32 devices in a mesh: blk: 4 (over z), lat: 4 (over y, x), depth: 2 (over core).
Axes of the slice: x: 2, y: 2, z: 4, core: 2. Of those that a mesh axis runs over, the one named last changes fastest.
Arguments:
- face_len: int32 [4, 4, 2, 6], P('blk', 'lat', 'depth'), may hold values from 0 to 128, as said below
- residual: float32 [4, 4, 2, 768, 512], P('blk', 'lat', 'depth'), as said below
- prev_direction: float32 [4, 4, 2, 768, 512], P('blk', 'lat', 'depth'), as said below
- prev_rho: float32 [512], replicated, may hold values from 0.5 to 4
- schur: float32 [4, 4, 2, 768, 768], P('blk', 'lat', 'depth'), as said below
- neumann: float32 [4, 4, 2, 768, 768], P('blk', 'lat', 'depth'), as said below
- coarse_basis: float32 [4, 4, 2, 768, 256], P('blk', 'lat', 'depth'), may hold values from -0.21875 to 0.21875
- coarse_inverse: float32 [4, 4, 2, 256, 256], P('blk', 'lat', 'depth'), as said below
- prim_owner: int32 [4, 4, 2, 256, 1], P('blk', 'lat', 'depth'), may hold values from 0 to 15; in each aligned block of 256 rows (0 to 255, 256 to 511, ..., all dimensions but the last counted through in order) at most 24 rows name the same one
- coarse_row: int32 [4, 4, 2, 256], P('blk', 'lat', 'depth'), may hold values from 0 to 255
Outputs:
- new_residual: float32 [4, 4, 2, 768, 512], P('blk', 'lat', 'depth')
- direction: float32 [4, 4, 2, 768, 512], P('blk', 'lat', 'depth')
- rho_now: float32 [512], replicated
- step_alpha: float32 [512], replicated
- res_norm: float32 [512], replicated
The draws below stay inside these ranges and needn't reach their ends.
Inputs may be any that keep to these rules, and one draw needn't show every extreme that they name: `face_len`: two subdomains that share a face have equal lengths on it; faces on the outer ends of lat and depth have length 0. `residual`: the two copies of a shared interface row are equal, and rows past a face's length are zero. `prev_direction`: the two copies of a shared interface row are equal, and rows past a face's length are zero. `schur`: each matrix has a positive definite symmetric part. `neumann`: each matrix has a positive definite symmetric part. `coarse_inverse`: each matrix has a positive definite symmetric part. `prim_owner`: at most 24 primal dofs of one subdomain have the same owner.
All inputs are finite; a program needn't handle non-finite values.
Results may differ from the reference program's by a relative error of at most 0.00005.
Values sent between devices are 32-bit elements; how exact they have to be, the bound alone decides.
No kernel may reach another device: no remote copies, remote signals or barrier semaphores. Data moves between devices by JAX's collectives and lax.ppermute only.
A program may use at most 64 MiB of HBM per device.

```python
import math
import jax
import jax.numpy as jnp
import numpy as np
from jax import lax

F = 128
NB = 768
NR = 512
NC = 256
CO = 256
CAP = 24
N_BLK = 4
N_LAT = 4
N_DEPTH = 2


def face_lengths(base_key):
    seed_key = jax.random.fold_in(base_key, 7)
    key_list = jax.random.split(seed_key, 3)
    full_shape = (N_BLK, N_LAT, N_DEPTH)
    pair_list = []
    for number in range(3):
        drawn_len = F - jax.random.randint(key_list[number], full_shape, 0, F // 2 + 1)
        pair_list.append(drawn_len.astype(jnp.int32))
    cycle_pairs = pair_list[0].at[0, 0, 0].set(F)
    lateral_pairs = pair_list[1].at[:, N_LAT - 1, :].set(0)
    depth_pairs = pair_list[2].at[:, :, N_DEPTH - 1].set(0)
    face_list = [jnp.roll(cycle_pairs, 1, axis=0), cycle_pairs, jnp.roll(lateral_pairs, 1, axis=1), lateral_pairs, jnp.roll(depth_pairs, 1, axis=2), depth_pairs]
    return jnp.stack(face_list, axis=-1)


def shared_field(base_key, salt):
    lengths = face_lengths(base_key)
    seed_key = jax.random.fold_in(base_key, salt)
    key_list = jax.random.split(seed_key, 4)
    full_shape = (N_BLK, N_LAT, N_DEPTH, F, NR)
    position = (jnp.arange(N_BLK)[:, None, None] * (N_LAT * N_DEPTH) + jnp.arange(N_LAT)[None, :, None] * N_DEPTH + jnp.arange(N_DEPTH)[None, None, :]).astype(jnp.float32)
    ramp_scale = 1.0 + 2.0 * position / (N_BLK * N_LAT * N_DEPTH - 1)
    pair_list = []
    for number in range(3):
        raw_values = jax.random.normal(key_list[number], full_shape, jnp.float32)
        pair_list.append(raw_values * ramp_scale[:, :, :, None, None])
    cycle_pairs, lateral_pairs, depth_pairs = pair_list
    face_list = [jnp.roll(cycle_pairs, 1, axis=0), cycle_pairs, jnp.roll(lateral_pairs, 1, axis=1), lateral_pairs, jnp.roll(depth_pairs, 1, axis=2), depth_pairs]
    stacked = jnp.stack(face_list, axis=3)
    live_mask = (jnp.arange(F)[None, None, None, None, :] < lengths[..., None]).astype(jnp.float32)
    return (stacked * live_mask[..., None]).reshape(N_BLK, N_LAT, N_DEPTH, 6 * F, NR)


def dominant(seed_key, order_n):
    key_list = jax.random.split(seed_key, 3)
    leading = (N_BLK, N_LAT, N_DEPTH)
    row_index = jnp.arange(order_n)[:, None]
    col_index = jnp.arange(order_n)[None, :]
    dense_part = jax.random.uniform(key_list[0], leading + (order_n, order_n), jnp.float32, -1.0, 1.0) * (0.4 / order_n)
    band_part = jax.random.uniform(key_list[1], leading + (order_n, order_n), jnp.float32, -1.0, 1.0) * 0.25
    band_part = jnp.where(jnp.abs(row_index - col_index) == 1, band_part, 0.0)
    off_diag = jnp.where(row_index == col_index, 0.0, dense_part) + band_part
    diagonal_part = 1.0 + 0.5 * jax.random.uniform(key_list[2], leading + (order_n,), jnp.float32)
    matrix = off_diag + jnp.where(row_index == col_index, 1.0, 0.0) * diagonal_part[..., :, None]
    return matrix


def draw_face_len(key, part):
    return face_lengths(key)


def draw_residual(key, part):
    return shared_field(key, 21)


def draw_prev_direction(key, part):
    return shared_field(key, 22)


def draw_schur(key, part):
    return dominant(jax.random.fold_in(key, 31), 6 * F)


def draw_neumann(key, part):
    return dominant(jax.random.fold_in(key, 32), 6 * F)


def draw_coarse_inverse(key, part):
    return dominant(jax.random.fold_in(key, 33), CO)


def set_ends(values, stream_key, least, top_value):
    dims = values.shape
    place = [jax.random.randint(jax.random.fold_in(stream_key, axis), (), 0, dims[axis]) for axis in range(len(dims))]
    values = values.at[tuple(place)].set(least)
    longest = dims.index(max(dims))
    place[longest] = (place[longest] + 1) % dims[longest]
    return values.at[tuple(place)].set(top_value)


def steps_of(own_key, dims, pieces, low, top_value):
    loudness, own = 1.0, jax.random.fold_in(own_key, 6)
    for axis_at, blocks in pieces:
        heights = jnp.exp(jax.random.uniform(jax.random.fold_in(own, axis_at), (blocks,), jnp.float32, low / len(pieces), top_value / len(pieces)))
        loudness = loudness * jnp.repeat(heights, dims[axis_at] // blocks).reshape([-1 if axis == axis_at else 1 for axis in range(len(dims))])
    return loudness


def deal_out(stream_key, own, number, rows, amount, top, bound, slope):
    sequence = jax.random.permutation(stream_key, amount)
    heavy_load, common = load_shares(amount, rows * top, bound, slope, True), load_shares(amount, rows * top, bound, slope, False)
    places = jnp.arange(amount)

    def named(sizes, offset_by):
        used = int((sizes > 0).sum())
        fixed = max(1, used // 4)
        moved = fixed + (places - fixed + offset_by * (used - fixed)) % max(1, amount - fixed)
        return jnp.zeros((amount,), jnp.int32).at[sequence[jnp.where(places < fixed, places, moved)]].set(jnp.asarray(sizes, jnp.int32))

    sizes = jnp.where(number % 4 == 0, named(heavy_load, number // 4), named(common, number - number // 4 - 1))
    mixed = jax.random.permutation(jax.random.fold_in(own, 3), amount)
    source_of, receiver = mixed[0:amount // 2 * 2:2], mixed[1:amount // 2 * 2:2]
    room = jnp.minimum(sizes[source_of] - 1, bound - sizes[receiver]) // 2
    room = jnp.where((source_of == sequence[0]) | (receiver == sequence[0]) | (sizes[receiver] == 0), 0, jnp.maximum(room, 0))
    moved = jax.random.randint(jax.random.fold_in(own, 4), (amount // 2,), 0, 1 << 20) % (room + 1)
    sizes = sizes.at[source_of].add(-moved).at[receiver].add(moved)
    labels = jnp.searchsorted(jnp.cumsum(sizes), jnp.arange(rows * top), side="right").astype(jnp.int32)
    grid = labels.reshape(top, rows).T
    grid = grid[jax.random.permutation(jax.random.fold_in(own, 1), rows)]
    offset_by = jax.random.randint(jax.random.fold_in(own, 2), (rows, 1), 0, top)
    return jnp.take_along_axis(grid, (jnp.arange(top)[None, :] + offset_by) % top, axis=1)


def load_shares(count, total, limit, slope, full):
    portions = [(1 << 20) // math.isqrt(standing ** slope) + 1 for standing in range(1, count + 1)]
    largest = limit if full else min(limit, max(-(-total // count), total * portions[0] // sum(portions)))
    least = 1 if total - largest >= count - 1 else 0
    given, spare = [largest] + [least] * (count - 1), total - largest - least * (count - 1)
    while spare > 0:
        free = [i for i in range(1, count) if given[i] < largest] or [i for i in range(1, count) if given[i] < limit]
        pool, budget = sum([portions[i] for i in free]), spare
        for i in free:
            more = min(limit - given[i], max(1, budget * portions[i] // pool), spare)
            given[i] = given[i] + more
            spare = spare - more
    return np.array(given)


def normal_values(own_key, dims, width, reach, pieces=(), kind=jnp.bfloat16):
    drawn = jax.random.normal(own_key, dims, jnp.float32) * width
    if len(pieces) > 0:
        drawn = steps_of(own_key, dims, pieces, -0.22, 0.18) * drawn
    return jnp.clip(drawn, min=-reach, max=reach).astype(kind)


def setup_inputs(seed: int = 0) -> dict:
    arg_keys = jax.random.split(jax.random.key(seed), 11)
    face_len = draw_face_len(jax.random.fold_in(arg_keys[10], 71), 0)
    residual = draw_residual(jax.random.fold_in(arg_keys[10], 71), 0)
    prev_direction = draw_prev_direction(jax.random.fold_in(arg_keys[10], 71), 0)
    prev_rho = jnp.clip(jnp.exp(jax.random.uniform(arg_keys[3], (NR,), jnp.float32, math.log(0.5), math.log(4.0))), 0.5, 4.0)
    schur = draw_schur(jax.random.fold_in(arg_keys[10], 71), 0)
    neumann = draw_neumann(jax.random.fold_in(arg_keys[10], 71), 0)
    coarse_basis = normal_values(arg_keys[6], (N_BLK, N_LAT, N_DEPTH, NB, NC), NB ** -0.5, 0.21875, ((0, 4), (1, 4), (2, 2)), jnp.float32)
    coarse_inverse = draw_coarse_inverse(jax.random.fold_in(arg_keys[10], 71), 0)
    prim_owner_keys = jax.random.split(jax.random.fold_in(arg_keys[8], 1), N_BLK * N_LAT * N_DEPTH * NC // NC)
    prim_owner_turns = jax.random.permutation(jax.random.fold_in(arg_keys[8], 3), N_BLK * N_LAT * N_DEPTH * NC // NC)
    prim_owner = jax.vmap(lambda own, number: deal_out(jax.random.fold_in(arg_keys[8], 2), own, number, NC, N_BLK * N_LAT, 1, CAP, 1))(prim_owner_keys, prim_owner_turns).reshape((N_BLK, N_LAT, N_DEPTH, NC, 1))
    coarse_row = set_ends(jax.random.randint(arg_keys[9], (N_BLK, N_LAT, N_DEPTH, NC), 0, CO), jax.random.fold_in(arg_keys[9], 1), 0, CO - 1).astype(jnp.int32)
    return dict(face_len=face_len, residual=residual, prev_direction=prev_direction, prev_rho=prev_rho, schur=schur, neumann=neumann, coarse_basis=coarse_basis, coarse_inverse=coarse_inverse, prim_owner=prim_owner, coarse_row=coarse_row)


exact_mode = lax.Precision.HIGHEST


def live_rows(face_len):
    positions = jnp.arange(F, dtype=jnp.int32)
    live_mask = (positions[None, None, None, None, :] < face_len[..., None]).astype(jnp.float32)
    return live_mask.reshape(N_BLK, N_LAT, N_DEPTH, 6 * F, 1)


def across(vector):
    face_list = vector.reshape(N_BLK, N_LAT, N_DEPTH, 6, F, -1)
    empty_lat = jnp.zeros_like(face_list[:, :1, :, 0])
    empty_dep = jnp.zeros_like(face_list[:, :, :1, 0])
    received = [jnp.roll(face_list[:, :, :, 1], 1, axis=0),
                jnp.roll(face_list[:, :, :, 0], -1, axis=0),
                jnp.concatenate([empty_lat, face_list[:, :-1, :, 3]], axis=1),
                jnp.concatenate([face_list[:, 1:, :, 2], empty_lat], axis=1),
                jnp.concatenate([empty_dep, face_list[:, :, :-1, 5]], axis=2),
                jnp.concatenate([face_list[:, :, 1:, 4], empty_dep], axis=2)]
    return jnp.stack(received, axis=3).reshape(vector.shape)


def batched(matrices, vectors):
    return jnp.einsum("abcnm,abcmr->abcnr", matrices, vectors, precision=exact_mode)


def reference(face_len, residual, prev_direction, prev_rho, schur, neumann, coarse_basis, coarse_inverse, prim_owner, coarse_row):
    live_mask = live_rows(face_len)
    residual_live = live_mask * residual
    weighted = 0.5 * residual_live
    local_part = batched(neumann, weighted)
    coarse_terms = jnp.einsum("abcnk,abcnr->abckr", coarse_basis, weighted, precision=exact_mode)
    owners = N_BLK * N_LAT
    depth_of = jnp.broadcast_to(jnp.arange(N_DEPTH, dtype=jnp.int32)[None, None, :, None], (N_BLK, N_LAT, N_DEPTH, NC))
    slot_ids = ((depth_of * owners + prim_owner[..., 0]) * CO + coarse_row).astype(jnp.int32).reshape(-1)
    coarse_sum = jax.ops.segment_sum(coarse_terms.reshape(-1, NR), slot_ids, num_segments=N_DEPTH * owners * CO)
    blocks = coarse_sum.reshape(N_DEPTH, owners, CO, NR)
    inverse = jnp.transpose(coarse_inverse, (2, 0, 1, 3, 4)).reshape(N_DEPTH, owners, CO, CO)
    solved = jnp.einsum("dopq,doqr->dopr", inverse, blocks, precision=exact_mode).reshape(-1, NR)
    correction = jnp.take(solved, slot_ids, axis=0).reshape(N_BLK, N_LAT, N_DEPTH, NC, NR)
    precond_image = local_part + jnp.einsum("abcnk,abckr->abcnr", coarse_basis, correction, precision=exact_mode)
    precond = 0.5 * live_mask * (precond_image + across(precond_image))
    norm_scale = 0.5 / (N_BLK * N_LAT * N_DEPTH * 6 * F)
    rho_now = norm_scale * jnp.sum(residual_live * precond, axis=(0, 1, 2, 3))
    direction = precond + (rho_now / prev_rho) * (live_mask * prev_direction)
    schur_image = batched(schur, direction)
    applied = live_mask * (schur_image + across(schur_image))
    curvature_value = norm_scale * jnp.sum(direction * applied, axis=(0, 1, 2, 3))
    step_alpha = rho_now / curvature_value
    new_residual = residual_live - step_alpha * applied
    res_norm = norm_scale * jnp.sum(new_residual * new_residual, axis=(0, 1, 2, 3))
    return (new_residual, direction, rho_now, step_alpha, res_norm)
```

```python
import functools

import jax
import jax.numpy as jnp
from jax import lax
from jax.experimental import pallas as pl
from jax.experimental.pallas import tpu as pltpu
from jax.sharding import PartitionSpec as P

CAP = 24
AXES = ("blk", "lat", "depth")
LAYER = ("blk", "lat")
LANES = 128
f32 = jnp.float32
bf16 = jnp.bfloat16

VMEM = pl.BlockSpec(memory_space=pltpu.VMEM)
SMEM = pl.BlockSpec(memory_space=pltpu.SMEM)


def shape_of(*dims, dtype=f32):
    return jax.ShapeDtypeStruct(dims, dtype)


def call(body, out_shape, operands, smem=(), flops=0, moved=0, scratch=()):
    in_specs = [SMEM if i in smem else VMEM for i in range(len(operands))]
    outs = list(out_shape)
    return pl.pallas_call(
        body,
        out_shape=outs,
        in_specs=in_specs,
        out_specs=[VMEM] * len(outs),
        scratch_shapes=list(scratch),
        compiler_params=pltpu.CompilerParams(vmem_limit_bytes=32 << 20),
        cost_estimate=pl.CostEstimate(flops=flops, bytes_accessed=moved, transcendentals=0),
    )(*operands)


def parts(x):
    high = x.astype(bf16)
    low = (x - high.astype(f32)).astype(bf16)
    return high, low


def mul(a, b, dims):
    return lax.dot_general(a, b, (dims, ((), ())), preferred_element_type=f32)


PLAIN = ((1,), (0,))
LEFT_T = ((0,), (0,))


def product(a, b, dims=PLAIN):
    ah, al = parts(a)
    bh, bl = parts(b)
    return mul(ah, bh, dims) + (mul(ah, bl, dims) + mul(al, bh, dims))


def select(table, x, dims=PLAIN):
    high, low = parts(x)
    return mul(table, high, dims) + mul(table, low, dims)


def live_rows(len_ref, face, rows):
    return lax.broadcasted_iota(jnp.int32, (rows, 1), 0) < len_ref[face]


def masked(len_ref, ref, face, rows):
    block = ref[face * rows : (face + 1) * rows, :]
    return jnp.where(live_rows(len_ref, face, rows), block, 0.0)


def spread(out_ref, vector):
    for j in range(out_ref.shape[1]):
        piece = vector[:, j * LANES : (j + 1) * LANES]
        out_ref[:, j, :] = jnp.broadcast_to(piece, (out_ref.shape[0], LANES))


def gathered_sum(ref):
    total = jnp.sum(ref[...], axis=0)
    return jnp.concatenate([total[j : j + 1, :] for j in range(total.shape[0])], axis=1)


def one_hot(hit):
    return jnp.where(hit, 1.0, 0.0).astype(bf16)


def pack_kernel(len_ref, residual_ref, basis_ref, owner_ref, out_ref, table_ref):
    rows = residual_ref.shape[0] // 6
    primal = basis_ref.shape[1]
    slots = out_ref.shape[0]
    weighted = jnp.concatenate(
        [0.5 * masked(len_ref, residual_ref, face, rows) for face in range(6)], axis=0
    )
    terms = product(basis_ref[...], weighted, LEFT_T)
    row_at = lax.broadcasted_iota(jnp.int32, (primal, primal), 0)
    col_at = lax.broadcasted_iota(jnp.int32, (primal, primal), 1)
    own_row = owner_ref[...].astype(f32)
    own_col = jnp.sum(jnp.where(row_at == col_at, own_row, 0.0), axis=1, keepdims=True)
    same = own_row == own_col
    rank_row = jnp.sum(jnp.where(same & (row_at < col_at), 1.0, 0.0), axis=0, keepdims=True)
    rank_col = jnp.sum(jnp.where(same & (col_at < row_at), 1.0, 0.0), axis=1, keepdims=True)
    slot_row = (own_row * CAP + rank_row).astype(jnp.int32)
    slot_col = (own_col * CAP + rank_col).astype(jnp.int32)
    packer = one_hot(lax.broadcasted_iota(jnp.int32, (slots, primal), 0) == slot_row)
    table_ref[...] = one_hot(lax.broadcasted_iota(jnp.int32, (primal, slots), 1) == slot_col)
    out_ref[...] = select(packer, terms)


def neumann_kernel(len_ref, residual_ref, matrix_ref, local_ref, part_ref):
    rows = residual_ref.shape[0] // 6
    live = jnp.concatenate(
        [masked(len_ref, residual_ref, face, rows) for face in range(6)], axis=0
    )
    local = product(matrix_ref[...], 0.5 * live)
    local_ref[...] = local
    part_ref[...] = jnp.sum(live * local, axis=0, keepdims=True)


def table_kernel(owner_ref, row_ref, picker_ref):
    owners, primal = owner_ref.shape
    owned = picker_ref.shape[1]
    me = lax.axis_index(LAYER)
    mine = jnp.where(owner_ref[...] == me, 1.0, 0.0)
    row_at = lax.broadcasted_iota(jnp.int32, (primal, primal), 0)
    col_at = lax.broadcasted_iota(jnp.int32, (primal, primal), 1)
    rank = mul(mine.astype(bf16), one_hot(row_at < col_at), PLAIN)
    rank = jnp.where(mine > 0.0, rank, -1.0).astype(jnp.int32)
    wanted = row_ref[...].astype(f32) + 1.0
    slot_at = lax.broadcasted_iota(jnp.int32, (CAP, primal), 0)
    out_at = lax.broadcasted_iota(jnp.int32, (CAP, owned), 1).astype(f32)
    for source in range(owners):
        hit = slot_at == rank[source : source + 1, :]
        named = jnp.sum(jnp.where(hit, wanted[source : source + 1, :], 0.0), axis=1, keepdims=True)
        picker_ref[source * CAP : (source + 1) * CAP, :] = jnp.where(
            out_at == named - 1.0, 1.0, 0.0
        )


def solve_kernel(incoming_ref, picker_ref, inverse_ref, part_ref, answer_ref, spread_ref):
    picker = picker_ref[...].astype(bf16)
    summed = select(picker, incoming_ref[...], LEFT_T)
    solved = product(inverse_ref[...], summed)
    answer_ref[...] = select(picker, solved)
    spread(spread_ref, part_ref[...] + 2.0 * jnp.sum(summed * solved, axis=0, keepdims=True))


def put_faces(image, rows, pair_depth, face_refs):
    for face in range(4):
        face_refs[face][...] = image[face * rows : (face + 1) * rows, :]
    minus, plus = image[4 * rows : 5 * rows, :], image[5 * rows :, :]
    if pair_depth:
        face_refs[4][...] = jnp.where(lax.axis_index("depth") == 0, plus, minus)
    else:
        face_refs[4][...] = minus
        face_refs[5][...] = plus


def got_face(refs, face, pair_depth):
    if face < 4 or not pair_depth:
        return refs[face][...]
    there = 1 if face == 4 else 0
    return jnp.where(lax.axis_index("depth") == there, refs[4][...], 0.0)


def image_kernel(pair_depth, returned_ref, table_ref, basis_ref, local_ref, image_ref, *face_refs):
    rows = local_ref.shape[0] // 6
    correction = select(table_ref[...], returned_ref[...])
    image = local_ref[...] + product(basis_ref[...], correction)
    image_ref[...] = image
    put_faces(image, rows, pair_depth, face_refs)


def direction_kernel(pair_depth, faces, scale, len_ref, rho_ref, prev_rho_ref, image_ref, prev_ref, schur_ref, *refs):
    got, (direction_ref, spread_ref, rho_out, schur_out), face_refs = (
        refs[:faces],
        refs[faces : faces + 4],
        refs[faces + 4 :],
    )
    rows = image_ref.shape[0] // 6
    rho = scale * gathered_sum(rho_ref)
    rho_out[...] = rho
    beta = rho / prev_rho_ref[...]
    for face in range(6):
        at = slice(face * rows, (face + 1) * rows)
        precond = 0.5 * (image_ref[at, :] + got_face(got, face, pair_depth))
        direction_ref[at, :] = jnp.where(
            live_rows(len_ref, face, rows), precond + beta * prev_ref[at, :], 0.0
        )
    direction = direction_ref[...]
    image = product(schur_ref[...], direction)
    schur_out[...] = image
    put_faces(image, rows, pair_depth, face_refs)
    spread(spread_ref, 2.0 * jnp.sum(direction * image, axis=0, keepdims=True))


def residual_kernel(pair_depth, faces, scale, len_ref, rho_ref, curve_ref, schur_ref, residual_ref, *refs):
    got, (new_ref, spread_ref, alpha_ref) = refs[:faces], refs[faces:]
    rows = schur_ref.shape[0] // 6
    alpha = rho_ref[...] / (scale * gathered_sum(curve_ref))
    alpha_ref[...] = alpha
    total = jnp.zeros(alpha.shape, f32)
    for face in range(6):
        at = slice(face * rows, (face + 1) * rows)
        applied = schur_ref[at, :] + got_face(got, face, pair_depth)
        new = jnp.where(live_rows(len_ref, face, rows), residual_ref[at, :] - alpha * applied, 0.0)
        new_ref[at, :] = new
        total += jnp.sum(new * new, axis=0, keepdims=True)
    spread(spread_ref, total)


def norm_kernel(scale, part_ref, norm_ref):
    norm_ref[...] = scale * gathered_sum(part_ref)


def around(x, axis, by):
    devices = lax.axis_size(axis)
    return lax.ppermute(x, axis, [(i, (i + by) % devices) for i in range(devices)])


def along(x, axis, by):
    devices = range(lax.axis_size(axis))
    return lax.ppermute(x, axis, [(i - by, i) for i in devices if i - by in devices])


def exchange(faces, pair_depth):
    got = [
        around(faces[1], "blk", 1),
        around(faces[0], "blk", -1),
        along(faces[3], "lat", 1),
        along(faces[2], "lat", -1),
    ]
    if pair_depth:
        got.append(lax.ppermute(faces[4], "depth", [(0, 1), (1, 0)]))
    else:
        got += [along(faces[5], "depth", 1), along(faces[4], "depth", -1)]
    return got


def to_all(x):
    return lax.all_to_all(x, AXES, split_axis=0, concat_axis=0, tiled=True)


def shards(
    face_len,
    residual,
    prev_direction,
    prev_rho,
    schur,
    neumann,
    coarse_basis,
    coarse_inverse,
    prim_owner,
    coarse_row,
):
    height, width = residual.shape[3:]
    rows = height // 6
    primal = coarse_basis.shape[4]
    owned = coarse_inverse.shape[3]
    owners = lax.axis_size(LAYER)
    slots = owners * CAP
    devices = lax.axis_size(AXES)
    pair_depth = lax.axis_size("depth") == 2
    faces = 5 if pair_depth else 6
    scale = 0.5 / (devices * height)

    lengths = face_len.reshape(6)
    residual = residual.reshape(height, width)
    prev_direction = prev_direction.reshape(height, width)
    schur = schur.reshape(height, height)
    neumann = neumann.reshape(height, height)
    basis = coarse_basis.reshape(height, primal)
    inverse = coarse_inverse.reshape(owned, owned)
    owner = prim_owner.reshape(1, primal)
    wanted = coarse_row.reshape(1, primal)
    whole = shape_of(height, width)
    row = shape_of(1, width)
    face = shape_of(rows, width)
    copies = shape_of(devices, width // LANES, LANES)

    outgoing, table = call(
        pack_kernel,
        [shape_of(slots, width), shape_of(primal, slots, dtype=bf16)],
        [lengths, residual, basis, owner],
        smem=(0,),
        flops=6 * height * primal * width,
        moved=4 * (height * (width + primal) + slots * width),
    )
    all_owner = lax.all_gather(owner, LAYER, axis=0, tiled=True)
    all_row = lax.all_gather(wanted, LAYER, axis=0, tiled=True)
    incoming = lax.all_to_all(
        outgoing.reshape(owners, CAP, width), LAYER, split_axis=0, concat_axis=0, tiled=True
    )
    local, local_part = call(
        neumann_kernel,
        [whole, row],
        [lengths, residual, neumann],
        smem=(0,),
        flops=6 * height * height * width,
        moved=4 * height * (height + 2 * width),
    )
    (picker,) = call(
        table_kernel,
        [shape_of(slots, owned)],
        [all_owner, all_row],
        flops=2 * owners * primal * primal,
        moved=4 * slots * owned,
    )
    answers, rho_parts = call(
        solve_kernel,
        [shape_of(slots, width), copies],
        [incoming.reshape(slots, width), picker, inverse, local_part],
        flops=(8 * slots + 6 * owned) * owned * width,
        moved=8 * slots * width,
    )
    returned = lax.all_to_all(
        answers.reshape(owners, CAP, width), LAYER, split_axis=0, concat_axis=0, tiled=True
    )
    rho_parts = to_all(rho_parts)
    image, *outward = call(
        functools.partial(image_kernel, pair_depth),
        [whole] + [face] * faces,
        [returned.reshape(slots, width), table, basis, local],
        flops=(6 * height + 4 * slots) * primal * width,
        moved=16 * height * width,
    )
    got = exchange(outward, pair_depth)
    direction, curve_parts, rho, schur_image, *outward = call(
        functools.partial(direction_kernel, pair_depth, faces, scale),
        [whole, copies, row, whole] + [face] * faces,
        [lengths, rho_parts, prev_rho.reshape(1, width), image, prev_direction, schur, *got],
        smem=(0,),
        flops=6 * height * height * width,
        moved=4 * height * (height + 6 * width),
    )
    got = exchange(outward, pair_depth)
    curve_parts = to_all(curve_parts)
    new_residual, norm_parts, alpha = call(
        functools.partial(residual_kernel, pair_depth, faces, scale),
        [whole, copies, row],
        [lengths, rho, curve_parts, schur_image, residual, *got],
        smem=(0,),
        flops=6 * height * width,
        moved=16 * height * width,
    )
    (norm,) = call(
        functools.partial(norm_kernel, scale),
        [row],
        [to_all(norm_parts)],
        moved=4 * devices * width,
    )
    out_shape = (1, 1, 1, height, width)
    return (
        new_residual.reshape(out_shape),
        direction.reshape(out_shape),
        rho.reshape(width),
        alpha.reshape(width),
        norm.reshape(width),
    )


def solution(mesh):
    tall = P("blk", "lat", "depth", None, None)
    flat = P("blk", "lat", "depth", None)
    in_specs = (flat, tall, tall, P(), tall, tall, tall, tall, tall, flat)
    out_specs = (tall, tall, P(), P(), P())
    return jax.shard_map(shards, mesh=mesh, in_specs=in_specs, out_specs=out_specs, check_vma=False)
```

```python
import functools

import jax
import jax.numpy as jnp
from jax import lax
from jax.experimental import pallas as pl
from jax.experimental.pallas import tpu as pltpu
from jax.sharding import PartitionSpec as P

CAP = 24
PARTS = 2
AXES = ("blk", "lat", "depth")
LAYER = ("blk", "lat")
LANES = 128
TILE = 8
f32 = jnp.float32
bf16 = jnp.bfloat16

VMEM = pl.BlockSpec(memory_space=pltpu.VMEM)
SMEM = pl.BlockSpec(memory_space=pltpu.SMEM)
ANY = pl.BlockSpec(memory_space=pl.ANY)


def shape_of(*dims, dtype=f32):
    return jax.ShapeDtypeStruct(dims, dtype)


def call(body, outs, operands, smem=(), far=(), far_out=(), flops=0, moved=0, scratch=(), room=32):
    in_specs = [SMEM if i in smem else ANY if i in far else VMEM for i in range(len(operands))]
    out_specs = [ANY if i in far_out else VMEM for i in range(len(outs))]
    return pl.pallas_call(
        body,
        out_shape=list(outs),
        in_specs=in_specs,
        out_specs=out_specs,
        scratch_shapes=list(scratch),
        compiler_params=pltpu.CompilerParams(vmem_limit_bytes=room << 20),
        cost_estimate=pl.CostEstimate(flops=flops, bytes_accessed=moved, transcendentals=0),
    )(*operands)


def parts(x):
    high = x.astype(bf16)
    low = (x - high.astype(f32)).astype(bf16)
    return high, low


def mul(a, b, dims):
    return lax.dot_general(a, b, (dims, ((), ())), preferred_element_type=f32)


PLAIN = ((1,), (0,))
LEFT_T = ((0,), (0,))


def product(a, b, dims=PLAIN):
    ah, al = parts(a)
    bh, bl = parts(b)
    return mul(ah, bh, dims) + (mul(ah, bl, dims) + mul(al, bh, dims))


def select(table, x, dims=PLAIN):
    high, low = parts(x)
    return mul(table, high, dims) + mul(table, low, dims)


def one_hot(hit):
    return jnp.where(hit, 1.0, 0.0).astype(bf16)


def live_rows(len_ref, face, rows):
    return lax.broadcasted_iota(jnp.int32, (rows, 1), 0) < len_ref[face]


def masked(len_ref, ref, face, rows):
    block = ref[face * rows : (face + 1) * rows, :]
    return jnp.where(live_rows(len_ref, face, rows), block, 0.0)


def folded(vector):
    pieces = vector.shape[1] // LANES
    return [vector[:, j * LANES : (j + 1) * LANES] for j in range(pieces)]


def unfolded(block, first, pieces):
    return jnp.concatenate([block[first + j : first + j + 1, :] for j in range(pieces)], axis=1)


def tiles(rows):
    return -(-rows // TILE) * TILE


def put_slab(out_ref, block):
    owners = out_ref.shape[0]
    for j in range(block.shape[1] // LANES):
        piece = block[:, j * LANES : (j + 1) * LANES]
        out_ref[:, j * CAP : (j + 1) * CAP, :] = piece.reshape(owners, CAP, LANES)


def get_slab(ref, pieces):
    slots = ref.shape[0] * CAP
    return jnp.concatenate(
        [ref[:, j * CAP : (j + 1) * CAP, :].reshape(slots, LANES) for j in range(pieces)], axis=1
    )


def pack_kernel(count, len_any, owner_any, row_any, residual_any, basis_any, *refs):
    slab_refs, table_ref = refs[:count], refs[count]
    len_ref, owner_ref, row_ref, residual_ref, basis_ref, sems, small_sems = refs[count + 1 :]
    rows = residual_ref.shape[0] // 6
    primal = basis_ref.shape[1]
    owners = slab_refs[0].shape[0]
    slots = owners * CAP
    small = [
        pltpu.make_async_copy(src, dst, small_sems.at[i])
        for i, (src, dst) in enumerate(
            [(owner_any, owner_ref), (row_any, row_ref), (len_any, len_ref)]
        )
    ]
    large = []
    for pair in range(3):
        at = pl.ds(2 * pair * rows, 2 * rows)
        large.append(
            (
                pltpu.make_async_copy(residual_any.at[at], residual_ref.at[at], sems.at[pair, 0]),
                pltpu.make_async_copy(basis_any.at[at], basis_ref.at[at], sems.at[pair, 1]),
            )
        )
    for copy in small:
        copy.start()
    for pair in large:
        for copy in pair:
            copy.start()
    for copy in small:
        copy.wait()
    row_at = lax.broadcasted_iota(jnp.int32, (primal, primal), 0)
    col_at = lax.broadcasted_iota(jnp.int32, (primal, primal), 1)
    own_row = owner_ref[...].astype(f32)
    wanted_row = row_ref[...].astype(f32) + 1.0
    own_col = jnp.sum(jnp.where(row_at == col_at, own_row, 0.0), axis=1, keepdims=True)
    wanted_col = jnp.sum(jnp.where(row_at == col_at, wanted_row, 0.0), axis=1, keepdims=True)
    same = own_row == own_col
    rank_row = jnp.sum(jnp.where(same & (row_at < col_at), 1.0, 0.0), axis=0, keepdims=True)
    rank_col = jnp.sum(jnp.where(same & (col_at < row_at), 1.0, 0.0), axis=1, keepdims=True)
    slot_row = (own_row * CAP + rank_row).astype(jnp.int32)
    slot_col = (own_col * CAP + rank_col).astype(jnp.int32)
    packer = one_hot(lax.broadcasted_iota(jnp.int32, (slots, primal), 0) == slot_row)
    table_ref[...] = one_hot(lax.broadcasted_iota(jnp.int32, (primal, slots), 1) == slot_col)
    to_owner = one_hot(
        lax.broadcasted_iota(jnp.int32, (owners, primal), 0) == owner_ref[...]
    )
    lane_at = lax.broadcasted_iota(jnp.int32, (primal, LANES), 1)
    ranked = jnp.where(lane_at == rank_col.astype(jnp.int32), wanted_col, 0.0)
    names = select(to_owner, ranked)
    terms = None
    for pair in range(3):
        for copy in large[pair]:
            copy.wait()
        weighted = jnp.concatenate(
            [0.5 * masked(len_ref, residual_ref, 2 * pair + side, rows) for side in range(2)],
            axis=0,
        )
        term = product(basis_ref[2 * pair * rows : 2 * (pair + 1) * rows, :], weighted, LEFT_T)
        terms = term if terms is None else terms + term
    packed = select(packer, terms)
    width = packed.shape[1] // count
    for i in range(count):
        put_slab(slab_refs[i], packed[:, i * width : (i + 1) * width])
    tail = slab_refs[0].shape[1] - TILE
    slab_refs[0][:, tail:, :] = jnp.broadcast_to(
        names.reshape(owners, 1, LANES), (owners, TILE, LANES)
    )


def neumann_kernel(len_ref, residual_ref, matrix_ref, local_ref, part_ref, square_ref):
    rows = residual_ref.shape[0] // 6
    live = jnp.concatenate(
        [masked(len_ref, residual_ref, face, rows) for face in range(6)], axis=0
    )
    local = product(matrix_ref[...], 0.5 * live)
    local_ref[...] = local
    part_ref[...] = jnp.sum(live * local, axis=0, keepdims=True)
    square_ref[...] = jnp.sum(live * live, axis=0, keepdims=True)


def picker_table(slab_ref, owned):
    owners, height, _ = slab_ref.shape
    lane_at = lax.broadcasted_iota(jnp.int32, (CAP, LANES), 1)
    rank_at = lax.broadcasted_iota(jnp.int32, (CAP, LANES), 0)
    out_at = lax.broadcasted_iota(jnp.int32, (CAP, owned), 1).astype(f32) + 1.0
    blocks = []
    for source in range(owners):
        names = slab_ref[source, height - TILE : height - TILE + 1, :]
        named = jnp.sum(jnp.where(lane_at == rank_at, names, 0.0), axis=1, keepdims=True)
        blocks.append(jnp.where(out_at == named, 1.0, 0.0))
    return jnp.concatenate(blocks, axis=0)


def solve_kernel(index, count, *refs):
    incoming_ref, inverse_ref, refs = refs[0], refs[1], refs[2:]
    owned = inverse_ref.shape[0]
    if index > 0:
        picker_ref, refs = refs[0], refs[1:]
        picker = picker_ref[...]
    else:
        picker = picker_table(incoming_ref, owned)
    before, refs = refs[:index], refs[index:]
    last = index == count - 1
    if last:
        (local_part_ref, square_ref), refs = refs[:2], refs[2:]
    answer_ref, refs = refs[0], refs[1:]
    if index == 0 and not last:
        refs[-1][...] = picker
    table = picker.astype(bf16)
    pieces = (incoming_ref.shape[1] // CAP) if index else (incoming_ref.shape[1] - TILE) // CAP
    summed = select(table, get_slab(incoming_ref, pieces), LEFT_T)
    solved = product(inverse_ref[...], summed)
    put_slab(answer_ref, select(table, solved))
    mine = 2.0 * jnp.sum(summed * solved, axis=0, keepdims=True)
    if not last:
        refs[0][...] = mine
        return
    total = jnp.concatenate([ref[...] for ref in before] + [mine], axis=1) + local_part_ref[...]
    sums = folded(total) + folded(square_ref[...])
    sums += [jnp.zeros((1, LANES), f32)] * (tiles(len(sums)) - len(sums))
    owners = answer_ref.shape[0]
    start = pieces * CAP
    answer_ref[:, start:, :] = jnp.broadcast_to(
        jnp.concatenate(sums, axis=0)[None], (owners, len(sums), LANES)
    )


def put_faces(image, rows, pair_depth, face_refs):
    for face in range(4):
        face_refs[face][...] = image[face * rows : (face + 1) * rows, :]
    minus, plus = image[4 * rows : 5 * rows, :], image[5 * rows :, :]
    if pair_depth:
        face_refs[4][:rows, :] = jnp.where(lax.axis_index("depth") == 0, plus, minus)
    else:
        face_refs[4][...] = minus
        face_refs[5][...] = plus


def got_face(refs, face, rows, pair_depth):
    if face < 4 or not pair_depth:
        return refs[face][...]
    there = 1 if face == 4 else 0
    return jnp.where(lax.axis_index("depth") == there, refs[4][:rows, :], 0.0)


def image_kernel(pair_depth, count, *refs):
    returned, refs = refs[:count], refs[count:]
    (table_ref, basis_ref, local_ref, image_ref, sums_ref), face_refs = refs[:5], refs[5:]
    rows = local_ref.shape[0] // 6
    width = local_ref.shape[1]
    pieces = width // LANES // count
    terms = jnp.concatenate([get_slab(ref, pieces) for ref in returned], axis=1)
    correction = select(table_ref[...], terms)
    image = local_ref[...] + product(basis_ref[...], correction)
    image_ref[...] = image
    put_faces(image, rows, pair_depth, face_refs)
    tail = jnp.sum(returned[-1][:, pieces * CAP :, :], axis=0)
    if pair_depth:
        folds = width // LANES
        sums = jnp.concatenate(
            [unfolded(tail, 0, folds), unfolded(tail, folds, folds)]
            + [jnp.zeros((TILE - 2, width), f32)],
            axis=0,
        )
        sums_ref[...] = sums
        face_refs[4][rows:, :] = sums
    else:
        sums_ref[...] = jnp.broadcast_to(tail[None], sums_ref.shape)


def direction_kernel(pair_depth, faces, scale, len_ref, sums_ref, prev_rho_ref, image_ref, prev_ref, schur_ref, *refs):
    got, refs = refs[:faces], refs[faces:]
    (direction_out, rho_out, square_out, schur_out), refs = refs[:4], refs[4:]
    face_refs, (direction_ref, sem) = refs[:faces], refs[faces:]
    rows = image_ref.shape[0] // 6
    width = image_ref.shape[1]
    if pair_depth:
        sums = sums_ref[...] + got[4][rows:, :]
        rho, square = sums[0:1, :], sums[1:2, :]
    else:
        folds = width // LANES
        sums = jnp.sum(sums_ref[...], axis=0)
        rho, square = unfolded(sums, 0, folds), unfolded(sums, folds, folds)
    rho = scale * rho
    rho_out[...] = rho
    square_out[...] = square
    beta = rho / prev_rho_ref[...]
    for face in range(6):
        at = slice(face * rows, (face + 1) * rows)
        precond = 0.5 * (image_ref[at, :] + got_face(got, face, rows, pair_depth))
        direction_ref[at, :] = jnp.where(
            live_rows(len_ref, face, rows), precond + beta * prev_ref[at, :], 0.0
        )
    copy = pltpu.make_async_copy(direction_ref, direction_out, sem)
    copy.start()
    image = product(schur_ref[...], direction_ref[...])
    schur_out[...] = image
    put_faces(image, rows, pair_depth, face_refs)
    copy.wait()


def products_kernel(len_ref, direction_ref, schur_ref, residual_ref, curve_ref, cross_ref):
    rows = schur_ref.shape[0] // 6
    image = schur_ref[...]
    live = jnp.concatenate(
        [masked(len_ref, residual_ref, face, rows) for face in range(6)], axis=0
    )
    curve_ref[...] = 2.0 * jnp.sum(direction_ref[...] * image, axis=0, keepdims=True)
    cross_ref[...] = 2.0 * jnp.sum(live * image, axis=0, keepdims=True)


def applied_kernel(pair_depth, faces, len_ref, curve_ref, cross_ref, schur_ref, *refs):
    got, (applied_ref, spread_ref) = refs[:faces], refs[faces:]
    rows = schur_ref.shape[0] // 6
    total = jnp.zeros(curve_ref.shape, f32)
    for face in range(6):
        at = slice(face * rows, (face + 1) * rows)
        applied = schur_ref[at, :] + got_face(got, face, rows, pair_depth)
        applied = jnp.where(live_rows(len_ref, face, rows), applied, 0.0)
        applied_ref[at, :] = applied
        total += jnp.sum(applied * applied, axis=0, keepdims=True)
    for i, vector in enumerate([curve_ref[...], cross_ref[...], total]):
        for j, piece in enumerate(folded(vector)):
            spread_ref[:, i, j, :] = jnp.broadcast_to(piece, (spread_ref.shape[0], LANES))


def finish_kernel(scale, len_ref, sums_ref, rho_ref, square_ref, residual_ref, applied_ref, new_out, alpha_ref, norm_ref, new_ref, sems):
    rows = applied_ref.shape[0] // 6
    folds = sums_ref.shape[2]
    sums = jnp.sum(sums_ref[...], axis=0)
    curve, cross, square = [unfolded(sums[i], 0, folds) for i in range(3)]
    alpha = rho_ref[...] / (scale * curve)
    alpha_ref[...] = alpha
    norm_ref[...] = scale * (square_ref[...] - 2.0 * alpha * cross + alpha * alpha * square)
    copies = []
    for face in range(6):
        at = slice(face * rows, (face + 1) * rows)
        new_ref[at, :] = masked(len_ref, residual_ref, face, rows) - alpha * applied_ref[at, :]
        where = pl.ds(face * rows, rows)
        copies.append(pltpu.make_async_copy(new_ref.at[where], new_out.at[where], sems.at[face]))
        copies[-1].start()
    for copy in copies:
        copy.wait()


def around(x, axis, by):
    devices = lax.axis_size(axis)
    return lax.ppermute(x, axis, [(i, (i + by) % devices) for i in range(devices)])


def along(x, axis, by):
    devices = range(lax.axis_size(axis))
    return lax.ppermute(x, axis, [(i - by, i) for i in devices if i - by in devices])


def exchange(faces, pair_depth):
    got = [
        around(faces[1], "blk", 1),
        around(faces[0], "blk", -1),
        along(faces[3], "lat", 1),
        along(faces[2], "lat", -1),
    ]
    if pair_depth:
        got.append(lax.ppermute(faces[4], "depth", [(0, 1), (1, 0)]))
    else:
        got += [along(faces[5], "depth", 1), along(faces[4], "depth", -1)]
    return got


def to_all(x, axes):
    return lax.all_to_all(x, axes, split_axis=0, concat_axis=0, tiled=True)


def shards(
    face_len,
    residual,
    prev_direction,
    prev_rho,
    schur,
    neumann,
    coarse_basis,
    coarse_inverse,
    prim_owner,
    coarse_row,
):
    height, width = residual.shape[3:]
    rows = height // 6
    primal = coarse_basis.shape[4]
    owned = coarse_inverse.shape[3]
    owners = lax.axis_size(LAYER)
    slots = owners * CAP
    devices = lax.axis_size(AXES)
    layers = lax.axis_size("depth")
    pair_depth = layers == 2
    faces = 5 if pair_depth else 6
    scale = 0.5 / (devices * height)
    count = PARTS
    folds = width // LANES
    pieces = folds // count
    tail = tiles(2 * folds)

    lengths = face_len.reshape(6)
    residual = residual.reshape(height, width)
    prev_direction = prev_direction.reshape(height, width)
    schur = schur.reshape(height, height)
    neumann = neumann.reshape(height, height)
    basis = coarse_basis.reshape(height, primal)
    inverse = coarse_inverse.reshape(owned, owned)
    owner = prim_owner.reshape(1, primal)
    wanted = coarse_row.reshape(1, primal)
    whole = shape_of(height, width)
    row = shape_of(1, width)
    part_row = shape_of(1, width // count)
    face = shape_of(rows, width)

    *outgoing, table = call(
        functools.partial(pack_kernel, count),
        [
            shape_of(owners, pieces * CAP + (0 if i else TILE), LANES) for i in range(count)
        ]
        + [shape_of(primal, slots, dtype=bf16)],
        [lengths, owner, wanted, residual, basis],
        far=range(5),
        flops=6 * height * primal * width,
        moved=4 * (height * (width + primal) + slots * width),
        scratch=[
            pltpu.SMEM((6,), jnp.int32),
            pltpu.VMEM((1, primal), jnp.int32),
            pltpu.VMEM((1, primal), jnp.int32),
            pltpu.VMEM((height, width), f32),
            pltpu.VMEM((height, primal), f32),
            pltpu.SemaphoreType.DMA((3, 2)),
            pltpu.SemaphoreType.DMA((3,)),
        ],
        room=60,
    )
    incoming = [to_all(x, LAYER) for x in outgoing]
    local, local_part, square = call(
        neumann_kernel,
        [whole, row, row],
        [lengths, residual, neumann],
        smem=(0,),
        flops=6 * height * height * width,
        moved=4 * height * (height + 2 * width),
    )
    picker, before, returned = None, [], []
    for i in range(count):
        last = i == count - 1
        operands = [incoming[i], inverse] + ([picker] if i else []) + before
        outs = [shape_of(owners, pieces * CAP + (tail if last else 0), LANES)]
        if last:
            operands += [local_part, square]
        else:
            outs.append(part_row)
            if i == 0:
                outs.append(shape_of(slots, owned))
        got = call(
            functools.partial(solve_kernel, i, count),
            outs,
            operands,
            flops=(8 * slots + 6 * owned) * owned * width // count,
            moved=8 * slots * width // count,
        )
        returned.append(to_all(got[0], LAYER))
        if not last:
            before.append(got[1])
            if i == 0:
                picker = got[2]
    extra = TILE if pair_depth else 0
    image, sums, *outward = call(
        functools.partial(image_kernel, pair_depth, count),
        [whole, shape_of(TILE, width) if pair_depth else shape_of(layers, tail, LANES)]
        + [face] * 4
        + ([shape_of(rows + extra, width)] if pair_depth else [face] * 2),
        [*returned, table, basis, local],
        flops=(6 * height + 4 * slots) * primal * width,
        moved=16 * height * width,
    )
    if not pair_depth:
        sums = to_all(sums, "depth")
    got = exchange(outward, pair_depth)
    direction, rho, square, schur_image, *outward = call(
        functools.partial(direction_kernel, pair_depth, faces, scale),
        [whole, row, row, whole] + [face] * faces,
        [lengths, sums, prev_rho.reshape(1, width), image, prev_direction, schur, *got],
        smem=(0,),
        far_out=(0,),
        flops=6 * height * height * width,
        moved=4 * height * (height + 6 * width),
        scratch=[pltpu.VMEM((height, width), f32), pltpu.SemaphoreType.DMA],
    )
    got = exchange(outward, pair_depth)
    curve, cross = call(
        products_kernel,
        [row, row],
        [lengths, direction, schur_image, residual],
        smem=(0,),
        flops=4 * height * width,
        moved=12 * height * width,
    )
    applied, spread = call(
        functools.partial(applied_kernel, pair_depth, faces),
        [whole, shape_of(devices, 3, folds, LANES)],
        [lengths, curve, cross, schur_image, *got],
        smem=(0,),
        flops=4 * height * width,
        moved=12 * height * width,
    )
    new_residual, alpha, norm = call(
        functools.partial(finish_kernel, scale),
        [whole, row, row],
        [lengths, to_all(spread, AXES), rho, square, residual, applied],
        smem=(0,),
        far_out=(0,),
        flops=4 * height * width,
        moved=12 * height * width,
        scratch=[pltpu.VMEM((height, width), f32), pltpu.SemaphoreType.DMA((6,))],
    )
    out_shape = (1, 1, 1, height, width)
    return (
        new_residual.reshape(out_shape),
        direction.reshape(out_shape),
        rho.reshape(width),
        alpha.reshape(width),
        norm.reshape(width),
    )


def solution(mesh):
    tall = P("blk", "lat", "depth", None, None)
    flat = P("blk", "lat", "depth", None)
    in_specs = (flat, tall, tall, P(), tall, tall, tall, tall, tall, flat)
    out_specs = (tall, tall, P(), P(), P())
    return jax.shard_map(shards, mesh=mesh, in_specs=in_specs, out_specs=out_specs, check_vma=False)
```

```python
import functools

import jax
import jax.numpy as jnp
from jax import lax
from jax.experimental import pallas as pl
from jax.experimental.pallas import tpu as pltpu
from jax.sharding import PartitionSpec as P

CAP = 24
AXES = ("blk", "lat", "depth")
LAYER = ("blk", "lat")
LANES = 128
TILE = 8
f32 = jnp.float32
bf16 = jnp.bfloat16

VMEM = pl.BlockSpec(memory_space=pltpu.VMEM)
SMEM = pl.BlockSpec(memory_space=pltpu.SMEM)
ANY = pl.BlockSpec(memory_space=pl.ANY)


def shape_of(*dims, dtype=f32):
    return jax.ShapeDtypeStruct(dims, dtype)


def call(body, outs, operands, smem=(), far=(), far_out=(), flops=0, moved=0, scratch=(), room=32):
    in_specs = [SMEM if i in smem else ANY if i in far else VMEM for i in range(len(operands))]
    out_specs = [ANY if i in far_out else VMEM for i in range(len(outs))]
    return pl.pallas_call(
        body,
        out_shape=list(outs),
        in_specs=in_specs,
        out_specs=out_specs,
        scratch_shapes=list(scratch),
        compiler_params=pltpu.CompilerParams(vmem_limit_bytes=room << 20),
        cost_estimate=pl.CostEstimate(flops=flops, bytes_accessed=moved, transcendentals=0),
    )(*operands)


def parts(x):
    high = x.astype(bf16)
    low = (x - high.astype(f32)).astype(bf16)
    return high, low


def mul(a, b, dims):
    return lax.dot_general(a, b, (dims, ((), ())), preferred_element_type=f32)


PLAIN = ((1,), (0,))
LEFT_T = ((0,), (0,))


def product(a, b, dims=PLAIN):
    (ah, al), (bh, bl) = a, b
    return mul(ah, bh, dims) + (mul(ah, bl, dims) + mul(al, bh, dims))


def select(table, x, dims=PLAIN):
    high, low = parts(x)
    return mul(table, high, dims) + mul(table, low, dims)


def one_hot(hit):
    return jnp.where(hit, 1.0, 0.0).astype(bf16)


def live_rows(len_ref, face, rows):
    return lax.broadcasted_iota(jnp.int32, (rows, 1), 0) < len_ref[face]


def masked(len_ref, ref, face, rows):
    block = ref[face * rows : (face + 1) * rows, :]
    return jnp.where(live_rows(len_ref, face, rows), block, 0.0)


def folded(vector):
    pieces = vector.shape[1] // LANES
    return [vector[:, j * LANES : (j + 1) * LANES] for j in range(pieces)]


def unfolded(block, first, pieces):
    return jnp.concatenate([block[first + j : first + j + 1, :] for j in range(pieces)], axis=1)


def tiles(rows):
    return -(-rows // TILE) * TILE


def put_slab(out_ref, block):
    owners = out_ref.shape[0]
    for j in range(block.shape[1] // LANES):
        piece = block[:, j * LANES : (j + 1) * LANES]
        out_ref[:, j * CAP : (j + 1) * CAP, :] = piece.reshape(owners, CAP, LANES)


def get_slab(ref, pieces):
    slots = ref.shape[0] * CAP
    return jnp.concatenate(
        [ref[:, j * CAP : (j + 1) * CAP, :].reshape(slots, LANES) for j in range(pieces)], axis=1
    )


def pack_kernel(len_any, owner_any, row_any, residual_any, basis_any, slab_ref, *refs):
    len_ref, owner_ref, row_ref, residual_ref, basis_ref, sems, small_sems = refs
    rows = residual_ref.shape[0] // 6
    primal = basis_ref.shape[1]
    owners = slab_ref.shape[0]
    slots = owners * CAP
    small = [
        pltpu.make_async_copy(src, dst, small_sems.at[i])
        for i, (src, dst) in enumerate(
            [(owner_any, owner_ref), (row_any, row_ref), (len_any, len_ref)]
        )
    ]
    large = []
    for pair in range(3):
        at = pl.ds(2 * pair * rows, 2 * rows)
        large.append(
            (
                pltpu.make_async_copy(residual_any.at[at], residual_ref.at[at], sems.at[pair, 0]),
                pltpu.make_async_copy(basis_any.at[at], basis_ref.at[at], sems.at[pair, 1]),
            )
        )
    for copy in small:
        copy.start()
    for pair in large:
        for copy in pair:
            copy.start()
    for copy in small:
        copy.wait()
    row_at = lax.broadcasted_iota(jnp.int32, (primal, primal), 0)
    col_at = lax.broadcasted_iota(jnp.int32, (primal, primal), 1)
    own_row = owner_ref[...].astype(f32)
    wanted_row = row_ref[...].astype(f32) + 1.0
    own_col = jnp.sum(jnp.where(row_at == col_at, own_row, 0.0), axis=1, keepdims=True)
    wanted_col = jnp.sum(jnp.where(row_at == col_at, wanted_row, 0.0), axis=1, keepdims=True)
    same = own_row == own_col
    rank_row = jnp.sum(jnp.where(same & (row_at < col_at), 1.0, 0.0), axis=0, keepdims=True)
    rank_col = jnp.sum(jnp.where(same & (col_at < row_at), 1.0, 0.0), axis=1, keepdims=True)
    slot_row = (own_row * CAP + rank_row).astype(jnp.int32)
    packer = one_hot(lax.broadcasted_iota(jnp.int32, (slots, primal), 0) == slot_row)
    to_owner = one_hot(lax.broadcasted_iota(jnp.int32, (owners, primal), 0) == owner_ref[...])
    lane_at = lax.broadcasted_iota(jnp.int32, (primal, LANES), 1)
    ranked = jnp.where(lane_at == rank_col.astype(jnp.int32), wanted_col, 0.0)
    names = select(to_owner, ranked)
    terms = None
    for pair in range(3):
        for copy in large[pair]:
            copy.wait()
        weighted = jnp.concatenate(
            [0.5 * masked(len_ref, residual_ref, 2 * pair + side, rows) for side in range(2)],
            axis=0,
        )
        basis = basis_ref[2 * pair * rows : 2 * (pair + 1) * rows, :]
        term = product(parts(basis), parts(weighted), LEFT_T)
        terms = term if terms is None else terms + term
    put_slab(slab_ref, select(packer, terms))
    tail = slab_ref.shape[1] - TILE
    slab_ref[:, tail:, :] = jnp.broadcast_to(
        names.reshape(owners, 1, LANES), (owners, TILE, LANES)
    )


def local_kernel(len_ref, residual_ref, matrix_ref, owner_ref, *refs):
    whole, refs = refs[:3], refs[3:]
    local_ref, part_ref, square_ref, table_ref, refs = *refs[:4], refs[4:]
    rows = residual_ref.shape[0] // 6
    live = jnp.concatenate(
        [masked(len_ref, residual_ref, face, rows) for face in range(6)], axis=0
    )
    local = product(parts(matrix_ref[...]), parts(0.5 * live))
    local_ref[...] = local
    part_ref[...] = jnp.sum(live * local, axis=0, keepdims=True)
    square_ref[...] = jnp.sum(live * live, axis=0, keepdims=True)
    for i in range(3):
        refs[2 * i][...], refs[2 * i + 1][...] = parts(whole[i][...])
    primal, slots = table_ref.shape
    row_at = lax.broadcasted_iota(jnp.int32, (primal, primal), 0)
    col_at = lax.broadcasted_iota(jnp.int32, (primal, primal), 1)
    own_row = owner_ref[...].astype(f32)
    own_col = jnp.sum(jnp.where(row_at == col_at, own_row, 0.0), axis=1, keepdims=True)
    before = (own_row == own_col) & (col_at < row_at)
    rank_col = jnp.sum(jnp.where(before, 1.0, 0.0), axis=1, keepdims=True)
    slot_col = (own_col * CAP + rank_col).astype(jnp.int32)
    table_ref[...] = one_hot(lax.broadcasted_iota(jnp.int32, (primal, slots), 1) == slot_col)


def picker_table(slab_ref, owned):
    owners, height, _ = slab_ref.shape
    lane_at = lax.broadcasted_iota(jnp.int32, (CAP, LANES), 1)
    rank_at = lax.broadcasted_iota(jnp.int32, (CAP, LANES), 0)
    out_at = lax.broadcasted_iota(jnp.int32, (CAP, owned), 1).astype(f32) + 1.0
    blocks = []
    for source in range(owners):
        names = slab_ref[source, height - TILE : height - TILE + 1, :]
        named = jnp.sum(jnp.where(lane_at == rank_at, names, 0.0), axis=1, keepdims=True)
        blocks.append(jnp.where(out_at == named, 1.0, 0.0))
    return jnp.concatenate(blocks, axis=0)


def solve_kernel(incoming_ref, high_ref, low_ref, local_part_ref, square_ref, answer_ref):
    owners, height, _ = incoming_ref.shape
    pieces = (height - TILE) // CAP
    table = picker_table(incoming_ref, high_ref.shape[0]).astype(bf16)
    summed = select(table, get_slab(incoming_ref, pieces), LEFT_T)
    solved = product((high_ref[...], low_ref[...]), parts(summed))
    put_slab(answer_ref, select(table, solved))
    total = local_part_ref[...] + 2.0 * jnp.sum(summed * solved, axis=0, keepdims=True)
    sums = folded(total) + folded(square_ref[...])
    sums += [jnp.zeros((1, LANES), f32)] * (tiles(len(sums)) - len(sums))
    answer_ref[:, pieces * CAP :, :] = jnp.broadcast_to(
        jnp.concatenate(sums, axis=0)[None], (owners, len(sums), LANES)
    )


AXIS_AT = {"blk": 0, "lat": 2, "depth": 4}


def swaps():
    order = [("blk", 0), ("lat", 1), ("blk", 1), ("lat", 0), ("depth", 0), ("depth", 1)]
    return [(axis, odd) for axis, odd in order if pairs(axis, odd)]


def pairs(axis, odd):
    devices = lax.axis_size(axis)
    ends = [(i, i + 1) for i in range(odd, devices - 1, 2)]
    if axis == "blk" and odd:
        ends.append((devices - 1, 0))
    return [pair for i, j in ends for pair in ((i, j), (j, i))]


def sends_plus(axis, odd):
    return lax.rem(lax.axis_index(axis), 2) == odd


def put_faces(image, rows, face_refs):
    for ref, (axis, odd) in zip(face_refs, swaps(), strict=True):
        at = AXIS_AT[axis] * rows
        minus, plus = image[at : at + rows, :], image[at + rows : at + 2 * rows, :]
        ref[:rows, :] = jnp.where(sends_plus(axis, odd), plus, minus)


def got_face(refs, face, rows):
    axis = ("blk", "lat", "depth")[face // 2]
    total = None
    for ref, (axis_of, odd) in zip(refs, swaps(), strict=True):
        if axis_of == axis:
            mine = sends_plus(axis, odd) == (face % 2 == 1)
            piece = jnp.where(mine, ref[:rows, :], 0.0)
            total = piece if total is None else total + piece
    return total


def exchange(faces):
    return [
        lax.ppermute(block, axis, pairs(axis, odd))
        for block, (axis, odd) in zip(faces, swaps(), strict=True)
    ]


def image_kernel(pair_depth, returned_ref, table_ref, high_ref, low_ref, local_ref, image_ref, sums_ref, *face_refs):
    rows = local_ref.shape[0] // 6
    width = local_ref.shape[1]
    folds = width // LANES
    correction = select(table_ref[...], get_slab(returned_ref, folds))
    image = local_ref[...] + product((high_ref[...], low_ref[...]), parts(correction))
    image_ref[...] = image
    put_faces(image, rows, face_refs)
    tail = jnp.sum(returned_ref[:, folds * CAP :, :], axis=0)
    if pair_depth:
        sums = jnp.concatenate(
            [unfolded(tail, 0, folds), unfolded(tail, folds, folds)]
            + [jnp.zeros((TILE - 2, width), f32)],
            axis=0,
        )
        sums_ref[...] = sums
        face_refs[-1][rows:, :] = sums
    else:
        sums_ref[...] = jnp.broadcast_to(tail[None], sums_ref.shape)


def direction_kernel(pair_depth, scale, len_ref, sums_ref, prev_rho_ref, image_ref, prev_ref, high_ref, low_ref, *refs):
    faces = len(swaps())
    got, refs = refs[:faces], refs[faces:]
    (direction_out, rho_out, square_out, schur_out), refs = refs[:4], refs[4:]
    face_refs, (direction_ref, sem) = refs[:faces], refs[faces:]
    rows = image_ref.shape[0] // 6
    width = image_ref.shape[1]
    if pair_depth:
        sums = sums_ref[...] + got[-1][rows:, :]
        rho, square = sums[0:1, :], sums[1:2, :]
    else:
        folds = width // LANES
        sums = jnp.sum(sums_ref[...], axis=0)
        rho, square = unfolded(sums, 0, folds), unfolded(sums, folds, folds)
    rho = scale * rho
    rho_out[...] = rho
    square_out[...] = square
    beta = rho / prev_rho_ref[...]
    for face in range(6):
        at = slice(face * rows, (face + 1) * rows)
        precond = 0.5 * (image_ref[at, :] + got_face(got, face, rows))
        direction_ref[at, :] = jnp.where(
            live_rows(len_ref, face, rows), precond + beta * prev_ref[at, :], 0.0
        )
    copy = pltpu.make_async_copy(direction_ref, direction_out, sem)
    copy.start()
    image = product((high_ref[...], low_ref[...]), parts(direction_ref[...]))
    schur_out[...] = image
    put_faces(image, rows, face_refs)
    copy.wait()


def products_kernel(len_ref, direction_ref, schur_ref, residual_ref, curve_ref, cross_ref):
    rows = schur_ref.shape[0] // 6
    image = schur_ref[...]
    live = jnp.concatenate(
        [masked(len_ref, residual_ref, face, rows) for face in range(6)], axis=0
    )
    curve_ref[...] = 2.0 * jnp.sum(direction_ref[...] * image, axis=0, keepdims=True)
    cross_ref[...] = 2.0 * jnp.sum(live * image, axis=0, keepdims=True)


def applied_kernel(len_ref, curve_ref, cross_ref, schur_ref, *refs):
    got, (applied_ref, spread_ref) = refs[:-2], refs[-2:]
    rows = schur_ref.shape[0] // 6
    total = jnp.zeros(curve_ref.shape, f32)
    for face in range(6):
        at = slice(face * rows, (face + 1) * rows)
        applied = schur_ref[at, :] + got_face(got, face, rows)
        applied = jnp.where(live_rows(len_ref, face, rows), applied, 0.0)
        applied_ref[at, :] = applied
        total += jnp.sum(applied * applied, axis=0, keepdims=True)
    for i, vector in enumerate([curve_ref[...], cross_ref[...], total]):
        for j, piece in enumerate(folded(vector)):
            spread_ref[:, i, j, :] = jnp.broadcast_to(piece, (spread_ref.shape[0], LANES))


def finish_kernel(scale, len_ref, sums_ref, rho_ref, square_ref, residual_ref, applied_ref, new_out, alpha_ref, norm_ref, new_ref, sems):
    rows = applied_ref.shape[0] // 6
    folds = sums_ref.shape[2]
    sums = jnp.sum(sums_ref[...], axis=0)
    curve, cross, square = [unfolded(sums[i], 0, folds) for i in range(3)]
    alpha = rho_ref[...] / (scale * curve)
    alpha_ref[...] = alpha
    norm_ref[...] = scale * (square_ref[...] - 2.0 * alpha * cross + alpha * alpha * square)
    copies = []
    for face in range(6):
        at = slice(face * rows, (face + 1) * rows)
        new_ref[at, :] = masked(len_ref, residual_ref, face, rows) - alpha * applied_ref[at, :]
        where = pl.ds(face * rows, rows)
        copies.append(pltpu.make_async_copy(new_ref.at[where], new_out.at[where], sems.at[face]))
        copies[-1].start()
    for copy in copies:
        copy.wait()


def to_all(x, axes):
    return lax.all_to_all(x, axes, split_axis=0, concat_axis=0, tiled=True)


def shards(
    face_len,
    residual,
    prev_direction,
    prev_rho,
    schur,
    neumann,
    coarse_basis,
    coarse_inverse,
    prim_owner,
    coarse_row,
):
    height, width = residual.shape[3:]
    rows = height // 6
    primal = coarse_basis.shape[4]
    owned = coarse_inverse.shape[3]
    owners = lax.axis_size(LAYER)
    slots = owners * CAP
    devices = lax.axis_size(AXES)
    layers = lax.axis_size("depth")
    pair_depth = layers == 2
    scale = 0.5 / (devices * height)
    folds = width // LANES
    tail = tiles(2 * folds)

    lengths = face_len.reshape(6)
    residual = residual.reshape(height, width)
    prev_direction = prev_direction.reshape(height, width)
    schur = schur.reshape(height, height)
    neumann = neumann.reshape(height, height)
    basis = coarse_basis.reshape(height, primal)
    inverse = coarse_inverse.reshape(owned, owned)
    owner = prim_owner.reshape(1, primal)
    wanted = coarse_row.reshape(1, primal)
    whole = shape_of(height, width)
    row = shape_of(1, width)
    face = shape_of(rows, width)

    (outgoing,) = call(
        pack_kernel,
        [shape_of(owners, folds * CAP + TILE, LANES)],
        [lengths, owner, wanted, residual, basis],
        far=range(5),
        flops=6 * height * primal * width,
        moved=4 * (height * (width + primal) + slots * width),
        scratch=[
            pltpu.SMEM((6,), jnp.int32),
            pltpu.VMEM((1, primal), jnp.int32),
            pltpu.VMEM((1, primal), jnp.int32),
            pltpu.VMEM((height, width), f32),
            pltpu.VMEM((height, primal), f32),
            pltpu.SemaphoreType.DMA((3, 2)),
            pltpu.SemaphoreType.DMA((3,)),
        ],
        room=60,
    )
    incoming = to_all(outgoing, LAYER)
    local, local_part, square, table, *halves = call(
        local_kernel,
        [whole, row, row, shape_of(primal, slots, dtype=bf16)]
        + [shape_of(height, primal, dtype=bf16)] * 2
        + [shape_of(owned, owned, dtype=bf16)] * 2
        + [shape_of(height, height, dtype=bf16)] * 2,
        [lengths, residual, neumann, owner, basis, inverse, schur],
        smem=(0,),
        flops=6 * height * height * width,
        moved=4 * height * (3 * height + 2 * width),
    )
    basis_halves, inverse_halves, schur_halves = halves[:2], halves[2:4], halves[4:]
    (answers,) = call(
        solve_kernel,
        [shape_of(owners, folds * CAP + tail, LANES)],
        [incoming, *inverse_halves, local_part, square],
        flops=(8 * slots + 6 * owned) * owned * width,
        moved=8 * slots * width,
    )
    returned = to_all(answers, LAYER)
    faces = len(swaps())
    last = shape_of(rows + TILE, width) if pair_depth else face
    image, sums, *outward = call(
        functools.partial(image_kernel, pair_depth),
        [whole, shape_of(TILE, width) if pair_depth else shape_of(layers, tail, LANES)]
        + [face] * (faces - 1)
        + [last],
        [returned, table, *basis_halves, local],
        flops=(6 * height + 4 * slots) * primal * width,
        moved=16 * height * width,
    )
    if not pair_depth:
        sums = to_all(sums, "depth")
    got = exchange(outward)
    direction, rho, square, schur_image, *outward = call(
        functools.partial(direction_kernel, pair_depth, scale),
        [whole, row, row, whole] + [face] * faces,
        [lengths, sums, prev_rho.reshape(1, width), image, prev_direction, *schur_halves, *got],
        smem=(0,),
        far_out=(0,),
        flops=6 * height * height * width,
        moved=4 * height * (height + 6 * width),
        scratch=[pltpu.VMEM((height, width), f32), pltpu.SemaphoreType.DMA],
    )
    got = exchange(outward)
    curve, cross = call(
        products_kernel,
        [row, row],
        [lengths, direction, schur_image, residual],
        smem=(0,),
        flops=4 * height * width,
        moved=12 * height * width,
    )
    applied, spread = call(
        applied_kernel,
        [whole, shape_of(devices, 3, folds, LANES)],
        [lengths, curve, cross, schur_image, *got],
        smem=(0,),
        flops=4 * height * width,
        moved=12 * height * width,
    )
    new_residual, alpha, norm = call(
        functools.partial(finish_kernel, scale),
        [whole, row, row],
        [lengths, to_all(spread, AXES), rho, square, residual, applied],
        smem=(0,),
        far_out=(0,),
        flops=4 * height * width,
        moved=12 * height * width,
        scratch=[pltpu.VMEM((height, width), f32), pltpu.SemaphoreType.DMA((6,))],
    )
    out_shape = (1, 1, 1, height, width)
    return (
        new_residual.reshape(out_shape),
        direction.reshape(out_shape),
        rho.reshape(width),
        alpha.reshape(width),
        norm.reshape(width),
    )


def solution(mesh):
    tall = P("blk", "lat", "depth", None, None)
    flat = P("blk", "lat", "depth", None)
    in_specs = (flat, tall, tall, P(), tall, tall, tall, tall, tall, flat)
    out_specs = (tall, tall, P(), P(), P())
    return jax.shard_map(shards, mesh=mesh, in_specs=in_specs, out_specs=out_specs, check_vma=False)
```

```python
import functools

import jax
import jax.numpy as jnp
from jax import lax
from jax.experimental import pallas as pl
from jax.experimental.pallas import tpu as pltpu
from jax.sharding import PartitionSpec as P

CAP = 24
AXES = ("blk", "lat", "depth")
LAYER = ("blk", "lat")
LANES = 128
TILE = 8
f32 = jnp.float32
bf16 = jnp.bfloat16

VMEM = pl.BlockSpec(memory_space=pltpu.VMEM)
SMEM = pl.BlockSpec(memory_space=pltpu.SMEM)
ANY = pl.BlockSpec(memory_space=pl.ANY)


def shape_of(*dims, dtype=f32):
    return jax.ShapeDtypeStruct(dims, dtype)


def call(body, outs, operands, smem=(), far=(), far_out=(), flops=0, moved=0, scratch=(), room=32):
    in_specs = [SMEM if i in smem else ANY if i in far else VMEM for i in range(len(operands))]
    out_specs = [ANY if i in far_out else VMEM for i in range(len(outs))]
    return pl.pallas_call(
        body,
        out_shape=list(outs),
        in_specs=in_specs,
        out_specs=out_specs,
        scratch_shapes=list(scratch),
        compiler_params=pltpu.CompilerParams(vmem_limit_bytes=room << 20),
        cost_estimate=pl.CostEstimate(flops=flops, bytes_accessed=moved, transcendentals=0),
    )(*operands)


def parts(x):
    high = x.astype(bf16)
    low = (x - high.astype(f32)).astype(bf16)
    return high, low


def mul(a, b, dims):
    return lax.dot_general(a, b, (dims, ((), ())), preferred_element_type=f32)


PLAIN = ((1,), (0,))
LEFT_T = ((0,), (0,))


def product(a, b, dims=PLAIN):
    (ah, al), (bh, bl) = a, b
    (along_a,), (along_b,) = dims
    left = jnp.concatenate([ah, ah, al], axis=along_a)
    right = jnp.concatenate([bh, bl, bh], axis=along_b)
    return mul(left, right, dims)


def select(table, x, dims=PLAIN):
    (along_a,), (along_b,) = dims
    left = jnp.concatenate([table, table], axis=along_a)
    return mul(left, jnp.concatenate(parts(x), axis=along_b), dims)


def one_hot(hit):
    return jnp.where(hit, 1.0, 0.0).astype(bf16)


def live_rows(len_ref, face, rows):
    return lax.broadcasted_iota(jnp.int32, (rows, 1), 0) < len_ref[face]


def masked(len_ref, ref, face, rows):
    block = ref[face * rows : (face + 1) * rows, :]
    return jnp.where(live_rows(len_ref, face, rows), block, 0.0)


def folded(vector):
    pieces = vector.shape[1] // LANES
    return [vector[:, j * LANES : (j + 1) * LANES] for j in range(pieces)]


def unfolded(block, first, pieces):
    return jnp.concatenate([block[first + j : first + j + 1, :] for j in range(pieces)], axis=1)


def tiles(rows):
    return -(-rows // TILE) * TILE


def put_slab(out_ref, block):
    owners = out_ref.shape[0]
    for j in range(block.shape[1] // LANES):
        piece = block[:, j * LANES : (j + 1) * LANES]
        out_ref[:, j * CAP : (j + 1) * CAP, :] = piece.reshape(owners, CAP, LANES)


def get_slab(ref, pieces):
    slots = ref.shape[0] * CAP
    return jnp.concatenate(
        [ref[:, j * CAP : (j + 1) * CAP, :].reshape(slots, LANES) for j in range(pieces)], axis=1
    )


def pack_kernel(len_any, owner_any, row_any, residual_any, basis_any, slab_ref, *refs):
    len_ref, owner_ref, row_ref, residual_ref, basis_ref, sems, small_sems = refs
    rows = residual_ref.shape[0] // 6
    primal = basis_ref.shape[1]
    owners = slab_ref.shape[0]
    slots = owners * CAP
    small = [
        pltpu.make_async_copy(src, dst, small_sems.at[i])
        for i, (src, dst) in enumerate(
            [(owner_any, owner_ref), (row_any, row_ref), (len_any, len_ref)]
        )
    ]
    large = []
    for pair in range(3):
        at = pl.ds(2 * pair * rows, 2 * rows)
        large.append(
            (
                pltpu.make_async_copy(residual_any.at[at], residual_ref.at[at], sems.at[pair, 0]),
                pltpu.make_async_copy(basis_any.at[at], basis_ref.at[at], sems.at[pair, 1]),
            )
        )
    for copy in small:
        copy.start()
    for pair in large:
        for copy in pair:
            copy.start()
    for copy in small:
        copy.wait()
    row_at = lax.broadcasted_iota(jnp.int32, (primal, primal), 0)
    col_at = lax.broadcasted_iota(jnp.int32, (primal, primal), 1)
    own_row = owner_ref[...].astype(f32)
    wanted_row = row_ref[...].astype(f32) + 1.0
    own_col = jnp.sum(jnp.where(row_at == col_at, own_row, 0.0), axis=1, keepdims=True)
    wanted_col = jnp.sum(jnp.where(row_at == col_at, wanted_row, 0.0), axis=1, keepdims=True)
    same = own_row == own_col
    rank_row = jnp.sum(jnp.where(same & (row_at < col_at), 1.0, 0.0), axis=0, keepdims=True)
    rank_col = jnp.sum(jnp.where(same & (col_at < row_at), 1.0, 0.0), axis=1, keepdims=True)
    slot_row = (own_row * CAP + rank_row).astype(jnp.int32)
    packer = one_hot(lax.broadcasted_iota(jnp.int32, (slots, primal), 0) == slot_row)
    to_owner = one_hot(lax.broadcasted_iota(jnp.int32, (owners, primal), 0) == owner_ref[...])
    lane_at = lax.broadcasted_iota(jnp.int32, (primal, LANES), 1)
    ranked = jnp.where(lane_at == rank_col.astype(jnp.int32), wanted_col, 0.0)
    names = select(to_owner, ranked)
    terms = None
    for pair in range(3):
        for copy in large[pair]:
            copy.wait()
        weighted = jnp.concatenate(
            [0.5 * masked(len_ref, residual_ref, 2 * pair + side, rows) for side in range(2)],
            axis=0,
        )
        basis = basis_ref[2 * pair * rows : 2 * (pair + 1) * rows, :]
        term = product(parts(basis), parts(weighted), LEFT_T)
        terms = term if terms is None else terms + term
    put_slab(slab_ref, select(packer, terms))
    tail = slab_ref.shape[1] - TILE
    slab_ref[:, tail:, :] = jnp.broadcast_to(
        names.reshape(owners, 1, LANES), (owners, TILE, LANES)
    )


def local_kernel(len_ref, residual_ref, matrix_ref, owner_ref, *refs):
    whole, refs = refs[:2], refs[2:]
    local_ref, part_ref, square_ref, table_ref, refs = *refs[:4], refs[4:]
    rows = residual_ref.shape[0] // 6
    live = jnp.concatenate(
        [masked(len_ref, residual_ref, face, rows) for face in range(6)], axis=0
    )
    local = product(parts(matrix_ref[...]), parts(0.5 * live))
    local_ref[...] = local
    part_ref[...] = jnp.sum(live * local, axis=0, keepdims=True)
    square_ref[...] = jnp.sum(live * live, axis=0, keepdims=True)
    for i in range(2):
        refs[2 * i][...], refs[2 * i + 1][...] = parts(whole[i][...])
    primal, slots = table_ref.shape
    row_at = lax.broadcasted_iota(jnp.int32, (primal, primal), 0)
    col_at = lax.broadcasted_iota(jnp.int32, (primal, primal), 1)
    own_row = owner_ref[...].astype(f32)
    own_col = jnp.sum(jnp.where(row_at == col_at, own_row, 0.0), axis=1, keepdims=True)
    before = (own_row == own_col) & (col_at < row_at)
    rank_col = jnp.sum(jnp.where(before, 1.0, 0.0), axis=1, keepdims=True)
    slot_col = (own_col * CAP + rank_col).astype(jnp.int32)
    table_ref[...] = one_hot(lax.broadcasted_iota(jnp.int32, (primal, slots), 1) == slot_col)


def picker_table(names_ref, owned):
    owners = names_ref.shape[0]
    lane_at = lax.broadcasted_iota(jnp.int32, (CAP, LANES), 1)
    rank_at = lax.broadcasted_iota(jnp.int32, (CAP, LANES), 0)
    out_at = lax.broadcasted_iota(jnp.int32, (CAP, owned), 1).astype(f32) + 1.0
    blocks = []
    for source in range(owners):
        names = names_ref[source, 0:1, :]
        named = jnp.sum(jnp.where(lane_at == rank_at, names, 0.0), axis=1, keepdims=True)
        blocks.append(jnp.where(out_at == named, 1.0, 0.0))
    return jnp.concatenate(blocks, axis=0)


def solve_kernel(incoming_any, inverse_any, local_part_ref, square_ref, answer_ref, *refs):
    names_ref, slab_ref, inverse_ref, sems = refs
    owners, height, _ = slab_ref.shape
    pieces = height // CAP
    half = pieces // 2 * CAP
    copies = [
        pltpu.make_async_copy(incoming_any.at[:, pl.ds(height, TILE)], names_ref, sems.at[0]),
        pltpu.make_async_copy(
            incoming_any.at[:, pl.ds(0, half)], slab_ref.at[:, pl.ds(0, half)], sems.at[1]
        ),
        pltpu.make_async_copy(
            incoming_any.at[:, pl.ds(half, height - half)],
            slab_ref.at[:, pl.ds(half, height - half)],
            sems.at[2],
        ),
        pltpu.make_async_copy(inverse_any, inverse_ref, sems.at[3]),
    ]
    for copy in copies:
        copy.start()
    copies[0].wait()
    table = picker_table(names_ref, inverse_ref.shape[0]).astype(bf16)
    for copy in copies[1:]:
        copy.wait()
    summed = select(table, get_slab(slab_ref, pieces), LEFT_T)
    solved = product(parts(inverse_ref[...]), parts(summed))
    put_slab(answer_ref, select(table, solved))
    total = local_part_ref[...] + 2.0 * jnp.sum(summed * solved, axis=0, keepdims=True)
    sums = folded(total) + folded(square_ref[...])
    sums += [jnp.zeros((1, LANES), f32)] * (tiles(len(sums)) - len(sums))
    answer_ref[:, pieces * CAP :, :] = jnp.broadcast_to(
        jnp.concatenate(sums, axis=0)[None], (owners, len(sums), LANES)
    )


AXIS_AT = {"blk": 0, "lat": 2, "depth": 4}


def swaps():
    order = [("blk", 1), ("lat", 1), ("blk", 0), ("lat", 0), ("depth", 1), ("depth", 0)]
    return [(axis, odd) for axis, odd in order if pairs(axis, odd)]


def pairs(axis, odd):
    devices = lax.axis_size(axis)
    ends = [(i, i + 1) for i in range(odd, devices - 1, 2)]
    if axis == "blk" and odd:
        ends.append((devices - 1, 0))
    return [pair for i, j in ends for pair in ((i, j), (j, i))]


def sends_plus(axis, odd):
    return lax.rem(lax.axis_index(axis), 2) == odd


def put_faces(image, rows, face_refs):
    for ref, (axis, odd) in zip(face_refs, swaps(), strict=True):
        at = AXIS_AT[axis] * rows
        minus, plus = image[at : at + rows, :], image[at + rows : at + 2 * rows, :]
        ref[:rows, :] = jnp.where(sends_plus(axis, odd), plus, minus)


def got_face(refs, face, rows):
    axis = ("blk", "lat", "depth")[face // 2]
    total = None
    for ref, (axis_of, odd) in zip(refs, swaps(), strict=True):
        if axis_of == axis:
            mine = sends_plus(axis, odd) == (face % 2 == 1)
            piece = jnp.where(mine, ref[:rows, :], 0.0)
            total = piece if total is None else total + piece
    return total


def exchange(faces):
    return [
        lax.ppermute(block, axis, pairs(axis, odd))
        for block, (axis, odd) in zip(faces, swaps(), strict=True)
    ]


def image_kernel(pair_depth, returned_ref, table_ref, high_ref, low_ref, local_ref, image_ref, sums_ref, *face_refs):
    rows = local_ref.shape[0] // 6
    width = local_ref.shape[1]
    folds = width // LANES
    correction = select(table_ref[...], get_slab(returned_ref, folds))
    image = local_ref[...] + product((high_ref[...], low_ref[...]), parts(correction))
    image_ref[...] = image
    put_faces(image, rows, face_refs)
    tail = jnp.sum(returned_ref[:, folds * CAP :, :], axis=0)
    if pair_depth:
        sums = jnp.concatenate(
            [unfolded(tail, 0, folds), unfolded(tail, folds, folds)]
            + [jnp.zeros((TILE - 2, width), f32)],
            axis=0,
        )
        sums_ref[...] = sums
        face_refs[-1][rows:, :] = sums
    else:
        sums_ref[...] = jnp.broadcast_to(tail[None], sums_ref.shape)


def direction_kernel(pair_depth, scale, len_ref, sums_ref, prev_rho_ref, image_ref, prev_ref, high_ref, low_ref, *refs):
    faces = len(swaps())
    got, refs = refs[:faces], refs[faces:]
    (direction_out, rho_out, square_out, schur_out), refs = refs[:4], refs[4:]
    face_refs, (direction_ref, sem) = refs[:faces], refs[faces:]
    rows = image_ref.shape[0] // 6
    width = image_ref.shape[1]
    if pair_depth:
        sums = sums_ref[...] + got[-1][rows:, :]
        rho, square = sums[0:1, :], sums[1:2, :]
    else:
        folds = width // LANES
        sums = jnp.sum(sums_ref[...], axis=0)
        rho, square = unfolded(sums, 0, folds), unfolded(sums, folds, folds)
    rho = scale * rho
    rho_out[...] = rho
    square_out[...] = square
    beta = rho / prev_rho_ref[...]
    for face in range(6):
        at = slice(face * rows, (face + 1) * rows)
        precond = 0.5 * (image_ref[at, :] + got_face(got, face, rows))
        direction_ref[at, :] = jnp.where(
            live_rows(len_ref, face, rows), precond + beta * prev_ref[at, :], 0.0
        )
    copy = pltpu.make_async_copy(direction_ref, direction_out, sem)
    copy.start()
    image = product((high_ref[...], low_ref[...]), parts(direction_ref[...]))
    schur_out[...] = image
    put_faces(image, rows, face_refs)
    copy.wait()


def products_kernel(len_ref, direction_ref, schur_ref, residual_ref, curve_ref, cross_ref):
    rows = schur_ref.shape[0] // 6
    image = schur_ref[...]
    live = jnp.concatenate(
        [masked(len_ref, residual_ref, face, rows) for face in range(6)], axis=0
    )
    curve_ref[...] = 2.0 * jnp.sum(direction_ref[...] * image, axis=0, keepdims=True)
    cross_ref[...] = 2.0 * jnp.sum(live * image, axis=0, keepdims=True)


def applied_kernel(len_ref, curve_ref, cross_ref, schur_ref, *refs):
    got, (applied_ref, spread_ref) = refs[:-2], refs[-2:]
    rows = schur_ref.shape[0] // 6
    total = jnp.zeros(curve_ref.shape, f32)
    for face in range(6):
        at = slice(face * rows, (face + 1) * rows)
        applied = schur_ref[at, :] + got_face(got, face, rows)
        applied = jnp.where(live_rows(len_ref, face, rows), applied, 0.0)
        applied_ref[at, :] = applied
        total += jnp.sum(applied * applied, axis=0, keepdims=True)
    for i, vector in enumerate([curve_ref[...], cross_ref[...], total]):
        for j, piece in enumerate(folded(vector)):
            spread_ref[:, i, j, :] = jnp.broadcast_to(piece, (spread_ref.shape[0], LANES))


def finish_kernel(scale, len_ref, sums_ref, rho_ref, square_ref, residual_ref, applied_ref, new_out, alpha_ref, norm_ref, new_ref, sems):
    rows = applied_ref.shape[0] // 6
    folds = sums_ref.shape[2]
    sums = jnp.sum(sums_ref[...], axis=0)
    curve, cross, square = [unfolded(sums[i], 0, folds) for i in range(3)]
    alpha = rho_ref[...] / (scale * curve)
    alpha_ref[...] = alpha
    norm_ref[...] = scale * (square_ref[...] - 2.0 * alpha * cross + alpha * alpha * square)
    copies = []
    for face in range(6):
        at = slice(face * rows, (face + 1) * rows)
        new_ref[at, :] = masked(len_ref, residual_ref, face, rows) - alpha * applied_ref[at, :]
        where = pl.ds(face * rows, rows)
        copies.append(pltpu.make_async_copy(new_ref.at[where], new_out.at[where], sems.at[face]))
        copies[-1].start()
    for copy in copies:
        copy.wait()


def to_all(x, axes):
    return lax.all_to_all(x, axes, split_axis=0, concat_axis=0, tiled=True)


def shards(
    face_len,
    residual,
    prev_direction,
    prev_rho,
    schur,
    neumann,
    coarse_basis,
    coarse_inverse,
    prim_owner,
    coarse_row,
):
    height, width = residual.shape[3:]
    rows = height // 6
    primal = coarse_basis.shape[4]
    owned = coarse_inverse.shape[3]
    owners = lax.axis_size(LAYER)
    slots = owners * CAP
    devices = lax.axis_size(AXES)
    layers = lax.axis_size("depth")
    pair_depth = layers == 2
    scale = 0.5 / (devices * height)
    folds = width // LANES
    tail = tiles(2 * folds)

    lengths = face_len.reshape(6)
    residual = residual.reshape(height, width)
    prev_direction = prev_direction.reshape(height, width)
    schur = schur.reshape(height, height)
    neumann = neumann.reshape(height, height)
    basis = coarse_basis.reshape(height, primal)
    inverse = coarse_inverse.reshape(owned, owned)
    owner = prim_owner.reshape(1, primal)
    wanted = coarse_row.reshape(1, primal)
    whole = shape_of(height, width)
    row = shape_of(1, width)
    face = shape_of(rows, width)

    (outgoing,) = call(
        pack_kernel,
        [shape_of(owners, folds * CAP + TILE, LANES)],
        [lengths, owner, wanted, residual, basis],
        far=range(5),
        flops=6 * height * primal * width,
        moved=4 * (height * (width + primal) + slots * width),
        scratch=[
            pltpu.SMEM((6,), jnp.int32),
            pltpu.VMEM((1, primal), jnp.int32),
            pltpu.VMEM((1, primal), jnp.int32),
            pltpu.VMEM((height, width), f32),
            pltpu.VMEM((height, primal), f32),
            pltpu.SemaphoreType.DMA((3, 2)),
            pltpu.SemaphoreType.DMA((3,)),
        ],
        room=60,
    )
    incoming = to_all(outgoing, LAYER)
    local, local_part, square, table, *halves = call(
        local_kernel,
        [whole, row, row, shape_of(primal, slots, dtype=bf16)]
        + [shape_of(height, primal, dtype=bf16)] * 2
        + [shape_of(height, height, dtype=bf16)] * 2,
        [lengths, residual, neumann, owner, basis, schur],
        smem=(0,),
        flops=6 * height * height * width,
        moved=4 * height * (3 * height + 2 * width),
    )
    basis_halves, schur_halves = halves[:2], halves[2:]
    (answers,) = call(
        solve_kernel,
        [shape_of(owners, folds * CAP + tail, LANES)],
        [incoming, inverse, local_part, square],
        far=range(2),
        flops=(8 * slots + 6 * owned) * owned * width,
        moved=8 * slots * width,
        scratch=[
            pltpu.VMEM((owners, TILE, LANES), f32),
            pltpu.VMEM((owners, folds * CAP, LANES), f32),
            pltpu.VMEM((owned, owned), f32),
            pltpu.SemaphoreType.DMA((4,)),
        ],
    )
    returned = to_all(answers, LAYER)
    faces = len(swaps())
    last = shape_of(rows + TILE, width) if pair_depth else face
    image, sums, *outward = call(
        functools.partial(image_kernel, pair_depth),
        [whole, shape_of(TILE, width) if pair_depth else shape_of(layers, tail, LANES)]
        + [face] * (faces - 1)
        + [last],
        [returned, table, *basis_halves, local],
        flops=(6 * height + 4 * slots) * primal * width,
        moved=16 * height * width,
    )
    if not pair_depth:
        sums = to_all(sums, "depth")
    got = exchange(outward)
    direction, rho, square, schur_image, *outward = call(
        functools.partial(direction_kernel, pair_depth, scale),
        [whole, row, row, whole] + [face] * faces,
        [lengths, sums, prev_rho.reshape(1, width), image, prev_direction, *schur_halves, *got],
        smem=(0,),
        far_out=(0,),
        flops=6 * height * height * width,
        moved=4 * height * (height + 6 * width),
        scratch=[pltpu.VMEM((height, width), f32), pltpu.SemaphoreType.DMA],
    )
    got = exchange(outward)
    curve, cross = call(
        products_kernel,
        [row, row],
        [lengths, direction, schur_image, residual],
        smem=(0,),
        flops=4 * height * width,
        moved=12 * height * width,
    )
    applied, spread = call(
        applied_kernel,
        [whole, shape_of(devices, 3, folds, LANES)],
        [lengths, curve, cross, schur_image, *got],
        smem=(0,),
        flops=4 * height * width,
        moved=12 * height * width,
    )
    new_residual, alpha, norm = call(
        functools.partial(finish_kernel, scale),
        [whole, row, row],
        [lengths, to_all(spread, AXES), rho, square, residual, applied],
        smem=(0,),
        far_out=(0,),
        flops=4 * height * width,
        moved=12 * height * width,
        scratch=[pltpu.VMEM((height, width), f32), pltpu.SemaphoreType.DMA((6,))],
    )
    out_shape = (1, 1, 1, height, width)
    return (
        new_residual.reshape(out_shape),
        direction.reshape(out_shape),
        rho.reshape(width),
        alpha.reshape(width),
        norm.reshape(width),
    )


def solution(mesh):
    tall = P("blk", "lat", "depth", None, None)
    flat = P("blk", "lat", "depth", None)
    in_specs = (flat, tall, tall, P(), tall, tall, tall, tall, tall, flat)
    out_specs = (tall, tall, P(), P(), P())
    return jax.shard_map(shards, mesh=mesh, in_specs=in_specs, out_specs=out_specs, check_vma=False)
```

```python
import functools

import jax
import jax.numpy as jnp
from jax import lax
from jax.experimental import pallas as pl
from jax.experimental.pallas import tpu as pltpu
from jax.sharding import PartitionSpec as P

CAP = 24
AXES = ("blk", "lat", "depth")
LAYER = ("blk", "lat")
LANES = 128
TILE = 8
f32 = jnp.float32
bf16 = jnp.bfloat16

VMEM = pl.BlockSpec(memory_space=pltpu.VMEM)
SMEM = pl.BlockSpec(memory_space=pltpu.SMEM)
ANY = pl.BlockSpec(memory_space=pl.ANY)


def shape_of(*dims, dtype=f32):
    return jax.ShapeDtypeStruct(dims, dtype)


def call(body, outs, operands, smem=(), far=(), far_out=(), flops=0, moved=0, scratch=(), room=32):
    in_specs = [SMEM if i in smem else ANY if i in far else VMEM for i in range(len(operands))]
    operands = [
        pltpu.with_memory_space_constraint(x, pltpu.HBM) if i in far else x
        for i, x in enumerate(operands)
    ]
    out_specs = [ANY if i in far_out else VMEM for i in range(len(outs))]
    return pl.pallas_call(
        body,
        out_shape=list(outs),
        in_specs=in_specs,
        out_specs=out_specs,
        scratch_shapes=list(scratch),
        compiler_params=pltpu.CompilerParams(vmem_limit_bytes=room << 20),
        cost_estimate=pl.CostEstimate(flops=flops, bytes_accessed=moved, transcendentals=0),
    )(*operands)


def parts(x):
    high = x.astype(bf16)
    low = (x - high.astype(f32)).astype(bf16)
    return high, low


def mul(a, b, dims):
    return lax.dot_general(a, b, (dims, ((), ())), preferred_element_type=f32)


PLAIN = ((1,), (0,))
LEFT_T = ((0,), (0,))


def product(a, b, dims=PLAIN):
    (ah, al), (bh, bl) = a, b
    return mul(ah, bh, dims) + (mul(ah, bl, dims) + mul(al, bh, dims))


def select(table, x, dims=PLAIN):
    high, low = parts(x)
    return mul(table, high, dims) + mul(table, low, dims)


def one_hot(hit):
    return jnp.where(hit, 1.0, 0.0).astype(bf16)


def live_rows(len_ref, face, rows):
    return lax.broadcasted_iota(jnp.int32, (rows, 1), 0) < len_ref[face]


def masked(len_ref, ref, face, rows):
    block = ref[face * rows : (face + 1) * rows, :]
    return jnp.where(live_rows(len_ref, face, rows), block, 0.0)


def folded(vector):
    pieces = vector.shape[1] // LANES
    return [vector[:, j * LANES : (j + 1) * LANES] for j in range(pieces)]


def unfolded(block, first, pieces):
    return jnp.concatenate([block[first + j : first + j + 1, :] for j in range(pieces)], axis=1)


def tiles(rows):
    return -(-rows // TILE) * TILE


def put_slab(out_ref, block):
    owners = out_ref.shape[0]
    for j in range(block.shape[1] // LANES):
        piece = block[:, j * LANES : (j + 1) * LANES]
        out_ref[:, j * CAP : (j + 1) * CAP, :] = piece.reshape(owners, CAP, LANES)


def get_slab(ref, pieces):
    slots = ref.shape[0] * CAP
    return jnp.concatenate(
        [ref[:, j * CAP : (j + 1) * CAP, :].reshape(slots, LANES) for j in range(pieces)], axis=1
    )


def columns(*rows):
    spare = [jnp.zeros_like(rows[0])] * (TILE - len(rows))
    turned = jnp.transpose(jnp.concatenate([*rows, *spare], axis=0))
    return [turned[:, i : i + 1] for i in range(len(rows))]


def ranks(own_row):
    primal = own_row.shape[1]
    (own_col,) = columns(own_row)
    row_at = lax.broadcasted_iota(jnp.int32, (primal, primal), 0)
    col_at = lax.broadcasted_iota(jnp.int32, (primal, primal), 1)
    before = (own_row == own_col) & (row_at < col_at)
    return jnp.sum(jnp.where(before, 1.0, 0.0), axis=0, keepdims=True), own_col


def pack_kernel(len_any, owner_any, row_any, residual_any, basis_any, slab_ref, *refs):
    len_ref, owner_ref, row_ref, residual_ref, basis_ref, sems, small_sems = refs
    rows = residual_ref.shape[0] // 6
    primal = basis_ref.shape[1]
    owners = slab_ref.shape[0]
    slots = owners * CAP
    small = [
        pltpu.make_async_copy(src, dst, small_sems.at[i])
        for i, (src, dst) in enumerate(
            [(owner_any, owner_ref), (row_any, row_ref), (len_any, len_ref)]
        )
    ]
    large = []
    for pair in range(3):
        at = pl.ds(2 * pair * rows, 2 * rows)
        large.append(
            (
                pltpu.make_async_copy(residual_any.at[at], residual_ref.at[at], sems.at[pair, 0]),
                pltpu.make_async_copy(basis_any.at[at], basis_ref.at[at], sems.at[pair, 1]),
            )
        )
    for copy in small:
        copy.start()
    for pair in large:
        for copy in pair:
            copy.start()
    for copy in small:
        copy.wait()
    own_row = owner_ref[...].astype(f32)
    wanted_row = row_ref[...].astype(f32) + 1.0
    rank_row, _ = ranks(own_row)
    slot_row = (own_row * CAP + rank_row).astype(jnp.int32)
    rank_col, wanted_col = columns(rank_row, wanted_row)
    packer = one_hot(lax.broadcasted_iota(jnp.int32, (slots, primal), 0) == slot_row)
    to_owner = one_hot(lax.broadcasted_iota(jnp.int32, (owners, primal), 0) == owner_ref[...])
    lane_at = lax.broadcasted_iota(jnp.int32, (primal, LANES), 1)
    ranked = jnp.where(lane_at == rank_col.astype(jnp.int32), wanted_col, 0.0)
    names = select(to_owner, ranked)
    terms = None
    for pair in range(3):
        for copy in large[pair]:
            copy.wait()
        weighted = jnp.concatenate(
            [0.5 * masked(len_ref, residual_ref, 2 * pair + side, rows) for side in range(2)],
            axis=0,
        )
        basis = basis_ref[2 * pair * rows : 2 * (pair + 1) * rows, :]
        term = product(parts(basis), parts(weighted), LEFT_T)
        terms = term if terms is None else terms + term
    put_slab(slab_ref, select(packer, terms))
    tail = slab_ref.shape[1] - TILE
    slab_ref[:, tail:, :] = jnp.broadcast_to(
        names.reshape(owners, 1, LANES), (owners, TILE, LANES)
    )


def local_kernel(len_ref, residual_ref, matrix_ref, owner_ref, *refs):
    whole, refs = refs[:2], refs[2:]
    local_ref, part_ref, square_ref, table_ref, refs = *refs[:4], refs[4:]
    rows = residual_ref.shape[0] // 6
    live = jnp.concatenate(
        [masked(len_ref, residual_ref, face, rows) for face in range(6)], axis=0
    )
    local = product(parts(matrix_ref[...]), parts(0.5 * live))
    local_ref[...] = local
    part_ref[...] = jnp.sum(live * local, axis=0, keepdims=True)
    square_ref[...] = jnp.sum(live * live, axis=0, keepdims=True)
    for i in range(2):
        refs[2 * i][...], refs[2 * i + 1][...] = parts(whole[i][...])
    primal, slots = table_ref.shape
    rank_row, own_col = ranks(owner_ref[...].astype(f32))
    (rank_col,) = columns(rank_row)
    slot_col = (own_col * CAP + rank_col).astype(jnp.int32)
    table_ref[...] = one_hot(lax.broadcasted_iota(jnp.int32, (primal, slots), 1) == slot_col)


def picker_table(names_ref, owned):
    owners = names_ref.shape[0]
    lane_at = lax.broadcasted_iota(jnp.int32, (CAP, LANES), 1)
    rank_at = lax.broadcasted_iota(jnp.int32, (CAP, LANES), 0)
    out_at = lax.broadcasted_iota(jnp.int32, (CAP, owned), 1).astype(f32) + 1.0
    blocks = []
    for source in range(owners):
        names = names_ref[source, 0:1, :]
        named = jnp.sum(jnp.where(lane_at == rank_at, names, 0.0), axis=1, keepdims=True)
        blocks.append(jnp.where(out_at == named, 1.0, 0.0))
    return jnp.concatenate(blocks, axis=0)


def solve_kernel(incoming_any, inverse_any, local_part_ref, square_ref, answer_ref, *refs):
    names_ref, slab_ref, inverse_ref, sems = refs
    owners, height, _ = slab_ref.shape
    pieces = height // CAP
    half = pieces // 2 * CAP
    copies = [
        pltpu.make_async_copy(incoming_any.at[:, pl.ds(height, TILE)], names_ref, sems.at[0]),
        pltpu.make_async_copy(
            incoming_any.at[:, pl.ds(0, half)], slab_ref.at[:, pl.ds(0, half)], sems.at[1]
        ),
        pltpu.make_async_copy(
            incoming_any.at[:, pl.ds(half, height - half)],
            slab_ref.at[:, pl.ds(half, height - half)],
            sems.at[2],
        ),
        pltpu.make_async_copy(inverse_any, inverse_ref, sems.at[3]),
    ]
    for copy in copies:
        copy.start()
    copies[0].wait()
    table = picker_table(names_ref, inverse_ref.shape[0]).astype(bf16)
    for copy in copies[1:]:
        copy.wait()
    summed = select(table, get_slab(slab_ref, pieces), LEFT_T)
    solved = product(parts(inverse_ref[...]), parts(summed))
    put_slab(answer_ref, select(table, solved))
    total = local_part_ref[...] + 2.0 * jnp.sum(summed * solved, axis=0, keepdims=True)
    sums = folded(total) + folded(square_ref[...])
    sums += [jnp.zeros((1, LANES), f32)] * (tiles(len(sums)) - len(sums))
    answer_ref[:, pieces * CAP :, :] = jnp.broadcast_to(
        jnp.concatenate(sums, axis=0)[None], (owners, len(sums), LANES)
    )


AXIS_AT = {"blk": 0, "lat": 2, "depth": 4}


def moves():
    order = [("blk", "up"), ("lat", 1), ("blk", "down"), ("lat", 0), ("depth", 1), ("depth", 0)]
    return [(axis, way) for axis, way in order if route(axis, way)]


def route(axis, way):
    devices = lax.axis_size(axis)
    if way in ("up", "down"):
        by = 1 if way == "up" else -1
        return [(i, (i + by) % devices) for i in range(devices)]
    return [pair for i in range(way, devices - 1, 2) for pair in ((i, i + 1), (i + 1, i))]


def sends_plus(axis, way):
    return lax.rem(lax.axis_index(axis), 2) == way


def put_faces(image, rows, face_refs):
    for ref, (axis, way) in zip(face_refs, moves(), strict=True):
        at = AXIS_AT[axis] * rows
        minus, plus = image[at : at + rows, :], image[at + rows : at + 2 * rows, :]
        if way in ("up", "down"):
            ref[...] = plus if way == "up" else minus
        else:
            ref[...] = jnp.where(sends_plus(axis, way), plus, minus)


def got_face(got, face):
    axis, side = ("blk", "lat", "depth")[face // 2], face % 2
    if axis == "blk":
        return got["blk", "down" if side else "up"][...]
    total = None
    for (axis_of, way), ref in got.items():
        if axis_of == axis:
            mine = sends_plus(axis, way) == (side == 1)
            piece = jnp.where(mine, ref[...], 0.0)
            total = piece if total is None else total + piece
    return total


def exchange(faces):
    return [
        lax.ppermute(block, axis, route(axis, way))
        for block, (axis, way) in zip(faces, moves(), strict=True)
    ]


def image_kernel(pair_depth, returned_ref, table_ref, high_ref, low_ref, local_ref, image_ref, sums_ref, *face_refs):
    rows = local_ref.shape[0] // 6
    width = local_ref.shape[1]
    folds = width // LANES
    correction = select(table_ref[...], get_slab(returned_ref, folds))
    image = local_ref[...] + product((high_ref[...], low_ref[...]), parts(correction))
    image_ref[...] = image
    put_faces(image, rows, face_refs)
    tail = jnp.sum(returned_ref[:, folds * CAP :, :], axis=0)
    if pair_depth:
        sums_ref[...] = tail
    else:
        sums_ref[...] = jnp.broadcast_to(tail[None], sums_ref.shape)


def new_direction(len_ref, beta, image_ref, prev_ref, got, face, rows):
    at = slice(face * rows, (face + 1) * rows)
    precond = 0.5 * (image_ref[at, :] + got_face(got, face))
    return jnp.where(live_rows(len_ref, face, rows), precond + beta * prev_ref[at, :], 0.0)


def near_kernel(pair_depth, scale, keys, len_ref, sums_ref, prev_rho_ref, image_ref, prev_ref, high_ref, low_ref, *refs):
    got, refs = dict(zip(keys, refs)), refs[len(keys) :]
    if pair_depth:
        sums, refs = sums_ref[...] + refs[0][...], refs[1:]
    else:
        sums = jnp.sum(sums_ref[...], axis=0)
    rho_out, beta_out, square_out, near_ref, image_out = refs
    rows = image_ref.shape[0] // 6
    folds = image_ref.shape[1] // LANES
    rho = scale * unfolded(sums, 0, folds)
    beta = rho / prev_rho_ref[...]
    rho_out[...] = rho
    beta_out[...] = beta
    square_out[...] = unfolded(sums, folds, folds)
    for i, face in enumerate((0, 1, 4, 5)):
        near_ref[i * rows : (i + 1) * rows, :] = new_direction(
            len_ref, beta, image_ref, prev_ref, got, face, rows
        )
    high, low = parts(near_ref[...])
    first, last = 2 * rows, 4 * rows
    image_out[...] = product(
        (high_ref[:, :first], low_ref[:, :first]), (high[:first], low[:first])
    ) + product((high_ref[:, last:], low_ref[:, last:]), (high[first:], low[first:]))


def far_kernel(keys, len_ref, beta_ref, image_ref, prev_ref, high_ref, low_ref, near_ref, near_image_ref, *refs):
    got, refs = dict(zip(keys, refs)), refs[len(keys) :]
    (direction_out, schur_out), face_refs, (far_ref, sems) = refs[:2], refs[2:-2], refs[-2:]
    rows = image_ref.shape[0] // 6
    first, last = 2 * rows, 4 * rows
    pair = pl.ds(0, first)
    copies = [
        pltpu.make_async_copy(near_ref.at[pair], direction_out.at[pair], sems.at[0]),
        pltpu.make_async_copy(
            near_ref.at[pl.ds(first, first)], direction_out.at[pl.ds(last, first)], sems.at[1]
        ),
        pltpu.make_async_copy(far_ref, direction_out.at[pl.ds(first, first)], sems.at[2]),
    ]
    copies[0].start()
    copies[1].start()
    beta = beta_ref[...]
    for face in (2, 3):
        far_ref[(face - 2) * rows : (face - 1) * rows, :] = new_direction(
            len_ref, beta, image_ref, prev_ref, got, face, rows
        )
    copies[2].start()
    image = near_image_ref[...] + product(
        (high_ref[:, first:last], low_ref[:, first:last]), parts(far_ref[...])
    )
    schur_out[...] = image
    put_faces(image, rows, face_refs)
    for copy in copies:
        copy.wait()


def products_kernel(len_ref, direction_ref, schur_ref, residual_ref, curve_ref, cross_ref):
    rows = schur_ref.shape[0] // 6
    image = schur_ref[...]
    live = jnp.concatenate(
        [masked(len_ref, residual_ref, face, rows) for face in range(6)], axis=0
    )
    curve_ref[...] = 2.0 * jnp.sum(direction_ref[...] * image, axis=0, keepdims=True)
    cross_ref[...] = 2.0 * jnp.sum(live * image, axis=0, keepdims=True)


def applied_kernel(len_ref, curve_ref, cross_ref, schur_ref, *refs):
    got, (applied_ref, spread_ref) = dict(zip(moves(), refs)), refs[-2:]
    rows = schur_ref.shape[0] // 6
    total = jnp.zeros(curve_ref.shape, f32)
    for face in range(6):
        at = slice(face * rows, (face + 1) * rows)
        applied = schur_ref[at, :] + got_face(got, face)
        applied = jnp.where(live_rows(len_ref, face, rows), applied, 0.0)
        applied_ref[at, :] = applied
        total += jnp.sum(applied * applied, axis=0, keepdims=True)
    for i, vector in enumerate([curve_ref[...], cross_ref[...], total]):
        for j, piece in enumerate(folded(vector)):
            spread_ref[:, i, j, :] = jnp.broadcast_to(piece, (spread_ref.shape[0], LANES))


def finish_kernel(scale, len_ref, sums_ref, rho_ref, square_ref, residual_ref, applied_ref, new_out, alpha_ref, norm_ref, new_ref, sems):
    rows = applied_ref.shape[0] // 6
    folds = sums_ref.shape[2]
    sums = jnp.sum(sums_ref[...], axis=0)
    curve, cross, square = [unfolded(sums[i], 0, folds) for i in range(3)]
    alpha = rho_ref[...] / (scale * curve)
    alpha_ref[...] = alpha
    norm_ref[...] = scale * (square_ref[...] - 2.0 * alpha * cross + alpha * alpha * square)
    copies = []
    for face in range(6):
        at = slice(face * rows, (face + 1) * rows)
        new_ref[at, :] = masked(len_ref, residual_ref, face, rows) - alpha * applied_ref[at, :]
        where = pl.ds(face * rows, rows)
        copies.append(pltpu.make_async_copy(new_ref.at[where], new_out.at[where], sems.at[face]))
        copies[-1].start()
    for copy in copies:
        copy.wait()


def to_all(x, axes):
    return lax.all_to_all(x, axes, split_axis=0, concat_axis=0, tiled=True)


def shards(
    face_len,
    residual,
    prev_direction,
    prev_rho,
    schur,
    neumann,
    coarse_basis,
    coarse_inverse,
    prim_owner,
    coarse_row,
):
    height, width = residual.shape[3:]
    rows = height // 6
    primal = coarse_basis.shape[4]
    owned = coarse_inverse.shape[3]
    owners = lax.axis_size(LAYER)
    slots = owners * CAP
    devices = lax.axis_size(AXES)
    layers = lax.axis_size("depth")
    pair_depth = layers == 2
    scale = 0.5 / (devices * height)
    folds = width // LANES
    tail = tiles(2 * folds)

    lengths = face_len.reshape(6)
    residual = residual.reshape(height, width)
    prev_direction = prev_direction.reshape(height, width)
    schur = schur.reshape(height, height)
    neumann = neumann.reshape(height, height)
    basis = coarse_basis.reshape(height, primal)
    inverse = coarse_inverse.reshape(owned, owned)
    owner = prim_owner.reshape(1, primal)
    wanted = coarse_row.reshape(1, primal)
    whole = shape_of(height, width)
    row = shape_of(1, width)
    face = shape_of(rows, width)

    (outgoing,) = call(
        pack_kernel,
        [shape_of(owners, folds * CAP + TILE, LANES)],
        [lengths, owner, wanted, residual, basis],
        far=range(5),
        flops=6 * height * primal * width,
        moved=4 * (height * (width + primal) + slots * width),
        scratch=[
            pltpu.SMEM((6,), jnp.int32),
            pltpu.VMEM((1, primal), jnp.int32),
            pltpu.VMEM((1, primal), jnp.int32),
            pltpu.VMEM((height, width), f32),
            pltpu.VMEM((height, primal), f32),
            pltpu.SemaphoreType.DMA((3, 2)),
            pltpu.SemaphoreType.DMA((3,)),
        ],
    )
    incoming = to_all(outgoing, LAYER)
    local, local_part, square, table, *halves = call(
        local_kernel,
        [whole, row, row, shape_of(primal, slots, dtype=bf16)]
        + [shape_of(height, primal, dtype=bf16)] * 2
        + [shape_of(height, height, dtype=bf16)] * 2,
        [lengths, residual, neumann, owner, basis, schur],
        smem=(0,),
        flops=6 * height * height * width,
        moved=4 * height * (3 * height + 2 * width),
    )
    basis_halves, schur_halves = halves[:2], halves[2:]
    (answers,) = call(
        solve_kernel,
        [shape_of(owners, folds * CAP + tail, LANES)],
        [incoming, inverse, local_part, square],
        far=range(2),
        flops=(8 * slots + 6 * owned) * owned * width,
        moved=8 * slots * width,
        scratch=[
            pltpu.VMEM((owners, TILE, LANES), f32),
            pltpu.VMEM((owners, folds * CAP, LANES), f32),
            pltpu.VMEM((owned, owned), f32),
            pltpu.SemaphoreType.DMA((4,)),
        ],
    )
    returned = to_all(answers, LAYER)
    keys = moves()
    faces = [face] * len(keys)
    image, sums, *outward = call(
        functools.partial(image_kernel, pair_depth),
        [whole, shape_of(tail, LANES) if pair_depth else shape_of(layers, tail, LANES), *faces],
        [returned, table, *basis_halves, local],
        flops=(6 * height + 4 * slots) * primal * width,
        moved=16 * height * width,
    )
    got = dict(zip(keys, exchange(outward)))
    if pair_depth:
        sums = [sums, lax.ppermute(sums, "depth", route("depth", 0))]
    else:
        sums = [to_all(sums, "depth")]
    near_keys = [key for key in keys if key[0] != "lat"]
    far_keys = [key for key in keys if key[0] == "lat"]
    rho, beta, square, near, near_image = call(
        functools.partial(near_kernel, pair_depth, scale, near_keys),
        [row, row, row, shape_of(4 * rows, width), whole],
        [lengths, sums[0], prev_rho.reshape(1, width), image, prev_direction, *schur_halves]
        + [got[key] for key in near_keys]
        + sums[1:],
        smem=(0,),
        flops=4 * height * height * width,
        moved=4 * height * (height + 4 * width),
    )
    direction, schur_image, *outward = call(
        functools.partial(far_kernel, far_keys),
        [whole, whole, *faces],
        [lengths, beta, image, prev_direction, *schur_halves, near, near_image]
        + [got[key] for key in far_keys],
        smem=(0,),
        far_out=(0,),
        flops=2 * height * height * width,
        moved=4 * height * (height + 4 * width),
        scratch=[pltpu.VMEM((2 * rows, width), f32), pltpu.SemaphoreType.DMA((3,))],
    )
    got = exchange(outward)
    curve, cross = call(
        products_kernel,
        [row, row],
        [lengths, direction, schur_image, residual],
        smem=(0,),
        flops=4 * height * width,
        moved=12 * height * width,
    )
    applied, spread = call(
        applied_kernel,
        [whole, shape_of(devices, 3, folds, LANES)],
        [lengths, curve, cross, schur_image, *got],
        smem=(0,),
        flops=4 * height * width,
        moved=12 * height * width,
    )
    new_residual, alpha, norm = call(
        functools.partial(finish_kernel, scale),
        [whole, row, row],
        [lengths, to_all(spread, AXES), rho, square, residual, applied],
        smem=(0,),
        far_out=(0,),
        flops=4 * height * width,
        moved=12 * height * width,
        scratch=[pltpu.VMEM((height, width), f32), pltpu.SemaphoreType.DMA((6,))],
    )
    out_shape = (1, 1, 1, height, width)
    return (
        new_residual.reshape(out_shape),
        direction.reshape(out_shape),
        rho.reshape(width),
        alpha.reshape(width),
        norm.reshape(width),
    )


def solution(mesh):
    tall = P("blk", "lat", "depth", None, None)
    flat = P("blk", "lat", "depth", None)
    in_specs = (flat, tall, tall, P(), tall, tall, tall, tall, tall, flat)
    out_specs = (tall, tall, P(), P(), P())
    return jax.shard_map(shards, mesh=mesh, in_specs=in_specs, out_specs=out_specs, check_vma=False)
```

```python
import functools

import jax
import jax.numpy as jnp
from jax import lax
from jax.experimental import pallas as pl
from jax.experimental.pallas import tpu as pltpu
from jax.sharding import PartitionSpec as P

CAP = 24
AXES = ("blk", "lat", "depth")
LAYER = ("blk", "lat")
LANES = 128
TILE = 8
f32 = jnp.float32
bf16 = jnp.bfloat16

VMEM = pl.BlockSpec(memory_space=pltpu.VMEM)
SMEM = pl.BlockSpec(memory_space=pltpu.SMEM)
ANY = pl.BlockSpec(memory_space=pl.ANY)


def shape_of(*dims, dtype=f32):
    return jax.ShapeDtypeStruct(dims, dtype)


def call(body, outs, operands, smem=(), far=(), far_out=(), flops=0, moved=0, scratch=(), room=32):
    in_specs = [SMEM if i in smem else ANY if i in far else VMEM for i in range(len(operands))]
    operands = [
        pltpu.with_memory_space_constraint(x, pltpu.HBM) if i in far else x
        for i, x in enumerate(operands)
    ]
    out_specs = [ANY if i in far_out else VMEM for i in range(len(outs))]
    return pl.pallas_call(
        body,
        out_shape=list(outs),
        in_specs=in_specs,
        out_specs=out_specs,
        scratch_shapes=list(scratch),
        compiler_params=pltpu.CompilerParams(vmem_limit_bytes=room << 20),
        cost_estimate=pl.CostEstimate(flops=flops, bytes_accessed=moved, transcendentals=0),
    )(*operands)


def parts(x):
    high = x.astype(bf16)
    low = (x - high.astype(f32)).astype(bf16)
    return high, low


def mul(a, b, dims):
    return lax.dot_general(a, b, (dims, ((), ())), preferred_element_type=f32)


PLAIN = ((1,), (0,))
LEFT_T = ((0,), (0,))


def product(a, b, dims=PLAIN):
    (ah, al), (bh, bl) = a, b
    return mul(ah, bh, dims) + (mul(ah, bl, dims) + mul(al, bh, dims))


def select(table, x, dims=PLAIN):
    high, low = parts(x)
    return mul(table, high, dims) + mul(table, low, dims)


def one_hot(hit):
    return jnp.where(hit, 1.0, 0.0).astype(bf16)


def live_rows(len_ref, face, rows):
    return lax.broadcasted_iota(jnp.int32, (rows, 1), 0) < len_ref[face]


def masked(len_ref, ref, face, rows):
    block = ref[face * rows : (face + 1) * rows, :]
    return jnp.where(live_rows(len_ref, face, rows), block, 0.0)


def spread(out_ref, vector):
    for j, piece in enumerate(folded(vector)):
        out_ref[:, j, :] = jnp.broadcast_to(piece, (out_ref.shape[0], LANES))


def gathered_sum(ref):
    total = jnp.sum(ref[...], axis=0)
    return unfolded(total, 0, total.shape[0])


def folded(vector):
    pieces = vector.shape[1] // LANES
    return [vector[:, j * LANES : (j + 1) * LANES] for j in range(pieces)]


def unfolded(block, first, pieces):
    return jnp.concatenate([block[first + j : first + j + 1, :] for j in range(pieces)], axis=1)


def tiles(rows):
    return -(-rows // TILE) * TILE


def put_slab(out_ref, block):
    owners = out_ref.shape[0]
    for j in range(block.shape[1] // LANES):
        piece = block[:, j * LANES : (j + 1) * LANES]
        out_ref[:, j * CAP : (j + 1) * CAP, :] = piece.reshape(owners, CAP, LANES)


def get_slab(ref, pieces):
    slots = ref.shape[0] * CAP
    return jnp.concatenate(
        [ref[:, j * CAP : (j + 1) * CAP, :].reshape(slots, LANES) for j in range(pieces)], axis=1
    )


def columns(*rows):
    spare = [jnp.zeros_like(rows[0])] * (TILE - len(rows))
    turned = jnp.transpose(jnp.concatenate([*rows, *spare], axis=0))
    return [turned[:, i : i + 1] for i in range(len(rows))]


def ranks(own_row):
    primal = own_row.shape[1]
    (own_col,) = columns(own_row)
    row_at = lax.broadcasted_iota(jnp.int32, (primal, primal), 0)
    col_at = lax.broadcasted_iota(jnp.int32, (primal, primal), 1)
    before = (own_row == own_col) & (row_at < col_at)
    return jnp.sum(jnp.where(before, 1.0, 0.0), axis=0, keepdims=True), own_col


def pack_kernel(len_any, owner_any, row_any, residual_any, basis_any, slab_ref, *refs):
    len_ref, owner_ref, row_ref, residual_ref, basis_ref, sems, small_sems = refs
    rows = residual_ref.shape[0] // 6
    primal = basis_ref.shape[1]
    owners = slab_ref.shape[0]
    slots = owners * CAP
    small = [
        pltpu.make_async_copy(src, dst, small_sems.at[i])
        for i, (src, dst) in enumerate(
            [(owner_any, owner_ref), (row_any, row_ref), (len_any, len_ref)]
        )
    ]
    large = []
    for pair in range(3):
        at = pl.ds(2 * pair * rows, 2 * rows)
        large.append(
            (
                pltpu.make_async_copy(residual_any.at[at], residual_ref.at[at], sems.at[pair, 0]),
                pltpu.make_async_copy(basis_any.at[at], basis_ref.at[at], sems.at[pair, 1]),
            )
        )
    for copy in small:
        copy.start()
    for pair in large:
        for copy in pair:
            copy.start()
    for copy in small:
        copy.wait()
    own_row = owner_ref[...].astype(f32)
    wanted_row = row_ref[...].astype(f32) + 1.0
    rank_row, _ = ranks(own_row)
    slot_row = (own_row * CAP + rank_row).astype(jnp.int32)
    rank_col, wanted_col = columns(rank_row, wanted_row)
    packer = one_hot(lax.broadcasted_iota(jnp.int32, (slots, primal), 0) == slot_row)
    to_owner = one_hot(lax.broadcasted_iota(jnp.int32, (owners, primal), 0) == owner_ref[...])
    lane_at = lax.broadcasted_iota(jnp.int32, (primal, LANES), 1)
    ranked = jnp.where(lane_at == rank_col.astype(jnp.int32), wanted_col, 0.0)
    names = select(to_owner, ranked)
    terms = None
    for pair in range(3):
        for copy in large[pair]:
            copy.wait()
        weighted = jnp.concatenate(
            [0.5 * masked(len_ref, residual_ref, 2 * pair + side, rows) for side in range(2)],
            axis=0,
        )
        basis = basis_ref[2 * pair * rows : 2 * (pair + 1) * rows, :]
        term = product(parts(basis), parts(weighted), LEFT_T)
        terms = term if terms is None else terms + term
    put_slab(slab_ref, select(packer, terms))
    tail = slab_ref.shape[1] - TILE
    slab_ref[:, tail:, :] = jnp.broadcast_to(
        names.reshape(owners, 1, LANES), (owners, TILE, LANES)
    )


def local_kernel(len_ref, residual_ref, matrix_ref, owner_ref, *refs):
    whole, refs = refs[:2], refs[2:]
    local_ref, part_ref, table_ref, refs = *refs[:3], refs[3:]
    rows = residual_ref.shape[0] // 6
    live = jnp.concatenate(
        [masked(len_ref, residual_ref, face, rows) for face in range(6)], axis=0
    )
    local = product(parts(matrix_ref[...]), parts(0.5 * live))
    local_ref[...] = local
    part_ref[...] = jnp.sum(live * local, axis=0, keepdims=True)
    for i in range(2):
        refs[2 * i][...], refs[2 * i + 1][...] = parts(whole[i][...])
    primal, slots = table_ref.shape
    rank_row, own_col = ranks(owner_ref[...].astype(f32))
    (rank_col,) = columns(rank_row)
    slot_col = (own_col * CAP + rank_col).astype(jnp.int32)
    table_ref[...] = one_hot(lax.broadcasted_iota(jnp.int32, (primal, slots), 1) == slot_col)


def picker_table(names_ref, owned):
    owners = names_ref.shape[0]
    lane_at = lax.broadcasted_iota(jnp.int32, (CAP, LANES), 1)
    rank_at = lax.broadcasted_iota(jnp.int32, (CAP, LANES), 0)
    out_at = lax.broadcasted_iota(jnp.int32, (CAP, owned), 1).astype(f32) + 1.0
    blocks = []
    for source in range(owners):
        names = names_ref[source, 0:1, :]
        named = jnp.sum(jnp.where(lane_at == rank_at, names, 0.0), axis=1, keepdims=True)
        blocks.append(jnp.where(out_at == named, 1.0, 0.0))
    return jnp.concatenate(blocks, axis=0)


def solve_kernel(incoming_any, inverse_any, local_part_ref, answer_ref, *refs):
    names_ref, slab_ref, inverse_ref, sems = refs
    owners, height, _ = slab_ref.shape
    pieces = height // CAP
    half = pieces // 2 * CAP
    copies = [
        pltpu.make_async_copy(incoming_any.at[:, pl.ds(height, TILE)], names_ref, sems.at[0]),
        pltpu.make_async_copy(
            incoming_any.at[:, pl.ds(0, half)], slab_ref.at[:, pl.ds(0, half)], sems.at[1]
        ),
        pltpu.make_async_copy(
            incoming_any.at[:, pl.ds(half, height - half)],
            slab_ref.at[:, pl.ds(half, height - half)],
            sems.at[2],
        ),
        pltpu.make_async_copy(inverse_any, inverse_ref, sems.at[3]),
    ]
    for copy in copies:
        copy.start()
    copies[0].wait()
    table = picker_table(names_ref, inverse_ref.shape[0]).astype(bf16)
    for copy in copies[1:]:
        copy.wait()
    summed = select(table, get_slab(slab_ref, pieces), LEFT_T)
    solved = product(parts(inverse_ref[...]), parts(summed))
    put_slab(answer_ref, select(table, solved))
    total = local_part_ref[...] + 2.0 * jnp.sum(summed * solved, axis=0, keepdims=True)
    sums = folded(total)
    sums += [jnp.zeros((1, LANES), f32)] * (tiles(len(sums)) - len(sums))
    answer_ref[:, pieces * CAP :, :] = jnp.broadcast_to(
        jnp.concatenate(sums, axis=0)[None], (owners, len(sums), LANES)
    )


AXIS_AT = {"blk": 0, "lat": 2, "depth": 4}


def moves():
    order = [("lat", 1), ("blk", "up"), ("lat", 0), ("depth", 1), ("depth", 0), ("blk", "down")]
    return [(axis, way) for axis, way in order if route(axis, way)]


def route(axis, way):
    devices = lax.axis_size(axis)
    if way in ("up", "down"):
        by = 1 if way == "up" else -1
        return [(i, (i + by) % devices) for i in range(devices)]
    return [pair for i in range(way, devices - 1, 2) for pair in ((i, i + 1), (i + 1, i))]


def sends_plus(axis, way):
    return lax.rem(lax.axis_index(axis), 2) == way


def put_faces(image, rows, face_refs):
    for ref, (axis, way) in zip(face_refs, moves(), strict=True):
        at = AXIS_AT[axis] * rows
        minus, plus = image[at : at + rows, :], image[at + rows : at + 2 * rows, :]
        if way in ("up", "down"):
            ref[...] = plus if way == "up" else minus
        else:
            ref[...] = jnp.where(sends_plus(axis, way), plus, minus)


def got_face(got, face):
    axis, side = ("blk", "lat", "depth")[face // 2], face % 2
    if axis == "blk":
        return got["blk", "down" if side else "up"][...]
    total = None
    for (axis_of, way), ref in got.items():
        if axis_of == axis:
            mine = sends_plus(axis, way) == (side == 1)
            piece = jnp.where(mine, ref[...], 0.0)
            total = piece if total is None else total + piece
    return total


def exchange(faces):
    return [
        lax.ppermute(block, axis, route(axis, way))
        for block, (axis, way) in zip(faces, moves(), strict=True)
    ]


def image_kernel(pair_depth, returned_ref, table_ref, high_ref, low_ref, local_ref, image_ref, sums_ref, *face_refs):
    rows = local_ref.shape[0] // 6
    width = local_ref.shape[1]
    folds = width // LANES
    correction = select(table_ref[...], get_slab(returned_ref, folds))
    image = local_ref[...] + product((high_ref[...], low_ref[...]), parts(correction))
    image_ref[...] = image
    put_faces(image, rows, face_refs)
    tail = jnp.sum(returned_ref[:, folds * CAP :, :], axis=0)
    if pair_depth:
        sums_ref[...] = tail
    else:
        sums_ref[...] = jnp.broadcast_to(tail[None], sums_ref.shape)


def new_direction(len_ref, beta, image_ref, prev_ref, got, face, rows):
    at = slice(face * rows, (face + 1) * rows)
    precond = 0.5 * (image_ref[at, :] + got_face(got, face))
    return jnp.where(live_rows(len_ref, face, rows), precond + beta * prev_ref[at, :], 0.0)


def near_kernel(pair_depth, scale, keys, len_ref, sums_ref, prev_rho_ref, image_ref, prev_ref, high_ref, low_ref, *refs):
    got, refs = dict(zip(keys, refs)), refs[len(keys) :]
    if pair_depth:
        sums, refs = sums_ref[...] + refs[0][...], refs[1:]
    else:
        sums = jnp.sum(sums_ref[...], axis=0)
    rho_out, beta_out, near_ref, image_out = refs
    rows = image_ref.shape[0] // 6
    folds = image_ref.shape[1] // LANES
    rho = scale * unfolded(sums, 0, folds)
    beta = rho / prev_rho_ref[...]
    rho_out[...] = rho
    beta_out[...] = beta
    for i, face in enumerate((0, 2, 3, 4, 5)):
        near_ref[i * rows : (i + 1) * rows, :] = new_direction(
            len_ref, beta, image_ref, prev_ref, got, face, rows
        )
    high, low = parts(near_ref[...])
    last = 2 * rows
    image_out[...] = product(
        (high_ref[:, last:], low_ref[:, last:]), (high[rows:], low[rows:])
    ) + product((high_ref[:, :rows], low_ref[:, :rows]), (high[:rows], low[:rows]))


def far_kernel(keys, len_ref, beta_ref, image_ref, prev_ref, high_ref, low_ref, near_ref, near_image_ref, *refs):
    got, refs = dict(zip(keys, refs)), refs[len(keys) :]
    far_ref, schur_out, spread_ref, *face_refs = refs
    rows = image_ref.shape[0] // 6
    far = new_direction(len_ref, beta_ref[...], image_ref, prev_ref, got, 1, rows)
    far_ref[...] = far
    at = slice(rows, 2 * rows)
    image = near_image_ref[...] + product((high_ref[:, at], low_ref[:, at]), parts(far))
    schur_out[...] = image
    put_faces(image, rows, face_refs)
    near = near_ref[...]
    curve = (
        jnp.sum(near[:rows] * image[:rows], axis=0, keepdims=True)
        + jnp.sum(far * image[at], axis=0, keepdims=True)
        + jnp.sum(near[rows:] * image[2 * rows :], axis=0, keepdims=True)
    )
    spread(spread_ref, 2.0 * curve)


def store_kernel(near_ref, far_ref, direction_out, sems):
    rows = far_ref.shape[0]
    copies = [
        pltpu.make_async_copy(
            near_ref.at[pl.ds(0, rows)], direction_out.at[pl.ds(0, rows)], sems.at[0]
        ),
        pltpu.make_async_copy(far_ref, direction_out.at[pl.ds(rows, rows)], sems.at[1]),
        pltpu.make_async_copy(
            near_ref.at[pl.ds(rows, 4 * rows)],
            direction_out.at[pl.ds(2 * rows, 4 * rows)],
            sems.at[2],
        ),
    ]
    for copy in copies:
        copy.start()
    for copy in copies:
        copy.wait()


def applied_kernel(scale, len_ref, curve_ref, rho_ref, schur_ref, residual_ref, *refs):
    got, (applied_ref, alpha_ref, spread_ref) = dict(zip(moves(), refs)), refs[-3:]
    rows = schur_ref.shape[0] // 6
    alpha = rho_ref[...] / (scale * gathered_sum(curve_ref))
    alpha_ref[...] = alpha
    total = jnp.zeros(alpha.shape, f32)
    for face in range(6):
        at = slice(face * rows, (face + 1) * rows)
        applied = schur_ref[at, :] + got_face(got, face)
        applied_ref[at, :] = applied
        new = jnp.where(
            live_rows(len_ref, face, rows), residual_ref[at, :] - alpha * applied, 0.0
        )
        total += jnp.sum(new * new, axis=0, keepdims=True)
    spread(spread_ref, total)


def residual_kernel(len_ref, alpha_ref, residual_ref, applied_ref, new_out, new_ref, sems):
    rows = applied_ref.shape[0] // 6
    alpha = alpha_ref[...]
    copies = []
    for face in range(6):
        at = slice(face * rows, (face + 1) * rows)
        new_ref[at, :] = jnp.where(
            live_rows(len_ref, face, rows), residual_ref[at, :] - alpha * applied_ref[at, :], 0.0
        )
        where = pl.ds(face * rows, rows)
        copies.append(pltpu.make_async_copy(new_ref.at[where], new_out.at[where], sems.at[face]))
        copies[-1].start()
    for copy in copies:
        copy.wait()


def norm_kernel(scale, part_ref, norm_ref):
    norm_ref[...] = scale * gathered_sum(part_ref)


def to_all(x, axes):
    return lax.all_to_all(x, axes, split_axis=0, concat_axis=0, tiled=True)


def shards(
    face_len,
    residual,
    prev_direction,
    prev_rho,
    schur,
    neumann,
    coarse_basis,
    coarse_inverse,
    prim_owner,
    coarse_row,
):
    height, width = residual.shape[3:]
    rows = height // 6
    primal = coarse_basis.shape[4]
    owned = coarse_inverse.shape[3]
    owners = lax.axis_size(LAYER)
    slots = owners * CAP
    devices = lax.axis_size(AXES)
    layers = lax.axis_size("depth")
    pair_depth = layers == 2
    scale = 0.5 / (devices * height)
    folds = width // LANES
    tail = tiles(folds)

    lengths = face_len.reshape(6)
    residual = residual.reshape(height, width)
    prev_direction = prev_direction.reshape(height, width)
    schur = schur.reshape(height, height)
    neumann = neumann.reshape(height, height)
    basis = coarse_basis.reshape(height, primal)
    inverse = coarse_inverse.reshape(owned, owned)
    owner = prim_owner.reshape(1, primal)
    wanted = coarse_row.reshape(1, primal)
    whole = shape_of(height, width)
    row = shape_of(1, width)
    face = shape_of(rows, width)
    copies = shape_of(devices, folds, LANES)

    (outgoing,) = call(
        pack_kernel,
        [shape_of(owners, folds * CAP + TILE, LANES)],
        [lengths, owner, wanted, residual, basis],
        far=range(5),
        flops=6 * height * primal * width,
        moved=4 * (height * (width + primal) + slots * width),
        scratch=[
            pltpu.SMEM((6,), jnp.int32),
            pltpu.VMEM((1, primal), jnp.int32),
            pltpu.VMEM((1, primal), jnp.int32),
            pltpu.VMEM((height, width), f32),
            pltpu.VMEM((height, primal), f32),
            pltpu.SemaphoreType.DMA((3, 2)),
            pltpu.SemaphoreType.DMA((3,)),
        ],
    )
    incoming = to_all(outgoing, LAYER)
    local, local_part, table, *halves = call(
        local_kernel,
        [whole, row, shape_of(primal, slots, dtype=bf16)]
        + [shape_of(height, primal, dtype=bf16)] * 2
        + [shape_of(height, height, dtype=bf16)] * 2,
        [lengths, residual, neumann, owner, basis, schur],
        smem=(0,),
        flops=6 * height * height * width,
        moved=4 * height * (3 * height + 2 * width),
    )
    basis_halves, schur_halves = halves[:2], halves[2:]
    (answers,) = call(
        solve_kernel,
        [shape_of(owners, folds * CAP + tail, LANES)],
        [incoming, inverse, local_part],
        far=range(2),
        flops=(8 * slots + 6 * owned) * owned * width,
        moved=8 * slots * width,
        scratch=[
            pltpu.VMEM((owners, TILE, LANES), f32),
            pltpu.VMEM((owners, folds * CAP, LANES), f32),
            pltpu.VMEM((owned, owned), f32),
            pltpu.SemaphoreType.DMA((4,)),
        ],
    )
    returned = to_all(answers, LAYER)
    keys = moves()
    faces = [face] * len(keys)
    image, sums, *outward = call(
        functools.partial(image_kernel, pair_depth),
        [whole, shape_of(tail, LANES) if pair_depth else shape_of(layers, tail, LANES), *faces],
        [returned, table, *basis_halves, local],
        flops=(6 * height + 4 * slots) * primal * width,
        moved=16 * height * width,
    )
    got = dict(zip(keys, exchange(outward)))
    if pair_depth:
        sums = [sums, lax.ppermute(sums, "depth", route("depth", 0))]
    else:
        sums = [to_all(sums, "depth")]
    near_keys = [key for key in keys if key != ("blk", "down")]
    far_keys = [("blk", "down")]
    rho, beta, near, near_image = call(
        functools.partial(near_kernel, pair_depth, scale, near_keys),
        [row, row, shape_of(5 * rows, width), whole],
        [lengths, sums[0], prev_rho.reshape(1, width), image, prev_direction, *schur_halves]
        + [got[key] for key in near_keys]
        + sums[1:],
        smem=(0,),
        flops=4 * height * height * width,
        moved=4 * height * (height + 4 * width),
    )
    far, schur_image, curve, *outward = call(
        functools.partial(far_kernel, far_keys),
        [face, whole, copies, *faces],
        [lengths, beta, image, prev_direction, *schur_halves, near, near_image]
        + [got[key] for key in far_keys],
        smem=(0,),
        flops=height * height * width,
        moved=4 * height * (height + 4 * width),
    )
    got = exchange(outward)
    curve = to_all(curve, AXES)
    (direction,) = call(
        store_kernel,
        [whole],
        [near, far],
        far_out=(0,),
        moved=8 * height * width,
        scratch=[pltpu.SemaphoreType.DMA((3,))],
    )
    applied, alpha, norm_parts = call(
        functools.partial(applied_kernel, scale),
        [whole, row, copies],
        [lengths, curve, rho, schur_image, residual, *got],
        smem=(0,),
        flops=4 * height * width,
        moved=12 * height * width,
    )
    norm_parts = to_all(norm_parts, AXES)
    (new_residual,) = call(
        residual_kernel,
        [whole],
        [lengths, alpha, residual, applied],
        smem=(0,),
        far_out=(0,),
        flops=4 * height * width,
        moved=12 * height * width,
        scratch=[pltpu.VMEM((height, width), f32), pltpu.SemaphoreType.DMA((6,))],
    )
    (norm,) = call(
        functools.partial(norm_kernel, scale), [row], [norm_parts], moved=4 * devices * width
    )
    out_shape = (1, 1, 1, height, width)
    return (
        new_residual.reshape(out_shape),
        direction.reshape(out_shape),
        rho.reshape(width),
        alpha.reshape(width),
        norm.reshape(width),
    )


def solution(mesh):
    tall = P("blk", "lat", "depth", None, None)
    flat = P("blk", "lat", "depth", None)
    in_specs = (flat, tall, tall, P(), tall, tall, tall, tall, tall, flat)
    out_specs = (tall, tall, P(), P(), P())
    return jax.shard_map(shards, mesh=mesh, in_specs=in_specs, out_specs=out_specs, check_vma=False)
```

```python
import functools

import jax
import jax.numpy as jnp
from jax import lax
from jax.experimental import pallas as pl
from jax.experimental.pallas import tpu as pltpu
from jax.sharding import PartitionSpec as P

CAP = 24
AXES = ("blk", "lat", "depth")
LAYER = ("blk", "lat")
LANES = 128
TILE = 8
f32 = jnp.float32
bf16 = jnp.bfloat16

VMEM = pl.BlockSpec(memory_space=pltpu.VMEM)
SMEM = pl.BlockSpec(memory_space=pltpu.SMEM)
ANY = pl.BlockSpec(memory_space=pl.ANY)


def shape_of(*dims, dtype=f32):
    return jax.ShapeDtypeStruct(dims, dtype)


def call(body, outs, operands, smem=(), far=(), loose=(), far_out=(), flops=0, moved=0, scratch=(), room=32):
    in_specs = [
        SMEM if i in smem else ANY if i in far or i in loose else VMEM
        for i in range(len(operands))
    ]
    operands = [
        pltpu.with_memory_space_constraint(x, pltpu.HBM) if i in far else x
        for i, x in enumerate(operands)
    ]
    out_specs = [ANY if i in far_out else VMEM for i in range(len(outs))]
    return pl.pallas_call(
        body,
        out_shape=list(outs),
        in_specs=in_specs,
        out_specs=out_specs,
        scratch_shapes=list(scratch),
        compiler_params=pltpu.CompilerParams(vmem_limit_bytes=room << 20),
        cost_estimate=pl.CostEstimate(flops=flops, bytes_accessed=moved, transcendentals=0),
    )(*operands)


def parts(x):
    high = x.astype(bf16)
    low = (x - high.astype(f32)).astype(bf16)
    return high, low


def mul(a, b, dims):
    return lax.dot_general(a, b, (dims, ((), ())), preferred_element_type=f32)


PLAIN = ((1,), (0,))
LEFT_T = ((0,), (0,))


def product(a, b, dims=PLAIN):
    (ah, al), (bh, bl) = a, b
    return mul(ah, bh, dims) + (mul(ah, bl, dims) + mul(al, bh, dims))


def select(table, x, dims=PLAIN):
    high, low = parts(x)
    return mul(table, high, dims) + mul(table, low, dims)


def one_hot(hit):
    return jnp.where(hit, 1.0, 0.0).astype(bf16)


def live_rows(len_ref, face, rows):
    return lax.broadcasted_iota(jnp.int32, (rows, 1), 0) < len_ref[face]


def masked(len_ref, ref, face, rows):
    block = ref[face * rows : (face + 1) * rows, :]
    return jnp.where(live_rows(len_ref, face, rows), block, 0.0)


def folded(vector):
    pieces = vector.shape[1] // LANES
    return [vector[:, j * LANES : (j + 1) * LANES] for j in range(pieces)]


def unfolded(block, first, pieces):
    return jnp.concatenate([block[first + j : first + j + 1, :] for j in range(pieces)], axis=1)


def tiles(rows):
    return -(-rows // TILE) * TILE


def put_slab(out_ref, block):
    owners = out_ref.shape[0]
    for j in range(block.shape[1] // LANES):
        piece = block[:, j * LANES : (j + 1) * LANES]
        out_ref[:, j * CAP : (j + 1) * CAP, :] = piece.reshape(owners, CAP, LANES)


def get_slab(ref, pieces):
    slots = ref.shape[0] * CAP
    return jnp.concatenate(
        [ref[:, j * CAP : (j + 1) * CAP, :].reshape(slots, LANES) for j in range(pieces)], axis=1
    )


def columns(*rows):
    spare = [jnp.zeros_like(rows[0])] * (TILE - len(rows))
    turned = jnp.transpose(jnp.concatenate([*rows, *spare], axis=0))
    return [turned[:, i : i + 1] for i in range(len(rows))]


def ranks(own_row):
    primal = own_row.shape[1]
    (own_col,) = columns(own_row)
    row_at = lax.broadcasted_iota(jnp.int32, (primal, primal), 0)
    col_at = lax.broadcasted_iota(jnp.int32, (primal, primal), 1)
    before = (own_row == own_col) & (row_at < col_at)
    return jnp.sum(jnp.where(before, 1.0, 0.0), axis=0, keepdims=True), own_col


def pack_kernel(len_any, owner_any, row_any, residual_any, basis_any, slab_ref, *refs):
    len_ref, owner_ref, row_ref, residual_ref, basis_ref, sems, small_sems = refs
    rows = residual_ref.shape[0] // 6
    primal = basis_ref.shape[1]
    owners = slab_ref.shape[0]
    slots = owners * CAP
    small = [
        pltpu.make_async_copy(src, dst, small_sems.at[i])
        for i, (src, dst) in enumerate(
            [(owner_any, owner_ref), (row_any, row_ref), (len_any, len_ref)]
        )
    ]
    large = []
    for pair in range(3):
        at = pl.ds(2 * pair * rows, 2 * rows)
        large.append(
            (
                pltpu.make_async_copy(residual_any.at[at], residual_ref.at[at], sems.at[pair, 0]),
                pltpu.make_async_copy(basis_any.at[at], basis_ref.at[at], sems.at[pair, 1]),
            )
        )
    for copy in small:
        copy.start()
    for pair in large:
        for copy in pair:
            copy.start()
    for copy in small:
        copy.wait()
    own_row = owner_ref[...].astype(f32)
    wanted_row = row_ref[...].astype(f32) + 1.0
    rank_row, _ = ranks(own_row)
    slot_row = (own_row * CAP + rank_row).astype(jnp.int32)
    rank_col, wanted_col = columns(rank_row, wanted_row)
    packer = one_hot(lax.broadcasted_iota(jnp.int32, (slots, primal), 0) == slot_row)
    to_owner = one_hot(lax.broadcasted_iota(jnp.int32, (owners, primal), 0) == owner_ref[...])
    lane_at = lax.broadcasted_iota(jnp.int32, (primal, LANES), 1)
    ranked = jnp.where(lane_at == rank_col.astype(jnp.int32), wanted_col, 0.0)
    names = select(to_owner, ranked)
    terms = None
    for pair in range(3):
        for copy in large[pair]:
            copy.wait()
        weighted = jnp.concatenate(
            [0.5 * masked(len_ref, residual_ref, 2 * pair + side, rows) for side in range(2)],
            axis=0,
        )
        basis = basis_ref[2 * pair * rows : 2 * (pair + 1) * rows, :]
        term = product(parts(basis), parts(weighted), LEFT_T)
        terms = term if terms is None else terms + term
    put_slab(slab_ref, select(packer, terms))
    tail = slab_ref.shape[1] - TILE
    slab_ref[:, tail:, :] = jnp.broadcast_to(
        names.reshape(owners, 1, LANES), (owners, TILE, LANES)
    )


def local_kernel(len_ref, residual_ref, matrix_ref, owner_ref, *refs):
    whole, refs = refs[:2], refs[2:]
    local_ref, part_ref, square_ref, table_ref, refs = *refs[:4], refs[4:]
    rows = residual_ref.shape[0] // 6
    live = jnp.concatenate(
        [masked(len_ref, residual_ref, face, rows) for face in range(6)], axis=0
    )
    local = product(parts(matrix_ref[...]), parts(0.5 * live))
    local_ref[...] = local
    part_ref[...] = jnp.sum(live * local, axis=0, keepdims=True)
    square_ref[...] = jnp.sum(live * live, axis=0, keepdims=True)
    for i in range(2):
        refs[2 * i][...], refs[2 * i + 1][...] = parts(whole[i][...])
    primal, slots = table_ref.shape
    rank_row, own_col = ranks(owner_ref[...].astype(f32))
    (rank_col,) = columns(rank_row)
    slot_col = (own_col * CAP + rank_col).astype(jnp.int32)
    table_ref[...] = one_hot(lax.broadcasted_iota(jnp.int32, (primal, slots), 1) == slot_col)


def picker_table(names_ref, owned):
    owners = names_ref.shape[0]
    lane_at = lax.broadcasted_iota(jnp.int32, (CAP, LANES), 1)
    rank_at = lax.broadcasted_iota(jnp.int32, (CAP, LANES), 0)
    out_at = lax.broadcasted_iota(jnp.int32, (CAP, owned), 1).astype(f32) + 1.0
    blocks = []
    for source in range(owners):
        names = names_ref[source, 0:1, :]
        named = jnp.sum(jnp.where(lane_at == rank_at, names, 0.0), axis=1, keepdims=True)
        blocks.append(jnp.where(out_at == named, 1.0, 0.0))
    return jnp.concatenate(blocks, axis=0)


def solve_kernel(incoming_any, inverse_any, local_part_ref, square_ref, answer_ref, *refs):
    names_ref, slab_ref, inverse_ref, sems = refs
    owners, height, _ = slab_ref.shape
    pieces = height // CAP
    half = pieces // 2 * CAP
    copies = [
        pltpu.make_async_copy(incoming_any.at[:, pl.ds(height, TILE)], names_ref, sems.at[0]),
        pltpu.make_async_copy(
            incoming_any.at[:, pl.ds(0, half)], slab_ref.at[:, pl.ds(0, half)], sems.at[1]
        ),
        pltpu.make_async_copy(
            incoming_any.at[:, pl.ds(half, height - half)],
            slab_ref.at[:, pl.ds(half, height - half)],
            sems.at[2],
        ),
        pltpu.make_async_copy(inverse_any, inverse_ref, sems.at[3]),
    ]
    for copy in copies:
        copy.start()
    copies[0].wait()
    table = picker_table(names_ref, inverse_ref.shape[0]).astype(bf16)
    for copy in copies[1:]:
        copy.wait()
    summed = select(table, get_slab(slab_ref, pieces), LEFT_T)
    solved = product(parts(inverse_ref[...]), parts(summed))
    put_slab(answer_ref, select(table, solved))
    total = local_part_ref[...] + 2.0 * jnp.sum(summed * solved, axis=0, keepdims=True)
    sums = folded(total) + folded(square_ref[...])
    sums += [jnp.zeros((1, LANES), f32)] * (tiles(len(sums)) - len(sums))
    answer_ref[:, pieces * CAP :, :] = jnp.broadcast_to(
        jnp.concatenate(sums, axis=0)[None], (owners, len(sums), LANES)
    )


AXIS_AT = {"blk": 0, "lat": 2, "depth": 4}


FIRST = [("lat", 1), ("blk", "up"), ("lat", 0), ("depth", 1), ("depth", 0), ("blk", "down")]
SECOND = [("blk", "up"), ("lat", 1), ("blk", "down"), ("lat", 0), ("depth", 1), ("depth", 0)]


def moves(order):
    return [(axis, way) for axis, way in order if route(axis, way)]


def route(axis, way):
    devices = lax.axis_size(axis)
    if way in ("up", "down"):
        by = 1 if way == "up" else -1
        return [(i, (i + by) % devices) for i in range(devices)]
    return [pair for i in range(way, devices - 1, 2) for pair in ((i, i + 1), (i + 1, i))]


def sends_plus(axis, way):
    return lax.rem(lax.axis_index(axis), 2) == way


def put_faces(image, rows, order, face_refs):
    for ref, (axis, way) in zip(face_refs, moves(order), strict=True):
        at = AXIS_AT[axis] * rows
        minus, plus = image[at : at + rows, :], image[at + rows : at + 2 * rows, :]
        if way in ("up", "down"):
            ref[...] = plus if way == "up" else minus
        else:
            ref[...] = jnp.where(sends_plus(axis, way), plus, minus)


def got_face(got, face):
    axis, side = ("blk", "lat", "depth")[face // 2], face % 2
    if axis == "blk":
        return got["blk", "down" if side else "up"][...]
    total = None
    for (axis_of, way), ref in got.items():
        if axis_of == axis:
            mine = sends_plus(axis, way) == (side == 1)
            piece = jnp.where(mine, ref[...], 0.0)
            total = piece if total is None else total + piece
    return total


def exchange(faces, order):
    return [
        lax.ppermute(block, axis, route(axis, way))
        for block, (axis, way) in zip(faces, moves(order), strict=True)
    ]


def image_kernel(pair_depth, returned_ref, table_ref, high_ref, low_ref, local_ref, image_ref, sums_ref, *face_refs):
    rows = local_ref.shape[0] // 6
    width = local_ref.shape[1]
    folds = width // LANES
    correction = select(table_ref[...], get_slab(returned_ref, folds))
    image = local_ref[...] + product((high_ref[...], low_ref[...]), parts(correction))
    image_ref[...] = image
    put_faces(image, rows, FIRST, face_refs)
    tail = jnp.sum(returned_ref[:, folds * CAP :, :], axis=0)
    if pair_depth:
        sums_ref[...] = tail
    else:
        sums_ref[...] = jnp.broadcast_to(tail[None], sums_ref.shape)


def new_direction(len_ref, beta, image_ref, prev_ref, got, face, rows):
    at = slice(face * rows, (face + 1) * rows)
    precond = 0.5 * (image_ref[at, :] + got_face(got, face))
    return jnp.where(live_rows(len_ref, face, rows), precond + beta * prev_ref[at, :], 0.0)


def near_kernel(pair_depth, scale, keys, len_ref, sums_ref, prev_rho_ref, image_ref, prev_ref, high_ref, low_ref, *refs):
    got, refs = dict(zip(keys, refs)), refs[len(keys) :]
    if pair_depth:
        sums, refs = sums_ref[...] + refs[0][...], refs[1:]
    else:
        sums = jnp.sum(sums_ref[...], axis=0)
    rho_out, beta_out, square_out, near_ref, image_out = refs
    rows = image_ref.shape[0] // 6
    folds = image_ref.shape[1] // LANES
    rho = scale * unfolded(sums, 0, folds)
    beta = rho / prev_rho_ref[...]
    rho_out[...] = rho
    beta_out[...] = beta
    square_out[...] = unfolded(sums, folds, folds)
    for i, face in enumerate((0, 2, 3, 4, 5)):
        near_ref[i * rows : (i + 1) * rows, :] = new_direction(
            len_ref, beta, image_ref, prev_ref, got, face, rows
        )
    high, low = parts(near_ref[...])
    last = 2 * rows
    image_out[...] = product(
        (high_ref[:, last:], low_ref[:, last:]), (high[rows:], low[rows:])
    ) + product((high_ref[:, :rows], low_ref[:, :rows]), (high[:rows], low[:rows]))


def far_kernel(keys, len_ref, beta_ref, image_ref, prev_ref, high_ref, low_ref, near_ref, near_image_ref, *refs):
    got, refs = dict(zip(keys, refs)), refs[len(keys) :]
    far_ref, schur_out, *face_refs = refs
    rows = image_ref.shape[0] // 6
    far = new_direction(len_ref, beta_ref[...], image_ref, prev_ref, got, 1, rows)
    far_ref[...] = far
    at = slice(rows, 2 * rows)
    image = near_image_ref[...] + product((high_ref[:, at], low_ref[:, at]), parts(far))
    schur_out[...] = image
    put_faces(image, rows, SECOND, face_refs)


def store_kernel(near_ref, far_ref, direction_out, sems):
    rows = far_ref.shape[0]
    copies = [
        pltpu.make_async_copy(
            near_ref.at[pl.ds(0, rows)], direction_out.at[pl.ds(0, rows)], sems.at[0]
        ),
        pltpu.make_async_copy(far_ref, direction_out.at[pl.ds(rows, rows)], sems.at[1]),
        pltpu.make_async_copy(
            near_ref.at[pl.ds(rows, 4 * rows)],
            direction_out.at[pl.ds(2 * rows, 4 * rows)],
            sems.at[2],
        ),
    ]
    for copy in copies:
        copy.start()
    for copy in copies:
        copy.wait()


def products_kernel(len_ref, near_ref, far_ref, schur_ref, residual_ref, arrived, out_ref):
    rows = far_ref.shape[0]
    image = schur_ref[...]
    near = near_ref[...]
    direction = jnp.concatenate([near[:rows], far_ref[...], near[rows:]], axis=0)
    live = jnp.concatenate(
        [masked(len_ref, residual_ref, face, rows) for face in range(6)], axis=0
    )
    curve = 2.0 * jnp.sum(direction * image, axis=0, keepdims=True)
    cross = 2.0 * jnp.sum(live * image, axis=0, keepdims=True)
    for j, piece in enumerate(folded(curve) + folded(cross)):
        out_ref[j : j + 1, :] = piece


def applied_kernel(pair_depth, len_ref, schur_ref, *refs):
    keys = moves(SECOND)
    got, refs = dict(zip(keys, refs)), refs[len(keys) :]
    products, (applied_ref, spread_ref) = refs[:-2], refs[-2:]
    rows = schur_ref.shape[0] // 6
    folds = schur_ref.shape[1] // LANES
    total = jnp.zeros((1, schur_ref.shape[1]), f32)
    for face in range(6):
        at = slice(face * rows, (face + 1) * rows)
        applied = schur_ref[at, :] + got_face(got, face)
        applied = jnp.where(live_rows(len_ref, face, rows), applied, 0.0)
        applied_ref[at, :] = applied
        total += jnp.sum(applied * applied, axis=0, keepdims=True)
    products = sum(ref[...] for ref in products)
    halves = [products[:folds], products[folds : 2 * folds]]
    if pair_depth:
        halves = [jnp.where(lax.axis_index("depth") == 0, *halves)]
    for i, half in enumerate([*halves, jnp.concatenate(folded(total), axis=0)]):
        spread_ref[:, i, :, :] = jnp.broadcast_to(half[None], (spread_ref.shape[0], folds, LANES))


def finish_kernel(pair_depth, scale, len_ref, sums_ref, rho_ref, square_ref, residual_ref, applied_ref, new_out, alpha_ref, norm_ref, new_ref, sems):
    rows = applied_ref.shape[0] // 6
    devices, _, folds, _ = sums_ref.shape
    if pair_depth:
        pairs = sums_ref[...].reshape(devices // 2, 2, 2, folds, LANES)
        pairs = jnp.sum(pairs, axis=0)
        sums = [pairs[0, 0], pairs[1, 0], pairs[0, 1] + pairs[1, 1]]
    else:
        total = jnp.sum(sums_ref[...], axis=0)
        sums = [total[i] for i in range(3)]
    curve, cross, applied_square = [unfolded(x, 0, folds) for x in sums]
    alpha = rho_ref[...] / (scale * curve)
    alpha_ref[...] = alpha
    norm_ref[...] = scale * (
        square_ref[...] - 2.0 * alpha * cross + alpha * alpha * applied_square
    )
    copies = []
    for face in range(6):
        at = slice(face * rows, (face + 1) * rows)
        new_ref[at, :] = masked(len_ref, residual_ref, face, rows) - alpha * applied_ref[at, :]
        where = pl.ds(face * rows, rows)
        copies.append(pltpu.make_async_copy(new_ref.at[where], new_out.at[where], sems.at[face]))
        copies[-1].start()
    for copy in copies:
        copy.wait()


def to_all(x, axes):
    return lax.all_to_all(x, axes, split_axis=0, concat_axis=0, tiled=True)


def shards(
    face_len,
    residual,
    prev_direction,
    prev_rho,
    schur,
    neumann,
    coarse_basis,
    coarse_inverse,
    prim_owner,
    coarse_row,
):
    height, width = residual.shape[3:]
    rows = height // 6
    primal = coarse_basis.shape[4]
    owned = coarse_inverse.shape[3]
    owners = lax.axis_size(LAYER)
    slots = owners * CAP
    devices = lax.axis_size(AXES)
    layers = lax.axis_size("depth")
    pair_depth = layers == 2
    scale = 0.5 / (devices * height)
    folds = width // LANES
    tail = tiles(2 * folds)

    lengths = face_len.reshape(6)
    residual = residual.reshape(height, width)
    prev_direction = prev_direction.reshape(height, width)
    schur = schur.reshape(height, height)
    neumann = neumann.reshape(height, height)
    basis = coarse_basis.reshape(height, primal)
    inverse = coarse_inverse.reshape(owned, owned)
    owner = prim_owner.reshape(1, primal)
    wanted = coarse_row.reshape(1, primal)
    whole = shape_of(height, width)
    row = shape_of(1, width)
    face = shape_of(rows, width)

    (outgoing,) = call(
        pack_kernel,
        [shape_of(owners, folds * CAP + TILE, LANES)],
        [lengths, owner, wanted, residual, basis],
        far=range(5),
        flops=6 * height * primal * width,
        moved=4 * (height * (width + primal) + slots * width),
        scratch=[
            pltpu.SMEM((6,), jnp.int32),
            pltpu.VMEM((1, primal), jnp.int32),
            pltpu.VMEM((1, primal), jnp.int32),
            pltpu.VMEM((height, width), f32),
            pltpu.VMEM((height, primal), f32),
            pltpu.SemaphoreType.DMA((3, 2)),
            pltpu.SemaphoreType.DMA((3,)),
        ],
    )
    incoming = to_all(outgoing, LAYER)
    local, local_part, square, table, *halves = call(
        local_kernel,
        [whole, row, row, shape_of(primal, slots, dtype=bf16)]
        + [shape_of(height, primal, dtype=bf16)] * 2
        + [shape_of(height, height, dtype=bf16)] * 2,
        [lengths, residual, neumann, owner, basis, schur],
        smem=(0,),
        flops=6 * height * height * width,
        moved=4 * height * (3 * height + 2 * width),
    )
    basis_halves, schur_halves = halves[:2], halves[2:]
    (answers,) = call(
        solve_kernel,
        [shape_of(owners, folds * CAP + tail, LANES)],
        [incoming, inverse, local_part, square],
        far=range(2),
        flops=(8 * slots + 6 * owned) * owned * width,
        moved=8 * slots * width,
        scratch=[
            pltpu.VMEM((owners, TILE, LANES), f32),
            pltpu.VMEM((owners, folds * CAP, LANES), f32),
            pltpu.VMEM((owned, owned), f32),
            pltpu.SemaphoreType.DMA((4,)),
        ],
    )
    returned = to_all(answers, LAYER)
    keys = moves(FIRST)
    faces = [face] * len(keys)
    image, sums, *outward = call(
        functools.partial(image_kernel, pair_depth),
        [whole, shape_of(tail, LANES) if pair_depth else shape_of(layers, tail, LANES), *faces],
        [returned, table, *basis_halves, local],
        flops=(6 * height + 4 * slots) * primal * width,
        moved=16 * height * width,
    )
    got = dict(zip(keys, exchange(outward, FIRST)))
    if pair_depth:
        sums = [sums, lax.ppermute(sums, "depth", route("depth", 0))]
    else:
        sums = [to_all(sums, "depth")]
    near_keys = [key for key in keys if key != ("blk", "down")]
    far_keys = [("blk", "down")]
    rho, beta, square, near, near_image = call(
        functools.partial(near_kernel, pair_depth, scale, near_keys),
        [row, row, row, shape_of(5 * rows, width), whole],
        [lengths, sums[0], prev_rho.reshape(1, width), image, prev_direction, *schur_halves]
        + [got[key] for key in near_keys]
        + sums[1:],
        smem=(0,),
        flops=4 * height * height * width,
        moved=4 * height * (height + 4 * width),
    )
    far, schur_image, *outward = call(
        functools.partial(far_kernel, far_keys),
        [face, whole, *faces],
        [lengths, beta, image, prev_direction, *schur_halves, near, near_image]
        + [got[key] for key in far_keys],
        smem=(0,),
        flops=height * height * width,
        moved=4 * height * (height + 4 * width),
    )
    got = exchange(outward, SECOND)
    (products,) = call(
        products_kernel,
        [shape_of(2 * folds, LANES)],
        [lengths, near, far, schur_image, residual, got[0]],
        smem=(0,),
        loose=(5,),
        flops=4 * height * width,
        moved=12 * height * width,
    )
    products = [products]
    if pair_depth:
        products.append(lax.ppermute(products[0], "depth", route("depth", 0)))
    (direction,) = call(
        store_kernel,
        [whole],
        [near, far],
        far_out=(0,),
        moved=8 * height * width,
        scratch=[pltpu.SemaphoreType.DMA((3,))],
    )
    applied, spread_sums = call(
        functools.partial(applied_kernel, pair_depth),
        [whole, shape_of(devices, 2 if pair_depth else 3, folds, LANES)],
        [lengths, schur_image, *got, *products],
        smem=(0,),
        flops=4 * height * width,
        moved=12 * height * width,
    )
    new_residual, alpha, norm = call(
        functools.partial(finish_kernel, pair_depth, scale),
        [whole, row, row],
        [lengths, to_all(spread_sums, AXES), rho, square, residual, applied],
        smem=(0,),
        far_out=(0,),
        flops=4 * height * width,
        moved=12 * height * width,
        scratch=[pltpu.VMEM((height, width), f32), pltpu.SemaphoreType.DMA((6,))],
    )
    out_shape = (1, 1, 1, height, width)
    return (
        new_residual.reshape(out_shape),
        direction.reshape(out_shape),
        rho.reshape(width),
        alpha.reshape(width),
        norm.reshape(width),
    )


def solution(mesh):
    tall = P("blk", "lat", "depth", None, None)
    flat = P("blk", "lat", "depth", None)
    in_specs = (flat, tall, tall, P(), tall, tall, tall, tall, tall, flat)
    out_specs = (tall, tall, P(), P(), P())
    return jax.shard_map(shards, mesh=mesh, in_specs=in_specs, out_specs=out_specs, check_vma=False)
```

```python
import functools

import jax
import jax.numpy as jnp
from jax import lax
from jax.experimental import pallas as pl
from jax.experimental.pallas import tpu as pltpu
from jax.sharding import PartitionSpec as P

CAP = 24
AXES = ("blk", "lat", "depth")
LAYER = ("blk", "lat")
LANES = 128
TILE = 8
f32 = jnp.float32
bf16 = jnp.bfloat16

VMEM = pl.BlockSpec(memory_space=pltpu.VMEM)
SMEM = pl.BlockSpec(memory_space=pltpu.SMEM)
ANY = pl.BlockSpec(memory_space=pl.ANY)


def shape_of(*dims, dtype=f32):
    return jax.ShapeDtypeStruct(dims, dtype)


def call(body, outs, operands, smem=(), far=(), loose=(), far_out=(), flops=0, moved=0, scratch=(), room=32):
    in_specs = [
        SMEM if i in smem else ANY if i in far or i in loose else VMEM
        for i in range(len(operands))
    ]
    operands = [
        pltpu.with_memory_space_constraint(x, pltpu.HBM) if i in far else x
        for i, x in enumerate(operands)
    ]
    out_specs = [ANY if i in far_out else VMEM for i in range(len(outs))]
    return pl.pallas_call(
        body,
        out_shape=list(outs),
        in_specs=in_specs,
        out_specs=out_specs,
        scratch_shapes=list(scratch),
        compiler_params=pltpu.CompilerParams(vmem_limit_bytes=room << 20),
        cost_estimate=pl.CostEstimate(flops=flops, bytes_accessed=moved, transcendentals=0),
    )(*operands)


def parts(x):
    high = x.astype(bf16)
    low = (x - high.astype(f32)).astype(bf16)
    return high, low


def mul(a, b, dims):
    return lax.dot_general(a, b, (dims, ((), ())), preferred_element_type=f32)


PLAIN = ((1,), (0,))
LEFT_T = ((0,), (0,))


def product(a, b, dims=PLAIN):
    (ah, al), (bh, bl) = a, b
    return mul(ah, bh, dims) + (mul(ah, bl, dims) + mul(al, bh, dims))


def select(table, x, dims=PLAIN):
    high, low = parts(x)
    return mul(table, high, dims) + mul(table, low, dims)


def one_hot(hit):
    return jnp.where(hit, 1.0, 0.0).astype(bf16)


def live_rows(len_ref, face, rows):
    return lax.broadcasted_iota(jnp.int32, (rows, 1), 0) < len_ref[face]


def masked(len_ref, ref, face, rows):
    block = ref[face * rows : (face + 1) * rows, :]
    return jnp.where(live_rows(len_ref, face, rows), block, 0.0)


def folded(vector):
    pieces = vector.shape[1] // LANES
    return [vector[:, j * LANES : (j + 1) * LANES] for j in range(pieces)]


def unfolded(block, first, pieces):
    return jnp.concatenate([block[first + j : first + j + 1, :] for j in range(pieces)], axis=1)


def tiles(rows):
    return -(-rows // TILE) * TILE


def put_slab(out_ref, block):
    owners = out_ref.shape[0]
    for j in range(block.shape[1] // LANES):
        piece = block[:, j * LANES : (j + 1) * LANES]
        out_ref[:, j * CAP : (j + 1) * CAP, :] = piece.reshape(owners, CAP, LANES)


def get_slab(ref, pieces):
    slots = ref.shape[0] * CAP
    return jnp.concatenate(
        [ref[:, j * CAP : (j + 1) * CAP, :].reshape(slots, LANES) for j in range(pieces)], axis=1
    )


def columns(*rows):
    spare = [jnp.zeros_like(rows[0])] * (TILE - len(rows))
    turned = jnp.transpose(jnp.concatenate([*rows, *spare], axis=0))
    return [turned[:, i : i + 1] for i in range(len(rows))]


def ranks(own_row):
    primal = own_row.shape[1]
    (own_col,) = columns(own_row)
    row_at = lax.broadcasted_iota(jnp.int32, (primal, primal), 0)
    col_at = lax.broadcasted_iota(jnp.int32, (primal, primal), 1)
    before = (own_row == own_col) & (row_at < col_at)
    return jnp.sum(jnp.where(before, 1.0, 0.0), axis=0, keepdims=True), own_col


def pack_kernel(len_any, owner_any, row_any, residual_any, basis_any, slab_ref, *refs):
    len_ref, owner_ref, row_ref, residual_ref, basis_ref, sems, small_sems = refs
    rows = residual_ref.shape[0] // 6
    primal = basis_ref.shape[1]
    owners = slab_ref.shape[0]
    slots = owners * CAP
    small = [
        pltpu.make_async_copy(src, dst, small_sems.at[i])
        for i, (src, dst) in enumerate(
            [(owner_any, owner_ref), (row_any, row_ref), (len_any, len_ref)]
        )
    ]
    large = []
    for pair in range(3):
        at = pl.ds(2 * pair * rows, 2 * rows)
        large.append(
            (
                pltpu.make_async_copy(residual_any.at[at], residual_ref.at[at], sems.at[pair, 0]),
                pltpu.make_async_copy(basis_any.at[at], basis_ref.at[at], sems.at[pair, 1]),
            )
        )
    for copy in small:
        copy.start()
    for pair in large:
        for copy in pair:
            copy.start()
    for copy in small:
        copy.wait()
    own_row = owner_ref[...].astype(f32)
    wanted_row = row_ref[...].astype(f32) + 1.0
    rank_row, _ = ranks(own_row)
    slot_row = (own_row * CAP + rank_row).astype(jnp.int32)
    rank_col, wanted_col = columns(rank_row, wanted_row)
    packer = one_hot(lax.broadcasted_iota(jnp.int32, (slots, primal), 0) == slot_row)
    to_owner = one_hot(lax.broadcasted_iota(jnp.int32, (owners, primal), 0) == owner_ref[...])
    lane_at = lax.broadcasted_iota(jnp.int32, (primal, LANES), 1)
    ranked = jnp.where(lane_at == rank_col.astype(jnp.int32), wanted_col, 0.0)
    names = select(to_owner, ranked)
    terms = None
    for pair in range(3):
        for copy in large[pair]:
            copy.wait()
        weighted = jnp.concatenate(
            [0.5 * masked(len_ref, residual_ref, 2 * pair + side, rows) for side in range(2)],
            axis=0,
        )
        basis = basis_ref[2 * pair * rows : 2 * (pair + 1) * rows, :]
        term = product(parts(basis), parts(weighted), LEFT_T)
        terms = term if terms is None else terms + term
    put_slab(slab_ref, select(packer, terms))
    tail = slab_ref.shape[1] - TILE
    slab_ref[:, tail:, :] = jnp.broadcast_to(
        names.reshape(owners, 1, LANES), (owners, TILE, LANES)
    )


def local_kernel(len_ref, residual_ref, matrix_ref, owner_ref, *refs):
    whole, refs = refs[:2], refs[2:]
    local_ref, part_ref, square_ref, table_ref, refs = *refs[:4], refs[4:]
    rows = residual_ref.shape[0] // 6
    live = jnp.concatenate(
        [masked(len_ref, residual_ref, face, rows) for face in range(6)], axis=0
    )
    local = product(parts(matrix_ref[...]), parts(0.5 * live))
    local_ref[...] = local
    part_ref[...] = jnp.sum(live * local, axis=0, keepdims=True)
    square_ref[...] = jnp.sum(live * live, axis=0, keepdims=True)
    refs[0][...], refs[1][...] = parts(whole[0][...])
    for i, face in enumerate(NEAR + FAR):
        at = slice(i * rows, (i + 1) * rows)
        refs[2][:, at], refs[3][:, at] = parts(whole[1][:, face * rows : (face + 1) * rows])
    primal, slots = table_ref.shape
    rank_row, own_col = ranks(owner_ref[...].astype(f32))
    (rank_col,) = columns(rank_row)
    slot_col = (own_col * CAP + rank_col).astype(jnp.int32)
    table_ref[...] = one_hot(lax.broadcasted_iota(jnp.int32, (primal, slots), 1) == slot_col)


def picker_table(names_ref, owned):
    owners = names_ref.shape[0]
    lane_at = lax.broadcasted_iota(jnp.int32, (CAP, LANES), 1)
    rank_at = lax.broadcasted_iota(jnp.int32, (CAP, LANES), 0)
    out_at = lax.broadcasted_iota(jnp.int32, (CAP, owned), 1).astype(f32) + 1.0
    blocks = []
    for source in range(owners):
        names = names_ref[source, 0:1, :]
        named = jnp.sum(jnp.where(lane_at == rank_at, names, 0.0), axis=1, keepdims=True)
        blocks.append(jnp.where(out_at == named, 1.0, 0.0))
    return jnp.concatenate(blocks, axis=0)


def solve_kernel(incoming_any, inverse_any, local_part_ref, square_ref, answer_ref, *refs):
    names_ref, slab_ref, inverse_ref, sems = refs
    owners, height, _ = slab_ref.shape
    pieces = height // CAP
    half = pieces // 2 * CAP
    copies = [
        pltpu.make_async_copy(incoming_any.at[:, pl.ds(height, TILE)], names_ref, sems.at[0]),
        pltpu.make_async_copy(
            incoming_any.at[:, pl.ds(0, half)], slab_ref.at[:, pl.ds(0, half)], sems.at[1]
        ),
        pltpu.make_async_copy(
            incoming_any.at[:, pl.ds(half, height - half)],
            slab_ref.at[:, pl.ds(half, height - half)],
            sems.at[2],
        ),
        pltpu.make_async_copy(inverse_any, inverse_ref, sems.at[3]),
    ]
    for copy in copies:
        copy.start()
    copies[0].wait()
    table = picker_table(names_ref, inverse_ref.shape[0]).astype(bf16)
    for copy in copies[1:]:
        copy.wait()
    summed = select(table, get_slab(slab_ref, pieces), LEFT_T)
    solved = product(parts(inverse_ref[...]), parts(summed))
    put_slab(answer_ref, select(table, solved))
    total = local_part_ref[...] + 2.0 * jnp.sum(summed * solved, axis=0, keepdims=True)
    sums = folded(total) + folded(square_ref[...])
    sums += [jnp.zeros((1, LANES), f32)] * (tiles(len(sums)) - len(sums))
    answer_ref[:, pieces * CAP :, :] = jnp.broadcast_to(
        jnp.concatenate(sums, axis=0)[None], (owners, len(sums), LANES)
    )


AXIS_AT = {"blk": 0, "lat": 2, "depth": 4}


FIRST = [("blk", "up"), ("lat", "up"), ("depth", 1), ("depth", 0), ("blk", "down"), ("lat", "down")]
SECOND = [("blk", "up"), ("lat", "up"), ("blk", "down"), ("lat", "down"), ("depth", 1), ("depth", 0)]
NEAR = (0, 2, 4, 5)
FAR = (1, 3)


def moves(order):
    return [(axis, way) for axis, way in order if route(axis, way)]


def route(axis, way):
    devices = lax.axis_size(axis)
    if way in ("up", "down"):
        by = 1 if way == "up" else -1
        ends = [(i, i + by) for i in range(devices)]
        return [(i, j % devices) for i, j in ends if axis == "blk" or j in range(devices)]
    return [pair for i in range(way, devices - 1, 2) for pair in ((i, i + 1), (i + 1, i))]


def sends_plus(axis, way):
    return lax.rem(lax.axis_index(axis), 2) == way


def put_faces(image, rows, order, face_refs):
    for ref, (axis, way) in zip(face_refs, moves(order), strict=True):
        at = AXIS_AT[axis] * rows
        minus, plus = image[at : at + rows, :], image[at + rows : at + 2 * rows, :]
        if way in ("up", "down"):
            ref[...] = plus if way == "up" else minus
        else:
            ref[...] = jnp.where(sends_plus(axis, way), plus, minus)


def got_face(got, face):
    axis, side = ("blk", "lat", "depth")[face // 2], face % 2
    if axis != "depth":
        return got[axis, "down" if side else "up"][...]
    total = None
    for way in (0, 1):
        if (axis, way) in got:
            mine = sends_plus(axis, way) == (side == 1)
            piece = jnp.where(mine, got[axis, way][...], 0.0)
            total = piece if total is None else total + piece
    return total


def exchange(faces, order):
    return [
        lax.ppermute(block, axis, route(axis, way))
        for block, (axis, way) in zip(faces, moves(order), strict=True)
    ]


def image_kernel(pair_depth, returned_ref, table_ref, high_ref, low_ref, local_ref, image_ref, sums_ref, *face_refs):
    rows = local_ref.shape[0] // 6
    width = local_ref.shape[1]
    folds = width // LANES
    correction = select(table_ref[...], get_slab(returned_ref, folds))
    image = local_ref[...] + product((high_ref[...], low_ref[...]), parts(correction))
    image_ref[...] = image
    put_faces(image, rows, FIRST, face_refs)
    tail = jnp.sum(returned_ref[:, folds * CAP :, :], axis=0)
    if pair_depth:
        sums_ref[...] = tail
    else:
        sums_ref[...] = jnp.broadcast_to(tail[None], sums_ref.shape)


def new_direction(len_ref, beta, image_ref, prev_ref, got, face, rows):
    at = slice(face * rows, (face + 1) * rows)
    precond = 0.5 * (image_ref[at, :] + got_face(got, face))
    return jnp.where(live_rows(len_ref, face, rows), precond + beta * prev_ref[at, :], 0.0)


def near_kernel(pair_depth, scale, keys, len_ref, sums_ref, prev_rho_ref, image_ref, prev_ref, high_ref, low_ref, *refs):
    got, refs = dict(zip(keys, refs)), refs[len(keys) :]
    if pair_depth:
        sums, refs = sums_ref[...] + refs[0][...], refs[1:]
    else:
        sums = jnp.sum(sums_ref[...], axis=0)
    rho_out, beta_out, square_out, near_ref, image_out = refs
    rows = image_ref.shape[0] // 6
    folds = image_ref.shape[1] // LANES
    rho = scale * unfolded(sums, 0, folds)
    beta = rho / prev_rho_ref[...]
    rho_out[...] = rho
    beta_out[...] = beta
    square_out[...] = unfolded(sums, folds, folds)
    for i, face in enumerate(NEAR):
        near_ref[i * rows : (i + 1) * rows, :] = new_direction(
            len_ref, beta, image_ref, prev_ref, got, face, rows
        )
    first = len(NEAR) * rows
    image_out[...] = product((high_ref[:, :first], low_ref[:, :first]), parts(near_ref[...]))


def far_kernel(keys, len_ref, beta_ref, image_ref, prev_ref, high_ref, low_ref, near_ref, near_image_ref, *refs):
    got, refs = dict(zip(keys, refs)), refs[len(keys) :]
    far_ref, schur_out, *face_refs = refs
    rows = image_ref.shape[0] // 6
    beta = beta_ref[...]
    for i, face in enumerate(FAR):
        far_ref[i * rows : (i + 1) * rows, :] = new_direction(
            len_ref, beta, image_ref, prev_ref, got, face, rows
        )
    first = len(NEAR) * rows
    image = near_image_ref[...] + product(
        (high_ref[:, first:], low_ref[:, first:]), parts(far_ref[...])
    )
    schur_out[...] = image
    put_faces(image, rows, SECOND, face_refs)


def store_kernel(near_ref, far_ref, direction_out, sems):
    rows = far_ref.shape[0] // len(FAR)
    copies = []
    for ref, faces in ((near_ref, NEAR), (far_ref, FAR)):
        for i, face in enumerate(faces):
            copies.append(
                pltpu.make_async_copy(
                    ref.at[pl.ds(i * rows, rows)],
                    direction_out.at[pl.ds(face * rows, rows)],
                    sems.at[face],
                )
            )
    for copy in copies:
        copy.start()
    for copy in copies:
        copy.wait()


def products_kernel(len_ref, near_ref, far_ref, schur_ref, residual_ref, arrived, out_ref):
    rows = schur_ref.shape[0] // 6
    image = schur_ref[...]
    blocks = {}
    for ref, faces in ((near_ref, NEAR), (far_ref, FAR)):
        for i, face in enumerate(faces):
            blocks[face] = ref[i * rows : (i + 1) * rows, :]
    direction = jnp.concatenate([blocks[face] for face in range(6)], axis=0)
    live = jnp.concatenate(
        [masked(len_ref, residual_ref, face, rows) for face in range(6)], axis=0
    )
    curve = 2.0 * jnp.sum(direction * image, axis=0, keepdims=True)
    cross = 2.0 * jnp.sum(live * image, axis=0, keepdims=True)
    for j, piece in enumerate(folded(curve) + folded(cross)):
        out_ref[j : j + 1, :] = piece


def applied_kernel(pair_depth, len_ref, stored, schur_ref, *refs):
    keys = moves(SECOND)
    got, refs = dict(zip(keys, refs)), refs[len(keys) :]
    products, (applied_ref, spread_ref) = refs[:-2], refs[-2:]
    rows = schur_ref.shape[0] // 6
    folds = schur_ref.shape[1] // LANES
    total = jnp.zeros((1, schur_ref.shape[1]), f32)
    for face in range(6):
        at = slice(face * rows, (face + 1) * rows)
        applied = schur_ref[at, :] + got_face(got, face)
        applied = jnp.where(live_rows(len_ref, face, rows), applied, 0.0)
        applied_ref[at, :] = applied
        total += jnp.sum(applied * applied, axis=0, keepdims=True)
    products = sum(ref[...] for ref in products)
    halves = [products[:folds], products[folds : 2 * folds]]
    if pair_depth:
        halves = [jnp.where(lax.axis_index("depth") == 0, *halves)]
    halves = [[half[j : j + 1] for j in range(folds)] for half in halves]
    for i, half in enumerate([*halves, folded(total)]):
        for j, piece in enumerate(half):
            spread_ref[:, i, j, :] = jnp.broadcast_to(piece, (spread_ref.shape[0], LANES))


def finish_kernel(pair_depth, scale, len_ref, sums_ref, rho_ref, square_ref, residual_ref, applied_ref, new_out, alpha_ref, norm_ref, new_ref, sems):
    rows = applied_ref.shape[0] // 6
    devices, _, folds, _ = sums_ref.shape
    if pair_depth:
        pairs = sums_ref[...].reshape(devices // 2, 2, 2, folds, LANES)
        pairs = jnp.sum(pairs, axis=0)
        sums = [pairs[0, 0], pairs[1, 0], pairs[0, 1] + pairs[1, 1]]
    else:
        total = jnp.sum(sums_ref[...], axis=0)
        sums = [total[i] for i in range(3)]
    curve, cross, applied_square = [unfolded(x, 0, folds) for x in sums]
    alpha = rho_ref[...] / (scale * curve)
    alpha_ref[...] = alpha
    norm_ref[...] = scale * (
        square_ref[...] - 2.0 * alpha * cross + alpha * alpha * applied_square
    )
    copies = []
    for face in range(6):
        at = slice(face * rows, (face + 1) * rows)
        new_ref[at, :] = masked(len_ref, residual_ref, face, rows) - alpha * applied_ref[at, :]
        where = pl.ds(face * rows, rows)
        copies.append(pltpu.make_async_copy(new_ref.at[where], new_out.at[where], sems.at[face]))
        copies[-1].start()
    for copy in copies:
        copy.wait()


def to_all(x, axes):
    return lax.all_to_all(x, axes, split_axis=0, concat_axis=0, tiled=True)


def shards(
    face_len,
    residual,
    prev_direction,
    prev_rho,
    schur,
    neumann,
    coarse_basis,
    coarse_inverse,
    prim_owner,
    coarse_row,
):
    height, width = residual.shape[3:]
    rows = height // 6
    primal = coarse_basis.shape[4]
    owned = coarse_inverse.shape[3]
    owners = lax.axis_size(LAYER)
    slots = owners * CAP
    devices = lax.axis_size(AXES)
    layers = lax.axis_size("depth")
    pair_depth = layers == 2
    scale = 0.5 / (devices * height)
    folds = width // LANES
    tail = tiles(2 * folds)

    lengths = face_len.reshape(6)
    residual = residual.reshape(height, width)
    prev_direction = prev_direction.reshape(height, width)
    schur = schur.reshape(height, height)
    neumann = neumann.reshape(height, height)
    basis = coarse_basis.reshape(height, primal)
    inverse = coarse_inverse.reshape(owned, owned)
    owner = prim_owner.reshape(1, primal)
    wanted = coarse_row.reshape(1, primal)
    whole = shape_of(height, width)
    row = shape_of(1, width)
    face = shape_of(rows, width)

    (outgoing,) = call(
        pack_kernel,
        [shape_of(owners, folds * CAP + TILE, LANES)],
        [lengths, owner, wanted, residual, basis],
        far=range(5),
        flops=6 * height * primal * width,
        moved=4 * (height * (width + primal) + slots * width),
        scratch=[
            pltpu.SMEM((6,), jnp.int32),
            pltpu.VMEM((1, primal), jnp.int32),
            pltpu.VMEM((1, primal), jnp.int32),
            pltpu.VMEM((height, width), f32),
            pltpu.VMEM((height, primal), f32),
            pltpu.SemaphoreType.DMA((3, 2)),
            pltpu.SemaphoreType.DMA((3,)),
        ],
    )
    incoming = to_all(outgoing, LAYER)
    local, local_part, square, table, *halves = call(
        local_kernel,
        [whole, row, row, shape_of(primal, slots, dtype=bf16)]
        + [shape_of(height, primal, dtype=bf16)] * 2
        + [shape_of(height, height, dtype=bf16)] * 2,
        [lengths, residual, neumann, owner, basis, schur],
        smem=(0,),
        flops=6 * height * height * width,
        moved=4 * height * (3 * height + 2 * width),
    )
    basis_halves, schur_halves = halves[:2], halves[2:]
    (answers,) = call(
        solve_kernel,
        [shape_of(owners, folds * CAP + tail, LANES)],
        [incoming, inverse, local_part, square],
        far=range(2),
        flops=(8 * slots + 6 * owned) * owned * width,
        moved=8 * slots * width,
        scratch=[
            pltpu.VMEM((owners, TILE, LANES), f32),
            pltpu.VMEM((owners, folds * CAP, LANES), f32),
            pltpu.VMEM((owned, owned), f32),
            pltpu.SemaphoreType.DMA((4,)),
        ],
    )
    returned = to_all(answers, LAYER)
    keys = moves(FIRST)
    faces = [face] * len(keys)
    image, sums, *outward = call(
        functools.partial(image_kernel, pair_depth),
        [whole, shape_of(tail, LANES) if pair_depth else shape_of(layers, tail, LANES), *faces],
        [returned, table, *basis_halves, local],
        flops=(6 * height + 4 * slots) * primal * width,
        moved=16 * height * width,
    )
    got = dict(zip(keys, exchange(outward, FIRST)))
    if pair_depth:
        sums = [sums, lax.ppermute(sums, "depth", route("depth", 0))]
    else:
        sums = [to_all(sums, "depth")]
    far_keys = [("blk", "down"), ("lat", "down")]
    near_keys = [key for key in keys if key not in far_keys]
    rho, beta, square, near, near_image = call(
        functools.partial(near_kernel, pair_depth, scale, near_keys),
        [row, row, row, shape_of(len(NEAR) * rows, width), whole],
        [lengths, sums[0], prev_rho.reshape(1, width), image, prev_direction, *schur_halves]
        + [got[key] for key in near_keys]
        + sums[1:],
        smem=(0,),
        flops=4 * height * height * width,
        moved=4 * height * (height + 4 * width),
    )
    far, schur_image, *outward = call(
        functools.partial(far_kernel, far_keys),
        [shape_of(len(FAR) * rows, width), whole, *faces],
        [lengths, beta, image, prev_direction, *schur_halves, near, near_image]
        + [got[key] for key in far_keys],
        smem=(0,),
        flops=2 * height * height * width,
        moved=4 * height * (height + 4 * width),
    )
    got = exchange(outward, SECOND)
    (products,) = call(
        products_kernel,
        [shape_of(2 * folds, LANES)],
        [lengths, near, far, schur_image, residual, got[0]],
        smem=(0,),
        loose=(5,),
        flops=4 * height * width,
        moved=12 * height * width,
    )
    products = [products]
    if pair_depth:
        products.append(lax.ppermute(products[0], "depth", route("depth", 0)))
    (direction,) = call(
        store_kernel,
        [whole],
        [near, far],
        far_out=(0,),
        moved=8 * height * width,
        scratch=[pltpu.SemaphoreType.DMA((6,))],
    )
    applied, spread_sums = call(
        functools.partial(applied_kernel, pair_depth),
        [whole, shape_of(devices, 2 if pair_depth else 3, folds, LANES)],
        [lengths, direction, schur_image, *got, *products],
        smem=(0,),
        far=(1,),
        flops=4 * height * width,
        moved=12 * height * width,
    )
    new_residual, alpha, norm = call(
        functools.partial(finish_kernel, pair_depth, scale),
        [whole, row, row],
        [lengths, to_all(spread_sums, AXES), rho, square, residual, applied],
        smem=(0,),
        far_out=(0,),
        flops=4 * height * width,
        moved=12 * height * width,
        scratch=[pltpu.VMEM((height, width), f32), pltpu.SemaphoreType.DMA((6,))],
    )
    out_shape = (1, 1, 1, height, width)
    return (
        new_residual.reshape(out_shape),
        direction.reshape(out_shape),
        rho.reshape(width),
        alpha.reshape(width),
        norm.reshape(width),
    )


def solution(mesh):
    tall = P("blk", "lat", "depth", None, None)
    flat = P("blk", "lat", "depth", None)
    in_specs = (flat, tall, tall, P(), tall, tall, tall, tall, tall, flat)
    out_specs = (tall, tall, P(), P(), P())
    return jax.shard_map(shards, mesh=mesh, in_specs=in_specs, out_specs=out_specs, check_vma=False)
```

```python
import functools

import jax
import jax.numpy as jnp
from jax import lax
from jax.experimental import pallas as pl
from jax.experimental.pallas import tpu as pltpu
from jax.sharding import PartitionSpec as P

CAP = 24
AXES = ("blk", "lat", "depth")
LAYER = ("blk", "lat")
LANES = 128
TILE = 8
f32 = jnp.float32
bf16 = jnp.bfloat16

VMEM = pl.BlockSpec(memory_space=pltpu.VMEM)
SMEM = pl.BlockSpec(memory_space=pltpu.SMEM)
ANY = pl.BlockSpec(memory_space=pl.ANY)


def shape_of(*dims, dtype=f32):
    return jax.ShapeDtypeStruct(dims, dtype)


def call(body, outs, operands, smem=(), far=(), loose=(), far_out=(), flops=0, moved=0, scratch=(), room=32):
    in_specs = [
        SMEM if i in smem else ANY if i in far or i in loose else VMEM
        for i in range(len(operands))
    ]
    operands = [
        pltpu.with_memory_space_constraint(x, pltpu.HBM) if i in far else x
        for i, x in enumerate(operands)
    ]
    out_specs = [ANY if i in far_out else VMEM for i in range(len(outs))]
    return pl.pallas_call(
        body,
        out_shape=list(outs),
        in_specs=in_specs,
        out_specs=out_specs,
        scratch_shapes=list(scratch),
        compiler_params=pltpu.CompilerParams(vmem_limit_bytes=room << 20),
        cost_estimate=pl.CostEstimate(flops=flops, bytes_accessed=moved, transcendentals=0),
    )(*operands)


def parts(x):
    high = x.astype(bf16)
    low = (x - high.astype(f32)).astype(bf16)
    return high, low


def mul(a, b, dims):
    return lax.dot_general(a, b, (dims, ((), ())), preferred_element_type=f32)


PLAIN = ((1,), (0,))
LEFT_T = ((0,), (0,))


def product(a, b, dims=PLAIN):
    (ah, al), (bh, bl) = a, b
    return mul(ah, bh, dims) + (mul(ah, bl, dims) + mul(al, bh, dims))


def select(table, x, dims=PLAIN):
    high, low = parts(x)
    return mul(table, high, dims) + mul(table, low, dims)


def one_hot(hit):
    return jnp.where(hit, 1.0, 0.0).astype(bf16)


def live_rows(len_ref, face, rows):
    return lax.broadcasted_iota(jnp.int32, (rows, 1), 0) < len_ref[face]


def masked(len_ref, ref, face, rows):
    block = ref[face * rows : (face + 1) * rows, :]
    return jnp.where(live_rows(len_ref, face, rows), block, 0.0)


def folded(vector):
    pieces = vector.shape[1] // LANES
    return [vector[:, j * LANES : (j + 1) * LANES] for j in range(pieces)]


def unfolded(block, first, pieces):
    return jnp.concatenate([block[first + j : first + j + 1, :] for j in range(pieces)], axis=1)


def tiles(rows):
    return -(-rows // TILE) * TILE


def put_slab(out_ref, block, first=0):
    owners = out_ref.shape[0]
    for j in range(block.shape[1] // LANES):
        piece = block[:, j * LANES : (j + 1) * LANES]
        at = (first + j) * CAP
        out_ref[:, at : at + CAP, :] = piece.reshape(owners, CAP, LANES)


def get_slab(ref, first, last):
    slots = ref.shape[0] * CAP
    return jnp.concatenate(
        [ref[:, j * CAP : (j + 1) * CAP, :].reshape(slots, LANES) for j in range(first, last)],
        axis=1,
    )


def columns(*rows):
    spare = [jnp.zeros_like(rows[0])] * (TILE - len(rows))
    turned = jnp.transpose(jnp.concatenate([*rows, *spare], axis=0))
    return [turned[:, i : i + 1] for i in range(len(rows))]


def ranks(own_row):
    primal = own_row.shape[1]
    (own_col,) = columns(own_row)
    row_at = lax.broadcasted_iota(jnp.int32, (primal, primal), 0)
    col_at = lax.broadcasted_iota(jnp.int32, (primal, primal), 1)
    before = (own_row == own_col) & (row_at < col_at)
    return jnp.sum(jnp.where(before, 1.0, 0.0), axis=0, keepdims=True), own_col


def pack_kernel(len_any, owner_any, row_any, residual_any, basis_any, slab_ref, *refs):
    len_ref, owner_ref, row_ref, residual_ref, basis_ref, sems, small_sems = refs
    rows = residual_ref.shape[0] // 6
    primal = basis_ref.shape[1]
    owners = slab_ref.shape[0]
    slots = owners * CAP
    small = [
        pltpu.make_async_copy(src, dst, small_sems.at[i])
        for i, (src, dst) in enumerate(
            [(owner_any, owner_ref), (row_any, row_ref), (len_any, len_ref)]
        )
    ]
    large = []
    for pair in range(3):
        at = pl.ds(2 * pair * rows, 2 * rows)
        large.append(
            (
                pltpu.make_async_copy(residual_any.at[at], residual_ref.at[at], sems.at[pair, 0]),
                pltpu.make_async_copy(basis_any.at[at], basis_ref.at[at], sems.at[pair, 1]),
            )
        )
    for copy in small:
        copy.start()
    for pair in large:
        for copy in pair:
            copy.start()
    for copy in small:
        copy.wait()
    own_row = owner_ref[...].astype(f32)
    wanted_row = row_ref[...].astype(f32) + 1.0
    rank_row, _ = ranks(own_row)
    slot_row = (own_row * CAP + rank_row).astype(jnp.int32)
    rank_col, wanted_col = columns(rank_row, wanted_row)
    packer = one_hot(lax.broadcasted_iota(jnp.int32, (slots, primal), 0) == slot_row)
    to_owner = one_hot(lax.broadcasted_iota(jnp.int32, (owners, primal), 0) == owner_ref[...])
    lane_at = lax.broadcasted_iota(jnp.int32, (primal, LANES), 1)
    ranked = jnp.where(lane_at == rank_col.astype(jnp.int32), wanted_col, 0.0)
    names = select(to_owner, ranked)
    terms = None
    for pair in range(3):
        for copy in large[pair]:
            copy.wait()
        weighted = jnp.concatenate(
            [0.5 * masked(len_ref, residual_ref, 2 * pair + side, rows) for side in range(2)],
            axis=0,
        )
        basis = basis_ref[2 * pair * rows : 2 * (pair + 1) * rows, :]
        term = product(parts(basis), parts(weighted), LEFT_T)
        terms = term if terms is None else terms + term
    put_slab(slab_ref, select(packer, terms))
    tail = slab_ref.shape[1] - TILE
    slab_ref[:, tail:, :] = jnp.broadcast_to(
        names.reshape(owners, 1, LANES), (owners, TILE, LANES)
    )


def local_kernel(len_ref, residual_ref, matrix_ref, owner_ref, *refs):
    whole, refs = refs[:2], refs[2:]
    local_ref, part_ref, square_ref, table_ref, refs = *refs[:4], refs[4:]
    rows = residual_ref.shape[0] // 6
    live = jnp.concatenate(
        [masked(len_ref, residual_ref, face, rows) for face in range(6)], axis=0
    )
    local = product(parts(matrix_ref[...]), parts(0.5 * live))
    local_ref[...] = local
    part_ref[...] = jnp.sum(live * local, axis=0, keepdims=True)
    square_ref[...] = jnp.sum(live * live, axis=0, keepdims=True)
    refs[0][...], refs[1][...] = parts(whole[0][...])
    for i, move in enumerate(NEAR + FAR):
        at = slice(i * rows, (i + 1) * rows)
        refs[2][:, at], refs[3][:, at] = parts(whole[1][:, rows_of(served(*move), rows)])
    primal, slots = table_ref.shape
    rank_row, own_col = ranks(owner_ref[...].astype(f32))
    (rank_col,) = columns(rank_row)
    slot_col = (own_col * CAP + rank_col).astype(jnp.int32)
    table_ref[...] = one_hot(lax.broadcasted_iota(jnp.int32, (primal, slots), 1) == slot_col)


def picker_table(names_ref, owned):
    owners = names_ref.shape[0]
    lane_at = lax.broadcasted_iota(jnp.int32, (CAP, LANES), 1)
    rank_at = lax.broadcasted_iota(jnp.int32, (CAP, LANES), 0)
    out_at = lax.broadcasted_iota(jnp.int32, (CAP, owned), 1).astype(f32) + 1.0
    blocks = []
    for source in range(owners):
        names = names_ref[source, 0:1, :]
        named = jnp.sum(jnp.where(lane_at == rank_at, names, 0.0), axis=1, keepdims=True)
        blocks.append(jnp.where(out_at == named, 1.0, 0.0))
    return jnp.concatenate(blocks, axis=0)


def solve_kernel(incoming_any, inverse_any, local_part_ref, square_ref, answer_ref, *refs):
    names_ref, slab_ref, inverse_ref, sems = refs
    owners, height, _ = slab_ref.shape
    pieces = height // CAP
    half = pieces // 2 * CAP
    copies = [
        pltpu.make_async_copy(incoming_any.at[:, pl.ds(height, TILE)], names_ref, sems.at[0]),
        pltpu.make_async_copy(
            incoming_any.at[:, pl.ds(0, half)], slab_ref.at[:, pl.ds(0, half)], sems.at[1]
        ),
        pltpu.make_async_copy(
            incoming_any.at[:, pl.ds(half, height - half)],
            slab_ref.at[:, pl.ds(half, height - half)],
            sems.at[2],
        ),
        pltpu.make_async_copy(inverse_any, inverse_ref, sems.at[3]),
    ]
    for copy in copies:
        copy.start()
    copies[0].wait()
    table = picker_table(names_ref, inverse_ref.shape[0]).astype(bf16)
    copies[3].wait()
    inverse = parts(inverse_ref[...])
    products = []
    for half, copy in enumerate(copies[1:3]):
        copy.wait()
        first, last = (0, pieces // 2) if half == 0 else (pieces // 2, pieces)
        summed = select(table, get_slab(slab_ref, first, last), LEFT_T)
        solved = product(inverse, parts(summed))
        put_slab(answer_ref, select(table, solved), first)
        products.append(jnp.sum(summed * solved, axis=0, keepdims=True))
    total = local_part_ref[...] + 2.0 * jnp.concatenate(products, axis=1)
    sums = folded(total) + folded(square_ref[...])
    sums += [jnp.zeros((1, LANES), f32)] * (tiles(len(sums)) - len(sums))
    answer_ref[:, pieces * CAP :, :] = jnp.broadcast_to(
        jnp.concatenate(sums, axis=0)[None], (owners, len(sums), LANES)
    )


NEAR = (("blk", "up"), ("lat", 0), ("depth", 0), ("depth", 1))
FAR = (("blk", "down"), ("lat", 1))
FIRST = NEAR + FAR
SECOND = (("blk", "up"), ("lat", 0), ("blk", "down"), ("lat", 1), ("depth", 0), ("depth", 1))


def moves(order):
    return [(axis, way) for axis, way in order if route(axis, way)]


def route(axis, way):
    devices = lax.axis_size(axis)
    if way in ("up", "down"):
        by = 1 if way == "up" else -1
        return [(i, (i + by) % devices) for i in range(devices)]
    return [pair for i in range(way, devices - 1, 2) for pair in ((i, i + 1), (i + 1, i))]


def served(axis, way):
    if way in ("up", "down"):
        return 0 if way == "up" else 1
    plus = (lax.rem(lax.axis_index(axis), 2) == way).astype(jnp.int32)
    return (2 if axis == "lat" else 4) + plus


def sent(axis, way):
    return 1 - served(axis, way) if axis == "blk" else served(axis, way)


def rows_of(face, rows):
    if isinstance(face, int):
        return pl.ds(face * rows, rows)
    return pl.ds(pl.multiple_of(face * rows, rows), rows)


def put_faces(image_ref, rows, order, face_refs):
    for ref, move in zip(face_refs, moves(order), strict=True):
        ref[...] = image_ref[rows_of(sent(*move), rows), :]


def exchange(faces, order):
    return [
        lax.ppermute(block, axis, route(axis, way))
        for block, (axis, way) in zip(faces, moves(order), strict=True)
    ]


def image_kernel(pair_depth, returned_ref, table_ref, high_ref, low_ref, local_ref, image_ref, sums_ref, *face_refs):
    rows = local_ref.shape[0] // 6
    width = local_ref.shape[1]
    folds = width // LANES
    correction = select(table_ref[...], get_slab(returned_ref, 0, folds))
    image = local_ref[...] + product((high_ref[...], low_ref[...]), parts(correction))
    image_ref[...] = image
    put_faces(image_ref, rows, FIRST, face_refs)
    tail = jnp.sum(returned_ref[:, folds * CAP :, :], axis=0)
    if pair_depth:
        sums_ref[...] = tail
    else:
        sums_ref[...] = jnp.broadcast_to(tail[None], sums_ref.shape)


def with_got(ref, at, got, move):
    return ref[at, :] + got[move][...] if move in got else ref[at, :]


def new_direction(len_ref, beta, image_ref, prev_ref, got, move, rows):
    face = served(*move)
    at = rows_of(face, rows)
    precond = 0.5 * with_got(image_ref, at, got, move)
    return jnp.where(live_rows(len_ref, face, rows), precond + beta * prev_ref[at, :], 0.0)


def near_kernel(pair_depth, scale, keys, len_ref, sums_ref, prev_rho_ref, image_ref, prev_ref, high_ref, low_ref, *refs):
    got, refs = dict(zip(keys, refs)), refs[len(keys) :]
    if pair_depth:
        sums, refs = sums_ref[...] + refs[0][...], refs[1:]
    else:
        sums = jnp.sum(sums_ref[...], axis=0)
    rho_out, beta_out, square_out, near_ref, image_out = refs
    rows = image_ref.shape[0] // 6
    folds = image_ref.shape[1] // LANES
    rho = scale * unfolded(sums, 0, folds)
    beta = rho / prev_rho_ref[...]
    rho_out[...] = rho
    beta_out[...] = beta
    square_out[...] = unfolded(sums, folds, folds)
    for i, move in enumerate(NEAR):
        near_ref[i * rows : (i + 1) * rows, :] = new_direction(
            len_ref, beta, image_ref, prev_ref, got, move, rows
        )
    first = len(NEAR) * rows
    image_out[...] = product((high_ref[:, :first], low_ref[:, :first]), parts(near_ref[...]))


def far_kernel(keys, len_ref, beta_ref, image_ref, prev_ref, high_ref, low_ref, near_ref, near_image_ref, *refs):
    got, refs = dict(zip(keys, refs)), refs[len(keys) :]
    far_ref, schur_out, *face_refs = refs
    rows = image_ref.shape[0] // 6
    beta = beta_ref[...]
    for i, move in enumerate(FAR):
        far_ref[i * rows : (i + 1) * rows, :] = new_direction(
            len_ref, beta, image_ref, prev_ref, got, move, rows
        )
    first = len(NEAR) * rows
    image = near_image_ref[...] + product(
        (high_ref[:, first:], low_ref[:, first:]), parts(far_ref[...])
    )
    schur_out[...] = image
    put_faces(schur_out, rows, SECOND, face_refs)


def store_kernel(near_ref, far_ref, direction_out, sems):
    rows = far_ref.shape[0] // len(FAR)
    copies = []
    for ref, served_moves in ((near_ref, NEAR), (far_ref, FAR)):
        for i, move in enumerate(served_moves):
            copies.append(
                pltpu.make_async_copy(
                    ref.at[pl.ds(i * rows, rows)],
                    direction_out.at[rows_of(served(*move), rows)],
                    sems.at[len(copies)],
                )
            )
    for copy in copies:
        copy.start()
    for copy in copies:
        copy.wait()


def products_kernel(len_ref, near_ref, far_ref, schur_ref, residual_ref, arrived, out_ref):
    rows = schur_ref.shape[0] // 6
    curve = cross = jnp.zeros((1, schur_ref.shape[1]), f32)
    for ref, served_moves in ((near_ref, NEAR), (far_ref, FAR)):
        for i, move in enumerate(served_moves):
            face = served(*move)
            at = rows_of(face, rows)
            image = schur_ref[at, :]
            live = jnp.where(live_rows(len_ref, face, rows), residual_ref[at, :], 0.0)
            direction = ref[i * rows : (i + 1) * rows, :]
            curve += 2.0 * jnp.sum(direction * image, axis=0, keepdims=True)
            cross += 2.0 * jnp.sum(live * image, axis=0, keepdims=True)
    for j, piece in enumerate(folded(curve) + folded(cross)):
        out_ref[j : j + 1, :] = piece


def applied_kernel(pair_depth, len_ref, stored, schur_ref, *refs):
    keys = moves(SECOND)
    got, refs = dict(zip(keys, refs)), refs[len(keys) :]
    products, (applied_ref, spread_ref) = refs[:-2], refs[-2:]
    rows = schur_ref.shape[0] // 6
    folds = schur_ref.shape[1] // LANES
    total = jnp.zeros((1, schur_ref.shape[1]), f32)
    for move in SECOND:
        face = served(*move)
        at = rows_of(face, rows)
        applied = with_got(schur_ref, at, got, move)
        applied = jnp.where(live_rows(len_ref, face, rows), applied, 0.0)
        applied_ref[at, :] = applied
        total += jnp.sum(applied * applied, axis=0, keepdims=True)
    products = sum(ref[...] for ref in products)
    halves = [products[:folds], products[folds : 2 * folds]]
    if pair_depth:
        halves = [jnp.where(lax.axis_index("depth") == 0, *halves)]
    halves = [[half[j : j + 1] for j in range(folds)] for half in halves]
    for i, half in enumerate([*halves, folded(total)]):
        for j, piece in enumerate(half):
            spread_ref[:, i, j, :] = jnp.broadcast_to(piece, (spread_ref.shape[0], LANES))


def finish_kernel(pair_depth, scale, len_ref, sums_ref, rho_ref, square_ref, residual_ref, applied_ref, new_out, alpha_ref, norm_ref, new_ref, sems):
    rows = applied_ref.shape[0] // 6
    devices, _, folds, _ = sums_ref.shape
    if pair_depth:
        pairs = sums_ref[...].reshape(devices // 2, 2, 2, folds, LANES)
        pairs = jnp.sum(pairs, axis=0)
        sums = [pairs[0, 0], pairs[1, 0], pairs[0, 1] + pairs[1, 1]]
    else:
        total = jnp.sum(sums_ref[...], axis=0)
        sums = [total[i] for i in range(3)]
    curve, cross, applied_square = [unfolded(x, 0, folds) for x in sums]
    alpha = rho_ref[...] / (scale * curve)
    alpha_ref[...] = alpha
    norm_ref[...] = scale * (
        square_ref[...] - 2.0 * alpha * cross + alpha * alpha * applied_square
    )
    copies = []
    for face in range(6):
        at = slice(face * rows, (face + 1) * rows)
        new_ref[at, :] = masked(len_ref, residual_ref, face, rows) - alpha * applied_ref[at, :]
        where = pl.ds(face * rows, rows)
        copies.append(pltpu.make_async_copy(new_ref.at[where], new_out.at[where], sems.at[face]))
        copies[-1].start()
    for copy in copies:
        copy.wait()


def to_all(x, axes):
    return lax.all_to_all(x, axes, split_axis=0, concat_axis=0, tiled=True)


def shards(
    face_len,
    residual,
    prev_direction,
    prev_rho,
    schur,
    neumann,
    coarse_basis,
    coarse_inverse,
    prim_owner,
    coarse_row,
):
    height, width = residual.shape[3:]
    rows = height // 6
    primal = coarse_basis.shape[4]
    owned = coarse_inverse.shape[3]
    owners = lax.axis_size(LAYER)
    slots = owners * CAP
    devices = lax.axis_size(AXES)
    layers = lax.axis_size("depth")
    pair_depth = layers == 2
    scale = 0.5 / (devices * height)
    folds = width // LANES
    tail = tiles(2 * folds)

    lengths = face_len.reshape(6)
    residual = residual.reshape(height, width)
    prev_direction = prev_direction.reshape(height, width)
    schur = schur.reshape(height, height)
    neumann = neumann.reshape(height, height)
    basis = coarse_basis.reshape(height, primal)
    inverse = coarse_inverse.reshape(owned, owned)
    owner = prim_owner.reshape(1, primal)
    wanted = coarse_row.reshape(1, primal)
    whole = shape_of(height, width)
    row = shape_of(1, width)
    face = shape_of(rows, width)

    (outgoing,) = call(
        pack_kernel,
        [shape_of(owners, folds * CAP + TILE, LANES)],
        [lengths, owner, wanted, residual, basis],
        far=range(5),
        flops=6 * height * primal * width,
        moved=4 * (height * (width + primal) + slots * width),
        scratch=[
            pltpu.SMEM((6,), jnp.int32),
            pltpu.VMEM((1, primal), jnp.int32),
            pltpu.VMEM((1, primal), jnp.int32),
            pltpu.VMEM((height, width), f32),
            pltpu.VMEM((height, primal), f32),
            pltpu.SemaphoreType.DMA((3, 2)),
            pltpu.SemaphoreType.DMA((3,)),
        ],
    )
    incoming = to_all(outgoing, LAYER)
    local, local_part, square, table, *halves = call(
        local_kernel,
        [whole, row, row, shape_of(primal, slots, dtype=bf16)]
        + [shape_of(height, primal, dtype=bf16)] * 2
        + [shape_of(height, height, dtype=bf16)] * 2,
        [lengths, residual, neumann, owner, basis, schur],
        smem=(0,),
        flops=6 * height * height * width,
        moved=4 * height * (3 * height + 2 * width),
    )
    basis_halves, schur_halves = halves[:2], halves[2:]
    (answers,) = call(
        solve_kernel,
        [shape_of(owners, folds * CAP + tail, LANES)],
        [incoming, inverse, local_part, square],
        far=range(2),
        flops=(8 * slots + 6 * owned) * owned * width,
        moved=8 * slots * width,
        scratch=[
            pltpu.VMEM((owners, TILE, LANES), f32),
            pltpu.VMEM((owners, folds * CAP, LANES), f32),
            pltpu.VMEM((owned, owned), f32),
            pltpu.SemaphoreType.DMA((4,)),
        ],
    )
    returned = to_all(answers, LAYER)
    keys = moves(FIRST)
    faces = [face] * len(keys)
    image, sums, *outward = call(
        functools.partial(image_kernel, pair_depth),
        [whole, shape_of(tail, LANES) if pair_depth else shape_of(layers, tail, LANES), *faces],
        [returned, table, *basis_halves, local],
        flops=(6 * height + 4 * slots) * primal * width,
        moved=16 * height * width,
    )
    got = dict(zip(keys, exchange(outward, FIRST)))
    if pair_depth:
        sums = [sums, lax.ppermute(sums, "depth", route("depth", 0))]
    else:
        sums = [to_all(sums, "depth")]
    near_keys, far_keys = moves(NEAR), moves(FAR)
    rho, beta, square, near, near_image = call(
        functools.partial(near_kernel, pair_depth, scale, near_keys),
        [row, row, row, shape_of(len(NEAR) * rows, width), whole],
        [lengths, sums[0], prev_rho.reshape(1, width), image, prev_direction, *schur_halves]
        + [got[key] for key in near_keys]
        + sums[1:],
        smem=(0,),
        flops=4 * height * height * width,
        moved=4 * height * (height + 4 * width),
    )
    far, schur_image, *outward = call(
        functools.partial(far_kernel, far_keys),
        [shape_of(len(FAR) * rows, width), whole, *faces],
        [lengths, beta, image, prev_direction, *schur_halves, near, near_image]
        + [got[key] for key in far_keys],
        smem=(0,),
        flops=2 * height * height * width,
        moved=4 * height * (height + 4 * width),
    )
    got = exchange(outward, SECOND)
    (products,) = call(
        products_kernel,
        [shape_of(2 * folds, LANES)],
        [lengths, near, far, schur_image, residual, got[0]],
        smem=(0,),
        loose=(5,),
        flops=4 * height * width,
        moved=12 * height * width,
    )
    products = [products]
    if pair_depth:
        products.append(lax.ppermute(products[0], "depth", route("depth", 0)))
    (direction,) = call(
        store_kernel,
        [whole],
        [near, far],
        far_out=(0,),
        moved=8 * height * width,
        scratch=[pltpu.SemaphoreType.DMA((6,))],
    )
    applied, spread_sums = call(
        functools.partial(applied_kernel, pair_depth),
        [whole, shape_of(devices, 2 if pair_depth else 3, folds, LANES)],
        [lengths, direction, schur_image, *got, *products],
        smem=(0,),
        far=(1,),
        flops=4 * height * width,
        moved=12 * height * width,
    )
    new_residual, alpha, norm = call(
        functools.partial(finish_kernel, pair_depth, scale),
        [whole, row, row],
        [lengths, to_all(spread_sums, AXES), rho, square, residual, applied],
        smem=(0,),
        far_out=(0,),
        flops=4 * height * width,
        moved=12 * height * width,
        scratch=[pltpu.VMEM((height, width), f32), pltpu.SemaphoreType.DMA((6,))],
    )
    out_shape = (1, 1, 1, height, width)
    return (
        new_residual.reshape(out_shape),
        direction.reshape(out_shape),
        rho.reshape(width),
        alpha.reshape(width),
        norm.reshape(width),
    )


def solution(mesh):
    tall = P("blk", "lat", "depth", None, None)
    flat = P("blk", "lat", "depth", None)
    in_specs = (flat, tall, tall, P(), tall, tall, tall, tall, tall, flat)
    out_specs = (tall, tall, P(), P(), P())
    return jax.shard_map(shards, mesh=mesh, in_specs=in_specs, out_specs=out_specs, check_vma=False)
```

```python
import functools

import jax
import jax.numpy as jnp
from jax import lax
from jax.experimental import pallas as pl
from jax.experimental.pallas import tpu as pltpu
from jax.sharding import PartitionSpec as P

CAP = 24
AXES = ("blk", "lat", "depth")
LAYER = ("blk", "lat")
LANES = 128
TILE = 8
f32 = jnp.float32
bf16 = jnp.bfloat16

VMEM = pl.BlockSpec(memory_space=pltpu.VMEM)
SMEM = pl.BlockSpec(memory_space=pltpu.SMEM)
ANY = pl.BlockSpec(memory_space=pl.ANY)


def shape_of(*dims, dtype=f32):
    return jax.ShapeDtypeStruct(dims, dtype)


def call(body, outs, operands, smem=(), far=(), loose=(), far_out=(), flops=0, moved=0, scratch=(), room=32):
    in_specs = [
        SMEM if i in smem else ANY if i in far or i in loose else VMEM
        for i in range(len(operands))
    ]
    operands = [
        pltpu.with_memory_space_constraint(x, pltpu.HBM) if i in far else x
        for i, x in enumerate(operands)
    ]
    out_specs = [ANY if i in far_out else VMEM for i in range(len(outs))]
    return pl.pallas_call(
        body,
        out_shape=list(outs),
        in_specs=in_specs,
        out_specs=out_specs,
        scratch_shapes=list(scratch),
        compiler_params=pltpu.CompilerParams(vmem_limit_bytes=room << 20),
        cost_estimate=pl.CostEstimate(flops=flops, bytes_accessed=moved, transcendentals=0),
    )(*operands)


def parts(x):
    high = x.astype(bf16)
    low = (x - high.astype(f32)).astype(bf16)
    return high, low


def mul(a, b, dims):
    return lax.dot_general(a, b, (dims, ((), ())), preferred_element_type=f32)


PLAIN = ((1,), (0,))


def product(a, b, dims=PLAIN):
    (ah, al), (bh, bl) = a, b
    return mul(ah, bh, dims) + (mul(ah, bl, dims) + mul(al, bh, dims))


def select(table, x, dims=PLAIN):
    high, low = parts(x)
    return mul(table, high, dims) + mul(table, low, dims)


def one_hot(hit):
    return jnp.where(hit, 1.0, 0.0).astype(bf16)


def live_rows(len_ref, face, rows):
    return lax.broadcasted_iota(jnp.int32, (rows, 1), 0) < len_ref[face]


def masked(len_ref, ref, face, rows):
    block = ref[face * rows : (face + 1) * rows, :]
    return jnp.where(live_rows(len_ref, face, rows), block, 0.0)


def folded(vector):
    pieces = vector.shape[1] // LANES
    return [vector[:, j * LANES : (j + 1) * LANES] for j in range(pieces)]


def unfolded(block, first, pieces):
    return jnp.concatenate([block[first + j : first + j + 1, :] for j in range(pieces)], axis=1)


def id_rows(slots):
    return -(-slots // LANES)


def tiles(rows):
    return -(-rows // TILE) * TILE


def put_slab(out_ref, block):
    owners = out_ref.shape[0]
    for j in range(block.shape[1] // LANES):
        piece = block[:, j * LANES : (j + 1) * LANES]
        out_ref[:, j * CAP : (j + 1) * CAP, :] = piece.reshape(owners, CAP, LANES)


def get_slab(ref, pieces):
    slots = ref.shape[0] * CAP
    return jnp.concatenate(
        [ref[:, j * CAP : (j + 1) * CAP, :].reshape(slots, LANES) for j in range(pieces)], axis=1
    )


def columns(*rows):
    spare = [jnp.zeros_like(rows[0])] * (TILE - len(rows))
    turned = jnp.transpose(jnp.concatenate([*rows, *spare], axis=0))
    return [turned[:, i : i + 1] for i in range(len(rows))]


def ranks(own_row):
    primal = own_row.shape[1]
    (own_col,) = columns(own_row)
    row_at = lax.broadcasted_iota(jnp.int32, (primal, primal), 0)
    col_at = lax.broadcasted_iota(jnp.int32, (primal, primal), 1)
    before = (own_row == own_col) & (row_at < col_at)
    return jnp.sum(jnp.where(before, 1.0, 0.0), axis=0, keepdims=True), own_col


def pack_kernel(len_any, owner_any, row_any, residual_any, basis_any, slab_ref, *refs):
    len_ref, owner_ref, row_ref, residual_ref, basis_ref, sems, small_sems = refs
    rows = residual_ref.shape[0] // 6
    primal = basis_ref.shape[1]
    owners = slab_ref.shape[0]
    slots = owners * CAP
    small = [
        pltpu.make_async_copy(src, dst, small_sems.at[i])
        for i, (src, dst) in enumerate(
            [(owner_any, owner_ref), (row_any, row_ref), (len_any, len_ref)]
        )
    ]
    large = []
    for pair in range(3):
        at = pl.ds(2 * pair * rows, 2 * rows)
        large.append(
            (
                pltpu.make_async_copy(residual_any.at[at], residual_ref.at[at], sems.at[pair, 0]),
                pltpu.make_async_copy(basis_any.at[at], basis_ref.at[at], sems.at[pair, 1]),
            )
        )
    for copy in small:
        copy.start()
    for pair in large:
        for copy in pair:
            copy.start()
    for copy in small:
        copy.wait()
    own_row = owner_ref[...].astype(f32)
    wanted_row = row_ref[...].astype(f32) + 1.0
    rank_row, _ = ranks(own_row)
    slot_row = (own_row * CAP + rank_row).astype(jnp.int32)
    rank_col, wanted_col = columns(rank_row, wanted_row)
    packer = one_hot(lax.broadcasted_iota(jnp.int32, (slots, primal), 0) == slot_row)
    to_owner = one_hot(lax.broadcasted_iota(jnp.int32, (owners, primal), 0) == owner_ref[...])
    at_owner = lax.axis_index(LAYER) * CAP + rank_col.astype(jnp.int32)
    place = lax.broadcasted_iota(jnp.int32, (primal, id_rows(slots) * LANES), 1)
    names = select(to_owner, jnp.where(place == at_owner, wanted_col, 0.0))
    terms = None
    for pair in range(3):
        for copy in large[pair]:
            copy.wait()
        weighted = jnp.concatenate(
            [0.5 * masked(len_ref, residual_ref, 2 * pair + side, rows) for side in range(2)],
            axis=0,
        )
        basis = basis_ref[2 * pair * rows : 2 * (pair + 1) * rows, :]
        term = product(parts(jnp.transpose(basis)), parts(weighted))
        terms = term if terms is None else terms + term
    put_slab(slab_ref, select(packer, terms))
    tail = slab_ref.shape[1] - tiles(id_rows(slots))
    names = jnp.concatenate(
        [names, jnp.zeros((owners, (slab_ref.shape[1] - tail) * LANES - names.shape[1]), f32)], axis=1
    )
    for j in range(slab_ref.shape[1] - tail):
        slab_ref[:, tail + j, :] = names[:, j * LANES : (j + 1) * LANES]


def local_kernel(len_ref, residual_ref, matrix_ref, owner_ref, *refs):
    whole, refs = refs[:2], refs[2:]
    local_ref, part_ref, square_ref, table_ref, refs = *refs[:4], refs[4:]
    rows = residual_ref.shape[0] // 6
    live = jnp.concatenate(
        [masked(len_ref, residual_ref, face, rows) for face in range(6)], axis=0
    )
    local = product(parts(matrix_ref[...]), parts(0.5 * live))
    local_ref[...] = local
    part_ref[...] = jnp.sum(live * local, axis=0, keepdims=True)
    square_ref[...] = jnp.sum(live * live, axis=0, keepdims=True)
    refs[0][...], refs[1][...] = parts(whole[0][...])
    for i, move in enumerate(NEAR + FAR):
        at = slice(i * rows, (i + 1) * rows)
        refs[2][:, at], refs[3][:, at] = parts(whole[1][:, rows_of(served(*move), rows)])
    primal, slots = table_ref.shape
    rank_row, own_col = ranks(owner_ref[...].astype(f32))
    (rank_col,) = columns(rank_row)
    slot_col = (own_col * CAP + rank_col).astype(jnp.int32)
    table_ref[...] = one_hot(lax.broadcasted_iota(jnp.int32, (primal, slots), 1) == slot_col)


def solve_kernel(incoming_any, inverse_any, local_part_ref, square_ref, answer_ref, *refs):
    names_ref, slab_ref, inverse_ref, sems = refs
    owners, height, _ = slab_ref.shape
    pieces = height // CAP
    half = pieces // 2 * CAP
    copies = [
        pltpu.make_async_copy(
            incoming_any.at[:, pl.ds(height, names_ref.shape[1])], names_ref, sems.at[0]
        ),
        pltpu.make_async_copy(
            incoming_any.at[:, pl.ds(0, half)], slab_ref.at[:, pl.ds(0, half)], sems.at[1]
        ),
        pltpu.make_async_copy(
            incoming_any.at[:, pl.ds(half, height - half)],
            slab_ref.at[:, pl.ds(half, height - half)],
            sems.at[2],
        ),
        pltpu.make_async_copy(inverse_any, inverse_ref, sems.at[3]),
    ]
    for copy in copies:
        copy.start()
    copies[0].wait()
    slots, owned = owners * CAP, inverse_ref.shape[0]
    wanted = unfolded(jnp.sum(names_ref[...], axis=0), 0, id_rows(slots))[:, :slots]
    (wanted_col,) = columns(wanted)
    row_at = lax.broadcasted_iota(jnp.int32, (owned, slots), 0).astype(f32) + 1.0
    col_at = lax.broadcasted_iota(jnp.int32, (slots, owned), 1).astype(f32) + 1.0
    gather = one_hot(row_at == wanted)
    table = one_hot(col_at == wanted_col)
    copies[3].wait()
    inverse = parts(inverse_ref[...])
    for copy in copies[1:3]:
        copy.wait()
    summed = select(gather, get_slab(slab_ref, pieces))
    solved = product(inverse, parts(summed))
    put_slab(answer_ref, select(table, solved))
    total = local_part_ref[...] + 2.0 * jnp.sum(summed * solved, axis=0, keepdims=True)
    sums = folded(total) + folded(square_ref[...])
    sums += [jnp.zeros((1, LANES), f32)] * (tiles(len(sums)) - len(sums))
    answer_ref[:, pieces * CAP :, :] = jnp.broadcast_to(
        jnp.concatenate(sums, axis=0)[None], (owners, len(sums), LANES)
    )


NEAR = (("blk", "up"), ("lat", 0), ("depth", 0), ("depth", 1))
FAR = (("blk", "down"), ("lat", 1))
FIRST = NEAR + FAR
SECOND = (("blk", "up"), ("lat", 0), ("blk", "down"), ("lat", 1), ("depth", 0), ("depth", 1))


def moves(order):
    return [(axis, way) for axis, way in order if route(axis, way)]


def route(axis, way):
    devices = lax.axis_size(axis)
    if way in ("up", "down"):
        by = 1 if way == "up" else -1
        return [(i, (i + by) % devices) for i in range(devices)]
    return [pair for i in range(way, devices - 1, 2) for pair in ((i, i + 1), (i + 1, i))]


def served(axis, way):
    if way in ("up", "down"):
        return 0 if way == "up" else 1
    plus = (lax.rem(lax.axis_index(axis), 2) == way).astype(jnp.int32)
    return (2 if axis == "lat" else 4) + plus


def sent(axis, way):
    return 1 - served(axis, way) if axis == "blk" else served(axis, way)


def rows_of(face, rows):
    if isinstance(face, int):
        return pl.ds(face * rows, rows)
    return pl.ds(pl.multiple_of(face * rows, rows), rows)


def put_faces(image_ref, rows, order, face_refs):
    for ref, move in zip(face_refs, moves(order), strict=True):
        ref[...] = image_ref[rows_of(sent(*move), rows), :]


def exchange(faces, order):
    return [
        lax.ppermute(block, axis, route(axis, way))
        for block, (axis, way) in zip(faces, moves(order), strict=True)
    ]


def image_kernel(pair_depth, returned_ref, table_ref, high_ref, low_ref, local_ref, image_ref, sums_ref, *face_refs):
    rows = local_ref.shape[0] // 6
    width = local_ref.shape[1]
    folds = width // LANES
    correction = select(table_ref[...], get_slab(returned_ref, folds))
    image = local_ref[...] + product((high_ref[...], low_ref[...]), parts(correction))
    image_ref[...] = image
    put_faces(image_ref, rows, FIRST, face_refs)
    tail = jnp.sum(returned_ref[:, folds * CAP :, :], axis=0)
    if pair_depth:
        sums_ref[...] = tail
    else:
        sums_ref[...] = jnp.broadcast_to(tail[None], sums_ref.shape)


def with_got(ref, at, got, move):
    return ref[at, :] + got[move][...] if move in got else ref[at, :]


def new_direction(len_ref, beta, image_ref, prev_ref, got, move, rows):
    face = served(*move)
    at = rows_of(face, rows)
    precond = 0.5 * with_got(image_ref, at, got, move)
    return jnp.where(live_rows(len_ref, face, rows), precond + beta * prev_ref[at, :], 0.0)


def near_kernel(pair_depth, scale, keys, len_ref, sums_ref, prev_rho_ref, image_ref, prev_ref, high_ref, low_ref, *refs):
    got, refs = dict(zip(keys, refs)), refs[len(keys) :]
    if pair_depth:
        sums, refs = sums_ref[...] + refs[0][...], refs[1:]
    else:
        sums = jnp.sum(sums_ref[...], axis=0)
    rho_out, beta_out, square_out, near_ref, image_out = refs
    rows = image_ref.shape[0] // 6
    folds = image_ref.shape[1] // LANES
    rho = scale * unfolded(sums, 0, folds)
    beta = rho / prev_rho_ref[...]
    rho_out[...] = rho
    beta_out[...] = beta
    square_out[...] = unfolded(sums, folds, folds)
    for i, move in enumerate(NEAR):
        near_ref[i * rows : (i + 1) * rows, :] = new_direction(
            len_ref, beta, image_ref, prev_ref, got, move, rows
        )
    first = len(NEAR) * rows
    image_out[...] = product((high_ref[:, :first], low_ref[:, :first]), parts(near_ref[...]))


def far_kernel(keys, len_ref, beta_ref, image_ref, prev_ref, high_ref, low_ref, near_ref, near_image_ref, *refs):
    got, refs = dict(zip(keys, refs)), refs[len(keys) :]
    far_ref, schur_out, *face_refs = refs
    rows = image_ref.shape[0] // 6
    beta = beta_ref[...]
    for i, move in enumerate(FAR):
        far_ref[i * rows : (i + 1) * rows, :] = new_direction(
            len_ref, beta, image_ref, prev_ref, got, move, rows
        )
    first = len(NEAR) * rows
    image = near_image_ref[...] + product(
        (high_ref[:, first:], low_ref[:, first:]), parts(far_ref[...])
    )
    schur_out[...] = image
    put_faces(schur_out, rows, SECOND, face_refs)


def store_kernel(near_ref, far_ref, direction_out, sems):
    rows = far_ref.shape[0] // len(FAR)
    copies = []
    for ref, served_moves in ((near_ref, NEAR), (far_ref, FAR)):
        for i, move in enumerate(served_moves):
            copies.append(
                pltpu.make_async_copy(
                    ref.at[pl.ds(i * rows, rows)],
                    direction_out.at[rows_of(served(*move), rows)],
                    sems.at[len(copies)],
                )
            )
    for copy in copies:
        copy.start()
    for copy in copies:
        copy.wait()


def products_kernel(len_ref, near_ref, far_ref, schur_ref, residual_ref, arrived, out_ref):
    rows = schur_ref.shape[0] // 6
    curve = cross = jnp.zeros((1, schur_ref.shape[1]), f32)
    for ref, served_moves in ((near_ref, NEAR), (far_ref, FAR)):
        for i, move in enumerate(served_moves):
            face = served(*move)
            at = rows_of(face, rows)
            image = schur_ref[at, :]
            live = jnp.where(live_rows(len_ref, face, rows), residual_ref[at, :], 0.0)
            direction = ref[i * rows : (i + 1) * rows, :]
            curve += 2.0 * jnp.sum(direction * image, axis=0, keepdims=True)
            cross += 2.0 * jnp.sum(live * image, axis=0, keepdims=True)
    for j, piece in enumerate(folded(curve) + folded(cross)):
        out_ref[j : j + 1, :] = piece


def applied_kernel(pair_depth, len_ref, stored, schur_ref, *refs):
    keys = moves(SECOND)
    got, refs = dict(zip(keys, refs)), refs[len(keys) :]
    products, (applied_ref, spread_ref) = refs[:-2], refs[-2:]
    rows = schur_ref.shape[0] // 6
    folds = schur_ref.shape[1] // LANES
    total = jnp.zeros((1, schur_ref.shape[1]), f32)
    for move in SECOND:
        face = served(*move)
        at = rows_of(face, rows)
        applied = with_got(schur_ref, at, got, move)
        applied = jnp.where(live_rows(len_ref, face, rows), applied, 0.0)
        applied_ref[at, :] = applied
        total += jnp.sum(applied * applied, axis=0, keepdims=True)
    products = sum(ref[...] for ref in products)
    halves = [products[:folds], products[folds : 2 * folds]]
    if pair_depth:
        halves = [jnp.where(lax.axis_index("depth") == 0, *halves)]
    halves = [[half[j : j + 1] for j in range(folds)] for half in halves]
    for i, half in enumerate([*halves, folded(total)]):
        for j, piece in enumerate(half):
            spread_ref[:, i, j, :] = jnp.broadcast_to(piece, (spread_ref.shape[0], LANES))


def finish_kernel(pair_depth, scale, len_ref, sums_ref, rho_ref, square_ref, residual_ref, applied_ref, new_out, alpha_ref, norm_ref, new_ref, sems):
    rows = applied_ref.shape[0] // 6
    devices, _, folds, _ = sums_ref.shape
    if pair_depth:
        pairs = sums_ref[...].reshape(devices // 2, 2, 2, folds, LANES)
        pairs = jnp.sum(pairs, axis=0)
        sums = [pairs[0, 0], pairs[1, 0], pairs[0, 1] + pairs[1, 1]]
    else:
        total = jnp.sum(sums_ref[...], axis=0)
        sums = [total[i] for i in range(3)]
    curve, cross, applied_square = [unfolded(x, 0, folds) for x in sums]
    alpha = rho_ref[...] / (scale * curve)
    alpha_ref[...] = alpha
    norm_ref[...] = scale * (
        square_ref[...] - 2.0 * alpha * cross + alpha * alpha * applied_square
    )
    copies = []
    for face in range(6):
        at = slice(face * rows, (face + 1) * rows)
        new_ref[at, :] = masked(len_ref, residual_ref, face, rows) - alpha * applied_ref[at, :]
        where = pl.ds(face * rows, rows)
        copies.append(pltpu.make_async_copy(new_ref.at[where], new_out.at[where], sems.at[face]))
        copies[-1].start()
    for copy in copies:
        copy.wait()


def to_all(x, axes):
    return lax.all_to_all(x, axes, split_axis=0, concat_axis=0, tiled=True)


def shards(
    face_len,
    residual,
    prev_direction,
    prev_rho,
    schur,
    neumann,
    coarse_basis,
    coarse_inverse,
    prim_owner,
    coarse_row,
):
    height, width = residual.shape[3:]
    rows = height // 6
    primal = coarse_basis.shape[4]
    owned = coarse_inverse.shape[3]
    owners = lax.axis_size(LAYER)
    slots = owners * CAP
    devices = lax.axis_size(AXES)
    layers = lax.axis_size("depth")
    pair_depth = layers == 2
    scale = 0.5 / (devices * height)
    folds = width // LANES
    tail = tiles(2 * folds)
    id_tail = tiles(id_rows(slots))

    lengths = face_len.reshape(6)
    residual = residual.reshape(height, width)
    prev_direction = prev_direction.reshape(height, width)
    schur = schur.reshape(height, height)
    neumann = neumann.reshape(height, height)
    basis = coarse_basis.reshape(height, primal)
    inverse = coarse_inverse.reshape(owned, owned)
    owner = prim_owner.reshape(1, primal)
    wanted = coarse_row.reshape(1, primal)
    whole = shape_of(height, width)
    row = shape_of(1, width)
    face = shape_of(rows, width)

    (outgoing,) = call(
        pack_kernel,
        [shape_of(owners, folds * CAP + id_tail, LANES)],
        [lengths, owner, wanted, residual, basis],
        far=range(5),
        flops=6 * height * primal * width,
        moved=4 * (height * (width + primal) + slots * width),
        scratch=[
            pltpu.SMEM((6,), jnp.int32),
            pltpu.VMEM((1, primal), jnp.int32),
            pltpu.VMEM((1, primal), jnp.int32),
            pltpu.VMEM((height, width), f32),
            pltpu.VMEM((height, primal), f32),
            pltpu.SemaphoreType.DMA((3, 2)),
            pltpu.SemaphoreType.DMA((3,)),
        ],
    )
    incoming = to_all(outgoing, LAYER)
    local, local_part, square, table, *halves = call(
        local_kernel,
        [whole, row, row, shape_of(primal, slots, dtype=bf16)]
        + [shape_of(height, primal, dtype=bf16)] * 2
        + [shape_of(height, height, dtype=bf16)] * 2,
        [lengths, residual, neumann, owner, basis, schur],
        smem=(0,),
        flops=6 * height * height * width,
        moved=4 * height * (3 * height + 2 * width),
    )
    basis_halves, schur_halves = halves[:2], halves[2:]
    (answers,) = call(
        solve_kernel,
        [shape_of(owners, folds * CAP + tail, LANES)],
        [incoming, inverse, local_part, square],
        far=range(2),
        flops=(8 * slots + 6 * owned) * owned * width,
        moved=8 * slots * width,
        scratch=[
            pltpu.VMEM((owners, id_tail, LANES), f32),
            pltpu.VMEM((owners, folds * CAP, LANES), f32),
            pltpu.VMEM((owned, owned), f32),
            pltpu.SemaphoreType.DMA((4,)),
        ],
    )
    returned = to_all(answers, LAYER)
    keys = moves(FIRST)
    faces = [face] * len(keys)
    image, sums, *outward = call(
        functools.partial(image_kernel, pair_depth),
        [whole, shape_of(tail, LANES) if pair_depth else shape_of(layers, tail, LANES), *faces],
        [returned, table, *basis_halves, local],
        flops=(6 * height + 4 * slots) * primal * width,
        moved=16 * height * width,
    )
    got = dict(zip(keys, exchange(outward, FIRST)))
    if pair_depth:
        sums = [sums, lax.ppermute(sums, "depth", route("depth", 0))]
    else:
        sums = [to_all(sums, "depth")]
    near_keys, far_keys = moves(NEAR), moves(FAR)
    rho, beta, square, near, near_image = call(
        functools.partial(near_kernel, pair_depth, scale, near_keys),
        [row, row, row, shape_of(len(NEAR) * rows, width), whole],
        [lengths, sums[0], prev_rho.reshape(1, width), image, prev_direction, *schur_halves]
        + [got[key] for key in near_keys]
        + sums[1:],
        smem=(0,),
        flops=4 * height * height * width,
        moved=4 * height * (height + 4 * width),
    )
    far, schur_image, *outward = call(
        functools.partial(far_kernel, far_keys),
        [shape_of(len(FAR) * rows, width), whole, *faces],
        [lengths, beta, image, prev_direction, *schur_halves, near, near_image]
        + [got[key] for key in far_keys],
        smem=(0,),
        flops=2 * height * height * width,
        moved=4 * height * (height + 4 * width),
    )
    got = exchange(outward, SECOND)
    (products,) = call(
        products_kernel,
        [shape_of(2 * folds, LANES)],
        [lengths, near, far, schur_image, residual, got[0]],
        smem=(0,),
        loose=(5,),
        flops=4 * height * width,
        moved=12 * height * width,
    )
    products = [products]
    if pair_depth:
        products.append(lax.ppermute(products[0], "depth", route("depth", 0)))
    (direction,) = call(
        store_kernel,
        [whole],
        [near, far],
        far_out=(0,),
        moved=8 * height * width,
        scratch=[pltpu.SemaphoreType.DMA((6,))],
    )
    applied, spread_sums = call(
        functools.partial(applied_kernel, pair_depth),
        [whole, shape_of(devices, 2 if pair_depth else 3, folds, LANES)],
        [lengths, direction, schur_image, *got, *products],
        smem=(0,),
        far=(1,),
        flops=4 * height * width,
        moved=12 * height * width,
    )
    new_residual, alpha, norm = call(
        functools.partial(finish_kernel, pair_depth, scale),
        [whole, row, row],
        [lengths, to_all(spread_sums, AXES), rho, square, residual, applied],
        smem=(0,),
        far_out=(0,),
        flops=4 * height * width,
        moved=12 * height * width,
        scratch=[pltpu.VMEM((height, width), f32), pltpu.SemaphoreType.DMA((6,))],
    )
    out_shape = (1, 1, 1, height, width)
    return (
        new_residual.reshape(out_shape),
        direction.reshape(out_shape),
        rho.reshape(width),
        alpha.reshape(width),
        norm.reshape(width),
    )


def solution(mesh):
    tall = P("blk", "lat", "depth", None, None)
    flat = P("blk", "lat", "depth", None)
    in_specs = (flat, tall, tall, P(), tall, tall, tall, tall, tall, flat)
    out_specs = (tall, tall, P(), P(), P())
    return jax.shard_map(shards, mesh=mesh, in_specs=in_specs, out_specs=out_specs, check_vma=False)
```

```python
import functools

import jax
import jax.numpy as jnp
from jax import lax
from jax.experimental import pallas as pl
from jax.experimental.pallas import tpu as pltpu
from jax.sharding import PartitionSpec as P

CAP = 24
AXES = ("blk", "lat", "depth")
LAYER = ("lat", "blk")
LANES = 128
TILE = 8
f32 = jnp.float32
bf16 = jnp.bfloat16

VMEM = pl.BlockSpec(memory_space=pltpu.VMEM)
SMEM = pl.BlockSpec(memory_space=pltpu.SMEM)
ANY = pl.BlockSpec(memory_space=pl.ANY)


def shape_of(*dims, dtype=f32):
    return jax.ShapeDtypeStruct(dims, dtype)


def call(body, outs, operands, smem=(), far=(), loose=(), far_out=(), flops=0, moved=0, scratch=(), room=32):
    in_specs = [
        SMEM if i in smem else ANY if i in far or i in loose else VMEM
        for i in range(len(operands))
    ]
    operands = [
        pltpu.with_memory_space_constraint(x, pltpu.HBM) if i in far else x
        for i, x in enumerate(operands)
    ]
    out_specs = [ANY if i in far_out else VMEM for i in range(len(outs))]
    return pl.pallas_call(
        body,
        out_shape=list(outs),
        in_specs=in_specs,
        out_specs=out_specs,
        scratch_shapes=list(scratch),
        compiler_params=pltpu.CompilerParams(vmem_limit_bytes=room << 20),
        cost_estimate=pl.CostEstimate(flops=flops, bytes_accessed=moved, transcendentals=0),
    )(*operands)


def parts(x):
    high = x.astype(bf16)
    low = (x - high.astype(f32)).astype(bf16)
    return high, low


def mul(a, b, dims):
    return lax.dot_general(a, b, (dims, ((), ())), preferred_element_type=f32)


PLAIN = ((1,), (0,))


def product(a, b, dims=PLAIN):
    (ah, al), (bh, bl) = a, b
    return mul(ah, bh, dims) + (mul(ah, bl, dims) + mul(al, bh, dims))


def select(table, x, dims=PLAIN):
    high, low = parts(x)
    return mul(table, high, dims) + mul(table, low, dims)


def one_hot(hit):
    return jnp.where(hit, 1.0, 0.0).astype(bf16)


def live_rows(len_ref, face, rows):
    return lax.broadcasted_iota(jnp.int32, (rows, 1), 0) < len_ref[face]


def masked(len_ref, ref, face, rows):
    block = ref[face * rows : (face + 1) * rows, :]
    return jnp.where(live_rows(len_ref, face, rows), block, 0.0)


def folded(vector):
    pieces = vector.shape[1] // LANES
    return [vector[:, j * LANES : (j + 1) * LANES] for j in range(pieces)]


def unfolded(block, first, pieces):
    return jnp.concatenate([block[first + j : first + j + 1, :] for j in range(pieces)], axis=1)


def id_rows(slots):
    return -(-slots // LANES)


def tiles(rows):
    return -(-rows // TILE) * TILE


def put_slab(out_ref, block):
    owners = out_ref.shape[0]
    for j in range(block.shape[1] // LANES):
        piece = block[:, j * LANES : (j + 1) * LANES]
        out_ref[:, j * CAP : (j + 1) * CAP, :] = piece.reshape(owners, CAP, LANES)


def get_slab(ref, pieces):
    slots = ref.shape[0] * CAP
    return jnp.concatenate(
        [ref[:, j * CAP : (j + 1) * CAP, :].reshape(slots, LANES) for j in range(pieces)], axis=1
    )


def columns(*rows):
    spare = [jnp.zeros_like(rows[0])] * (TILE - len(rows))
    turned = jnp.transpose(jnp.concatenate([*rows, *spare], axis=0))
    return [turned[:, i : i + 1] for i in range(len(rows))]


def position(owner):
    lats = lax.axis_size("lat")
    blk = jnp.floor((owner.astype(f32) + 0.5) * (1.0 / lats))
    return (owner.astype(f32) - lats * blk) * lax.axis_size("blk") + blk


def ranks(own_row):
    primal = own_row.shape[1]
    (own_col,) = columns(own_row)
    row_at = lax.broadcasted_iota(jnp.int32, (primal, primal), 0)
    col_at = lax.broadcasted_iota(jnp.int32, (primal, primal), 1)
    before = (own_row == own_col) & (row_at < col_at)
    return jnp.sum(jnp.where(before, 1.0, 0.0), axis=0, keepdims=True), own_col


def pack_kernel(len_any, owner_any, row_any, residual_any, basis_any, slab_ref, *refs):
    len_ref, owner_ref, row_ref, residual_ref, basis_ref, sems, small_sems = refs
    rows = residual_ref.shape[0] // 6
    primal = basis_ref.shape[1]
    owners = slab_ref.shape[0]
    slots = owners * CAP
    small = [
        pltpu.make_async_copy(src, dst, small_sems.at[i])
        for i, (src, dst) in enumerate(
            [(owner_any, owner_ref), (row_any, row_ref), (len_any, len_ref)]
        )
    ]
    large = []
    for pair in range(3):
        at = pl.ds(2 * pair * rows, 2 * rows)
        large.append(
            (
                pltpu.make_async_copy(residual_any.at[at], residual_ref.at[at], sems.at[pair, 0]),
                pltpu.make_async_copy(basis_any.at[at], basis_ref.at[at], sems.at[pair, 1]),
            )
        )
    for copy in small:
        copy.start()
    for pair in large:
        for copy in pair:
            copy.start()
    for copy in small:
        copy.wait()
    own_row = position(owner_ref[...])
    wanted_row = row_ref[...].astype(f32) + 1.0
    rank_row, _ = ranks(own_row)
    slot_row = (own_row * CAP + rank_row).astype(jnp.int32)
    rank_col, wanted_col = columns(rank_row, wanted_row)
    packer = one_hot(lax.broadcasted_iota(jnp.int32, (slots, primal), 0) == slot_row)
    to_owner = one_hot(
        lax.broadcasted_iota(jnp.int32, (owners, primal), 0) == own_row.astype(jnp.int32)
    )
    at_owner = lax.axis_index(LAYER) * CAP + rank_col.astype(jnp.int32)
    place = lax.broadcasted_iota(jnp.int32, (primal, id_rows(slots) * LANES), 1)
    names = select(to_owner, jnp.where(place == at_owner, wanted_col, 0.0))
    terms = None
    for pair in range(3):
        for copy in large[pair]:
            copy.wait()
        weighted = jnp.concatenate(
            [0.5 * masked(len_ref, residual_ref, 2 * pair + side, rows) for side in range(2)],
            axis=0,
        )
        basis = basis_ref[2 * pair * rows : 2 * (pair + 1) * rows, :]
        term = product(parts(jnp.transpose(basis)), parts(weighted))
        terms = term if terms is None else terms + term
    put_slab(slab_ref, select(packer, terms))
    tail = slab_ref.shape[1] - tiles(id_rows(slots))
    names = jnp.concatenate(
        [names, jnp.zeros((owners, (slab_ref.shape[1] - tail) * LANES - names.shape[1]), f32)], axis=1
    )
    for j in range(slab_ref.shape[1] - tail):
        slab_ref[:, tail + j, :] = names[:, j * LANES : (j + 1) * LANES]


def local_kernel(len_ref, residual_ref, matrix_ref, owner_ref, *refs):
    whole, refs = refs[:2], refs[2:]
    local_ref, part_ref, square_ref, table_ref, refs = *refs[:4], refs[4:]
    rows = residual_ref.shape[0] // 6
    live = jnp.concatenate(
        [masked(len_ref, residual_ref, face, rows) for face in range(6)], axis=0
    )
    local = product(parts(matrix_ref[...]), parts(0.5 * live))
    local_ref[...] = local
    part_ref[...] = jnp.sum(live * local, axis=0, keepdims=True)
    square_ref[...] = jnp.sum(live * live, axis=0, keepdims=True)
    refs[0][...], refs[1][...] = parts(whole[0][...])
    for i, move in enumerate(NEAR + FAR):
        at = slice(i * rows, (i + 1) * rows)
        refs[2][:, at], refs[3][:, at] = parts(whole[1][:, rows_of(served(*move), rows)])
    primal, slots = table_ref.shape
    rank_row, own_col = ranks(position(owner_ref[...]))
    (rank_col,) = columns(rank_row)
    slot_col = (own_col * CAP + rank_col).astype(jnp.int32)
    table_ref[...] = one_hot(lax.broadcasted_iota(jnp.int32, (primal, slots), 1) == slot_col)


def solve_kernel(incoming_any, inverse_any, local_part_ref, square_ref, answer_ref, *refs):
    names_ref, slab_ref, inverse_ref, sems = refs
    owners, height, _ = slab_ref.shape
    pieces = height // CAP
    half = pieces // 2 * CAP
    copies = [
        pltpu.make_async_copy(
            incoming_any.at[:, pl.ds(height, names_ref.shape[1])], names_ref, sems.at[0]
        ),
        pltpu.make_async_copy(
            incoming_any.at[:, pl.ds(0, half)], slab_ref.at[:, pl.ds(0, half)], sems.at[1]
        ),
        pltpu.make_async_copy(
            incoming_any.at[:, pl.ds(half, height - half)],
            slab_ref.at[:, pl.ds(half, height - half)],
            sems.at[2],
        ),
        pltpu.make_async_copy(inverse_any, inverse_ref, sems.at[3]),
    ]
    for copy in copies:
        copy.start()
    copies[0].wait()
    slots, owned = owners * CAP, inverse_ref.shape[0]
    wanted = unfolded(jnp.sum(names_ref[...], axis=0), 0, id_rows(slots))[:, :slots]
    (wanted_col,) = columns(wanted)
    row_at = lax.broadcasted_iota(jnp.int32, (owned, slots), 0).astype(f32) + 1.0
    col_at = lax.broadcasted_iota(jnp.int32, (slots, owned), 1).astype(f32) + 1.0
    gather = one_hot(row_at == wanted)
    table = one_hot(col_at == wanted_col)
    copies[3].wait()
    inverse = parts(inverse_ref[...])
    for copy in copies[1:3]:
        copy.wait()
    summed = select(gather, get_slab(slab_ref, pieces))
    solved = product(inverse, parts(summed))
    put_slab(answer_ref, select(table, solved))
    total = local_part_ref[...] + 2.0 * jnp.sum(summed * solved, axis=0, keepdims=True)
    sums = folded(total) + folded(square_ref[...])
    sums += [jnp.zeros((1, LANES), f32)] * (tiles(len(sums)) - len(sums))
    answer_ref[:, pieces * CAP :, :] = jnp.broadcast_to(
        jnp.concatenate(sums, axis=0)[None], (owners, len(sums), LANES)
    )


NEAR = (("blk", "up"), ("lat", 0), ("depth", 0), ("depth", 1))
FAR = (("blk", "down"), ("lat", 1))
FIRST = NEAR + FAR
SECOND = (("blk", "up"), ("lat", 0), ("blk", "down"), ("lat", 1), ("depth", 0), ("depth", 1))


def moves(order):
    return [(axis, way) for axis, way in order if route(axis, way)]


def route(axis, way):
    devices = lax.axis_size(axis)
    if way in ("up", "down"):
        by = 1 if way == "up" else -1
        return [(i, (i + by) % devices) for i in range(devices)]
    return [pair for i in range(way, devices - 1, 2) for pair in ((i, i + 1), (i + 1, i))]


def served(axis, way):
    if way in ("up", "down"):
        return 0 if way == "up" else 1
    plus = (lax.rem(lax.axis_index(axis), 2) == way).astype(jnp.int32)
    return (2 if axis == "lat" else 4) + plus


def sent(axis, way):
    return 1 - served(axis, way) if axis == "blk" else served(axis, way)


def rows_of(face, rows):
    if isinstance(face, int):
        return pl.ds(face * rows, rows)
    return pl.ds(pl.multiple_of(face * rows, rows), rows)


def put_faces(image_ref, rows, order, face_refs):
    for ref, move in zip(face_refs, moves(order), strict=True):
        ref[...] = image_ref[rows_of(sent(*move), rows), :]


def exchange(faces, order):
    return [
        lax.ppermute(block, axis, route(axis, way))
        for block, (axis, way) in zip(faces, moves(order), strict=True)
    ]


def image_kernel(pair_depth, returned_ref, table_ref, high_ref, low_ref, local_ref, image_ref, sums_ref, *face_refs):
    rows = local_ref.shape[0] // 6
    width = local_ref.shape[1]
    folds = width // LANES
    correction = select(table_ref[...], get_slab(returned_ref, folds))
    image = local_ref[...] + product((high_ref[...], low_ref[...]), parts(correction))
    image_ref[...] = image
    put_faces(image_ref, rows, FIRST, face_refs)
    tail = jnp.sum(returned_ref[:, folds * CAP :, :], axis=0)
    if pair_depth:
        sums_ref[...] = tail
    else:
        sums_ref[...] = jnp.broadcast_to(tail[None], sums_ref.shape)


def with_got(ref, at, got, move):
    return ref[at, :] + got[move][...] if move in got else ref[at, :]


def new_direction(len_ref, beta, image_ref, prev_ref, got, move, rows):
    face = served(*move)
    at = rows_of(face, rows)
    precond = 0.5 * with_got(image_ref, at, got, move)
    return jnp.where(live_rows(len_ref, face, rows), precond + beta * prev_ref[at, :], 0.0)


def near_kernel(pair_depth, scale, keys, len_ref, sums_ref, prev_rho_ref, image_ref, prev_ref, high_ref, low_ref, *refs):
    got, refs = dict(zip(keys, refs)), refs[len(keys) :]
    if pair_depth:
        sums, refs = sums_ref[...] + refs[0][...], refs[1:]
    else:
        sums = jnp.sum(sums_ref[...], axis=0)
    rho_out, beta_out, square_out, near_ref, image_out = refs
    rows = image_ref.shape[0] // 6
    folds = image_ref.shape[1] // LANES
    rho = scale * unfolded(sums, 0, folds)
    beta = rho / prev_rho_ref[...]
    rho_out[...] = rho
    beta_out[...] = beta
    square_out[...] = unfolded(sums, folds, folds)
    for i, move in enumerate(NEAR):
        near_ref[i * rows : (i + 1) * rows, :] = new_direction(
            len_ref, beta, image_ref, prev_ref, got, move, rows
        )
    first = len(NEAR) * rows
    image_out[...] = product((high_ref[:, :first], low_ref[:, :first]), parts(near_ref[...]))


def far_kernel(keys, len_ref, beta_ref, image_ref, prev_ref, high_ref, low_ref, near_ref, near_image_ref, *refs):
    got, refs = dict(zip(keys, refs)), refs[len(keys) :]
    far_ref, schur_out, *face_refs = refs
    rows = image_ref.shape[0] // 6
    beta = beta_ref[...]
    for i, move in enumerate(FAR):
        far_ref[i * rows : (i + 1) * rows, :] = new_direction(
            len_ref, beta, image_ref, prev_ref, got, move, rows
        )
    first = len(NEAR) * rows
    image = near_image_ref[...] + product(
        (high_ref[:, first:], low_ref[:, first:]), parts(far_ref[...])
    )
    schur_out[...] = image
    put_faces(schur_out, rows, SECOND, face_refs)


def store_kernel(near_ref, far_ref, direction_out, sems):
    rows = far_ref.shape[0] // len(FAR)
    copies = []
    for ref, served_moves in ((near_ref, NEAR), (far_ref, FAR)):
        for i, move in enumerate(served_moves):
            copies.append(
                pltpu.make_async_copy(
                    ref.at[pl.ds(i * rows, rows)],
                    direction_out.at[rows_of(served(*move), rows)],
                    sems.at[len(copies)],
                )
            )
    for copy in copies:
        copy.start()
    for copy in copies:
        copy.wait()


def products_kernel(len_ref, near_ref, far_ref, schur_ref, residual_ref, arrived, out_ref):
    rows = schur_ref.shape[0] // 6
    curve = cross = jnp.zeros((1, schur_ref.shape[1]), f32)
    for ref, served_moves in ((near_ref, NEAR), (far_ref, FAR)):
        for i, move in enumerate(served_moves):
            face = served(*move)
            at = rows_of(face, rows)
            image = schur_ref[at, :]
            live = jnp.where(live_rows(len_ref, face, rows), residual_ref[at, :], 0.0)
            direction = ref[i * rows : (i + 1) * rows, :]
            curve += 2.0 * jnp.sum(direction * image, axis=0, keepdims=True)
            cross += 2.0 * jnp.sum(live * image, axis=0, keepdims=True)
    for j, piece in enumerate(folded(curve) + folded(cross)):
        out_ref[j : j + 1, :] = piece


def applied_kernel(pair_depth, len_ref, stored, schur_ref, *refs):
    keys = moves(SECOND)
    got, refs = dict(zip(keys, refs)), refs[len(keys) :]
    products, (applied_ref, spread_ref) = refs[:-2], refs[-2:]
    rows = schur_ref.shape[0] // 6
    folds = schur_ref.shape[1] // LANES
    total = jnp.zeros((1, schur_ref.shape[1]), f32)
    for move in SECOND:
        face = served(*move)
        at = rows_of(face, rows)
        applied = with_got(schur_ref, at, got, move)
        applied = jnp.where(live_rows(len_ref, face, rows), applied, 0.0)
        applied_ref[at, :] = applied
        total += jnp.sum(applied * applied, axis=0, keepdims=True)
    products = sum(ref[...] for ref in products)
    halves = [products[:folds], products[folds : 2 * folds]]
    if pair_depth:
        halves = [jnp.where(lax.axis_index("depth") == 0, *halves)]
    halves = [[half[j : j + 1] for j in range(folds)] for half in halves]
    for i, half in enumerate([*halves, folded(total)]):
        for j, piece in enumerate(half):
            spread_ref[:, i, j, :] = jnp.broadcast_to(piece, (spread_ref.shape[0], LANES))


def finish_kernel(pair_depth, scale, len_ref, sums_ref, rho_ref, square_ref, residual_ref, applied_ref, new_out, alpha_ref, norm_ref, new_ref, sems):
    rows = applied_ref.shape[0] // 6
    devices, _, folds, _ = sums_ref.shape
    if pair_depth:
        pairs = sums_ref[...].reshape(devices // 2, 2, 2, folds, LANES)
        pairs = jnp.sum(pairs, axis=0)
        sums = [pairs[0, 0], pairs[1, 0], pairs[0, 1] + pairs[1, 1]]
    else:
        total = jnp.sum(sums_ref[...], axis=0)
        sums = [total[i] for i in range(3)]
    curve, cross, applied_square = [unfolded(x, 0, folds) for x in sums]
    alpha = rho_ref[...] / (scale * curve)
    alpha_ref[...] = alpha
    norm_ref[...] = scale * (
        square_ref[...] - 2.0 * alpha * cross + alpha * alpha * applied_square
    )
    copies = []
    for face in range(6):
        at = slice(face * rows, (face + 1) * rows)
        new_ref[at, :] = masked(len_ref, residual_ref, face, rows) - alpha * applied_ref[at, :]
        where = pl.ds(face * rows, rows)
        copies.append(pltpu.make_async_copy(new_ref.at[where], new_out.at[where], sems.at[face]))
        copies[-1].start()
    for copy in copies:
        copy.wait()


def to_all(x, axes):
    return lax.all_to_all(x, axes, split_axis=0, concat_axis=0, tiled=True)


def shards(
    face_len,
    residual,
    prev_direction,
    prev_rho,
    schur,
    neumann,
    coarse_basis,
    coarse_inverse,
    prim_owner,
    coarse_row,
):
    height, width = residual.shape[3:]
    rows = height // 6
    primal = coarse_basis.shape[4]
    owned = coarse_inverse.shape[3]
    owners = lax.axis_size(LAYER)
    slots = owners * CAP
    devices = lax.axis_size(AXES)
    layers = lax.axis_size("depth")
    pair_depth = layers == 2
    scale = 0.5 / (devices * height)
    folds = width // LANES
    tail = tiles(2 * folds)
    id_tail = tiles(id_rows(slots))

    lengths = face_len.reshape(6)
    residual = residual.reshape(height, width)
    prev_direction = prev_direction.reshape(height, width)
    schur = schur.reshape(height, height)
    neumann = neumann.reshape(height, height)
    basis = coarse_basis.reshape(height, primal)
    inverse = coarse_inverse.reshape(owned, owned)
    owner = prim_owner.reshape(1, primal)
    wanted = coarse_row.reshape(1, primal)
    whole = shape_of(height, width)
    row = shape_of(1, width)
    face = shape_of(rows, width)

    (outgoing,) = call(
        pack_kernel,
        [shape_of(owners, folds * CAP + id_tail, LANES)],
        [lengths, owner, wanted, residual, basis],
        far=range(5),
        flops=6 * height * primal * width,
        moved=4 * (height * (width + primal) + slots * width),
        scratch=[
            pltpu.SMEM((6,), jnp.int32),
            pltpu.VMEM((1, primal), jnp.int32),
            pltpu.VMEM((1, primal), jnp.int32),
            pltpu.VMEM((height, width), f32),
            pltpu.VMEM((height, primal), f32),
            pltpu.SemaphoreType.DMA((3, 2)),
            pltpu.SemaphoreType.DMA((3,)),
        ],
    )
    incoming = to_all(outgoing, LAYER)
    local, local_part, square, table, *halves = call(
        local_kernel,
        [whole, row, row, shape_of(primal, slots, dtype=bf16)]
        + [shape_of(height, primal, dtype=bf16)] * 2
        + [shape_of(height, height, dtype=bf16)] * 2,
        [lengths, residual, neumann, owner, basis, schur],
        smem=(0,),
        flops=6 * height * height * width,
        moved=4 * height * (3 * height + 2 * width),
    )
    basis_halves, schur_halves = halves[:2], halves[2:]
    (answers,) = call(
        solve_kernel,
        [shape_of(owners, folds * CAP + tail, LANES)],
        [incoming, inverse, local_part, square],
        far=range(2),
        flops=(8 * slots + 6 * owned) * owned * width,
        moved=8 * slots * width,
        scratch=[
            pltpu.VMEM((owners, id_tail, LANES), f32),
            pltpu.VMEM((owners, folds * CAP, LANES), f32),
            pltpu.VMEM((owned, owned), f32),
            pltpu.SemaphoreType.DMA((4,)),
        ],
    )
    returned = to_all(answers, LAYER)
    keys = moves(FIRST)
    faces = [face] * len(keys)
    image, sums, *outward = call(
        functools.partial(image_kernel, pair_depth),
        [whole, shape_of(tail, LANES) if pair_depth else shape_of(layers, tail, LANES), *faces],
        [returned, table, *basis_halves, local],
        flops=(6 * height + 4 * slots) * primal * width,
        moved=16 * height * width,
    )
    got = dict(zip(keys, exchange(outward, FIRST)))
    if pair_depth:
        sums = [sums, lax.ppermute(sums, "depth", route("depth", 0))]
    else:
        sums = [to_all(sums, "depth")]
    near_keys, far_keys = moves(NEAR), moves(FAR)
    rho, beta, square, near, near_image = call(
        functools.partial(near_kernel, pair_depth, scale, near_keys),
        [row, row, row, shape_of(len(NEAR) * rows, width), whole],
        [lengths, sums[0], prev_rho.reshape(1, width), image, prev_direction, *schur_halves]
        + [got[key] for key in near_keys]
        + sums[1:],
        smem=(0,),
        flops=4 * height * height * width,
        moved=4 * height * (height + 4 * width),
    )
    far, schur_image, *outward = call(
        functools.partial(far_kernel, far_keys),
        [shape_of(len(FAR) * rows, width), whole, *faces],
        [lengths, beta, image, prev_direction, *schur_halves, near, near_image]
        + [got[key] for key in far_keys],
        smem=(0,),
        flops=2 * height * height * width,
        moved=4 * height * (height + 4 * width),
    )
    got = exchange(outward, SECOND)
    (products,) = call(
        products_kernel,
        [shape_of(2 * folds, LANES)],
        [lengths, near, far, schur_image, residual, got[0]],
        smem=(0,),
        loose=(5,),
        flops=4 * height * width,
        moved=12 * height * width,
    )
    products = [products]
    if pair_depth:
        products.append(lax.ppermute(products[0], "depth", route("depth", 0)))
    (direction,) = call(
        store_kernel,
        [whole],
        [near, far],
        far_out=(0,),
        moved=8 * height * width,
        scratch=[pltpu.SemaphoreType.DMA((6,))],
    )
    applied, spread_sums = call(
        functools.partial(applied_kernel, pair_depth),
        [whole, shape_of(devices, 2 if pair_depth else 3, folds, LANES)],
        [lengths, direction, schur_image, *got, *products],
        smem=(0,),
        far=(1,),
        flops=4 * height * width,
        moved=12 * height * width,
    )
    new_residual, alpha, norm = call(
        functools.partial(finish_kernel, pair_depth, scale),
        [whole, row, row],
        [lengths, to_all(spread_sums, AXES), rho, square, residual, applied],
        smem=(0,),
        far_out=(0,),
        flops=4 * height * width,
        moved=12 * height * width,
        scratch=[pltpu.VMEM((height, width), f32), pltpu.SemaphoreType.DMA((6,))],
    )
    out_shape = (1, 1, 1, height, width)
    return (
        new_residual.reshape(out_shape),
        direction.reshape(out_shape),
        rho.reshape(width),
        alpha.reshape(width),
        norm.reshape(width),
    )


def solution(mesh):
    tall = P("blk", "lat", "depth", None, None)
    flat = P("blk", "lat", "depth", None)
    in_specs = (flat, tall, tall, P(), tall, tall, tall, tall, tall, flat)
    out_specs = (tall, tall, P(), P(), P())
    return jax.shard_map(shards, mesh=mesh, in_specs=in_specs, out_specs=out_specs, check_vma=False)
```

```python
import functools

import jax
import jax.numpy as jnp
from jax import lax
from jax.experimental import pallas as pl
from jax.experimental.pallas import tpu as pltpu
from jax.sharding import PartitionSpec as P

CAP = 24
AXES = ("blk", "lat", "depth")
LAYER = ("blk", "lat")
LANES = 128
TILE = 8
f32 = jnp.float32
bf16 = jnp.bfloat16

VMEM = pl.BlockSpec(memory_space=pltpu.VMEM)
SMEM = pl.BlockSpec(memory_space=pltpu.SMEM)
ANY = pl.BlockSpec(memory_space=pl.ANY)


def shape_of(*dims, dtype=f32):
    return jax.ShapeDtypeStruct(dims, dtype)


def call(body, outs, operands, smem=(), far=(), loose=(), far_out=(), flops=0, moved=0, scratch=(), room=32):
    in_specs = [
        SMEM if i in smem else ANY if i in far or i in loose else VMEM
        for i in range(len(operands))
    ]
    operands = [
        pltpu.with_memory_space_constraint(x, pltpu.HBM) if i in far else x
        for i, x in enumerate(operands)
    ]
    out_specs = [ANY if i in far_out else VMEM for i in range(len(outs))]
    return pl.pallas_call(
        body,
        out_shape=list(outs),
        in_specs=in_specs,
        out_specs=out_specs,
        scratch_shapes=list(scratch),
        compiler_params=pltpu.CompilerParams(vmem_limit_bytes=room << 20),
        cost_estimate=pl.CostEstimate(flops=flops, bytes_accessed=moved, transcendentals=0),
    )(*operands)


def parts(x):
    high = x.astype(bf16)
    low = (x - high.astype(f32)).astype(bf16)
    return high, low


def mul(a, b, dims):
    return lax.dot_general(a, b, (dims, ((), ())), preferred_element_type=f32)


PLAIN = ((1,), (0,))


def product(a, b, dims=PLAIN):
    (ah, al), (bh, bl) = a, b
    return mul(ah, bh, dims) + (mul(ah, bl, dims) + mul(al, bh, dims))


def select(table, x, dims=PLAIN):
    high, low = parts(x)
    return mul(table, high, dims) + mul(table, low, dims)


def one_hot(hit):
    return jnp.where(hit, 1.0, 0.0).astype(bf16)


def live_rows(len_ref, face, rows):
    return lax.broadcasted_iota(jnp.int32, (rows, 1), 0) < len_ref[face]


def masked(len_ref, ref, face, rows):
    block = ref[face * rows : (face + 1) * rows, :]
    return jnp.where(live_rows(len_ref, face, rows), block, 0.0)


def folded(vector):
    pieces = vector.shape[1] // LANES
    return [vector[:, j * LANES : (j + 1) * LANES] for j in range(pieces)]


def unfolded(block, first, pieces):
    return jnp.concatenate([block[first + j : first + j + 1, :] for j in range(pieces)], axis=1)


def id_rows(slots):
    return -(-slots // LANES)


def tiles(rows):
    return -(-rows // TILE) * TILE


def put_slab(out_ref, block):
    owners = out_ref.shape[0]
    for j in range(block.shape[1] // LANES):
        piece = block[:, j * LANES : (j + 1) * LANES]
        out_ref[:, j * CAP : (j + 1) * CAP, :] = piece.reshape(owners, CAP, LANES)


def get_slab(ref, pieces):
    slots = ref.shape[0] * CAP
    return jnp.concatenate(
        [ref[:, j * CAP : (j + 1) * CAP, :].reshape(slots, LANES) for j in range(pieces)], axis=1
    )


def columns(*rows):
    spare = [jnp.zeros_like(rows[0])] * (TILE - len(rows))
    turned = jnp.transpose(jnp.concatenate([*rows, *spare], axis=0))
    return [turned[:, i : i + 1] for i in range(len(rows))]


def ranks(own_row):
    primal = own_row.shape[1]
    (own_col,) = columns(own_row)
    row_at = lax.broadcasted_iota(jnp.int32, (primal, primal), 0)
    col_at = lax.broadcasted_iota(jnp.int32, (primal, primal), 1)
    before = (own_row == own_col) & (row_at < col_at)
    return jnp.sum(jnp.where(before, 1.0, 0.0), axis=0, keepdims=True), own_col


def pack_kernel(len_any, owner_any, row_any, residual_any, basis_any, slab_ref, *refs):
    len_ref, owner_ref, row_ref, residual_ref, basis_ref, sems, small_sems = refs
    rows = residual_ref.shape[0] // 6
    primal = basis_ref.shape[1]
    owners = slab_ref.shape[0]
    slots = owners * CAP
    small = [
        pltpu.make_async_copy(src, dst, small_sems.at[i])
        for i, (src, dst) in enumerate(
            [(owner_any, owner_ref), (row_any, row_ref), (len_any, len_ref)]
        )
    ]
    large = []
    for face in range(6):
        at = pl.ds(face * rows, rows)
        large += [
            pltpu.make_async_copy(residual_any.at[at], residual_ref.at[at], sems.at[face, 0]),
            pltpu.make_async_copy(basis_any.at[at], basis_ref.at[at], sems.at[face, 1]),
        ]
    for copy in small:
        copy.start()
    for copy in large:
        copy.start()
    for copy in small:
        copy.wait()
    own_row = owner_ref[...].astype(f32)
    wanted_row = row_ref[...].astype(f32) + 1.0
    rank_row, _ = ranks(own_row)
    slot_row = (own_row * CAP + rank_row).astype(jnp.int32)
    rank_col, wanted_col = columns(rank_row, wanted_row)
    packer = one_hot(lax.broadcasted_iota(jnp.int32, (slots, primal), 0) == slot_row)
    to_owner = one_hot(lax.broadcasted_iota(jnp.int32, (owners, primal), 0) == owner_ref[...])
    at_owner = lax.axis_index(LAYER) * CAP + rank_col.astype(jnp.int32)
    place = lax.broadcasted_iota(jnp.int32, (primal, id_rows(slots) * LANES), 1)
    names = select(to_owner, jnp.where(place == at_owner, wanted_col, 0.0))
    terms = None
    for pair in range(3):
        for copy in large[4 * pair : 4 * pair + 4]:
            copy.wait()
        weighted = jnp.concatenate(
            [0.5 * masked(len_ref, residual_ref, 2 * pair + side, rows) for side in range(2)],
            axis=0,
        )
        basis = basis_ref[2 * pair * rows : 2 * (pair + 1) * rows, :]
        term = product(parts(jnp.transpose(basis)), parts(weighted))
        terms = term if terms is None else terms + term
    put_slab(slab_ref, select(packer, terms))
    tail = slab_ref.shape[1] - tiles(id_rows(slots))
    names = jnp.concatenate(
        [names, jnp.zeros((owners, (slab_ref.shape[1] - tail) * LANES - names.shape[1]), f32)], axis=1
    )
    for j in range(slab_ref.shape[1] - tail):
        slab_ref[:, tail + j, :] = names[:, j * LANES : (j + 1) * LANES]


def local_kernel(len_ref, residual_ref, matrix_ref, owner_ref, *refs):
    whole, refs = refs[:2], refs[2:]
    local_ref, part_ref, square_ref, table_ref, refs = *refs[:4], refs[4:]
    rows = residual_ref.shape[0] // 6
    weighted = parts(
        jnp.concatenate(
            [0.5 * masked(len_ref, residual_ref, face, rows) for face in range(6)], axis=0
        )
    )
    part = square = jnp.zeros((1, residual_ref.shape[1]), f32)
    for i, move in enumerate(FIRST):
        face = served(*move)
        at, to = rows_of(face, rows), slice(i * rows, (i + 1) * rows)
        local = product(parts(matrix_ref[at, :]), weighted)
        local_ref[to, :] = local
        live = jnp.where(live_rows(len_ref, face, rows), residual_ref[at, :], 0.0)
        part += jnp.sum(live * local, axis=0, keepdims=True)
        square += jnp.sum(live * live, axis=0, keepdims=True)
        refs[0][to, :], refs[1][to, :] = parts(whole[0][at, :])
        for j, other in enumerate(FIRST):
            across = rows_of(served(*other), rows)
            over = slice(j * rows, (j + 1) * rows)
            refs[2][to, over], refs[3][to, over] = parts(whole[1][at, across])
    part_ref[...] = part
    square_ref[...] = square
    primal, slots = table_ref.shape
    rank_row, own_col = ranks(owner_ref[...].astype(f32))
    (rank_col,) = columns(rank_row)
    slot_col = (own_col * CAP + rank_col).astype(jnp.int32)
    table_ref[...] = one_hot(lax.broadcasted_iota(jnp.int32, (primal, slots), 1) == slot_col)


def solve_kernel(incoming_any, inverse_any, local_part_ref, square_ref, answer_ref, *refs):
    names_ref, slab_ref, inverse_ref, sems = refs
    owners, height, _ = slab_ref.shape
    pieces = height // CAP
    half = pieces // 2 * CAP
    copies = [
        pltpu.make_async_copy(
            incoming_any.at[:, pl.ds(height, names_ref.shape[1])], names_ref, sems.at[0]
        ),
        pltpu.make_async_copy(
            incoming_any.at[:, pl.ds(0, half)], slab_ref.at[:, pl.ds(0, half)], sems.at[1]
        ),
        pltpu.make_async_copy(
            incoming_any.at[:, pl.ds(half, height - half)],
            slab_ref.at[:, pl.ds(half, height - half)],
            sems.at[2],
        ),
        pltpu.make_async_copy(inverse_any, inverse_ref, sems.at[3]),
    ]
    for copy in copies:
        copy.start()
    copies[0].wait()
    slots, owned = owners * CAP, inverse_ref.shape[0]
    wanted = unfolded(jnp.sum(names_ref[...], axis=0), 0, id_rows(slots))[:, :slots]
    (wanted_col,) = columns(wanted)
    row_at = lax.broadcasted_iota(jnp.int32, (owned, slots), 0).astype(f32) + 1.0
    col_at = lax.broadcasted_iota(jnp.int32, (slots, owned), 1).astype(f32) + 1.0
    gather = one_hot(row_at == wanted)
    table = one_hot(col_at == wanted_col)
    copies[3].wait()
    inverse = parts(inverse_ref[...])
    for copy in copies[1:3]:
        copy.wait()
    summed = select(gather, get_slab(slab_ref, pieces))
    solved = product(inverse, parts(summed))
    put_slab(answer_ref, select(table, solved))
    total = local_part_ref[...] + 2.0 * jnp.sum(summed * solved, axis=0, keepdims=True)
    sums = folded(total) + folded(square_ref[...])
    sums += [jnp.zeros((1, LANES), f32)] * (tiles(len(sums)) - len(sums))
    answer_ref[:, pieces * CAP :, :] = jnp.broadcast_to(
        jnp.concatenate(sums, axis=0)[None], (owners, len(sums), LANES)
    )


NEAR = (("blk", "up"), ("lat", 0), ("depth", 0), ("depth", 1))
FAR = (("blk", "down"), ("lat", 1))
FIRST = NEAR + FAR
SECOND = (("blk", "up"), ("lat", 0), ("blk", "down"), ("lat", 1), ("depth", 0), ("depth", 1))


def moves(order):
    return [(axis, way) for axis, way in order if route(axis, way)]


def route(axis, way):
    devices = lax.axis_size(axis)
    if way in ("up", "down"):
        by = 1 if way == "up" else -1
        return [(i, (i + by) % devices) for i in range(devices)]
    return [pair for i in range(way, devices - 1, 2) for pair in ((i, i + 1), (i + 1, i))]


def served(axis, way):
    if way in ("up", "down"):
        return 0 if way == "up" else 1
    plus = (lax.rem(lax.axis_index(axis), 2) == way).astype(jnp.int32)
    return (2 if axis == "lat" else 4) + plus


def sent(axis, way):
    return (axis, "down" if way == "up" else "up") if axis == "blk" else (axis, way)


def rows_of(face, rows):
    if isinstance(face, int):
        return pl.ds(face * rows, rows)
    return pl.ds(pl.multiple_of(face * rows, rows), rows)


def sending(order):
    return [sent(*move) for move in order]


def put_blocks(image, refs, order):
    rows = refs[0].shape[0]
    for ref, move in zip(refs, sending(order), strict=True):
        i = FIRST.index(move)
        ref[...] = image[i * rows : (i + 1) * rows, :]


def exchange(blocks, order):
    return {
        (axis, way): lax.ppermute(blocks[sent(axis, way)], axis, route(axis, way))
        for axis, way in moves(order)
    }


def image_kernel(pair_depth, returned_ref, table_ref, high_ref, low_ref, local_ref, sums_ref, *image_refs):
    width = local_ref.shape[1]
    folds = width // LANES
    correction = select(table_ref[...], get_slab(returned_ref, folds))
    image = local_ref[...] + product((high_ref[...], low_ref[...]), parts(correction))
    put_blocks(image, image_refs, FIRST)
    tail = jnp.sum(returned_ref[:, folds * CAP :, :], axis=0)
    if pair_depth:
        sums_ref[...] = tail
    else:
        sums_ref[...] = jnp.broadcast_to(tail[None], sums_ref.shape)


def with_got(block, got, move):
    return block + got[move][...] if move in got else block


def new_direction(len_ref, beta, image_ref, prev_ref, got, move, rows):
    face = served(*move)
    precond = 0.5 * with_got(image_ref[...], got, move)
    return jnp.where(
        live_rows(len_ref, face, rows), precond + beta * prev_ref[rows_of(face, rows), :], 0.0
    )


def near_kernel(pair_depth, scale, keys, len_ref, sums_ref, prev_rho_ref, prev_ref, high_ref, low_ref, *refs):
    images, refs = refs[: len(NEAR)], refs[len(NEAR) :]
    got, refs = dict(zip(keys, refs)), refs[len(keys) :]
    if pair_depth:
        sums, refs = sums_ref[...] + refs[0][...], refs[1:]
    else:
        sums = jnp.sum(sums_ref[...], axis=0)
    rho_out, beta_out, square_out, near_ref, image_out = refs
    rows = images[0].shape[0]
    folds = images[0].shape[1] // LANES
    rho = scale * unfolded(sums, 0, folds)
    beta = rho / prev_rho_ref[...]
    rho_out[...] = rho
    beta_out[...] = beta
    square_out[...] = unfolded(sums, folds, folds)
    for i, move in enumerate(NEAR):
        near_ref[i * rows : (i + 1) * rows, :] = new_direction(
            len_ref, beta, images[i], prev_ref, got, move, rows
        )
    first = len(NEAR) * rows
    image_out[...] = product((high_ref[:, :first], low_ref[:, :first]), parts(near_ref[...]))


def far_kernel(keys, len_ref, beta_ref, prev_ref, high_ref, low_ref, near_image_ref, *refs):
    images, refs = refs[: len(FAR)], refs[len(FAR) :]
    got, (far_ref, *schur_refs) = dict(zip(keys, refs)), refs[len(keys) :]
    rows = images[0].shape[0]
    beta = beta_ref[...]
    for i, move in enumerate(FAR):
        far_ref[i * rows : (i + 1) * rows, :] = new_direction(
            len_ref, beta, images[i], prev_ref, got, move, rows
        )
    first = len(NEAR) * rows
    image = near_image_ref[...] + product(
        (high_ref[:, first:], low_ref[:, first:]), parts(far_ref[...])
    )
    put_blocks(image, schur_refs, SECOND)


def store_kernel(near_ref, far_ref, direction_out, sems):
    rows = far_ref.shape[0] // len(FAR)
    copies = []
    for ref, served_moves in ((near_ref, NEAR), (far_ref, FAR)):
        for i, move in enumerate(served_moves):
            copies.append(
                pltpu.make_async_copy(
                    ref.at[pl.ds(i * rows, rows)],
                    direction_out.at[rows_of(served(*move), rows)],
                    sems.at[len(copies)],
                )
            )
    for copy in copies:
        copy.start()
    for copy in copies:
        copy.wait()


def products_kernel(len_ref, near_ref, far_ref, residual_ref, arrived, *refs):
    schur_refs, out_ref = refs[:-1], refs[-1]
    rows, width = schur_refs[0].shape
    curve = cross = jnp.zeros((1, width), f32)
    for i, (move, schur_ref) in enumerate(zip(FIRST, schur_refs, strict=True)):
        face = served(*move)
        image = schur_ref[...]
        live = jnp.where(live_rows(len_ref, face, rows), residual_ref[rows_of(face, rows), :], 0.0)
        ref, first = (near_ref, i) if i < len(NEAR) else (far_ref, i - len(NEAR))
        direction = ref[first * rows : (first + 1) * rows, :]
        curve += 2.0 * jnp.sum(direction * image, axis=0, keepdims=True)
        cross += 2.0 * jnp.sum(live * image, axis=0, keepdims=True)
    for j, piece in enumerate(folded(curve) + folded(cross)):
        out_ref[j : j + 1, :] = piece


def applied_kernel(pair_depth, keys, len_ref, stored, *refs):
    schur_refs, refs = refs[: len(FIRST)], refs[len(FIRST) :]
    got, refs = dict(zip(keys, refs)), refs[len(keys) :]
    products, (applied_ref, spread_ref) = refs[:-2], refs[-2:]
    rows, width = schur_refs[0].shape
    folds = width // LANES
    total = jnp.zeros((1, width), f32)
    for i, (move, schur_ref) in enumerate(zip(FIRST, schur_refs, strict=True)):
        applied = with_got(schur_ref[...], got, move)
        applied = jnp.where(live_rows(len_ref, served(*move), rows), applied, 0.0)
        applied_ref[i * rows : (i + 1) * rows, :] = applied
        total += jnp.sum(applied * applied, axis=0, keepdims=True)
    products = sum(ref[...] for ref in products)
    halves = [products[:folds], products[folds : 2 * folds]]
    if pair_depth:
        halves = [jnp.where(lax.axis_index("depth") == 0, *halves)]
    halves = [[half[j : j + 1] for j in range(folds)] for half in halves]
    for i, half in enumerate([*halves, folded(total)]):
        for j, piece in enumerate(half):
            spread_ref[:, i, j, :] = jnp.broadcast_to(piece, (spread_ref.shape[0], LANES))


def finish_kernel(pair_depth, scale, len_ref, sums_ref, rho_ref, square_ref, residual_ref, applied_ref, new_out, alpha_ref, norm_ref, new_ref, sems):
    rows = applied_ref.shape[0] // 6
    devices, _, folds, _ = sums_ref.shape
    if pair_depth:
        pairs = sums_ref[...].reshape(devices // 2, 2, 2, folds, LANES)
        pairs = jnp.sum(pairs, axis=0)
        sums = [pairs[0, 0], pairs[1, 0], pairs[0, 1] + pairs[1, 1]]
    else:
        total = jnp.sum(sums_ref[...], axis=0)
        sums = [total[i] for i in range(3)]
    curve, cross, applied_square = [unfolded(x, 0, folds) for x in sums]
    alpha = rho_ref[...] / (scale * curve)
    alpha_ref[...] = alpha
    norm_ref[...] = scale * (
        square_ref[...] - 2.0 * alpha * cross + alpha * alpha * applied_square
    )
    copies = []
    for i, move in enumerate(FIRST):
        face = served(*move)
        at, to = rows_of(face, rows), pl.ds(i * rows, rows)
        live = jnp.where(live_rows(len_ref, face, rows), residual_ref[at, :], 0.0)
        new_ref[to, :] = live - alpha * applied_ref[to, :]
        copies.append(pltpu.make_async_copy(new_ref.at[to], new_out.at[at], sems.at[i]))
        copies[-1].start()
    for copy in copies:
        copy.wait()


def to_all(x, axes):
    return lax.all_to_all(x, axes, split_axis=0, concat_axis=0, tiled=True)


def shards(
    face_len,
    residual,
    prev_direction,
    prev_rho,
    schur,
    neumann,
    coarse_basis,
    coarse_inverse,
    prim_owner,
    coarse_row,
):
    height, width = residual.shape[3:]
    rows = height // 6
    primal = coarse_basis.shape[4]
    owned = coarse_inverse.shape[3]
    owners = lax.axis_size(LAYER)
    slots = owners * CAP
    devices = lax.axis_size(AXES)
    layers = lax.axis_size("depth")
    pair_depth = layers == 2
    scale = 0.5 / (devices * height)
    folds = width // LANES
    tail = tiles(2 * folds)
    id_tail = tiles(id_rows(slots))

    lengths = face_len.reshape(6)
    residual = residual.reshape(height, width)
    prev_direction = prev_direction.reshape(height, width)
    schur = schur.reshape(height, height)
    neumann = neumann.reshape(height, height)
    basis = coarse_basis.reshape(height, primal)
    inverse = coarse_inverse.reshape(owned, owned)
    owner = prim_owner.reshape(1, primal)
    wanted = coarse_row.reshape(1, primal)
    whole = shape_of(height, width)
    row = shape_of(1, width)
    face = shape_of(rows, width)

    (outgoing,) = call(
        pack_kernel,
        [shape_of(owners, folds * CAP + id_tail, LANES)],
        [lengths, owner, wanted, residual, basis],
        far=range(5),
        flops=6 * height * primal * width,
        moved=4 * (height * (width + primal) + slots * width),
        scratch=[
            pltpu.SMEM((6,), jnp.int32),
            pltpu.VMEM((1, primal), jnp.int32),
            pltpu.VMEM((1, primal), jnp.int32),
            pltpu.VMEM((height, width), f32),
            pltpu.VMEM((height, primal), f32),
            pltpu.SemaphoreType.DMA((6, 2)),
            pltpu.SemaphoreType.DMA((3,)),
        ],
    )
    incoming = to_all(outgoing, LAYER)
    local, local_part, square, table, *halves = call(
        local_kernel,
        [whole, row, row, shape_of(primal, slots, dtype=bf16)]
        + [shape_of(height, primal, dtype=bf16)] * 2
        + [shape_of(height, height, dtype=bf16)] * 2,
        [lengths, residual, neumann, owner, basis, schur],
        smem=(0,),
        flops=6 * height * height * width,
        moved=4 * height * (3 * height + 2 * width),
    )
    basis_halves, schur_halves = halves[:2], halves[2:]
    (answers,) = call(
        solve_kernel,
        [shape_of(owners, folds * CAP + tail, LANES)],
        [incoming, inverse, local_part, square],
        far=range(2),
        flops=(8 * slots + 6 * owned) * owned * width,
        moved=8 * slots * width,
        scratch=[
            pltpu.VMEM((owners, id_tail, LANES), f32),
            pltpu.VMEM((owners, folds * CAP, LANES), f32),
            pltpu.VMEM((owned, owned), f32),
            pltpu.SemaphoreType.DMA((4,)),
        ],
    )
    returned = to_all(answers, LAYER)
    faces = [face] * len(FIRST)
    sums, *image = call(
        functools.partial(image_kernel, pair_depth),
        [shape_of(tail, LANES) if pair_depth else shape_of(layers, tail, LANES), *faces],
        [returned, table, *basis_halves, local],
        flops=(6 * height + 4 * slots) * primal * width,
        moved=16 * height * width,
    )
    image = dict(zip(sending(FIRST), image))
    got = exchange(image, FIRST)
    if pair_depth:
        sums = [sums, lax.ppermute(sums, "depth", route("depth", 0))]
    else:
        sums = [to_all(sums, "depth")]
    near_keys, far_keys = moves(NEAR), moves(FAR)
    rho, beta, square, near, near_image = call(
        functools.partial(near_kernel, pair_depth, scale, near_keys),
        [row, row, row, shape_of(len(NEAR) * rows, width), whole],
        [lengths, sums[0], prev_rho.reshape(1, width), prev_direction, *schur_halves]
        + [image[move] for move in NEAR]
        + [got[key] for key in near_keys]
        + sums[1:],
        smem=(0,),
        flops=4 * height * height * width,
        moved=4 * height * (height + 4 * width),
    )
    far, *schur_image = call(
        functools.partial(far_kernel, far_keys),
        [shape_of(len(FAR) * rows, width), *faces],
        [lengths, beta, prev_direction, *schur_halves, near_image]
        + [image[move] for move in FAR]
        + [got[key] for key in far_keys],
        smem=(0,),
        flops=2 * height * height * width,
        moved=4 * height * (height + 4 * width),
    )
    schur_image = dict(zip(sending(SECOND), schur_image))
    got = exchange(schur_image, SECOND)
    schur_image = [schur_image[move] for move in FIRST]
    (products,) = call(
        products_kernel,
        [shape_of(2 * folds, LANES)],
        [lengths, near, far, residual, got[SECOND[0]], *schur_image],
        smem=(0,),
        loose=(4,),
        flops=4 * height * width,
        moved=12 * height * width,
    )
    products = [products]
    if pair_depth:
        products.append(lax.ppermute(products[0], "depth", route("depth", 0)))
    (direction,) = call(
        store_kernel,
        [whole],
        [near, far],
        far_out=(0,),
        moved=8 * height * width,
        scratch=[pltpu.SemaphoreType.DMA((6,))],
    )
    applied, spread_sums = call(
        functools.partial(applied_kernel, pair_depth, list(got)),
        [whole, shape_of(devices, 2 if pair_depth else 3, folds, LANES)],
        [lengths, direction, *schur_image, *got.values(), *products],
        smem=(0,),
        far=(1,),
        flops=4 * height * width,
        moved=12 * height * width,
    )
    new_residual, alpha, norm = call(
        functools.partial(finish_kernel, pair_depth, scale),
        [whole, row, row],
        [lengths, to_all(spread_sums, AXES), rho, square, residual, applied],
        smem=(0,),
        far_out=(0,),
        flops=4 * height * width,
        moved=12 * height * width,
        scratch=[pltpu.VMEM((height, width), f32), pltpu.SemaphoreType.DMA((6,))],
    )
    out_shape = (1, 1, 1, height, width)
    return (
        new_residual.reshape(out_shape),
        direction.reshape(out_shape),
        rho.reshape(width),
        alpha.reshape(width),
        norm.reshape(width),
    )


def solution(mesh):
    tall = P("blk", "lat", "depth", None, None)
    flat = P("blk", "lat", "depth", None)
    in_specs = (flat, tall, tall, P(), tall, tall, tall, tall, tall, flat)
    out_specs = (tall, tall, P(), P(), P())
    return jax.shard_map(shards, mesh=mesh, in_specs=in_specs, out_specs=out_specs, check_vma=False)
```

```python
import functools

import jax
import jax.numpy as jnp
from jax import lax
from jax.experimental import pallas as pl
from jax.experimental.pallas import tpu as pltpu
from jax.sharding import PartitionSpec as P

CAP = 24
AXES = ("depth", "blk", "lat")
LAYER = ("blk", "lat")
LANES = 128
TILE = 8
f32 = jnp.float32
bf16 = jnp.bfloat16

VMEM = pl.BlockSpec(memory_space=pltpu.VMEM)
SMEM = pl.BlockSpec(memory_space=pltpu.SMEM)
ANY = pl.BlockSpec(memory_space=pl.ANY)


def shape_of(*dims, dtype=f32):
    return jax.ShapeDtypeStruct(dims, dtype)


def call(body, outs, operands, smem=(), far=(), loose=(), far_out=(), flops=0, moved=0, scratch=(), room=32):
    in_specs = [
        SMEM if i in smem else ANY if i in far or i in loose else VMEM
        for i in range(len(operands))
    ]
    operands = [
        pltpu.with_memory_space_constraint(x, pltpu.HBM) if i in far else x
        for i, x in enumerate(operands)
    ]
    out_specs = [ANY if i in far_out else VMEM for i in range(len(outs))]
    return pl.pallas_call(
        body,
        out_shape=list(outs),
        in_specs=in_specs,
        out_specs=out_specs,
        scratch_shapes=list(scratch),
        compiler_params=pltpu.CompilerParams(vmem_limit_bytes=room << 20),
        cost_estimate=pl.CostEstimate(flops=flops, bytes_accessed=moved, transcendentals=0),
    )(*operands)


def parts(x):
    high = x.astype(bf16)
    low = (x - high.astype(f32)).astype(bf16)
    return high, low


def mul(a, b, dims):
    return lax.dot_general(a, b, (dims, ((), ())), preferred_element_type=f32)


PLAIN = ((1,), (0,))


def product(a, b, dims=PLAIN):
    (ah, al), (bh, bl) = a, b
    return mul(ah, bh, dims) + (mul(ah, bl, dims) + mul(al, bh, dims))


def select(table, x, dims=PLAIN):
    high, low = parts(x)
    return mul(table, high, dims) + mul(table, low, dims)


def one_hot(hit):
    return jnp.where(hit, 1.0, 0.0).astype(bf16)


def live_rows(len_ref, face, rows):
    return lax.broadcasted_iota(jnp.int32, (rows, 1), 0) < len_ref[face]


def masked(len_ref, ref, face, rows):
    block = ref[face * rows : (face + 1) * rows, :]
    return jnp.where(live_rows(len_ref, face, rows), block, 0.0)


def folded(vector):
    pieces = vector.shape[1] // LANES
    return [vector[:, j * LANES : (j + 1) * LANES] for j in range(pieces)]


def unfolded(block, first, pieces):
    return jnp.concatenate([block[first + j : first + j + 1, :] for j in range(pieces)], axis=1)


def id_rows(slots):
    return -(-slots // LANES)


def tiles(rows):
    return -(-rows // TILE) * TILE


def put_slab(out_ref, block):
    owners = out_ref.shape[0]
    for j in range(block.shape[1] // LANES):
        piece = block[:, j * LANES : (j + 1) * LANES]
        out_ref[:, j * CAP : (j + 1) * CAP, :] = piece.reshape(owners, CAP, LANES)


def get_slab(ref, pieces):
    slots = ref.shape[0] * CAP
    return jnp.concatenate(
        [ref[:, j * CAP : (j + 1) * CAP, :].reshape(slots, LANES) for j in range(pieces)], axis=1
    )


def columns(*rows):
    spare = [jnp.zeros_like(rows[0])] * (TILE - len(rows))
    turned = jnp.transpose(jnp.concatenate([*rows, *spare], axis=0))
    return [turned[:, i : i + 1] for i in range(len(rows))]


def ranks(own_row):
    primal = own_row.shape[1]
    (own_col,) = columns(own_row)
    row_at = lax.broadcasted_iota(jnp.int32, (primal, primal), 0)
    col_at = lax.broadcasted_iota(jnp.int32, (primal, primal), 1)
    before = (own_row == own_col) & (row_at < col_at)
    return jnp.sum(jnp.where(before, 1.0, 0.0), axis=0, keepdims=True), own_col


def pack_kernel(len_any, owner_any, row_any, residual_any, basis_any, slab_ref, *refs):
    len_ref, owner_ref, row_ref, residual_ref, basis_ref, sems, small_sems = refs
    rows = residual_ref.shape[0] // 6
    primal = basis_ref.shape[1]
    owners = slab_ref.shape[0]
    slots = owners * CAP
    small = [
        pltpu.make_async_copy(src, dst, small_sems.at[i])
        for i, (src, dst) in enumerate(
            [(owner_any, owner_ref), (row_any, row_ref), (len_any, len_ref)]
        )
    ]
    large = []
    for pair in range(3):
        at = pl.ds(2 * pair * rows, 2 * rows)
        large.append(
            (
                pltpu.make_async_copy(residual_any.at[at], residual_ref.at[at], sems.at[pair, 0]),
                pltpu.make_async_copy(basis_any.at[at], basis_ref.at[at], sems.at[pair, 1]),
            )
        )
    for copy in small:
        copy.start()
    for pair in large:
        for copy in pair:
            copy.start()
    for copy in small:
        copy.wait()

    def term_of(pair):
        for copy in large[pair]:
            copy.wait()
        weighted = jnp.concatenate(
            [0.5 * masked(len_ref, residual_ref, 2 * pair + side, rows) for side in range(2)],
            axis=0,
        )
        basis = basis_ref[2 * pair * rows : 2 * (pair + 1) * rows, :]
        return product(parts(jnp.transpose(basis)), parts(weighted))

    terms = term_of(0)
    own_row = owner_ref[...].astype(f32)
    wanted_row = row_ref[...].astype(f32) + 1.0
    rank_row, _ = ranks(own_row)
    slot_row = (own_row * CAP + rank_row).astype(jnp.int32)
    rank_col, wanted_col = columns(rank_row, wanted_row)
    packer = one_hot(lax.broadcasted_iota(jnp.int32, (slots, primal), 0) == slot_row)
    to_owner = one_hot(lax.broadcasted_iota(jnp.int32, (owners, primal), 0) == owner_ref[...])
    at_owner = lax.axis_index(LAYER) * CAP + rank_col.astype(jnp.int32)
    place = lax.broadcasted_iota(jnp.int32, (primal, id_rows(slots) * LANES), 1)
    names = select(to_owner, jnp.where(place == at_owner, wanted_col, 0.0))
    terms += term_of(1)
    terms += term_of(2)
    put_slab(slab_ref, select(packer, terms))
    tail = slab_ref.shape[1] - tiles(id_rows(slots))
    names = jnp.concatenate(
        [names, jnp.zeros((owners, (slab_ref.shape[1] - tail) * LANES - names.shape[1]), f32)], axis=1
    )
    for j in range(slab_ref.shape[1] - tail):
        slab_ref[:, tail + j, :] = names[:, j * LANES : (j + 1) * LANES]


def local_kernel(len_ref, residual_ref, matrix_ref, owner_ref, *refs):
    whole, refs = refs[:2], refs[2:]
    local_ref, part_ref, square_ref, table_ref, refs = *refs[:4], refs[4:]
    rows = residual_ref.shape[0] // 6
    live = jnp.concatenate(
        [masked(len_ref, residual_ref, face, rows) for face in range(6)], axis=0
    )
    local = product(parts(matrix_ref[...]), parts(0.5 * live))
    local_ref[...] = local
    part_ref[...] = jnp.sum(live * local, axis=0, keepdims=True)
    square_ref[...] = jnp.sum(live * live, axis=0, keepdims=True)
    refs[0][...], refs[1][...] = parts(whole[0][...])
    for i, move in enumerate(NEAR + FAR):
        at = slice(i * rows, (i + 1) * rows)
        refs[2][:, at], refs[3][:, at] = parts(whole[1][:, rows_of(served(*move), rows)])
    primal, slots = table_ref.shape
    rank_row, own_col = ranks(owner_ref[...].astype(f32))
    (rank_col,) = columns(rank_row)
    slot_col = (own_col * CAP + rank_col).astype(jnp.int32)
    table_ref[...] = one_hot(lax.broadcasted_iota(jnp.int32, (primal, slots), 1) == slot_col)


def solve_kernel(incoming_any, inverse_any, local_part_ref, square_ref, answer_ref, *refs):
    names_ref, slab_ref, inverse_ref, sems = refs
    owners, height, _ = slab_ref.shape
    pieces = height // CAP
    half = pieces // 2 * CAP
    copies = [
        pltpu.make_async_copy(
            incoming_any.at[:, pl.ds(height, names_ref.shape[1])], names_ref, sems.at[0]
        ),
        pltpu.make_async_copy(
            incoming_any.at[:, pl.ds(0, half)], slab_ref.at[:, pl.ds(0, half)], sems.at[1]
        ),
        pltpu.make_async_copy(
            incoming_any.at[:, pl.ds(half, height - half)],
            slab_ref.at[:, pl.ds(half, height - half)],
            sems.at[2],
        ),
        pltpu.make_async_copy(inverse_any, inverse_ref, sems.at[3]),
    ]
    for copy in copies:
        copy.start()
    copies[0].wait()
    slots, owned = owners * CAP, inverse_ref.shape[0]
    wanted = unfolded(jnp.sum(names_ref[...], axis=0), 0, id_rows(slots))[:, :slots]
    (wanted_col,) = columns(wanted)
    row_at = lax.broadcasted_iota(jnp.int32, (owned, slots), 0).astype(f32) + 1.0
    col_at = lax.broadcasted_iota(jnp.int32, (slots, owned), 1).astype(f32) + 1.0
    gather = one_hot(row_at == wanted)
    table = one_hot(col_at == wanted_col)
    copies[3].wait()
    inverse = parts(inverse_ref[...])
    for copy in copies[1:3]:
        copy.wait()
    summed = select(gather, get_slab(slab_ref, pieces))
    solved = product(inverse, parts(summed))
    put_slab(answer_ref, select(table, solved))
    total = local_part_ref[...] + 2.0 * jnp.sum(summed * solved, axis=0, keepdims=True)
    sums = folded(total) + folded(square_ref[...])
    sums += [jnp.zeros((1, LANES), f32)] * (tiles(len(sums)) - len(sums))
    answer_ref[:, pieces * CAP :, :] = jnp.broadcast_to(
        jnp.concatenate(sums, axis=0)[None], (owners, len(sums), LANES)
    )


NEAR = (("blk", "up"), ("lat", 0), ("depth", 0), ("depth", 1))
FAR = (("blk", "down"), ("lat", 1))
FIRST = NEAR + FAR
SECOND = (("blk", "up"), ("lat", 0), ("blk", "down"), ("lat", 1), ("depth", 0), ("depth", 1))


def moves(order):
    return [(axis, way) for axis, way in order if route(axis, way)]


def route(axis, way):
    devices = lax.axis_size(axis)
    if way in ("up", "down"):
        by = 1 if way == "up" else -1
        return [(i, (i + by) % devices) for i in range(devices)]
    return [pair for i in range(way, devices - 1, 2) for pair in ((i, i + 1), (i + 1, i))]


def served(axis, way):
    if way in ("up", "down"):
        return 0 if way == "up" else 1
    plus = (lax.rem(lax.axis_index(axis), 2) == way).astype(jnp.int32)
    return (2 if axis == "lat" else 4) + plus


def sent(axis, way):
    return 1 - served(axis, way) if axis == "blk" else served(axis, way)


def rows_of(face, rows):
    if isinstance(face, int):
        return pl.ds(face * rows, rows)
    return pl.ds(pl.multiple_of(face * rows, rows), rows)


def put_faces(image_ref, rows, order, face_refs):
    for ref, move in zip(face_refs, moves(order), strict=True):
        ref[...] = image_ref[rows_of(sent(*move), rows), :]


def exchange(faces, order):
    return [
        lax.ppermute(block, axis, route(axis, way))
        for block, (axis, way) in zip(faces, moves(order), strict=True)
    ]


def image_kernel(pair_depth, returned_ref, table_ref, high_ref, low_ref, local_ref, image_ref, sums_ref, *face_refs):
    rows = local_ref.shape[0] // 6
    width = local_ref.shape[1]
    folds = width // LANES
    correction = select(table_ref[...], get_slab(returned_ref, folds))
    image = local_ref[...] + product((high_ref[...], low_ref[...]), parts(correction))
    image_ref[...] = image
    put_faces(image_ref, rows, FIRST, face_refs)
    tail = jnp.sum(returned_ref[:, folds * CAP :, :], axis=0)
    if pair_depth:
        sums_ref[...] = tail
    else:
        sums_ref[...] = jnp.broadcast_to(tail[None], sums_ref.shape)


def with_got(ref, at, got, move):
    return ref[at, :] + got[move][...] if move in got else ref[at, :]


def new_direction(len_ref, beta, image_ref, prev_ref, got, move, rows):
    face = served(*move)
    at = rows_of(face, rows)
    precond = 0.5 * with_got(image_ref, at, got, move)
    return jnp.where(live_rows(len_ref, face, rows), precond + beta * prev_ref[at, :], 0.0)


def near_kernel(pair_depth, scale, keys, len_ref, sums_ref, prev_rho_ref, image_ref, prev_ref, high_ref, low_ref, *refs):
    got, refs = dict(zip(keys, refs)), refs[len(keys) :]
    if pair_depth:
        sums, refs = sums_ref[...] + refs[0][...], refs[1:]
    else:
        sums = jnp.sum(sums_ref[...], axis=0)
    rho_out, beta_out, square_out, near_ref, image_out = refs
    rows = image_ref.shape[0] // 6
    folds = image_ref.shape[1] // LANES
    rho = scale * unfolded(sums, 0, folds)
    beta = rho / prev_rho_ref[...]
    rho_out[...] = rho
    beta_out[...] = beta
    square_out[...] = unfolded(sums, folds, folds)
    for i, move in enumerate(NEAR):
        near_ref[i * rows : (i + 1) * rows, :] = new_direction(
            len_ref, beta, image_ref, prev_ref, got, move, rows
        )
    first = len(NEAR) * rows
    image_out[...] = product((high_ref[:, :first], low_ref[:, :first]), parts(near_ref[...]))


def far_kernel(keys, len_ref, beta_ref, image_ref, prev_ref, high_ref, low_ref, near_ref, near_image_ref, *refs):
    got, refs = dict(zip(keys, refs)), refs[len(keys) :]
    far_ref, schur_out, *face_refs = refs
    rows = image_ref.shape[0] // 6
    beta = beta_ref[...]
    for i, move in enumerate(FAR):
        far_ref[i * rows : (i + 1) * rows, :] = new_direction(
            len_ref, beta, image_ref, prev_ref, got, move, rows
        )
    first = len(NEAR) * rows
    image = near_image_ref[...] + product(
        (high_ref[:, first:], low_ref[:, first:]), parts(far_ref[...])
    )
    schur_out[...] = image
    put_faces(schur_out, rows, SECOND, face_refs)


def store_kernel(near_ref, far_ref, direction_out, sems):
    rows = far_ref.shape[0] // len(FAR)
    copies = []
    for ref, served_moves in ((near_ref, NEAR), (far_ref, FAR)):
        for i, move in enumerate(served_moves):
            copies.append(
                pltpu.make_async_copy(
                    ref.at[pl.ds(i * rows, rows)],
                    direction_out.at[rows_of(served(*move), rows)],
                    sems.at[len(copies)],
                )
            )
    for copy in copies:
        copy.start()
    for copy in copies:
        copy.wait()


def products_kernel(len_ref, near_ref, far_ref, schur_ref, residual_ref, arrived, out_ref):
    rows = schur_ref.shape[0] // 6
    curve = cross = jnp.zeros((1, schur_ref.shape[1]), f32)
    for ref, served_moves in ((near_ref, NEAR), (far_ref, FAR)):
        for i, move in enumerate(served_moves):
            face = served(*move)
            at = rows_of(face, rows)
            image = schur_ref[at, :]
            live = jnp.where(live_rows(len_ref, face, rows), residual_ref[at, :], 0.0)
            direction = ref[i * rows : (i + 1) * rows, :]
            curve += 2.0 * jnp.sum(direction * image, axis=0, keepdims=True)
            cross += 2.0 * jnp.sum(live * image, axis=0, keepdims=True)
    for j, piece in enumerate(folded(curve) + folded(cross)):
        out_ref[j : j + 1, :] = piece


def applied_kernel(pair_depth, len_ref, stored, schur_ref, *refs):
    keys = moves(SECOND)
    got, refs = dict(zip(keys, refs)), refs[len(keys) :]
    products, (applied_ref, spread_ref) = refs[:-2], refs[-2:]
    rows = schur_ref.shape[0] // 6
    folds = schur_ref.shape[1] // LANES
    total = jnp.zeros((1, schur_ref.shape[1]), f32)
    for move in SECOND:
        face = served(*move)
        at = rows_of(face, rows)
        applied = with_got(schur_ref, at, got, move)
        applied = jnp.where(live_rows(len_ref, face, rows), applied, 0.0)
        applied_ref[at, :] = applied
        total += jnp.sum(applied * applied, axis=0, keepdims=True)
    products = sum(ref[...] for ref in products)
    halves = [products[:folds], products[folds : 2 * folds]]
    if pair_depth:
        halves = [jnp.where(lax.axis_index("depth") == 0, *halves)]
    block = jnp.concatenate([*halves, *folded(total)], axis=0)
    spread_ref[...] = jnp.broadcast_to(block[None], spread_ref.shape)


def finish_kernel(pair_depth, scale, len_ref, sums_ref, rho_ref, square_ref, residual_ref, applied_ref, new_out, alpha_ref, norm_ref, new_ref, sems):
    rows = applied_ref.shape[0] // 6
    devices, height, _ = sums_ref.shape
    if pair_depth:
        folds = height // 2
        layers = [jnp.sum(sums_ref[: devices // 2], axis=0), jnp.sum(sums_ref[devices // 2 :], axis=0)]
        curve, cross = [unfolded(layer, 0, folds) for layer in layers]
        applied_square = unfolded(layers[0] + layers[1], folds, folds)
    else:
        folds = height // 3
        total = jnp.sum(sums_ref[...], axis=0)
        curve, cross, applied_square = [unfolded(total, i * folds, folds) for i in range(3)]
    alpha = rho_ref[...] / (scale * curve)
    alpha_ref[...] = alpha
    norm_ref[...] = scale * (
        square_ref[...] - 2.0 * alpha * cross + alpha * alpha * applied_square
    )
    copies = []
    for face in range(6):
        at = slice(face * rows, (face + 1) * rows)
        new_ref[at, :] = masked(len_ref, residual_ref, face, rows) - alpha * applied_ref[at, :]
        where = pl.ds(face * rows, rows)
        copies.append(pltpu.make_async_copy(new_ref.at[where], new_out.at[where], sems.at[face]))
        copies[-1].start()
    for copy in copies:
        copy.wait()


def to_all(x, axes):
    return lax.all_to_all(x, axes, split_axis=0, concat_axis=0, tiled=True)


def shards(
    face_len,
    residual,
    prev_direction,
    prev_rho,
    schur,
    neumann,
    coarse_basis,
    coarse_inverse,
    prim_owner,
    coarse_row,
):
    height, width = residual.shape[3:]
    rows = height // 6
    primal = coarse_basis.shape[4]
    owned = coarse_inverse.shape[3]
    owners = lax.axis_size(LAYER)
    slots = owners * CAP
    devices = lax.axis_size(AXES)
    layers = lax.axis_size("depth")
    pair_depth = layers == 2
    scale = 0.5 / (devices * height)
    folds = width // LANES
    tail = tiles(2 * folds)
    id_tail = tiles(id_rows(slots))

    lengths = face_len.reshape(6)
    residual = residual.reshape(height, width)
    prev_direction = prev_direction.reshape(height, width)
    schur = schur.reshape(height, height)
    neumann = neumann.reshape(height, height)
    basis = coarse_basis.reshape(height, primal)
    inverse = coarse_inverse.reshape(owned, owned)
    owner = prim_owner.reshape(1, primal)
    wanted = coarse_row.reshape(1, primal)
    whole = shape_of(height, width)
    row = shape_of(1, width)
    face = shape_of(rows, width)

    (outgoing,) = call(
        pack_kernel,
        [shape_of(owners, folds * CAP + id_tail, LANES)],
        [lengths, owner, wanted, residual, basis],
        far=range(5),
        flops=6 * height * primal * width,
        moved=4 * (height * (width + primal) + slots * width),
        scratch=[
            pltpu.SMEM((6,), jnp.int32),
            pltpu.VMEM((1, primal), jnp.int32),
            pltpu.VMEM((1, primal), jnp.int32),
            pltpu.VMEM((height, width), f32),
            pltpu.VMEM((height, primal), f32),
            pltpu.SemaphoreType.DMA((3, 2)),
            pltpu.SemaphoreType.DMA((3,)),
        ],
    )
    incoming = to_all(outgoing, LAYER)
    local, local_part, square, table, *halves = call(
        local_kernel,
        [whole, row, row, shape_of(primal, slots, dtype=bf16)]
        + [shape_of(height, primal, dtype=bf16)] * 2
        + [shape_of(height, height, dtype=bf16)] * 2,
        [lengths, residual, neumann, owner, basis, schur],
        smem=(0,),
        flops=6 * height * height * width,
        moved=4 * height * (3 * height + 2 * width),
    )
    basis_halves, schur_halves = halves[:2], halves[2:]
    (answers,) = call(
        solve_kernel,
        [shape_of(owners, folds * CAP + tail, LANES)],
        [incoming, inverse, local_part, square],
        far=range(2),
        flops=(8 * slots + 6 * owned) * owned * width,
        moved=8 * slots * width,
        scratch=[
            pltpu.VMEM((owners, id_tail, LANES), f32),
            pltpu.VMEM((owners, folds * CAP, LANES), f32),
            pltpu.VMEM((owned, owned), f32),
            pltpu.SemaphoreType.DMA((4,)),
        ],
    )
    returned = to_all(answers, LAYER)
    keys = moves(FIRST)
    faces = [face] * len(keys)
    image, sums, *outward = call(
        functools.partial(image_kernel, pair_depth),
        [whole, shape_of(tail, LANES) if pair_depth else shape_of(layers, tail, LANES), *faces],
        [returned, table, *basis_halves, local],
        flops=(6 * height + 4 * slots) * primal * width,
        moved=16 * height * width,
    )
    got = dict(zip(keys, exchange(outward, FIRST)))
    if pair_depth:
        sums = [sums, lax.ppermute(sums, "depth", route("depth", 0))]
    else:
        sums = [to_all(sums, "depth")]
    near_keys, far_keys = moves(NEAR), moves(FAR)
    rho, beta, square, near, near_image = call(
        functools.partial(near_kernel, pair_depth, scale, near_keys),
        [row, row, row, shape_of(len(NEAR) * rows, width), whole],
        [lengths, sums[0], prev_rho.reshape(1, width), image, prev_direction, *schur_halves]
        + [got[key] for key in near_keys]
        + sums[1:],
        smem=(0,),
        flops=4 * height * height * width,
        moved=4 * height * (height + 4 * width),
    )
    far, schur_image, *outward = call(
        functools.partial(far_kernel, far_keys),
        [shape_of(len(FAR) * rows, width), whole, *faces],
        [lengths, beta, image, prev_direction, *schur_halves, near, near_image]
        + [got[key] for key in far_keys],
        smem=(0,),
        flops=2 * height * height * width,
        moved=4 * height * (height + 4 * width),
    )
    got = exchange(outward, SECOND)
    (products,) = call(
        products_kernel,
        [shape_of(2 * folds, LANES)],
        [lengths, near, far, schur_image, residual, got[0]],
        smem=(0,),
        loose=(5,),
        flops=4 * height * width,
        moved=12 * height * width,
    )
    products = [products]
    if pair_depth:
        products.append(lax.ppermute(products[0], "depth", route("depth", 0)))
    (direction,) = call(
        store_kernel,
        [whole],
        [near, far],
        far_out=(0,),
        moved=8 * height * width,
        scratch=[pltpu.SemaphoreType.DMA((6,))],
    )
    applied, spread_sums = call(
        functools.partial(applied_kernel, pair_depth),
        [whole, shape_of(devices, (2 if pair_depth else 3) * folds, LANES)],
        [lengths, direction, schur_image, *got, *products],
        smem=(0,),
        far=(1,),
        flops=4 * height * width,
        moved=12 * height * width,
    )
    new_residual, alpha, norm = call(
        functools.partial(finish_kernel, pair_depth, scale),
        [whole, row, row],
        [lengths, to_all(spread_sums, AXES), rho, square, residual, applied],
        smem=(0,),
        far_out=(0,),
        flops=4 * height * width,
        moved=12 * height * width,
        scratch=[pltpu.VMEM((height, width), f32), pltpu.SemaphoreType.DMA((6,))],
    )
    out_shape = (1, 1, 1, height, width)
    return (
        new_residual.reshape(out_shape),
        direction.reshape(out_shape),
        rho.reshape(width),
        alpha.reshape(width),
        norm.reshape(width),
    )


def solution(mesh):
    tall = P("blk", "lat", "depth", None, None)
    flat = P("blk", "lat", "depth", None)
    in_specs = (flat, tall, tall, P(), tall, tall, tall, tall, tall, flat)
    out_specs = (tall, tall, P(), P(), P())
    return jax.shard_map(shards, mesh=mesh, in_specs=in_specs, out_specs=out_specs, check_vma=False)
```

```python
import functools

import jax
import jax.numpy as jnp
from jax import lax
from jax.experimental import pallas as pl
from jax.experimental.pallas import tpu as pltpu
from jax.sharding import PartitionSpec as P

CAP = 24
AXES = ("depth", "blk", "lat")
LAYER = ("blk", "lat")
LANES = 128
TILE = 8
f32 = jnp.float32
bf16 = jnp.bfloat16

VMEM = pl.BlockSpec(memory_space=pltpu.VMEM)
SMEM = pl.BlockSpec(memory_space=pltpu.SMEM)
ANY = pl.BlockSpec(memory_space=pl.ANY)


def shape_of(*dims, dtype=f32):
    return jax.ShapeDtypeStruct(dims, dtype)


def call(body, outs, operands, smem=(), far=(), loose=(), far_out=(), flops=0, moved=0, scratch=(), room=32):
    in_specs = [
        SMEM if i in smem else ANY if i in far or i in loose else VMEM
        for i in range(len(operands))
    ]
    operands = [
        pltpu.with_memory_space_constraint(x, pltpu.HBM) if i in far else x
        for i, x in enumerate(operands)
    ]
    out_specs = [ANY if i in far_out else VMEM for i in range(len(outs))]
    return pl.pallas_call(
        body,
        out_shape=list(outs),
        in_specs=in_specs,
        out_specs=out_specs,
        scratch_shapes=list(scratch),
        compiler_params=pltpu.CompilerParams(vmem_limit_bytes=room << 20),
        cost_estimate=pl.CostEstimate(flops=flops, bytes_accessed=moved, transcendentals=0),
    )(*operands)


def parts(x):
    high = x.astype(bf16)
    low = (x - high.astype(f32)).astype(bf16)
    return high, low


def mul(a, b, dims):
    return lax.dot_general(a, b, (dims, ((), ())), preferred_element_type=f32)


PLAIN = ((1,), (0,))


def product(a, b, dims=PLAIN):
    (ah, al), (bh, bl) = a, b
    return mul(ah, bh, dims) + (mul(ah, bl, dims) + mul(al, bh, dims))


def select(table, x, dims=PLAIN):
    high, low = parts(x)
    return mul(table, high, dims) + mul(table, low, dims)


def one_hot(hit):
    return jnp.where(hit, 1.0, 0.0).astype(bf16)


def live_rows(len_ref, face, rows):
    return lax.broadcasted_iota(jnp.int32, (rows, 1), 0) < len_ref[face]


def masked(len_ref, ref, face, rows):
    block = ref[face * rows : (face + 1) * rows, :]
    return jnp.where(live_rows(len_ref, face, rows), block, 0.0)


def folded(vector):
    pieces = vector.shape[1] // LANES
    return [vector[:, j * LANES : (j + 1) * LANES] for j in range(pieces)]


def unfolded(block, first, pieces):
    return jnp.concatenate([block[first + j : first + j + 1, :] for j in range(pieces)], axis=1)


def id_rows(slots):
    return -(-slots // LANES)


def tiles(rows):
    return -(-rows // TILE) * TILE


def put_slab(out_ref, block):
    owners = out_ref.shape[0]
    for j in range(block.shape[1] // LANES):
        piece = block[:, j * LANES : (j + 1) * LANES]
        out_ref[:, j * CAP : (j + 1) * CAP, 0, :] = piece.reshape(owners, CAP, LANES)


def get_slab(ref, pieces):
    slots = ref.shape[0] * CAP
    return jnp.concatenate(
        [ref[:, j * CAP : (j + 1) * CAP, 0, :].reshape(slots, LANES) for j in range(pieces)], axis=1
    )


def columns(*rows):
    spare = [jnp.zeros_like(rows[0])] * (TILE - len(rows))
    turned = jnp.transpose(jnp.concatenate([*rows, *spare], axis=0))
    return [turned[:, i : i + 1] for i in range(len(rows))]


def ranks(own_row):
    primal = own_row.shape[1]
    (own_col,) = columns(own_row)
    row_at = lax.broadcasted_iota(jnp.int32, (primal, primal), 0)
    col_at = lax.broadcasted_iota(jnp.int32, (primal, primal), 1)
    before = (own_row == own_col) & (row_at < col_at)
    return jnp.sum(jnp.where(before, 1.0, 0.0), axis=0, keepdims=True), own_col


def pack_kernel(len_any, owner_any, row_any, residual_any, basis_any, slab_ref, *refs):
    len_ref, owner_ref, row_ref, residual_ref, basis_ref, sems, small_sems = refs
    rows = residual_ref.shape[0] // 6
    primal = basis_ref.shape[1]
    owners = slab_ref.shape[0]
    slots = owners * CAP
    small = [
        pltpu.make_async_copy(src, dst, small_sems.at[i])
        for i, (src, dst) in enumerate(
            [(owner_any, owner_ref), (row_any, row_ref), (len_any, len_ref)]
        )
    ]
    large = []
    for pair in range(3):
        at = pl.ds(2 * pair * rows, 2 * rows)
        large.append(
            (
                pltpu.make_async_copy(residual_any.at[at], residual_ref.at[at], sems.at[pair, 0]),
                pltpu.make_async_copy(basis_any.at[at], basis_ref.at[at], sems.at[pair, 1]),
            )
        )
    for copy in small:
        copy.start()
    for pair in large:
        for copy in pair:
            copy.start()
    for copy in small:
        copy.wait()

    squares = []

    def term_of(pair):
        for copy in large[pair]:
            copy.wait()
        weighted = jnp.concatenate(
            [0.5 * masked(len_ref, residual_ref, 2 * pair + side, rows) for side in range(2)],
            axis=0,
        )
        basis = basis_ref[2 * pair * rows : 2 * (pair + 1) * rows, :]
        squares.append(jnp.sum(weighted * weighted, axis=0, keepdims=True))
        return product(parts(jnp.transpose(basis)), parts(weighted))

    terms = term_of(0)
    own_row = owner_ref[...].astype(f32)
    wanted_row = row_ref[...].astype(f32) + 1.0
    rank_row, _ = ranks(own_row)
    slot_row = (own_row * CAP + rank_row).astype(jnp.int32)
    rank_col, wanted_col = columns(rank_row, wanted_row)
    packer = one_hot(lax.broadcasted_iota(jnp.int32, (slots, primal), 0) == slot_row)
    to_owner = one_hot(lax.broadcasted_iota(jnp.int32, (owners, primal), 0) == owner_ref[...])
    at_owner = lax.axis_index(LAYER) * CAP + rank_col.astype(jnp.int32)
    place = lax.broadcasted_iota(jnp.int32, (primal, id_rows(slots) * LANES), 1)
    names = select(to_owner, jnp.where(place == at_owner, wanted_col, 0.0))
    terms += term_of(1)
    terms += term_of(2)
    put_slab(slab_ref, select(packer, terms))
    square = 4.0 * (squares[0] + squares[1] + squares[2])
    pieces = folded(names) + [jnp.broadcast_to(x, (owners, LANES)) for x in folded(square)]
    for j, piece in enumerate(pieces):
        slab_ref[:, slab_ref.shape[1] - len(pieces) + j, 0, :] = piece


def local_kernel(len_ref, residual_ref, matrix_ref, owner_ref, *refs):
    whole, refs = refs[:2], refs[2:]
    local_ref, part_ref, table_ref, refs = *refs[:3], refs[3:]
    rows = residual_ref.shape[0] // 6
    live = jnp.concatenate(
        [masked(len_ref, residual_ref, face, rows) for face in range(6)], axis=0
    )
    local = product(parts(matrix_ref[...]), parts(0.5 * live))
    local_ref[...] = local
    part_ref[...] = jnp.sum(live * local, axis=0, keepdims=True)
    refs[0][...], refs[1][...] = parts(whole[0][...])
    for i, move in enumerate(NEAR + FAR):
        at = slice(i * rows, (i + 1) * rows)
        refs[2][:, at], refs[3][:, at] = parts(whole[1][:, rows_of(served(*move), rows)])
    primal, slots = table_ref.shape
    rank_row, own_col = ranks(owner_ref[...].astype(f32))
    (rank_col,) = columns(rank_row)
    slot_col = (own_col * CAP + rank_col).astype(jnp.int32)
    table_ref[...] = one_hot(lax.broadcasted_iota(jnp.int32, (primal, slots), 1) == slot_col)


def solve_kernel(incoming_any, inverse_any, local_part_ref, answer_ref, square_ref, *refs):
    names_ref, slab_ref, inverse_ref, sems = refs
    owners, height, _, _ = slab_ref.shape
    pieces = height // CAP
    half = pieces // 2 * CAP
    copies = [
        pltpu.make_async_copy(
            incoming_any.at[:, pl.ds(height, names_ref.shape[1])], names_ref, sems.at[0]
        ),
        pltpu.make_async_copy(
            incoming_any.at[:, pl.ds(0, half)], slab_ref.at[:, pl.ds(0, half)], sems.at[1]
        ),
        pltpu.make_async_copy(
            incoming_any.at[:, pl.ds(half, height - half)],
            slab_ref.at[:, pl.ds(half, height - half)],
            sems.at[2],
        ),
        pltpu.make_async_copy(inverse_any, inverse_ref, sems.at[3]),
    ]
    for copy in copies:
        copy.start()
    copies[0].wait()
    slots, owned = owners * CAP, inverse_ref.shape[0]
    told = [jnp.sum(names_ref[:, j, 0, :], axis=0, keepdims=True) for j in range(names_ref.shape[1])]
    for j, piece in enumerate(told[id_rows(slots) :]):
        square_ref[j : j + 1, :] = piece
    wanted = jnp.concatenate(told[: id_rows(slots)], axis=1)[:, :slots]
    (wanted_col,) = columns(wanted)
    row_at = lax.broadcasted_iota(jnp.int32, (owned, slots), 0).astype(f32) + 1.0
    col_at = lax.broadcasted_iota(jnp.int32, (slots, owned), 1).astype(f32) + 1.0
    gather = one_hot(row_at == wanted)
    table = one_hot(col_at == wanted_col)
    copies[3].wait()
    inverse = parts(inverse_ref[...])
    for copy in copies[1:3]:
        copy.wait()
    summed = select(gather, get_slab(slab_ref, pieces))
    solved = product(inverse, parts(summed))
    put_slab(answer_ref, select(table, solved))
    total = local_part_ref[...] + 2.0 * jnp.sum(summed * solved, axis=0, keepdims=True)
    for j, piece in enumerate(folded(total)):
        answer_ref[:, height + j, 0, :] = jnp.broadcast_to(piece, (owners, LANES))


NEAR = (("blk", "up"), ("lat", 0), ("depth", 0), ("depth", 1))
FAR = (("blk", "down"), ("lat", 1))
FIRST = NEAR + FAR
SECOND = (("blk", "up"), ("lat", 0), ("blk", "down"), ("lat", 1), ("depth", 0), ("depth", 1))


def moves(order):
    return [(axis, way) for axis, way in order if route(axis, way)]


def route(axis, way):
    devices = lax.axis_size(axis)
    if way in ("up", "down"):
        by = 1 if way == "up" else -1
        return [(i, (i + by) % devices) for i in range(devices)]
    return [pair for i in range(way, devices - 1, 2) for pair in ((i, i + 1), (i + 1, i))]


def served(axis, way):
    if way in ("up", "down"):
        return 0 if way == "up" else 1
    plus = (lax.rem(lax.axis_index(axis), 2) == way).astype(jnp.int32)
    return (2 if axis == "lat" else 4) + plus


def sent(axis, way):
    return 1 - served(axis, way) if axis == "blk" else served(axis, way)


def rows_of(face, rows):
    if isinstance(face, int):
        return pl.ds(face * rows, rows)
    return pl.ds(pl.multiple_of(face * rows, rows), rows)


def put_faces(image_ref, rows, order, face_refs):
    for ref, move in zip(face_refs, moves(order), strict=True):
        ref[...] = image_ref[rows_of(sent(*move), rows), :]


def exchange(faces, order):
    return [
        lax.ppermute(block, axis, route(axis, way))
        for block, (axis, way) in zip(faces, moves(order), strict=True)
    ]


def image_kernel(pair_depth, returned_ref, square_ref, table_ref, high_ref, low_ref, local_ref, image_ref, sums_ref, *face_refs):
    rows = local_ref.shape[0] // 6
    width = local_ref.shape[1]
    folds = width // LANES
    correction = select(table_ref[...], get_slab(returned_ref, folds))
    image = local_ref[...] + product((high_ref[...], low_ref[...]), parts(correction))
    image_ref[...] = image
    put_faces(image_ref, rows, FIRST, face_refs)
    tail = jnp.concatenate(
        [
            jnp.sum(returned_ref[:, folds * CAP + j, 0, :], axis=0, keepdims=True)
            for j in range(folds)
        ]
        + [square_ref[...]],
        axis=0,
    )
    if pair_depth:
        sums_ref[...] = tail
    else:
        sums_ref[...] = jnp.broadcast_to(tail[None], sums_ref.shape)


def with_got(ref, at, got, move):
    return ref[at, :] + got[move][...] if move in got else ref[at, :]


def new_direction(len_ref, beta, image_ref, prev_ref, got, move, rows):
    face = served(*move)
    at = rows_of(face, rows)
    precond = 0.5 * with_got(image_ref, at, got, move)
    return jnp.where(live_rows(len_ref, face, rows), precond + beta * prev_ref[at, :], 0.0)


def near_kernel(pair_depth, scale, keys, len_ref, sums_ref, prev_rho_ref, image_ref, prev_ref, high_ref, low_ref, *refs):
    got, refs = dict(zip(keys, refs)), refs[len(keys) :]
    if pair_depth:
        sums, refs = sums_ref[...] + refs[0][...], refs[1:]
    else:
        sums = jnp.sum(sums_ref[...], axis=0)
    rho_out, beta_out, square_out, near_ref, image_out = refs
    rows = image_ref.shape[0] // 6
    folds = image_ref.shape[1] // LANES
    rho = scale * unfolded(sums, 0, folds)
    beta = rho / prev_rho_ref[...]
    rho_out[...] = rho
    beta_out[...] = beta
    square_out[...] = unfolded(sums, folds, folds)
    for i, move in enumerate(NEAR):
        near_ref[i * rows : (i + 1) * rows, :] = new_direction(
            len_ref, beta, image_ref, prev_ref, got, move, rows
        )
    first = len(NEAR) * rows
    image_out[...] = product((high_ref[:, :first], low_ref[:, :first]), parts(near_ref[...]))


def far_kernel(keys, len_ref, beta_ref, image_ref, prev_ref, high_ref, low_ref, near_ref, near_image_ref, *refs):
    got, refs = dict(zip(keys, refs)), refs[len(keys) :]
    far_ref, schur_out, *face_refs = refs
    rows = image_ref.shape[0] // 6
    beta = beta_ref[...]
    for i, move in enumerate(FAR):
        far_ref[i * rows : (i + 1) * rows, :] = new_direction(
            len_ref, beta, image_ref, prev_ref, got, move, rows
        )
    first = len(NEAR) * rows
    image = near_image_ref[...] + product(
        (high_ref[:, first:], low_ref[:, first:]), parts(far_ref[...])
    )
    schur_out[...] = image
    put_faces(schur_out, rows, SECOND, face_refs)


def store_kernel(near_ref, far_ref, direction_out, sems):
    rows = far_ref.shape[0] // len(FAR)
    copies = []
    for ref, served_moves in ((near_ref, NEAR), (far_ref, FAR)):
        for i, move in enumerate(served_moves):
            copies.append(
                pltpu.make_async_copy(
                    ref.at[pl.ds(i * rows, rows)],
                    direction_out.at[rows_of(served(*move), rows)],
                    sems.at[len(copies)],
                )
            )
    for copy in copies:
        copy.start()
    for copy in copies:
        copy.wait()


def products_kernel(len_ref, near_ref, far_ref, schur_ref, residual_ref, arrived, out_ref):
    rows = schur_ref.shape[0] // 6
    curve = cross = jnp.zeros((1, schur_ref.shape[1]), f32)
    for ref, served_moves in ((near_ref, NEAR), (far_ref, FAR)):
        for i, move in enumerate(served_moves):
            face = served(*move)
            at = rows_of(face, rows)
            image = schur_ref[at, :]
            live = jnp.where(live_rows(len_ref, face, rows), residual_ref[at, :], 0.0)
            direction = ref[i * rows : (i + 1) * rows, :]
            curve += 2.0 * jnp.sum(direction * image, axis=0, keepdims=True)
            cross += 2.0 * jnp.sum(live * image, axis=0, keepdims=True)
    for j, piece in enumerate(folded(curve) + folded(cross)):
        out_ref[j : j + 1, :] = piece


def applied_kernel(pair_depth, len_ref, stored, schur_ref, *refs):
    keys = moves(SECOND)
    got, refs = dict(zip(keys, refs)), refs[len(keys) :]
    products, (applied_ref, spread_ref) = refs[:-2], refs[-2:]
    rows = schur_ref.shape[0] // 6
    folds = schur_ref.shape[1] // LANES
    total = jnp.zeros((1, schur_ref.shape[1]), f32)
    for move in SECOND:
        face = served(*move)
        at = rows_of(face, rows)
        applied = with_got(schur_ref, at, got, move)
        applied = jnp.where(live_rows(len_ref, face, rows), applied, 0.0)
        applied_ref[at, :] = applied
        total += jnp.sum(applied * applied, axis=0, keepdims=True)
    products = sum(ref[...] for ref in products)
    halves = [products[:folds], products[folds : 2 * folds]]
    if pair_depth:
        halves = [jnp.where(lax.axis_index("depth") == 0, *halves)]
    block = jnp.concatenate([*halves, *folded(total)], axis=0)
    spread_ref[...] = jnp.broadcast_to(block[None], spread_ref.shape)


def finish_kernel(pair_depth, scale, len_ref, sums_ref, rho_ref, square_ref, residual_ref, applied_ref, new_out, alpha_ref, norm_ref, new_ref, sems):
    rows = applied_ref.shape[0] // 6
    devices, height, _ = sums_ref.shape
    if pair_depth:
        folds = height // 2
        layers = [jnp.sum(sums_ref[: devices // 2], axis=0), jnp.sum(sums_ref[devices // 2 :], axis=0)]
        curve, cross = [unfolded(layer, 0, folds) for layer in layers]
        applied_square = unfolded(layers[0] + layers[1], folds, folds)
    else:
        folds = height // 3
        total = jnp.sum(sums_ref[...], axis=0)
        curve, cross, applied_square = [unfolded(total, i * folds, folds) for i in range(3)]
    alpha = rho_ref[...] / (scale * curve)
    alpha_ref[...] = alpha
    norm_ref[...] = scale * (
        square_ref[...] - 2.0 * alpha * cross + alpha * alpha * applied_square
    )
    copies = []
    for face in range(6):
        at = slice(face * rows, (face + 1) * rows)
        new_ref[at, :] = masked(len_ref, residual_ref, face, rows) - alpha * applied_ref[at, :]
        where = pl.ds(face * rows, rows)
        copies.append(pltpu.make_async_copy(new_ref.at[where], new_out.at[where], sems.at[face]))
        copies[-1].start()
    for copy in copies:
        copy.wait()


def to_all(x, axes):
    return lax.all_to_all(x, axes, split_axis=0, concat_axis=0, tiled=True)


def shards(
    face_len,
    residual,
    prev_direction,
    prev_rho,
    schur,
    neumann,
    coarse_basis,
    coarse_inverse,
    prim_owner,
    coarse_row,
):
    height, width = residual.shape[3:]
    rows = height // 6
    primal = coarse_basis.shape[4]
    owned = coarse_inverse.shape[3]
    owners = lax.axis_size(LAYER)
    slots = owners * CAP
    devices = lax.axis_size(AXES)
    layers = lax.axis_size("depth")
    pair_depth = layers == 2
    scale = 0.5 / (devices * height)
    folds = width // LANES
    tail = 2 * folds
    id_tail = id_rows(slots) + folds

    lengths = face_len.reshape(6)
    residual = residual.reshape(height, width)
    prev_direction = prev_direction.reshape(height, width)
    schur = schur.reshape(height, height)
    neumann = neumann.reshape(height, height)
    basis = coarse_basis.reshape(height, primal)
    inverse = coarse_inverse.reshape(owned, owned)
    owner = prim_owner.reshape(1, primal)
    wanted = coarse_row.reshape(1, primal)
    whole = shape_of(height, width)
    row = shape_of(1, width)
    face = shape_of(rows, width)

    (outgoing,) = call(
        pack_kernel,
        [shape_of(owners, folds * CAP + id_tail, 1, LANES)],
        [lengths, owner, wanted, residual, basis],
        far=range(5),
        flops=6 * height * primal * width,
        moved=4 * (height * (width + primal) + slots * width),
        scratch=[
            pltpu.SMEM((6,), jnp.int32),
            pltpu.VMEM((1, primal), jnp.int32),
            pltpu.VMEM((1, primal), jnp.int32),
            pltpu.VMEM((height, width), f32),
            pltpu.VMEM((height, primal), f32),
            pltpu.SemaphoreType.DMA((3, 2)),
            pltpu.SemaphoreType.DMA((3,)),
        ],
    )
    incoming = to_all(outgoing, LAYER)
    local, local_part, table, *halves = call(
        local_kernel,
        [whole, row, shape_of(primal, slots, dtype=bf16)]
        + [shape_of(height, primal, dtype=bf16)] * 2
        + [shape_of(height, height, dtype=bf16)] * 2,
        [lengths, residual, neumann, owner, basis, schur],
        smem=(0,),
        flops=6 * height * height * width,
        moved=4 * height * (3 * height + 2 * width),
    )
    basis_halves, schur_halves = halves[:2], halves[2:]
    answers, square = call(
        solve_kernel,
        [shape_of(owners, folds * CAP + folds, 1, LANES), shape_of(folds, LANES)],
        [incoming, inverse, local_part],
        far=range(2),
        flops=(8 * slots + 6 * owned) * owned * width,
        moved=8 * slots * width,
        scratch=[
            pltpu.VMEM((owners, id_tail, 1, LANES), f32),
            pltpu.VMEM((owners, folds * CAP, 1, LANES), f32),
            pltpu.VMEM((owned, owned), f32),
            pltpu.SemaphoreType.DMA((4,)),
        ],
    )
    returned = to_all(answers, LAYER)
    keys = moves(FIRST)
    faces = [face] * len(keys)
    image, sums, *outward = call(
        functools.partial(image_kernel, pair_depth),
        [whole, shape_of(tail, LANES) if pair_depth else shape_of(layers, tail, LANES), *faces],
        [returned, square, table, *basis_halves, local],
        flops=(6 * height + 4 * slots) * primal * width,
        moved=16 * height * width,
    )
    got = dict(zip(keys, exchange(outward, FIRST)))
    if pair_depth:
        sums = [sums, lax.ppermute(sums, "depth", route("depth", 0))]
    else:
        sums = [to_all(sums, "depth")]
    near_keys, far_keys = moves(NEAR), moves(FAR)
    rho, beta, square, near, near_image = call(
        functools.partial(near_kernel, pair_depth, scale, near_keys),
        [row, row, row, shape_of(len(NEAR) * rows, width), whole],
        [lengths, sums[0], prev_rho.reshape(1, width), image, prev_direction, *schur_halves]
        + [got[key] for key in near_keys]
        + sums[1:],
        smem=(0,),
        flops=4 * height * height * width,
        moved=4 * height * (height + 4 * width),
    )
    far, schur_image, *outward = call(
        functools.partial(far_kernel, far_keys),
        [shape_of(len(FAR) * rows, width), whole, *faces],
        [lengths, beta, image, prev_direction, *schur_halves, near, near_image]
        + [got[key] for key in far_keys],
        smem=(0,),
        flops=2 * height * height * width,
        moved=4 * height * (height + 4 * width),
    )
    got = exchange(outward, SECOND)
    (products,) = call(
        products_kernel,
        [shape_of(2 * folds, LANES)],
        [lengths, near, far, schur_image, residual, got[0]],
        smem=(0,),
        loose=(5,),
        flops=4 * height * width,
        moved=12 * height * width,
    )
    products = [products]
    if pair_depth:
        products.append(lax.ppermute(products[0], "depth", route("depth", 0)))
    (direction,) = call(
        store_kernel,
        [whole],
        [near, far],
        far_out=(0,),
        moved=8 * height * width,
        scratch=[pltpu.SemaphoreType.DMA((6,))],
    )
    applied, spread_sums = call(
        functools.partial(applied_kernel, pair_depth),
        [whole, shape_of(devices, (2 if pair_depth else 3) * folds, LANES)],
        [lengths, direction, schur_image, *got, *products],
        smem=(0,),
        far=(1,),
        flops=4 * height * width,
        moved=12 * height * width,
    )
    new_residual, alpha, norm = call(
        functools.partial(finish_kernel, pair_depth, scale),
        [whole, row, row],
        [lengths, to_all(spread_sums, AXES), rho, square, residual, applied],
        smem=(0,),
        far_out=(0,),
        flops=4 * height * width,
        moved=12 * height * width,
        scratch=[pltpu.VMEM((height, width), f32), pltpu.SemaphoreType.DMA((6,))],
    )
    out_shape = (1, 1, 1, height, width)
    return (
        new_residual.reshape(out_shape),
        direction.reshape(out_shape),
        rho.reshape(width),
        alpha.reshape(width),
        norm.reshape(width),
    )


def solution(mesh):
    tall = P("blk", "lat", "depth", None, None)
    flat = P("blk", "lat", "depth", None)
    in_specs = (flat, tall, tall, P(), tall, tall, tall, tall, tall, flat)
    out_specs = (tall, tall, P(), P(), P())
    return jax.shard_map(shards, mesh=mesh, in_specs=in_specs, out_specs=out_specs, check_vma=False)
```

```python
import functools

import jax
import jax.numpy as jnp
from jax import lax
from jax.experimental import pallas as pl
from jax.experimental.pallas import tpu as pltpu
from jax.sharding import PartitionSpec as P

CAP = 24
AXES = ("depth", "blk", "lat")
LAYER = ("blk", "lat")
LANES = 128
TILE = 8
f32 = jnp.float32
bf16 = jnp.bfloat16

VMEM = pl.BlockSpec(memory_space=pltpu.VMEM)
SMEM = pl.BlockSpec(memory_space=pltpu.SMEM)
ANY = pl.BlockSpec(memory_space=pl.ANY)


def shape_of(*dims, dtype=f32):
    return jax.ShapeDtypeStruct(dims, dtype)


def call(body, outs, operands, smem=(), far=(), loose=(), far_out=(), flops=0, moved=0, scratch=(), room=32):
    in_specs = [
        SMEM if i in smem else ANY if i in far or i in loose else VMEM
        for i in range(len(operands))
    ]
    operands = [
        pltpu.with_memory_space_constraint(x, pltpu.HBM) if i in far else x
        for i, x in enumerate(operands)
    ]
    out_specs = [ANY if i in far_out else VMEM for i in range(len(outs))]
    return pl.pallas_call(
        body,
        out_shape=list(outs),
        in_specs=in_specs,
        out_specs=out_specs,
        scratch_shapes=list(scratch),
        compiler_params=pltpu.CompilerParams(vmem_limit_bytes=room << 20),
        cost_estimate=pl.CostEstimate(flops=flops, bytes_accessed=moved, transcendentals=0),
    )(*operands)


def parts(x):
    high = x.astype(bf16)
    low = (x - high.astype(f32)).astype(bf16)
    return high, low


def mul(a, b, dims):
    return lax.dot_general(a, b, (dims, ((), ())), preferred_element_type=f32)


PLAIN = ((1,), (0,))


def product(a, b, dims=PLAIN):
    (ah, al), (bh, bl) = a, b
    return mul(ah, bh, dims) + (mul(ah, bl, dims) + mul(al, bh, dims))


def select(table, x, dims=PLAIN):
    high, low = parts(x)
    return mul(table, high, dims) + mul(table, low, dims)


def one_hot(hit):
    return jnp.where(hit, 1.0, 0.0).astype(bf16)


def live_rows(len_ref, face, rows):
    return lax.broadcasted_iota(jnp.int32, (rows, 1), 0) < len_ref[face]


def masked(len_ref, ref, face, rows):
    block = ref[face * rows : (face + 1) * rows, :]
    return jnp.where(live_rows(len_ref, face, rows), block, 0.0)


def folded(vector):
    pieces = vector.shape[1] // LANES
    return [vector[:, j * LANES : (j + 1) * LANES] for j in range(pieces)]


def unfolded(block, first, pieces):
    return jnp.concatenate([block[first + j : first + j + 1, :] for j in range(pieces)], axis=1)


def id_rows(slots):
    return -(-slots // LANES)


def tiles(rows):
    return -(-rows // TILE) * TILE


def put_slab(out_ref, block):
    owners = out_ref.shape[0]
    for j in range(block.shape[1] // LANES):
        piece = block[:, j * LANES : (j + 1) * LANES]
        out_ref[:, j * CAP : (j + 1) * CAP, :] = piece.reshape(owners, CAP, LANES)


def get_slab(ref, pieces):
    slots = ref.shape[0] * CAP
    return jnp.concatenate(
        [ref[:, j * CAP : (j + 1) * CAP, :].reshape(slots, LANES) for j in range(pieces)], axis=1
    )


def columns(*rows):
    spare = [jnp.zeros_like(rows[0])] * (TILE - len(rows))
    turned = jnp.transpose(jnp.concatenate([*rows, *spare], axis=0))
    return [turned[:, i : i + 1] for i in range(len(rows))]


def position(owner):
    blks, lats = lax.axis_size("blk"), lax.axis_size("lat")
    owner = owner.astype(f32)
    blk = jnp.floor((owner + 0.5) * (1.0 / lats))
    turned = (owner - lats * blk) * blks + blk
    return jnp.where(lax.rem(lax.axis_index("depth"), 2) == 0, owner, turned)


def own_position():
    blk, lat, depth = (lax.axis_index(axis) for axis in ("blk", "lat", "depth"))
    blks, lats = lax.axis_size("blk"), lax.axis_size("lat")
    return jnp.where(lax.rem(depth, 2) == 0, blk * lats + lat, lat * blks + blk)


def to_layer(x):
    blks, lats, layers = (lax.axis_size(axis) for axis in ("blk", "lat", "depth"))
    groups = []
    for layer in range(layers):
        if layer % 2 == 0:
            order = [(blk, lat) for blk in range(blks) for lat in range(lats)]
        else:
            order = [(blk, lat) for lat in range(lats) for blk in range(blks)]
        groups.append([(blk * lats + lat) * layers + layer for blk, lat in order])
    return lax.all_to_all(
        x, ("blk", "lat", "depth"), 0, 0, axis_index_groups=groups, tiled=True
    )


def ranks(own_row):
    primal = own_row.shape[1]
    (own_col,) = columns(own_row)
    row_at = lax.broadcasted_iota(jnp.int32, (primal, primal), 0)
    col_at = lax.broadcasted_iota(jnp.int32, (primal, primal), 1)
    before = (own_row == own_col) & (row_at < col_at)
    return jnp.sum(jnp.where(before, 1.0, 0.0), axis=0, keepdims=True), own_col


def pack_kernel(len_any, owner_any, row_any, residual_any, basis_any, slab_ref, *refs):
    len_ref, owner_ref, row_ref, residual_ref, basis_ref, sems, small_sems = refs
    rows = residual_ref.shape[0] // 6
    primal = basis_ref.shape[1]
    owners = slab_ref.shape[0]
    slots = owners * CAP
    small = [
        pltpu.make_async_copy(src, dst, small_sems.at[i])
        for i, (src, dst) in enumerate(
            [(owner_any, owner_ref), (row_any, row_ref), (len_any, len_ref)]
        )
    ]
    large = []
    for pair in range(3):
        at = pl.ds(2 * pair * rows, 2 * rows)
        large.append(
            (
                pltpu.make_async_copy(residual_any.at[at], residual_ref.at[at], sems.at[pair, 0]),
                pltpu.make_async_copy(basis_any.at[at], basis_ref.at[at], sems.at[pair, 1]),
            )
        )
    for copy in small:
        copy.start()
    for pair in large:
        for copy in pair:
            copy.start()
    for copy in small:
        copy.wait()

    def term_of(pair):
        for copy in large[pair]:
            copy.wait()
        weighted = jnp.concatenate(
            [0.5 * masked(len_ref, residual_ref, 2 * pair + side, rows) for side in range(2)],
            axis=0,
        )
        basis = basis_ref[2 * pair * rows : 2 * (pair + 1) * rows, :]
        return product(parts(jnp.transpose(basis)), parts(weighted))

    terms = term_of(0)
    own_row = position(owner_ref[...])
    wanted_row = row_ref[...].astype(f32) + 1.0
    rank_row, _ = ranks(own_row)
    slot_row = (own_row * CAP + rank_row).astype(jnp.int32)
    rank_col, wanted_col = columns(rank_row, wanted_row)
    packer = one_hot(lax.broadcasted_iota(jnp.int32, (slots, primal), 0) == slot_row)
    to_owner = one_hot(
        lax.broadcasted_iota(jnp.int32, (owners, primal), 0) == own_row.astype(jnp.int32)
    )
    at_owner = own_position() * CAP + rank_col.astype(jnp.int32)
    place = lax.broadcasted_iota(jnp.int32, (primal, id_rows(slots) * LANES), 1)
    names = select(to_owner, jnp.where(place == at_owner, wanted_col, 0.0))
    terms += term_of(1)
    terms += term_of(2)
    put_slab(slab_ref, select(packer, terms))
    tail = slab_ref.shape[1] - tiles(id_rows(slots))
    names = jnp.concatenate(
        [names, jnp.zeros((owners, (slab_ref.shape[1] - tail) * LANES - names.shape[1]), f32)], axis=1
    )
    for j in range(slab_ref.shape[1] - tail):
        slab_ref[:, tail + j, :] = names[:, j * LANES : (j + 1) * LANES]


def local_kernel(len_ref, residual_ref, matrix_ref, owner_ref, *refs):
    whole, refs = refs[:2], refs[2:]
    local_ref, part_ref, square_ref, table_ref, refs = *refs[:4], refs[4:]
    rows = residual_ref.shape[0] // 6
    live = jnp.concatenate(
        [masked(len_ref, residual_ref, face, rows) for face in range(6)], axis=0
    )
    local = product(parts(matrix_ref[...]), parts(0.5 * live))
    local_ref[...] = local
    part_ref[...] = jnp.sum(live * local, axis=0, keepdims=True)
    square_ref[...] = jnp.sum(live * live, axis=0, keepdims=True)
    refs[0][...], refs[1][...] = parts(whole[0][...])
    for i, move in enumerate(NEAR + FAR):
        at = slice(i * rows, (i + 1) * rows)
        refs[2][:, at], refs[3][:, at] = parts(whole[1][:, rows_of(served(*move), rows)])
    primal, slots = table_ref.shape
    rank_row, own_col = ranks(position(owner_ref[...]))
    (rank_col,) = columns(rank_row)
    slot_col = (own_col * CAP + rank_col).astype(jnp.int32)
    table_ref[...] = one_hot(lax.broadcasted_iota(jnp.int32, (primal, slots), 1) == slot_col)


def solve_kernel(incoming_any, inverse_any, local_part_ref, square_ref, answer_ref, *refs):
    names_ref, slab_ref, inverse_ref, sems = refs
    owners, height, _ = slab_ref.shape
    pieces = height // CAP
    half = pieces // 2 * CAP
    copies = [
        pltpu.make_async_copy(
            incoming_any.at[:, pl.ds(height, names_ref.shape[1])], names_ref, sems.at[0]
        ),
        pltpu.make_async_copy(
            incoming_any.at[:, pl.ds(0, half)], slab_ref.at[:, pl.ds(0, half)], sems.at[1]
        ),
        pltpu.make_async_copy(
            incoming_any.at[:, pl.ds(half, height - half)],
            slab_ref.at[:, pl.ds(half, height - half)],
            sems.at[2],
        ),
        pltpu.make_async_copy(inverse_any, inverse_ref, sems.at[3]),
    ]
    for copy in copies:
        copy.start()
    copies[0].wait()
    slots, owned = owners * CAP, inverse_ref.shape[0]
    wanted = unfolded(jnp.sum(names_ref[...], axis=0), 0, id_rows(slots))[:, :slots]
    (wanted_col,) = columns(wanted)
    row_at = lax.broadcasted_iota(jnp.int32, (owned, slots), 0).astype(f32) + 1.0
    col_at = lax.broadcasted_iota(jnp.int32, (slots, owned), 1).astype(f32) + 1.0
    gather = one_hot(row_at == wanted)
    table = one_hot(col_at == wanted_col)
    copies[3].wait()
    inverse = parts(inverse_ref[...])
    for copy in copies[1:3]:
        copy.wait()
    summed = select(gather, get_slab(slab_ref, pieces))
    solved = product(inverse, parts(summed))
    put_slab(answer_ref, select(table, solved))
    total = local_part_ref[...] + 2.0 * jnp.sum(summed * solved, axis=0, keepdims=True)
    sums = folded(total) + folded(square_ref[...])
    sums += [jnp.zeros((1, LANES), f32)] * (tiles(len(sums)) - len(sums))
    answer_ref[:, pieces * CAP :, :] = jnp.broadcast_to(
        jnp.concatenate(sums, axis=0)[None], (owners, len(sums), LANES)
    )


NEAR = (("blk", "up"), ("lat", 0), ("depth", 0), ("depth", 1))
FAR = (("blk", "down"), ("lat", 1))
FIRST = NEAR + FAR
SECOND = (("blk", "up"), ("lat", 0), ("blk", "down"), ("lat", 1), ("depth", 0), ("depth", 1))


def moves(order):
    return [(axis, way) for axis, way in order if route(axis, way)]


def route(axis, way):
    devices = lax.axis_size(axis)
    if way in ("up", "down"):
        by = 1 if way == "up" else -1
        return [(i, (i + by) % devices) for i in range(devices)]
    return [pair for i in range(way, devices - 1, 2) for pair in ((i, i + 1), (i + 1, i))]


def served(axis, way):
    if way in ("up", "down"):
        return 0 if way == "up" else 1
    plus = (lax.rem(lax.axis_index(axis), 2) == way).astype(jnp.int32)
    return (2 if axis == "lat" else 4) + plus


def sent(axis, way):
    return 1 - served(axis, way) if axis == "blk" else served(axis, way)


def rows_of(face, rows):
    if isinstance(face, int):
        return pl.ds(face * rows, rows)
    return pl.ds(pl.multiple_of(face * rows, rows), rows)


def put_faces(image_ref, rows, order, face_refs):
    for ref, move in zip(face_refs, moves(order), strict=True):
        ref[...] = image_ref[rows_of(sent(*move), rows), :]


def exchange(faces, order):
    return [
        lax.ppermute(block, axis, route(axis, way))
        for block, (axis, way) in zip(faces, moves(order), strict=True)
    ]


def image_kernel(pair_depth, returned_ref, table_ref, high_ref, low_ref, local_ref, image_ref, sums_ref, *face_refs):
    rows = local_ref.shape[0] // 6
    width = local_ref.shape[1]
    folds = width // LANES
    correction = select(table_ref[...], get_slab(returned_ref, folds))
    image = local_ref[...] + product((high_ref[...], low_ref[...]), parts(correction))
    image_ref[...] = image
    put_faces(image_ref, rows, FIRST, face_refs)
    tail = jnp.sum(returned_ref[:, folds * CAP :, :], axis=0)
    if pair_depth:
        sums_ref[...] = tail
    else:
        sums_ref[...] = jnp.broadcast_to(tail[None], sums_ref.shape)


def with_got(ref, at, got, move):
    return ref[at, :] + got[move][...] if move in got else ref[at, :]


def new_direction(len_ref, beta, image_ref, prev_ref, got, move, rows):
    face = served(*move)
    at = rows_of(face, rows)
    precond = 0.5 * with_got(image_ref, at, got, move)
    return jnp.where(live_rows(len_ref, face, rows), precond + beta * prev_ref[at, :], 0.0)


def near_kernel(pair_depth, scale, keys, len_ref, sums_ref, prev_rho_ref, image_ref, prev_ref, high_ref, low_ref, *refs):
    got, refs = dict(zip(keys, refs)), refs[len(keys) :]
    if pair_depth:
        sums, refs = sums_ref[...] + refs[0][...], refs[1:]
    else:
        sums = jnp.sum(sums_ref[...], axis=0)
    rho_out, beta_out, square_out, near_ref, image_out = refs
    rows = image_ref.shape[0] // 6
    folds = image_ref.shape[1] // LANES
    rho = scale * unfolded(sums, 0, folds)
    beta = rho / prev_rho_ref[...]
    rho_out[...] = rho
    beta_out[...] = beta
    square_out[...] = unfolded(sums, folds, folds)
    for i, move in enumerate(NEAR):
        near_ref[i * rows : (i + 1) * rows, :] = new_direction(
            len_ref, beta, image_ref, prev_ref, got, move, rows
        )
    first = len(NEAR) * rows
    image_out[...] = product((high_ref[:, :first], low_ref[:, :first]), parts(near_ref[...]))


def far_kernel(keys, len_ref, beta_ref, image_ref, prev_ref, high_ref, low_ref, near_ref, near_image_ref, *refs):
    got, refs = dict(zip(keys, refs)), refs[len(keys) :]
    far_ref, schur_out, *face_refs = refs
    rows = image_ref.shape[0] // 6
    beta = beta_ref[...]
    for i, move in enumerate(FAR):
        far_ref[i * rows : (i + 1) * rows, :] = new_direction(
            len_ref, beta, image_ref, prev_ref, got, move, rows
        )
    first = len(NEAR) * rows
    image = near_image_ref[...] + product(
        (high_ref[:, first:], low_ref[:, first:]), parts(far_ref[...])
    )
    schur_out[...] = image
    put_faces(schur_out, rows, SECOND, face_refs)


def store_kernel(near_ref, far_ref, direction_out, sems):
    rows = far_ref.shape[0] // len(FAR)
    copies = []
    for ref, served_moves in ((near_ref, NEAR), (far_ref, FAR)):
        for i, move in enumerate(served_moves):
            copies.append(
                pltpu.make_async_copy(
                    ref.at[pl.ds(i * rows, rows)],
                    direction_out.at[rows_of(served(*move), rows)],
                    sems.at[len(copies)],
                )
            )
    for copy in copies:
        copy.start()
    for copy in copies:
        copy.wait()


def products_kernel(len_ref, near_ref, far_ref, schur_ref, residual_ref, arrived, out_ref):
    rows = schur_ref.shape[0] // 6
    curve = cross = jnp.zeros((1, schur_ref.shape[1]), f32)
    for ref, served_moves in ((near_ref, NEAR), (far_ref, FAR)):
        for i, move in enumerate(served_moves):
            face = served(*move)
            at = rows_of(face, rows)
            image = schur_ref[at, :]
            live = jnp.where(live_rows(len_ref, face, rows), residual_ref[at, :], 0.0)
            direction = ref[i * rows : (i + 1) * rows, :]
            curve += 2.0 * jnp.sum(direction * image, axis=0, keepdims=True)
            cross += 2.0 * jnp.sum(live * image, axis=0, keepdims=True)
    for j, piece in enumerate(folded(curve) + folded(cross)):
        out_ref[j : j + 1, :] = piece


def applied_kernel(pair_depth, len_ref, stored, schur_ref, *refs):
    keys = moves(SECOND)
    got, refs = dict(zip(keys, refs)), refs[len(keys) :]
    products, (applied_ref, spread_ref) = refs[:-2], refs[-2:]
    rows = schur_ref.shape[0] // 6
    folds = schur_ref.shape[1] // LANES
    total = jnp.zeros((1, schur_ref.shape[1]), f32)
    for move in SECOND:
        face = served(*move)
        at = rows_of(face, rows)
        applied = with_got(schur_ref, at, got, move)
        applied = jnp.where(live_rows(len_ref, face, rows), applied, 0.0)
        applied_ref[at, :] = applied
        total += jnp.sum(applied * applied, axis=0, keepdims=True)
    products = sum(ref[...] for ref in products)
    halves = [products[:folds], products[folds : 2 * folds]]
    if pair_depth:
        halves = [jnp.where(lax.axis_index("depth") == 0, *halves)]
    block = jnp.concatenate([*halves, *folded(total)], axis=0)
    spread_ref[...] = jnp.broadcast_to(block[None], spread_ref.shape)


def finish_kernel(pair_depth, scale, len_ref, sums_ref, rho_ref, square_ref, residual_ref, applied_ref, new_out, alpha_ref, norm_ref, new_ref, sems):
    rows = applied_ref.shape[0] // 6
    devices, height, _ = sums_ref.shape
    if pair_depth:
        folds = height // 2
        layers = [jnp.sum(sums_ref[: devices // 2], axis=0), jnp.sum(sums_ref[devices // 2 :], axis=0)]
        curve, cross = [unfolded(layer, 0, folds) for layer in layers]
        applied_square = unfolded(layers[0] + layers[1], folds, folds)
    else:
        folds = height // 3
        total = jnp.sum(sums_ref[...], axis=0)
        curve, cross, applied_square = [unfolded(total, i * folds, folds) for i in range(3)]
    alpha = rho_ref[...] / (scale * curve)
    alpha_ref[...] = alpha
    norm_ref[...] = scale * (
        square_ref[...] - 2.0 * alpha * cross + alpha * alpha * applied_square
    )
    copies = []
    for face in range(6):
        at = slice(face * rows, (face + 1) * rows)
        new_ref[at, :] = masked(len_ref, residual_ref, face, rows) - alpha * applied_ref[at, :]
        where = pl.ds(face * rows, rows)
        copies.append(pltpu.make_async_copy(new_ref.at[where], new_out.at[where], sems.at[face]))
        copies[-1].start()
    for copy in copies:
        copy.wait()


def to_all(x, axes):
    return lax.all_to_all(x, axes, split_axis=0, concat_axis=0, tiled=True)


def shards(
    face_len,
    residual,
    prev_direction,
    prev_rho,
    schur,
    neumann,
    coarse_basis,
    coarse_inverse,
    prim_owner,
    coarse_row,
):
    height, width = residual.shape[3:]
    rows = height // 6
    primal = coarse_basis.shape[4]
    owned = coarse_inverse.shape[3]
    owners = lax.axis_size(LAYER)
    slots = owners * CAP
    devices = lax.axis_size(AXES)
    layers = lax.axis_size("depth")
    pair_depth = layers == 2
    scale = 0.5 / (devices * height)
    folds = width // LANES
    tail = tiles(2 * folds)
    id_tail = tiles(id_rows(slots))

    lengths = face_len.reshape(6)
    residual = residual.reshape(height, width)
    prev_direction = prev_direction.reshape(height, width)
    schur = schur.reshape(height, height)
    neumann = neumann.reshape(height, height)
    basis = coarse_basis.reshape(height, primal)
    inverse = coarse_inverse.reshape(owned, owned)
    owner = prim_owner.reshape(1, primal)
    wanted = coarse_row.reshape(1, primal)
    whole = shape_of(height, width)
    row = shape_of(1, width)
    face = shape_of(rows, width)

    (outgoing,) = call(
        pack_kernel,
        [shape_of(owners, folds * CAP + id_tail, LANES)],
        [lengths, owner, wanted, residual, basis],
        far=range(5),
        flops=6 * height * primal * width,
        moved=4 * (height * (width + primal) + slots * width),
        scratch=[
            pltpu.SMEM((6,), jnp.int32),
            pltpu.VMEM((1, primal), jnp.int32),
            pltpu.VMEM((1, primal), jnp.int32),
            pltpu.VMEM((height, width), f32),
            pltpu.VMEM((height, primal), f32),
            pltpu.SemaphoreType.DMA((3, 2)),
            pltpu.SemaphoreType.DMA((3,)),
        ],
    )
    incoming = to_layer(outgoing)
    local, local_part, square, table, *halves = call(
        local_kernel,
        [whole, row, row, shape_of(primal, slots, dtype=bf16)]
        + [shape_of(height, primal, dtype=bf16)] * 2
        + [shape_of(height, height, dtype=bf16)] * 2,
        [lengths, residual, neumann, owner, basis, schur],
        smem=(0,),
        flops=6 * height * height * width,
        moved=4 * height * (3 * height + 2 * width),
    )
    basis_halves, schur_halves = halves[:2], halves[2:]
    (answers,) = call(
        solve_kernel,
        [shape_of(owners, folds * CAP + tail, LANES)],
        [incoming, inverse, local_part, square],
        far=range(2),
        flops=(8 * slots + 6 * owned) * owned * width,
        moved=8 * slots * width,
        scratch=[
            pltpu.VMEM((owners, id_tail, LANES), f32),
            pltpu.VMEM((owners, folds * CAP, LANES), f32),
            pltpu.VMEM((owned, owned), f32),
            pltpu.SemaphoreType.DMA((4,)),
        ],
    )
    returned = to_layer(answers)
    keys = moves(FIRST)
    faces = [face] * len(keys)
    image, sums, *outward = call(
        functools.partial(image_kernel, pair_depth),
        [whole, shape_of(tail, LANES) if pair_depth else shape_of(layers, tail, LANES), *faces],
        [returned, table, *basis_halves, local],
        flops=(6 * height + 4 * slots) * primal * width,
        moved=16 * height * width,
    )
    got = dict(zip(keys, exchange(outward, FIRST)))
    if pair_depth:
        sums = [sums, lax.ppermute(sums, "depth", route("depth", 0))]
    else:
        sums = [to_all(sums, "depth")]
    near_keys, far_keys = moves(NEAR), moves(FAR)
    rho, beta, square, near, near_image = call(
        functools.partial(near_kernel, pair_depth, scale, near_keys),
        [row, row, row, shape_of(len(NEAR) * rows, width), whole],
        [lengths, sums[0], prev_rho.reshape(1, width), image, prev_direction, *schur_halves]
        + [got[key] for key in near_keys]
        + sums[1:],
        smem=(0,),
        flops=4 * height * height * width,
        moved=4 * height * (height + 4 * width),
    )
    far, schur_image, *outward = call(
        functools.partial(far_kernel, far_keys),
        [shape_of(len(FAR) * rows, width), whole, *faces],
        [lengths, beta, image, prev_direction, *schur_halves, near, near_image]
        + [got[key] for key in far_keys],
        smem=(0,),
        flops=2 * height * height * width,
        moved=4 * height * (height + 4 * width),
    )
    got = exchange(outward, SECOND)
    (products,) = call(
        products_kernel,
        [shape_of(2 * folds, LANES)],
        [lengths, near, far, schur_image, residual, got[0]],
        smem=(0,),
        loose=(5,),
        flops=4 * height * width,
        moved=12 * height * width,
    )
    products = [products]
    if pair_depth:
        products.append(lax.ppermute(products[0], "depth", route("depth", 0)))
    (direction,) = call(
        store_kernel,
        [whole],
        [near, far],
        far_out=(0,),
        moved=8 * height * width,
        scratch=[pltpu.SemaphoreType.DMA((6,))],
    )
    applied, spread_sums = call(
        functools.partial(applied_kernel, pair_depth),
        [whole, shape_of(devices, (2 if pair_depth else 3) * folds, LANES)],
        [lengths, direction, schur_image, *got, *products],
        smem=(0,),
        far=(1,),
        flops=4 * height * width,
        moved=12 * height * width,
    )
    new_residual, alpha, norm = call(
        functools.partial(finish_kernel, pair_depth, scale),
        [whole, row, row],
        [lengths, to_all(spread_sums, AXES), rho, square, residual, applied],
        smem=(0,),
        far_out=(0,),
        flops=4 * height * width,
        moved=12 * height * width,
        scratch=[pltpu.VMEM((height, width), f32), pltpu.SemaphoreType.DMA((6,))],
    )
    out_shape = (1, 1, 1, height, width)
    return (
        new_residual.reshape(out_shape),
        direction.reshape(out_shape),
        rho.reshape(width),
        alpha.reshape(width),
        norm.reshape(width),
    )


def solution(mesh):
    tall = P("blk", "lat", "depth", None, None)
    flat = P("blk", "lat", "depth", None)
    in_specs = (flat, tall, tall, P(), tall, tall, tall, tall, tall, flat)
    out_specs = (tall, tall, P(), P(), P())
    return jax.shard_map(shards, mesh=mesh, in_specs=in_specs, out_specs=out_specs, check_vma=False)
```

```python
import functools

import jax
import jax.numpy as jnp
from jax import lax
from jax.experimental import pallas as pl
from jax.experimental.pallas import tpu as pltpu
from jax.sharding import PartitionSpec as P

CAP = 24
AXES = ("depth", "blk", "lat")
LAYER = ("blk", "lat")
LANES = 128
TILE = 8
f32 = jnp.float32
bf16 = jnp.bfloat16

VMEM = pl.BlockSpec(memory_space=pltpu.VMEM)
SMEM = pl.BlockSpec(memory_space=pltpu.SMEM)
ANY = pl.BlockSpec(memory_space=pl.ANY)


def shape_of(*dims, dtype=f32):
    return jax.ShapeDtypeStruct(dims, dtype)


def call(body, outs, operands, smem=(), far=(), loose=(), far_out=(), flops=0, moved=0, scratch=(), room=32):
    in_specs = [
        SMEM if i in smem else ANY if i in far or i in loose else VMEM
        for i in range(len(operands))
    ]
    operands = [
        pltpu.with_memory_space_constraint(x, pltpu.HBM) if i in far else x
        for i, x in enumerate(operands)
    ]
    out_specs = [ANY if i in far_out else VMEM for i in range(len(outs))]
    return pl.pallas_call(
        body,
        out_shape=list(outs),
        in_specs=in_specs,
        out_specs=out_specs,
        scratch_shapes=list(scratch),
        compiler_params=pltpu.CompilerParams(vmem_limit_bytes=room << 20),
        cost_estimate=pl.CostEstimate(flops=flops, bytes_accessed=moved, transcendentals=0),
    )(*operands)


def parts(x):
    high = x.astype(bf16)
    low = (x - high.astype(f32)).astype(bf16)
    return high, low


def mul(a, b, dims):
    return lax.dot_general(a, b, (dims, ((), ())), preferred_element_type=f32)


PLAIN = ((1,), (0,))


def product(a, b, dims=PLAIN):
    (ah, al), (bh, bl) = a, b
    return mul(ah, bh, dims) + (mul(ah, bl, dims) + mul(al, bh, dims))


def select(table, x, dims=PLAIN):
    high, low = parts(x)
    return mul(table, high, dims) + mul(table, low, dims)


def one_hot(hit):
    return jnp.where(hit, 1.0, 0.0).astype(bf16)


def live_rows(len_ref, face, rows):
    return lax.broadcasted_iota(jnp.int32, (rows, 1), 0) < len_ref[face]


def masked(len_ref, ref, face, rows):
    block = ref[face * rows : (face + 1) * rows, :]
    return jnp.where(live_rows(len_ref, face, rows), block, 0.0)


def folded(vector):
    pieces = vector.shape[1] // LANES
    return [vector[:, j * LANES : (j + 1) * LANES] for j in range(pieces)]


def unfolded(block, first, pieces):
    return jnp.concatenate([block[first + j : first + j + 1, :] for j in range(pieces)], axis=1)


def id_rows(slots):
    return -(-slots // LANES)


def tiles(rows):
    return -(-rows // TILE) * TILE


def put_slab(out_ref, block):
    owners = out_ref.shape[0]
    for j in range(block.shape[1] // LANES):
        piece = block[:, j * LANES : (j + 1) * LANES]
        out_ref[:, j * CAP : (j + 1) * CAP, :] = piece.reshape(owners, CAP, LANES)


def get_slab(ref, pieces, first=0, last=None):
    last = ref.shape[0] if last is None else last
    columns_of = [ref[first:last, j * CAP : (j + 1) * CAP, :] for j in range(pieces)]
    return jnp.concatenate([x.reshape((last - first) * CAP, LANES) for x in columns_of], axis=1)


def columns(*rows):
    spare = [jnp.zeros_like(rows[0])] * (TILE - len(rows))
    turned = jnp.transpose(jnp.concatenate([*rows, *spare], axis=0))
    return [turned[:, i : i + 1] for i in range(len(rows))]


def turn(lat):
    return lat ^ (lat >> 1)


def position(owner):
    lats = lax.axis_size("lat")
    owner = owner.astype(f32)
    lat = owner - lats * jnp.floor((owner + 0.5) * (1.0 / lats))
    for one in range(lats):
        owner = owner + jnp.where(lat == one, float(turn(one) - one), 0.0)
    return owner


def own_position():
    lat = lax.axis_index("lat")
    return lax.axis_index("blk") * lax.axis_size("lat") + turn(lat)


def to_layer(x):
    lats = lax.axis_size("lat")
    order = [
        blk * lats + lat
        for blk in range(lax.axis_size("blk"))
        for lat in sorted(range(lats), key=turn)
    ]
    return lax.all_to_all(x, LAYER, 0, 0, axis_index_groups=[order], tiled=True)


def ranks(own_row):
    primal = own_row.shape[1]
    (own_col,) = columns(own_row)
    row_at = lax.broadcasted_iota(jnp.int32, (primal, primal), 0)
    col_at = lax.broadcasted_iota(jnp.int32, (primal, primal), 1)
    before = (own_row == own_col) & (row_at < col_at)
    return jnp.sum(jnp.where(before, 1.0, 0.0), axis=0, keepdims=True), own_col


def pack_kernel(len_any, owner_any, row_any, residual_any, basis_any, slab_ref, *refs):
    len_ref, owner_ref, row_ref, residual_ref, basis_ref, sems, small_sems = refs
    rows = residual_ref.shape[0] // 6
    primal = basis_ref.shape[1]
    owners = slab_ref.shape[0]
    slots = owners * CAP
    small = [
        pltpu.make_async_copy(src, dst, small_sems.at[i])
        for i, (src, dst) in enumerate(
            [(owner_any, owner_ref), (row_any, row_ref), (len_any, len_ref)]
        )
    ]
    large = []
    for pair in range(3):
        at = pl.ds(2 * pair * rows, 2 * rows)
        large.append(
            (
                pltpu.make_async_copy(residual_any.at[at], residual_ref.at[at], sems.at[pair, 0]),
                pltpu.make_async_copy(basis_any.at[at], basis_ref.at[at], sems.at[pair, 1]),
            )
        )
    for copy in small:
        copy.start()
    for pair in large:
        for copy in pair:
            copy.start()
    for copy in small:
        copy.wait()

    def term_of(*pairs):
        for pair in pairs:
            for copy in large[pair]:
                copy.wait()
        first, last = 2 * pairs[0], 2 * pairs[-1] + 2
        weighted = jnp.concatenate(
            [0.5 * masked(len_ref, residual_ref, face, rows) for face in range(first, last)],
            axis=0,
        )
        basis = basis_ref[first * rows : last * rows, :]
        return product(parts(jnp.transpose(basis)), parts(weighted))

    terms = term_of(0)
    own_row = position(owner_ref[...])
    wanted_row = row_ref[...].astype(f32) + 1.0
    rank_row, _ = ranks(own_row)
    slot_row = (own_row * CAP + rank_row).astype(jnp.int32)
    rank_col, wanted_col = columns(rank_row, wanted_row)
    packer = one_hot(lax.broadcasted_iota(jnp.int32, (slots, primal), 0) == slot_row)
    to_owner = one_hot(
        lax.broadcasted_iota(jnp.int32, (owners, primal), 0) == own_row.astype(jnp.int32)
    )
    at_owner = own_position() * CAP + rank_col.astype(jnp.int32)
    place = lax.broadcasted_iota(jnp.int32, (primal, id_rows(slots) * LANES), 1)
    names = select(to_owner, jnp.where(place == at_owner, wanted_col, 0.0))
    terms += term_of(1, 2)
    put_slab(slab_ref, select(packer, terms))
    tail = slab_ref.shape[1] - tiles(id_rows(slots))
    names = jnp.concatenate(
        [names, jnp.zeros((owners, (slab_ref.shape[1] - tail) * LANES - names.shape[1]), f32)], axis=1
    )
    for j in range(slab_ref.shape[1] - tail):
        slab_ref[:, tail + j, :] = names[:, j * LANES : (j + 1) * LANES]


def local_kernel(len_ref, residual_ref, matrix_ref, owner_ref, *refs):
    whole, refs = refs[:2], refs[2:]
    local_ref, part_ref, square_ref, table_ref, refs = *refs[:4], refs[4:]
    rows = residual_ref.shape[0] // 6
    live = jnp.concatenate(
        [masked(len_ref, residual_ref, face, rows) for face in range(6)], axis=0
    )
    local = product(parts(matrix_ref[...]), parts(0.5 * live))
    local_ref[...] = local
    part_ref[...] = jnp.sum(live * local, axis=0, keepdims=True)
    square_ref[...] = jnp.sum(live * live, axis=0, keepdims=True)
    refs[0][...], refs[1][...] = parts(whole[0][...])
    for i, move in enumerate(NEAR + FAR):
        at = slice(i * rows, (i + 1) * rows)
        refs[2][:, at], refs[3][:, at] = parts(whole[1][:, rows_of(served(*move), rows)])
    primal, slots = table_ref.shape
    rank_row, own_col = ranks(position(owner_ref[...]))
    (rank_col,) = columns(rank_row)
    slot_col = (own_col * CAP + rank_col).astype(jnp.int32)
    table_ref[...] = one_hot(lax.broadcasted_iota(jnp.int32, (primal, slots), 1) == slot_col)


def solve_kernel(incoming_any, inverse_any, local_part_ref, square_ref, answer_ref, *refs):
    names_ref, slab_ref, inverse_ref, sems = refs
    owners, height, _ = slab_ref.shape
    pieces = height // CAP
    slots, owned = owners * CAP, inverse_ref.shape[0]
    cut = 2 * slots // 3 // LANES * LANES
    lead = -(-cut // CAP)
    copies = [
        pltpu.make_async_copy(
            incoming_any.at[:, pl.ds(height, names_ref.shape[1])], names_ref, sems.at[0]
        ),
        pltpu.make_async_copy(
            incoming_any.at[pl.ds(0, lead), pl.ds(0, height)],
            slab_ref.at[pl.ds(0, lead)],
            sems.at[1],
        ),
        pltpu.make_async_copy(
            incoming_any.at[pl.ds(lead, owners - lead), pl.ds(0, height)],
            slab_ref.at[pl.ds(lead, owners - lead)],
            sems.at[2],
        ),
        pltpu.make_async_copy(inverse_any, inverse_ref, sems.at[3]),
    ]
    for copy in copies:
        copy.start()
    copies[0].wait()
    wanted = unfolded(jnp.sum(names_ref[...], axis=0), 0, id_rows(slots))[:, :slots]
    (wanted_col,) = columns(wanted)
    row_at = lax.broadcasted_iota(jnp.int32, (owned, slots), 0).astype(f32) + 1.0
    col_at = lax.broadcasted_iota(jnp.int32, (slots, owned), 1).astype(f32) + 1.0
    gather = one_hot(row_at == wanted)
    table = one_hot(col_at == wanted_col)
    copies[3].wait()
    inverse = parts(inverse_ref[...])
    copies[1].wait()
    head = get_slab(slab_ref, pieces, 0, lead)
    summed = select(gather[:, :cut], head[:cut])
    copies[2].wait()
    rest = jnp.concatenate([head[cut:], get_slab(slab_ref, pieces, lead, owners)], axis=0)
    summed += select(gather[:, cut:], rest)
    solved = product(inverse, parts(summed))
    put_slab(answer_ref, select(table, solved))
    total = local_part_ref[...] + 2.0 * jnp.sum(summed * solved, axis=0, keepdims=True)
    sums = folded(total) + folded(square_ref[...])
    sums += [jnp.zeros((1, LANES), f32)] * (tiles(len(sums)) - len(sums))
    answer_ref[:, pieces * CAP :, :] = jnp.broadcast_to(
        jnp.concatenate(sums, axis=0)[None], (owners, len(sums), LANES)
    )


NEAR = (("blk", "up"), ("lat", 0), ("depth", 0), ("depth", 1))
FAR = (("blk", "down"), ("lat", 1))
FIRST = NEAR + FAR
SECOND = (("blk", "up"), ("lat", 0), ("blk", "down"), ("lat", 1), ("depth", 0), ("depth", 1))


def moves(order):
    return [(axis, way) for axis, way in order if route(axis, way)]


def route(axis, way):
    devices = lax.axis_size(axis)
    if way in ("up", "down"):
        by = 1 if way == "up" else -1
        return [(i, (i + by) % devices) for i in range(devices)]
    return [pair for i in range(way, devices - 1, 2) for pair in ((i, i + 1), (i + 1, i))]


def served(axis, way):
    if way in ("up", "down"):
        return 0 if way == "up" else 1
    plus = (lax.rem(lax.axis_index(axis), 2) == way).astype(jnp.int32)
    return (2 if axis == "lat" else 4) + plus


def sent(axis, way):
    return 1 - served(axis, way) if axis == "blk" else served(axis, way)


def rows_of(face, rows):
    if isinstance(face, int):
        return pl.ds(face * rows, rows)
    return pl.ds(pl.multiple_of(face * rows, rows), rows)


def put_faces(image_ref, rows, order, face_refs):
    for ref, move in zip(face_refs, moves(order), strict=True):
        ref[...] = image_ref[rows_of(sent(*move), rows), :]


def exchange(faces, order):
    return [
        lax.ppermute(block, axis, route(axis, way))
        for block, (axis, way) in zip(faces, moves(order), strict=True)
    ]


def image_kernel(pair_depth, returned_ref, table_ref, high_ref, low_ref, local_ref, image_ref, sums_ref, *face_refs):
    rows = local_ref.shape[0] // 6
    width = local_ref.shape[1]
    folds = width // LANES
    correction = select(table_ref[...], get_slab(returned_ref, folds))
    image = local_ref[...] + product((high_ref[...], low_ref[...]), parts(correction))
    image_ref[...] = image
    put_faces(image_ref, rows, FIRST, face_refs)
    tail = jnp.sum(returned_ref[:, folds * CAP :, :], axis=0)
    if pair_depth:
        sums_ref[...] = tail
    else:
        sums_ref[...] = jnp.broadcast_to(tail[None], sums_ref.shape)


def with_got(ref, at, got, move):
    return ref[at, :] + got[move][...] if move in got else ref[at, :]


def new_direction(len_ref, beta, image_ref, prev_ref, got, move, rows):
    face = served(*move)
    at = rows_of(face, rows)
    precond = 0.5 * with_got(image_ref, at, got, move)
    return jnp.where(live_rows(len_ref, face, rows), precond + beta * prev_ref[at, :], 0.0)


def near_kernel(pair_depth, scale, keys, len_ref, sums_ref, prev_rho_ref, image_ref, prev_ref, high_ref, low_ref, *refs):
    got, refs = dict(zip(keys, refs)), refs[len(keys) :]
    if pair_depth:
        sums, refs = sums_ref[...] + refs[0][...], refs[1:]
    else:
        sums = jnp.sum(sums_ref[...], axis=0)
    rho_out, beta_out, square_out, near_ref, image_out = refs
    rows = image_ref.shape[0] // 6
    folds = image_ref.shape[1] // LANES
    rho = scale * unfolded(sums, 0, folds)
    beta = rho / prev_rho_ref[...]
    rho_out[...] = rho
    beta_out[...] = beta
    square_out[...] = unfolded(sums, folds, folds)
    for i, move in enumerate(NEAR):
        near_ref[i * rows : (i + 1) * rows, :] = new_direction(
            len_ref, beta, image_ref, prev_ref, got, move, rows
        )
    first = len(NEAR) * rows
    image_out[...] = product((high_ref[:, :first], low_ref[:, :first]), parts(near_ref[...]))


def far_kernel(keys, len_ref, beta_ref, image_ref, prev_ref, high_ref, low_ref, near_ref, near_image_ref, *refs):
    got, refs = dict(zip(keys, refs)), refs[len(keys) :]
    far_ref, schur_out, *face_refs = refs
    rows = image_ref.shape[0] // 6
    beta = beta_ref[...]
    for i, move in enumerate(FAR):
        far_ref[i * rows : (i + 1) * rows, :] = new_direction(
            len_ref, beta, image_ref, prev_ref, got, move, rows
        )
    first = len(NEAR) * rows
    image = near_image_ref[...] + product(
        (high_ref[:, first:], low_ref[:, first:]), parts(far_ref[...])
    )
    schur_out[...] = image
    put_faces(schur_out, rows, SECOND, face_refs)


def store_kernel(near_ref, far_ref, direction_out, sems):
    rows = far_ref.shape[0] // len(FAR)
    copies = []
    for ref, served_moves in ((near_ref, NEAR), (far_ref, FAR)):
        for i, move in enumerate(served_moves):
            copies.append(
                pltpu.make_async_copy(
                    ref.at[pl.ds(i * rows, rows)],
                    direction_out.at[rows_of(served(*move), rows)],
                    sems.at[len(copies)],
                )
            )
    for copy in copies:
        copy.start()
    for copy in copies:
        copy.wait()


def products_kernel(len_ref, near_ref, far_ref, schur_ref, residual_ref, arrived, out_ref):
    rows = schur_ref.shape[0] // 6
    curve = cross = jnp.zeros((1, schur_ref.shape[1]), f32)
    for ref, served_moves in ((near_ref, NEAR), (far_ref, FAR)):
        for i, move in enumerate(served_moves):
            face = served(*move)
            at = rows_of(face, rows)
            image = schur_ref[at, :]
            live = jnp.where(live_rows(len_ref, face, rows), residual_ref[at, :], 0.0)
            direction = ref[i * rows : (i + 1) * rows, :]
            curve += 2.0 * jnp.sum(direction * image, axis=0, keepdims=True)
            cross += 2.0 * jnp.sum(live * image, axis=0, keepdims=True)
    for j, piece in enumerate(folded(curve) + folded(cross)):
        out_ref[j : j + 1, :] = piece


def applied_kernel(pair_depth, len_ref, stored, schur_ref, *refs):
    keys = moves(SECOND)
    got, refs = dict(zip(keys, refs)), refs[len(keys) :]
    products, (applied_ref, spread_ref) = refs[:-2], refs[-2:]
    rows = schur_ref.shape[0] // 6
    folds = schur_ref.shape[1] // LANES
    total = jnp.zeros((1, schur_ref.shape[1]), f32)
    for move in SECOND:
        face = served(*move)
        at = rows_of(face, rows)
        applied = with_got(schur_ref, at, got, move)
        applied = jnp.where(live_rows(len_ref, face, rows), applied, 0.0)
        applied_ref[at, :] = applied
        total += jnp.sum(applied * applied, axis=0, keepdims=True)
    products = sum(ref[...] for ref in products)
    halves = [products[:folds], products[folds : 2 * folds]]
    if pair_depth:
        halves = [jnp.where(lax.axis_index("depth") == 0, *halves)]
    block = jnp.concatenate([*halves, *folded(total)], axis=0)
    spread_ref[...] = jnp.broadcast_to(block[None], spread_ref.shape)


def finish_kernel(pair_depth, scale, len_ref, sums_ref, rho_ref, square_ref, residual_ref, applied_ref, new_out, alpha_ref, norm_ref, new_ref, sems):
    rows = applied_ref.shape[0] // 6
    devices, height, _ = sums_ref.shape
    if pair_depth:
        folds = height // 2
        layers = [jnp.sum(sums_ref[: devices // 2], axis=0), jnp.sum(sums_ref[devices // 2 :], axis=0)]
        curve, cross = [unfolded(layer, 0, folds) for layer in layers]
        applied_square = unfolded(layers[0] + layers[1], folds, folds)
    else:
        folds = height // 3
        total = jnp.sum(sums_ref[...], axis=0)
        curve, cross, applied_square = [unfolded(total, i * folds, folds) for i in range(3)]
    alpha = rho_ref[...] / (scale * curve)
    alpha_ref[...] = alpha
    norm_ref[...] = scale * (
        square_ref[...] - 2.0 * alpha * cross + alpha * alpha * applied_square
    )
    copies = []
    for face in range(6):
        at = slice(face * rows, (face + 1) * rows)
        new_ref[at, :] = masked(len_ref, residual_ref, face, rows) - alpha * applied_ref[at, :]
        where = pl.ds(face * rows, rows)
        copies.append(pltpu.make_async_copy(new_ref.at[where], new_out.at[where], sems.at[face]))
        copies[-1].start()
    for copy in copies:
        copy.wait()


def to_all(x, axes):
    return lax.all_to_all(x, axes, split_axis=0, concat_axis=0, tiled=True)


def shards(
    face_len,
    residual,
    prev_direction,
    prev_rho,
    schur,
    neumann,
    coarse_basis,
    coarse_inverse,
    prim_owner,
    coarse_row,
):
    height, width = residual.shape[3:]
    rows = height // 6
    primal = coarse_basis.shape[4]
    owned = coarse_inverse.shape[3]
    owners = lax.axis_size(LAYER)
    slots = owners * CAP
    devices = lax.axis_size(AXES)
    layers = lax.axis_size("depth")
    pair_depth = layers == 2
    scale = 0.5 / (devices * height)
    folds = width // LANES
    tail = tiles(2 * folds)
    id_tail = tiles(id_rows(slots))

    lengths = face_len.reshape(6)
    residual = residual.reshape(height, width)
    prev_direction = prev_direction.reshape(height, width)
    schur = schur.reshape(height, height)
    neumann = neumann.reshape(height, height)
    basis = coarse_basis.reshape(height, primal)
    inverse = coarse_inverse.reshape(owned, owned)
    owner = prim_owner.reshape(1, primal)
    wanted = coarse_row.reshape(1, primal)
    whole = shape_of(height, width)
    row = shape_of(1, width)
    face = shape_of(rows, width)

    (outgoing,) = call(
        pack_kernel,
        [shape_of(owners, folds * CAP + id_tail, LANES)],
        [lengths, owner, wanted, residual, basis],
        far=range(5),
        flops=6 * height * primal * width,
        moved=4 * (height * (width + primal) + slots * width),
        scratch=[
            pltpu.SMEM((6,), jnp.int32),
            pltpu.VMEM((1, primal), jnp.int32),
            pltpu.VMEM((1, primal), jnp.int32),
            pltpu.VMEM((height, width), f32),
            pltpu.VMEM((height, primal), f32),
            pltpu.SemaphoreType.DMA((3, 2)),
            pltpu.SemaphoreType.DMA((3,)),
        ],
    )
    incoming = to_layer(outgoing)
    local, local_part, square, table, *halves = call(
        local_kernel,
        [whole, row, row, shape_of(primal, slots, dtype=bf16)]
        + [shape_of(height, primal, dtype=bf16)] * 2
        + [shape_of(height, height, dtype=bf16)] * 2,
        [lengths, residual, neumann, owner, basis, schur],
        smem=(0,),
        flops=6 * height * height * width,
        moved=4 * height * (3 * height + 2 * width),
    )
    basis_halves, schur_halves = halves[:2], halves[2:]
    (answers,) = call(
        solve_kernel,
        [shape_of(owners, folds * CAP + tail, LANES)],
        [incoming, inverse, local_part, square],
        far=range(2),
        flops=(8 * slots + 6 * owned) * owned * width,
        moved=8 * slots * width,
        scratch=[
            pltpu.VMEM((owners, id_tail, LANES), f32),
            pltpu.VMEM((owners, folds * CAP, LANES), f32),
            pltpu.VMEM((owned, owned), f32),
            pltpu.SemaphoreType.DMA((4,)),
        ],
    )
    returned = to_layer(answers)
    keys = moves(FIRST)
    faces = [face] * len(keys)
    image, sums, *outward = call(
        functools.partial(image_kernel, pair_depth),
        [whole, shape_of(tail, LANES) if pair_depth else shape_of(layers, tail, LANES), *faces],
        [returned, table, *basis_halves, local],
        flops=(6 * height + 4 * slots) * primal * width,
        moved=16 * height * width,
    )
    got = dict(zip(keys, exchange(outward, FIRST)))
    if pair_depth:
        sums = [sums, lax.ppermute(sums, "depth", route("depth", 0))]
    else:
        sums = [to_all(sums, "depth")]
    near_keys, far_keys = moves(NEAR), moves(FAR)
    rho, beta, square, near, near_image = call(
        functools.partial(near_kernel, pair_depth, scale, near_keys),
        [row, row, row, shape_of(len(NEAR) * rows, width), whole],
        [lengths, sums[0], prev_rho.reshape(1, width), image, prev_direction, *schur_halves]
        + [got[key] for key in near_keys]
        + sums[1:],
        smem=(0,),
        flops=4 * height * height * width,
        moved=4 * height * (height + 4 * width),
    )
    far, schur_image, *outward = call(
        functools.partial(far_kernel, far_keys),
        [shape_of(len(FAR) * rows, width), whole, *faces],
        [lengths, beta, image, prev_direction, *schur_halves, near, near_image]
        + [got[key] for key in far_keys],
        smem=(0,),
        flops=2 * height * height * width,
        moved=4 * height * (height + 4 * width),
    )
    got = exchange(outward, SECOND)
    (products,) = call(
        products_kernel,
        [shape_of(2 * folds, LANES)],
        [lengths, near, far, schur_image, residual, got[0]],
        smem=(0,),
        loose=(5,),
        flops=4 * height * width,
        moved=12 * height * width,
    )
    products = [products]
    if pair_depth:
        products.append(lax.ppermute(products[0], "depth", route("depth", 0)))
    (direction,) = call(
        store_kernel,
        [whole],
        [near, far],
        far_out=(0,),
        moved=8 * height * width,
        scratch=[pltpu.SemaphoreType.DMA((6,))],
    )
    applied, spread_sums = call(
        functools.partial(applied_kernel, pair_depth),
        [whole, shape_of(devices, (2 if pair_depth else 3) * folds, LANES)],
        [lengths, direction, schur_image, *got, *products],
        smem=(0,),
        far=(1,),
        flops=4 * height * width,
        moved=12 * height * width,
    )
    new_residual, alpha, norm = call(
        functools.partial(finish_kernel, pair_depth, scale),
        [whole, row, row],
        [lengths, to_all(spread_sums, AXES), rho, square, residual, applied],
        smem=(0,),
        far_out=(0,),
        flops=4 * height * width,
        moved=12 * height * width,
        scratch=[pltpu.VMEM((height, width), f32), pltpu.SemaphoreType.DMA((6,))],
    )
    out_shape = (1, 1, 1, height, width)
    return (
        new_residual.reshape(out_shape),
        direction.reshape(out_shape),
        rho.reshape(width),
        alpha.reshape(width),
        norm.reshape(width),
    )


def solution(mesh):
    tall = P("blk", "lat", "depth", None, None)
    flat = P("blk", "lat", "depth", None)
    in_specs = (flat, tall, tall, P(), tall, tall, tall, tall, tall, flat)
    out_specs = (tall, tall, P(), P(), P())
    return jax.shard_map(shards, mesh=mesh, in_specs=in_specs, out_specs=out_specs, check_vma=False)
```

```python
import functools

import jax
import jax.numpy as jnp
from jax import lax
from jax.experimental import pallas as pl
from jax.experimental.pallas import tpu as pltpu
from jax.sharding import PartitionSpec as P

CAP = 24
AXES = ("depth", "blk", "lat")
LAYER = ("blk", "lat")
LANES = 128
TILE = 8
f32 = jnp.float32
bf16 = jnp.bfloat16

VMEM = pl.BlockSpec(memory_space=pltpu.VMEM)
SMEM = pl.BlockSpec(memory_space=pltpu.SMEM)
ANY = pl.BlockSpec(memory_space=pl.ANY)


def shape_of(*dims, dtype=f32):
    return jax.ShapeDtypeStruct(dims, dtype)


def call(body, outs, operands, smem=(), far=(), loose=(), far_out=(), flops=0, moved=0, scratch=(), room=32):
    in_specs = [
        SMEM if i in smem else ANY if i in far or i in loose else VMEM
        for i in range(len(operands))
    ]
    operands = [
        pltpu.with_memory_space_constraint(x, pltpu.HBM) if i in far else x
        for i, x in enumerate(operands)
    ]
    out_specs = [ANY if i in far_out else VMEM for i in range(len(outs))]
    return pl.pallas_call(
        body,
        out_shape=list(outs),
        in_specs=in_specs,
        out_specs=out_specs,
        scratch_shapes=list(scratch),
        compiler_params=pltpu.CompilerParams(vmem_limit_bytes=room << 20),
        cost_estimate=pl.CostEstimate(flops=flops, bytes_accessed=moved, transcendentals=0),
    )(*operands)


def parts(x):
    high = x.astype(bf16)
    low = (x - high.astype(f32)).astype(bf16)
    return high, low


def mul(a, b, dims):
    return lax.dot_general(a, b, (dims, ((), ())), preferred_element_type=f32)


PLAIN = ((1,), (0,))


def product(a, b, dims=PLAIN):
    (ah, al), (bh, bl) = a, b
    return mul(ah, bh, dims) + (mul(ah, bl, dims) + mul(al, bh, dims))


def select(table, x, dims=PLAIN):
    high, low = parts(x)
    return mul(table, high, dims) + mul(table, low, dims)


def one_hot(hit):
    return jnp.where(hit, 1.0, 0.0).astype(bf16)


def live_rows(len_ref, face, rows):
    return lax.broadcasted_iota(jnp.int32, (rows, 1), 0) < len_ref[face]


def masked(len_ref, ref, face, rows):
    block = ref[face * rows : (face + 1) * rows, :]
    return jnp.where(live_rows(len_ref, face, rows), block, 0.0)


def folded(vector):
    pieces = vector.shape[1] // LANES
    return [vector[:, j * LANES : (j + 1) * LANES] for j in range(pieces)]


def unfolded(block, first, pieces):
    return jnp.concatenate([block[first + j : first + j + 1, :] for j in range(pieces)], axis=1)


def id_rows(slots):
    return -(-slots // LANES)


def tiles(rows):
    return -(-rows // TILE) * TILE


def put_slab(out_ref, block):
    owners = out_ref.shape[0]
    for j in range(block.shape[1] // LANES):
        piece = block[:, j * LANES : (j + 1) * LANES]
        out_ref[:, j * CAP : (j + 1) * CAP, :] = piece.reshape(owners, CAP, LANES)


def get_slab(ref, pieces, first=0, last=None):
    last = ref.shape[0] if last is None else last
    columns_of = [ref[first:last, j * CAP : (j + 1) * CAP, :] for j in range(pieces)]
    return jnp.concatenate([x.reshape((last - first) * CAP, LANES) for x in columns_of], axis=1)


def columns(*rows):
    spare = [jnp.zeros_like(rows[0])] * (TILE - len(rows))
    turned = jnp.transpose(jnp.concatenate([*rows, *spare], axis=0))
    return [turned[:, i : i + 1] for i in range(len(rows))]


def turn(lat):
    return lat ^ (lat >> 1)


def position(owner):
    lats = lax.axis_size("lat")
    owner = owner.astype(f32)
    lat = owner - lats * jnp.floor((owner + 0.5) * (1.0 / lats))
    for one in range(lats):
        owner = owner + jnp.where(lat == one, float(turn(one) - one), 0.0)
    return owner


def own_position():
    lat = lax.axis_index("lat")
    return lax.axis_index("blk") * lax.axis_size("lat") + turn(lat)


def to_layer(x):
    lats = lax.axis_size("lat")
    order = [
        blk * lats + lat
        for blk in range(lax.axis_size("blk"))
        for lat in sorted(range(lats), key=turn)
    ]
    return lax.all_to_all(x, LAYER, 0, 0, axis_index_groups=[order], tiled=True)


def ranks(own_row):
    primal = own_row.shape[1]
    (own_col,) = columns(own_row)
    row_at = lax.broadcasted_iota(jnp.int32, (primal, primal), 0)
    col_at = lax.broadcasted_iota(jnp.int32, (primal, primal), 1)
    before = (own_row == own_col) & (row_at < col_at)
    return jnp.sum(jnp.where(before, 1.0, 0.0), axis=0, keepdims=True), own_col


def pack_kernel(len_any, owner_any, row_any, residual_any, basis_any, slab_ref, *refs):
    len_ref, owner_ref, row_ref, residual_ref, basis_ref, sems, small_sems = refs
    rows = residual_ref.shape[0] // 6
    primal = basis_ref.shape[1]
    owners = slab_ref.shape[0]
    slots = owners * CAP
    small = [
        pltpu.make_async_copy(src, dst, small_sems.at[i])
        for i, (src, dst) in enumerate(
            [(owner_any, owner_ref), (row_any, row_ref), (len_any, len_ref)]
        )
    ]
    large = []
    for pair in range(3):
        at = pl.ds(2 * pair * rows, 2 * rows)
        large.append(
            (
                pltpu.make_async_copy(residual_any.at[at], residual_ref.at[at], sems.at[pair, 0]),
                pltpu.make_async_copy(basis_any.at[at], basis_ref.at[at], sems.at[pair, 1]),
            )
        )
    for copy in small:
        copy.start()
    for pair in large:
        for copy in pair:
            copy.start()
    for copy in small:
        copy.wait()

    def term_of(*pairs):
        for pair in pairs:
            for copy in large[pair]:
                copy.wait()
        first, last = 2 * pairs[0], 2 * pairs[-1] + 2
        weighted = jnp.concatenate(
            [0.5 * masked(len_ref, residual_ref, face, rows) for face in range(first, last)],
            axis=0,
        )
        basis = basis_ref[first * rows : last * rows, :]
        return product(parts(jnp.transpose(basis)), parts(weighted))

    terms = term_of(0)
    own_row = position(owner_ref[...])
    wanted_row = row_ref[...].astype(f32) + 1.0
    rank_row, _ = ranks(own_row)
    slot_row = (own_row * CAP + rank_row).astype(jnp.int32)
    rank_col, wanted_col = columns(rank_row, wanted_row)
    packer = one_hot(lax.broadcasted_iota(jnp.int32, (slots, primal), 0) == slot_row)
    to_owner = one_hot(
        lax.broadcasted_iota(jnp.int32, (owners, primal), 0) == own_row.astype(jnp.int32)
    )
    at_owner = own_position() * CAP + rank_col.astype(jnp.int32)
    place = lax.broadcasted_iota(jnp.int32, (primal, id_rows(slots) * LANES), 1)
    names = select(to_owner, jnp.where(place == at_owner, wanted_col, 0.0))
    terms += term_of(1, 2)
    put_slab(slab_ref, select(packer, terms))
    tail = slab_ref.shape[1] - tiles(id_rows(slots))
    names = jnp.concatenate(
        [names, jnp.zeros((owners, (slab_ref.shape[1] - tail) * LANES - names.shape[1]), f32)], axis=1
    )
    for j in range(slab_ref.shape[1] - tail):
        slab_ref[:, tail + j, :] = names[:, j * LANES : (j + 1) * LANES]


def local_kernel(len_ref, residual_ref, matrix_ref, owner_ref, *refs):
    whole, refs = refs[:2], refs[2:]
    local_ref, part_ref, square_ref, table_ref, refs = *refs[:4], refs[4:]
    rows = residual_ref.shape[0] // 6
    live = jnp.concatenate(
        [masked(len_ref, residual_ref, face, rows) for face in range(6)], axis=0
    )
    local = product(parts(matrix_ref[...]), parts(0.5 * live))
    local_ref[...] = local
    part_ref[...] = jnp.sum(live * local, axis=0, keepdims=True)
    square_ref[...] = jnp.sum(live * live, axis=0, keepdims=True)
    refs[0][...], refs[1][...] = parts(whole[0][...])
    for i, move in enumerate(NEAR + FAR):
        at = slice(i * rows, (i + 1) * rows)
        refs[2][:, at], refs[3][:, at] = parts(whole[1][:, rows_of(served(*move), rows)])
    primal, slots = table_ref.shape
    rank_row, own_col = ranks(position(owner_ref[...]))
    (rank_col,) = columns(rank_row)
    slot_col = (own_col * CAP + rank_col).astype(jnp.int32)
    table_ref[...] = one_hot(lax.broadcasted_iota(jnp.int32, (primal, slots), 1) == slot_col)


def solve_kernel(incoming_any, inverse_any, local_part_ref, square_ref, answer_ref, *refs):
    names_ref, slab_ref, inverse_ref, sems = refs
    owners, height, _ = slab_ref.shape
    pieces = height // CAP
    slots, owned = owners * CAP, inverse_ref.shape[0]
    cut = 2 * slots // 3 // LANES * LANES
    lead = -(-cut // CAP)
    copies = [
        pltpu.make_async_copy(
            incoming_any.at[:, pl.ds(height, names_ref.shape[1])], names_ref, sems.at[0]
        ),
        pltpu.make_async_copy(
            incoming_any.at[pl.ds(0, lead), pl.ds(0, height)],
            slab_ref.at[pl.ds(0, lead)],
            sems.at[1],
        ),
        pltpu.make_async_copy(
            incoming_any.at[pl.ds(lead, owners - lead), pl.ds(0, height)],
            slab_ref.at[pl.ds(lead, owners - lead)],
            sems.at[2],
        ),
        pltpu.make_async_copy(inverse_any, inverse_ref, sems.at[3]),
    ]
    for copy in copies:
        copy.start()
    copies[0].wait()
    wanted = unfolded(jnp.sum(names_ref[...], axis=0), 0, id_rows(slots))[:, :slots]
    (wanted_col,) = columns(wanted)
    row_at = lax.broadcasted_iota(jnp.int32, (owned, slots), 0).astype(f32) + 1.0
    col_at = lax.broadcasted_iota(jnp.int32, (slots, owned), 1).astype(f32) + 1.0
    gather = one_hot(row_at == wanted)
    table = one_hot(col_at == wanted_col)
    copies[3].wait()
    inverse = parts(inverse_ref[...])
    copies[1].wait()
    head = get_slab(slab_ref, pieces, 0, lead)
    summed = select(gather[:, :cut], head[:cut])
    copies[2].wait()
    rest = jnp.concatenate([head[cut:], get_slab(slab_ref, pieces, lead, owners)], axis=0)
    summed += select(gather[:, cut:], rest)
    solved = product(inverse, parts(summed))
    put_slab(answer_ref, select(table, solved))
    total = local_part_ref[...] + 2.0 * jnp.sum(summed * solved, axis=0, keepdims=True)
    sums = folded(total) + folded(square_ref[...])
    sums += [jnp.zeros((1, LANES), f32)] * (tiles(len(sums)) - len(sums))
    answer_ref[:, pieces * CAP :, :] = jnp.broadcast_to(
        jnp.concatenate(sums, axis=0)[None], (owners, len(sums), LANES)
    )


NEAR = (("blk", "up"), ("lat", 0), ("depth", 0), ("depth", 1))
FAR = (("blk", "down"), ("lat", 1))
FIRST = NEAR + FAR
SECOND = (("blk", "up"), ("lat", 0), ("blk", "down"), ("lat", 1), ("depth", 0), ("depth", 1))


def moves(order):
    return [(axis, way) for axis, way in order if route(axis, way)]


def route(axis, way):
    devices = lax.axis_size(axis)
    if way in ("up", "down"):
        by = 1 if way == "up" else -1
        return [(i, (i + by) % devices) for i in range(devices)]
    return [pair for i in range(way, devices - 1, 2) for pair in ((i, i + 1), (i + 1, i))]


def served(axis, way):
    if way in ("up", "down"):
        return 0 if way == "up" else 1
    plus = (lax.rem(lax.axis_index(axis), 2) == way).astype(jnp.int32)
    return (2 if axis == "lat" else 4) + plus


def sent(axis, way):
    return 1 - served(axis, way) if axis == "blk" else served(axis, way)


def rows_of(face, rows):
    if isinstance(face, int):
        return pl.ds(face * rows, rows)
    return pl.ds(pl.multiple_of(face * rows, rows), rows)


def put_faces(image_ref, rows, order, face_refs):
    for ref, move in zip(face_refs, moves(order), strict=True):
        ref[...] = image_ref[rows_of(sent(*move), rows), :]


def exchange(faces, order):
    return [
        lax.ppermute(block, axis, route(axis, way))
        for block, (axis, way) in zip(faces, moves(order), strict=True)
    ]


def image_kernel(pair_depth, returned_ref, table_ref, high_ref, low_ref, local_ref, image_ref, sums_ref, *face_refs):
    rows = local_ref.shape[0] // 6
    width = local_ref.shape[1]
    folds = width // LANES
    correction = select(table_ref[...], get_slab(returned_ref, folds))
    image = local_ref[...] + product((high_ref[...], low_ref[...]), parts(correction))
    image_ref[...] = image
    put_faces(image_ref, rows, FIRST, face_refs)
    tail = jnp.sum(returned_ref[:, folds * CAP :, :], axis=0)
    if pair_depth:
        sums_ref[...] = tail
    else:
        sums_ref[...] = jnp.broadcast_to(tail[None], sums_ref.shape)


def with_got(ref, at, got, move):
    return ref[at, :] + got[move][...] if move in got else ref[at, :]


def new_direction(len_ref, beta, image_ref, prev_ref, got, move, rows):
    face = served(*move)
    at = rows_of(face, rows)
    precond = 0.5 * with_got(image_ref, at, got, move)
    return jnp.where(live_rows(len_ref, face, rows), precond + beta * prev_ref[at, :], 0.0)


def near_kernel(pair_depth, scale, keys, len_ref, sums_ref, prev_rho_ref, image_ref, prev_ref, high_ref, low_ref, *refs):
    got, refs = dict(zip(keys, refs)), refs[len(keys) :]
    if pair_depth:
        sums, refs = sums_ref[...] + refs[0][...], refs[1:]
    else:
        sums = jnp.sum(sums_ref[...], axis=0)
    rho_out, beta_out, square_out, near_ref, image_out = refs
    rows = image_ref.shape[0] // 6
    folds = image_ref.shape[1] // LANES
    rho = scale * unfolded(sums, 0, folds)
    beta = rho / prev_rho_ref[...]
    rho_out[...] = rho
    beta_out[...] = beta
    square_out[...] = unfolded(sums, folds, folds)
    for i, move in enumerate(NEAR):
        near_ref[i * rows : (i + 1) * rows, :] = new_direction(
            len_ref, beta, image_ref, prev_ref, got, move, rows
        )
    first = len(NEAR) * rows
    image_out[...] = product((high_ref[:, :first], low_ref[:, :first]), parts(near_ref[...]))


def far_kernel(keys, len_ref, beta_ref, image_ref, prev_ref, high_ref, low_ref, near_ref, near_image_ref, *refs):
    got, refs = dict(zip(keys, refs)), refs[len(keys) :]
    far_ref, schur_out, *face_refs = refs
    rows = image_ref.shape[0] // 6
    beta = beta_ref[...]
    for i, move in enumerate(FAR):
        far_ref[i * rows : (i + 1) * rows, :] = new_direction(
            len_ref, beta, image_ref, prev_ref, got, move, rows
        )
    first = len(NEAR) * rows
    image = near_image_ref[...] + product(
        (high_ref[:, first:], low_ref[:, first:]), parts(far_ref[...])
    )
    schur_out[...] = image
    put_faces(schur_out, rows, SECOND, face_refs)


def store_kernel(near_ref, far_ref, direction_out, sems):
    rows = far_ref.shape[0] // len(FAR)
    copies = []
    for ref, served_moves in ((near_ref, NEAR), (far_ref, FAR)):
        for i, move in enumerate(served_moves):
            copies.append(
                pltpu.make_async_copy(
                    ref.at[pl.ds(i * rows, rows)],
                    direction_out.at[rows_of(served(*move), rows)],
                    sems.at[len(copies)],
                )
            )
    for copy in copies:
        copy.start()
    for copy in copies:
        copy.wait()


def products_kernel(len_ref, near_ref, far_ref, schur_ref, residual_ref, arrived, stored, out_ref):
    rows = schur_ref.shape[0] // 6
    curve = cross = jnp.zeros((1, schur_ref.shape[1]), f32)
    for ref, served_moves in ((near_ref, NEAR), (far_ref, FAR)):
        for i, move in enumerate(served_moves):
            face = served(*move)
            at = rows_of(face, rows)
            image = schur_ref[at, :]
            live = jnp.where(live_rows(len_ref, face, rows), residual_ref[at, :], 0.0)
            direction = ref[i * rows : (i + 1) * rows, :]
            curve += 2.0 * jnp.sum(direction * image, axis=0, keepdims=True)
            cross += 2.0 * jnp.sum(live * image, axis=0, keepdims=True)
    for j, piece in enumerate(folded(curve) + folded(cross)):
        out_ref[j : j + 1, :] = piece


def applied_kernel(pair_depth, len_ref, schur_ref, *refs):
    keys = moves(SECOND)
    got, refs = dict(zip(keys, refs)), refs[len(keys) :]
    products, (applied_ref, spread_ref) = refs[:-2], refs[-2:]
    rows = schur_ref.shape[0] // 6
    folds = schur_ref.shape[1] // LANES
    total = jnp.zeros((1, schur_ref.shape[1]), f32)
    for move in SECOND:
        face = served(*move)
        at = rows_of(face, rows)
        applied = with_got(schur_ref, at, got, move)
        applied = jnp.where(live_rows(len_ref, face, rows), applied, 0.0)
        applied_ref[at, :] = applied
        total += jnp.sum(applied * applied, axis=0, keepdims=True)
    products = sum(ref[...] for ref in products)
    halves = [products[:folds], products[folds : 2 * folds]]
    if pair_depth:
        halves = [jnp.where(lax.axis_index("depth") == 0, *halves)]
    block = jnp.concatenate([*halves, *folded(total)], axis=0)
    spread_ref[...] = jnp.broadcast_to(block[None], spread_ref.shape)


def finish_kernel(pair_depth, scale, len_ref, sums_ref, rho_ref, square_ref, residual_ref, applied_ref, new_out, alpha_ref, norm_ref, new_ref, sems):
    rows = applied_ref.shape[0] // 6
    devices, height, _ = sums_ref.shape
    if pair_depth:
        folds = height // 2
        layers = [jnp.sum(sums_ref[: devices // 2], axis=0), jnp.sum(sums_ref[devices // 2 :], axis=0)]
        curve, cross = [unfolded(layer, 0, folds) for layer in layers]
        applied_square = unfolded(layers[0] + layers[1], folds, folds)
    else:
        folds = height // 3
        total = jnp.sum(sums_ref[...], axis=0)
        curve, cross, applied_square = [unfolded(total, i * folds, folds) for i in range(3)]
    alpha = rho_ref[...] / (scale * curve)
    alpha_ref[...] = alpha
    norm_ref[...] = scale * (
        square_ref[...] - 2.0 * alpha * cross + alpha * alpha * applied_square
    )
    copies = []
    for face in range(6):
        at = slice(face * rows, (face + 1) * rows)
        new_ref[at, :] = masked(len_ref, residual_ref, face, rows) - alpha * applied_ref[at, :]
        where = pl.ds(face * rows, rows)
        copies.append(pltpu.make_async_copy(new_ref.at[where], new_out.at[where], sems.at[face]))
        copies[-1].start()
    for copy in copies:
        copy.wait()


def to_all(x, axes):
    return lax.all_to_all(x, axes, split_axis=0, concat_axis=0, tiled=True)


def shards(
    face_len,
    residual,
    prev_direction,
    prev_rho,
    schur,
    neumann,
    coarse_basis,
    coarse_inverse,
    prim_owner,
    coarse_row,
):
    height, width = residual.shape[3:]
    rows = height // 6
    primal = coarse_basis.shape[4]
    owned = coarse_inverse.shape[3]
    owners = lax.axis_size(LAYER)
    slots = owners * CAP
    devices = lax.axis_size(AXES)
    layers = lax.axis_size("depth")
    pair_depth = layers == 2
    scale = 0.5 / (devices * height)
    folds = width // LANES
    tail = tiles(2 * folds)
    id_tail = tiles(id_rows(slots))

    lengths = face_len.reshape(6)
    residual = residual.reshape(height, width)
    prev_direction = prev_direction.reshape(height, width)
    schur = schur.reshape(height, height)
    neumann = neumann.reshape(height, height)
    basis = coarse_basis.reshape(height, primal)
    inverse = coarse_inverse.reshape(owned, owned)
    owner = prim_owner.reshape(1, primal)
    wanted = coarse_row.reshape(1, primal)
    whole = shape_of(height, width)
    row = shape_of(1, width)
    face = shape_of(rows, width)

    (outgoing,) = call(
        pack_kernel,
        [shape_of(owners, folds * CAP + id_tail, LANES)],
        [lengths, owner, wanted, residual, basis],
        far=range(5),
        flops=6 * height * primal * width,
        moved=4 * (height * (width + primal) + slots * width),
        scratch=[
            pltpu.SMEM((6,), jnp.int32),
            pltpu.VMEM((1, primal), jnp.int32),
            pltpu.VMEM((1, primal), jnp.int32),
            pltpu.VMEM((height, width), f32),
            pltpu.VMEM((height, primal), f32),
            pltpu.SemaphoreType.DMA((3, 2)),
            pltpu.SemaphoreType.DMA((3,)),
        ],
    )
    incoming = to_layer(outgoing)
    local, local_part, square, table, *halves = call(
        local_kernel,
        [whole, row, row, shape_of(primal, slots, dtype=bf16)]
        + [shape_of(height, primal, dtype=bf16)] * 2
        + [shape_of(height, height, dtype=bf16)] * 2,
        [lengths, residual, neumann, owner, basis, schur],
        smem=(0,),
        flops=6 * height * height * width,
        moved=4 * height * (3 * height + 2 * width),
    )
    basis_halves, schur_halves = halves[:2], halves[2:]
    (answers,) = call(
        solve_kernel,
        [shape_of(owners, folds * CAP + tail, LANES)],
        [incoming, inverse, local_part, square],
        far=range(2),
        flops=(8 * slots + 6 * owned) * owned * width,
        moved=8 * slots * width,
        scratch=[
            pltpu.VMEM((owners, id_tail, LANES), f32),
            pltpu.VMEM((owners, folds * CAP, LANES), f32),
            pltpu.VMEM((owned, owned), f32),
            pltpu.SemaphoreType.DMA((4,)),
        ],
    )
    returned = to_layer(answers)
    keys = moves(FIRST)
    faces = [face] * len(keys)
    image, sums, *outward = call(
        functools.partial(image_kernel, pair_depth),
        [whole, shape_of(tail, LANES) if pair_depth else shape_of(layers, tail, LANES), *faces],
        [returned, table, *basis_halves, local],
        flops=(6 * height + 4 * slots) * primal * width,
        moved=16 * height * width,
    )
    got = dict(zip(keys, exchange(outward, FIRST)))
    if pair_depth:
        sums = [sums, lax.ppermute(sums, "depth", route("depth", 0))]
    else:
        sums = [to_all(sums, "depth")]
    near_keys, far_keys = moves(NEAR), moves(FAR)
    rho, beta, square, near, near_image = call(
        functools.partial(near_kernel, pair_depth, scale, near_keys),
        [row, row, row, shape_of(len(NEAR) * rows, width), whole],
        [lengths, sums[0], prev_rho.reshape(1, width), image, prev_direction, *schur_halves]
        + [got[key] for key in near_keys]
        + sums[1:],
        smem=(0,),
        flops=4 * height * height * width,
        moved=4 * height * (height + 4 * width),
    )
    far, schur_image, *outward = call(
        functools.partial(far_kernel, far_keys),
        [shape_of(len(FAR) * rows, width), whole, *faces],
        [lengths, beta, image, prev_direction, *schur_halves, near, near_image]
        + [got[key] for key in far_keys],
        smem=(0,),
        flops=2 * height * height * width,
        moved=4 * height * (height + 4 * width),
    )
    got = exchange(outward, SECOND)
    (direction,) = call(
        store_kernel,
        [whole],
        [near, far],
        far_out=(0,),
        moved=8 * height * width,
        scratch=[pltpu.SemaphoreType.DMA((6,))],
    )
    (products,) = call(
        products_kernel,
        [shape_of(2 * folds, LANES)],
        [lengths, near, far, schur_image, residual, got[0], direction],
        smem=(0,),
        loose=(5,),
        far=(6,),
        flops=4 * height * width,
        moved=12 * height * width,
    )
    products = [products]
    if pair_depth:
        products.append(lax.ppermute(products[0], "depth", route("depth", 0)))
    applied, spread_sums = call(
        functools.partial(applied_kernel, pair_depth),
        [whole, shape_of(devices, (2 if pair_depth else 3) * folds, LANES)],
        [lengths, schur_image, *got, *products],
        smem=(0,),
        flops=4 * height * width,
        moved=12 * height * width,
    )
    new_residual, alpha, norm = call(
        functools.partial(finish_kernel, pair_depth, scale),
        [whole, row, row],
        [lengths, to_all(spread_sums, AXES), rho, square, residual, applied],
        smem=(0,),
        far_out=(0,),
        flops=4 * height * width,
        moved=12 * height * width,
        scratch=[pltpu.VMEM((height, width), f32), pltpu.SemaphoreType.DMA((6,))],
    )
    out_shape = (1, 1, 1, height, width)
    return (
        new_residual.reshape(out_shape),
        direction.reshape(out_shape),
        rho.reshape(width),
        alpha.reshape(width),
        norm.reshape(width),
    )


def solution(mesh):
    tall = P("blk", "lat", "depth", None, None)
    flat = P("blk", "lat", "depth", None)
    in_specs = (flat, tall, tall, P(), tall, tall, tall, tall, tall, flat)
    out_specs = (tall, tall, P(), P(), P())
    return jax.shard_map(shards, mesh=mesh, in_specs=in_specs, out_specs=out_specs, check_vma=False)
```

```python
import functools

import jax
import jax.numpy as jnp
from jax import lax
from jax.experimental import pallas as pl
from jax.experimental.pallas import tpu as pltpu
from jax.sharding import PartitionSpec as P

CAP = 24
AXES = ("depth", "blk", "lat")
LAYER = ("blk", "lat")
LANES = 128
TILE = 8
f32 = jnp.float32
bf16 = jnp.bfloat16

VMEM = pl.BlockSpec(memory_space=pltpu.VMEM)
SMEM = pl.BlockSpec(memory_space=pltpu.SMEM)
ANY = pl.BlockSpec(memory_space=pl.ANY)


def shape_of(*dims, dtype=f32):
    return jax.ShapeDtypeStruct(dims, dtype)


def call(body, outs, operands, smem=(), far=(), loose=(), far_out=(), flops=0, moved=0, scratch=(), room=32):
    in_specs = [
        SMEM if i in smem else ANY if i in far or i in loose else VMEM
        for i in range(len(operands))
    ]
    operands = [
        pltpu.with_memory_space_constraint(x, pltpu.HBM) if i in far else x
        for i, x in enumerate(operands)
    ]
    out_specs = [ANY if i in far_out else VMEM for i in range(len(outs))]
    return pl.pallas_call(
        body,
        out_shape=list(outs),
        in_specs=in_specs,
        out_specs=out_specs,
        scratch_shapes=list(scratch),
        compiler_params=pltpu.CompilerParams(vmem_limit_bytes=room << 20),
        cost_estimate=pl.CostEstimate(flops=flops, bytes_accessed=moved, transcendentals=0),
    )(*operands)


def parts(x):
    high = x.astype(bf16)
    low = (x - high.astype(f32)).astype(bf16)
    return high, low


def mul(a, b, dims):
    return lax.dot_general(a, b, (dims, ((), ())), preferred_element_type=f32)


PLAIN = ((1,), (0,))


def product(a, b, dims=PLAIN):
    (ah, al), (bh, bl) = a, b
    return mul(ah, bh, dims) + (mul(ah, bl, dims) + mul(al, bh, dims))


def select(table, x, dims=PLAIN):
    high, low = parts(x)
    return mul(table, high, dims) + mul(table, low, dims)


def one_hot(hit):
    return jnp.where(hit, 1.0, 0.0).astype(bf16)


def live_rows(len_ref, face, rows):
    return lax.broadcasted_iota(jnp.int32, (rows, 1), 0) < len_ref[face]


def masked(len_ref, ref, face, rows):
    block = ref[face * rows : (face + 1) * rows, :]
    return jnp.where(live_rows(len_ref, face, rows), block, 0.0)


def folded(vector):
    pieces = vector.shape[1] // LANES
    return [vector[:, j * LANES : (j + 1) * LANES] for j in range(pieces)]


def unfolded(block, first, pieces):
    return jnp.concatenate([block[first + j : first + j + 1, :] for j in range(pieces)], axis=1)


def id_rows(slots):
    return -(-slots // LANES)


def tiles(rows):
    return -(-rows // TILE) * TILE


def put_slab(out_ref, block):
    owners = out_ref.shape[0]
    for j in range(block.shape[1] // LANES):
        piece = block[:, j * LANES : (j + 1) * LANES]
        out_ref[:, j * CAP : (j + 1) * CAP, :] = piece.reshape(owners, CAP, LANES)


def get_slab(ref, pieces, first=0, last=None):
    last = ref.shape[0] if last is None else last
    columns_of = [ref[first:last, j * CAP : (j + 1) * CAP, :] for j in range(pieces)]
    return jnp.concatenate([x.reshape((last - first) * CAP, LANES) for x in columns_of], axis=1)


def columns(*rows):
    spare = [jnp.zeros_like(rows[0])] * (TILE - len(rows))
    turned = jnp.transpose(jnp.concatenate([*rows, *spare], axis=0))
    return [turned[:, i : i + 1] for i in range(len(rows))]


def ranks(own_row):
    primal = own_row.shape[1]
    (own_col,) = columns(own_row)
    row_at = lax.broadcasted_iota(jnp.int32, (primal, primal), 0)
    col_at = lax.broadcasted_iota(jnp.int32, (primal, primal), 1)
    before = (own_row == own_col) & (row_at < col_at)
    return jnp.sum(jnp.where(before, 1.0, 0.0), axis=0, keepdims=True), own_col


def pack_kernel(len_any, owner_any, row_any, residual_any, basis_any, slab_ref, *refs):
    len_ref, owner_ref, row_ref, residual_ref, basis_ref, sems, small_sems = refs
    rows = residual_ref.shape[0] // 6
    primal = basis_ref.shape[1]
    owners = slab_ref.shape[0]
    slots = owners * CAP
    small = [
        pltpu.make_async_copy(src, dst, small_sems.at[i])
        for i, (src, dst) in enumerate(
            [(len_any, len_ref), (owner_any, owner_ref), (row_any, row_ref)]
        )
    ]
    large = []
    for pair in range(3):
        at = pl.ds(2 * pair * rows, 2 * rows)
        large.append(
            (
                pltpu.make_async_copy(residual_any.at[at], residual_ref.at[at], sems.at[pair, 0]),
                pltpu.make_async_copy(basis_any.at[at], basis_ref.at[at], sems.at[pair, 1]),
            )
        )
    for copy in [small[0], *large[0], *small[1:], *large[1], *large[2]]:
        copy.start()
    small[0].wait()

    def term_of(*pairs):
        for pair in pairs:
            for copy in large[pair]:
                copy.wait()
        first, last = 2 * pairs[0], 2 * pairs[-1] + 2
        weighted = jnp.concatenate(
            [0.5 * masked(len_ref, residual_ref, face, rows) for face in range(first, last)],
            axis=0,
        )
        basis = basis_ref[first * rows : last * rows, :]
        return product(parts(jnp.transpose(basis)), parts(weighted))

    terms = term_of(0)
    for copy in small[1:]:
        copy.wait()
    own_row = owner_ref[...].astype(f32)
    wanted_row = row_ref[...].astype(f32) + 1.0
    rank_row, _ = ranks(own_row)
    slot_row = (own_row * CAP + rank_row).astype(jnp.int32)
    rank_col, wanted_col = columns(rank_row, wanted_row)
    packer = one_hot(lax.broadcasted_iota(jnp.int32, (slots, primal), 0) == slot_row)
    to_owner = one_hot(lax.broadcasted_iota(jnp.int32, (owners, primal), 0) == owner_ref[...])
    at_owner = lax.axis_index(LAYER) * CAP + rank_col.astype(jnp.int32)
    place = lax.broadcasted_iota(jnp.int32, (primal, id_rows(slots) * LANES), 1)
    names = select(to_owner, jnp.where(place == at_owner, wanted_col, 0.0))
    terms += term_of(1, 2)
    put_slab(slab_ref, select(packer, terms))
    tail = slab_ref.shape[1] - tiles(id_rows(slots))
    names = jnp.concatenate(
        [names, jnp.zeros((owners, (slab_ref.shape[1] - tail) * LANES - names.shape[1]), f32)], axis=1
    )
    for j in range(slab_ref.shape[1] - tail):
        slab_ref[:, tail + j, :] = names[:, j * LANES : (j + 1) * LANES]


def local_kernel(len_ref, residual_ref, matrix_ref, owner_ref, *refs):
    whole, refs = refs[:2], refs[2:]
    local_ref, part_ref, square_ref, table_ref, refs = *refs[:4], refs[4:]
    rows = residual_ref.shape[0] // 6
    live = jnp.concatenate(
        [masked(len_ref, residual_ref, face, rows) for face in range(6)], axis=0
    )
    local = product(parts(matrix_ref[...]), parts(0.5 * live))
    local_ref[...] = local
    part_ref[...] = jnp.sum(live * local, axis=0, keepdims=True)
    square_ref[...] = jnp.sum(live * live, axis=0, keepdims=True)
    refs[0][...], refs[1][...] = parts(whole[0][...])
    for i, move in enumerate(NEAR + FAR):
        at = slice(i * rows, (i + 1) * rows)
        refs[2][:, at], refs[3][:, at] = parts(whole[1][:, rows_of(served(*move), rows)])
    primal, slots = table_ref.shape
    rank_row, own_col = ranks(owner_ref[...].astype(f32))
    (rank_col,) = columns(rank_row)
    slot_col = (own_col * CAP + rank_col).astype(jnp.int32)
    table_ref[...] = one_hot(lax.broadcasted_iota(jnp.int32, (primal, slots), 1) == slot_col)


def solve_kernel(incoming_any, inverse_any, local_part_ref, square_ref, answer_ref, *refs):
    names_ref, slab_ref, inverse_ref, sems = refs
    owners, height, _ = slab_ref.shape
    pieces = height // CAP
    slots, owned = owners * CAP, inverse_ref.shape[0]
    cut = 2 * slots // 3 // LANES * LANES
    lead = -(-cut // CAP)
    copies = [
        pltpu.make_async_copy(
            incoming_any.at[:, pl.ds(height, names_ref.shape[1])], names_ref, sems.at[0]
        ),
        pltpu.make_async_copy(
            incoming_any.at[pl.ds(0, lead), pl.ds(0, height)],
            slab_ref.at[pl.ds(0, lead)],
            sems.at[1],
        ),
        pltpu.make_async_copy(
            incoming_any.at[pl.ds(lead, owners - lead), pl.ds(0, height)],
            slab_ref.at[pl.ds(lead, owners - lead)],
            sems.at[2],
        ),
        pltpu.make_async_copy(inverse_any, inverse_ref, sems.at[3]),
    ]
    for copy in copies:
        copy.start()
    copies[0].wait()
    wanted = unfolded(jnp.sum(names_ref[...], axis=0), 0, id_rows(slots))[:, :slots]
    (wanted_col,) = columns(wanted)
    row_at = lax.broadcasted_iota(jnp.int32, (owned, slots), 0).astype(f32) + 1.0
    col_at = lax.broadcasted_iota(jnp.int32, (slots, owned), 1).astype(f32) + 1.0
    gather = one_hot(row_at == wanted)
    table = one_hot(col_at == wanted_col)
    copies[3].wait()
    inverse = parts(inverse_ref[...])
    copies[1].wait()
    head = get_slab(slab_ref, pieces, 0, lead)
    summed = select(gather[:, :cut], head[:cut])
    copies[2].wait()
    rest = jnp.concatenate([head[cut:], get_slab(slab_ref, pieces, lead, owners)], axis=0)
    summed += select(gather[:, cut:], rest)
    solved = product(inverse, parts(summed))
    put_slab(answer_ref, select(table, solved))
    total = local_part_ref[...] + 2.0 * jnp.sum(summed * solved, axis=0, keepdims=True)
    sums = folded(total) + folded(square_ref[...])
    sums += [jnp.zeros((1, LANES), f32)] * (tiles(len(sums)) - len(sums))
    answer_ref[:, pieces * CAP :, :] = jnp.broadcast_to(
        jnp.concatenate(sums, axis=0)[None], (owners, len(sums), LANES)
    )


NEAR = (("blk", "up"), ("lat", 0), ("depth", 0), ("depth", 1))
FAR = (("blk", "down"), ("lat", 1))
FIRST = NEAR + FAR
SECOND = (("blk", "up"), ("lat", 0), ("blk", "down"), ("lat", 1), ("depth", 0), ("depth", 1))


def moves(order):
    return [(axis, way) for axis, way in order if route(axis, way)]


def route(axis, way):
    devices = lax.axis_size(axis)
    if way in ("up", "down"):
        by = 1 if way == "up" else -1
        return [(i, (i + by) % devices) for i in range(devices)]
    return [pair for i in range(way, devices - 1, 2) for pair in ((i, i + 1), (i + 1, i))]


def served(axis, way):
    if way in ("up", "down"):
        return 0 if way == "up" else 1
    plus = (lax.rem(lax.axis_index(axis), 2) == way).astype(jnp.int32)
    return (2 if axis == "lat" else 4) + plus


def sent(axis, way):
    return 1 - served(axis, way) if axis == "blk" else served(axis, way)


def rows_of(face, rows):
    if isinstance(face, int):
        return pl.ds(face * rows, rows)
    return pl.ds(pl.multiple_of(face * rows, rows), rows)


def put_faces(image_ref, rows, order, face_refs):
    for ref, move in zip(face_refs, moves(order), strict=True):
        ref[...] = image_ref[rows_of(sent(*move), rows), :]


def exchange(faces, order):
    return [
        lax.ppermute(block, axis, route(axis, way))
        for block, (axis, way) in zip(faces, moves(order), strict=True)
    ]


def image_kernel(pair_depth, returned_ref, table_ref, high_ref, low_ref, local_ref, image_ref, sums_ref, *face_refs):
    rows = local_ref.shape[0] // 6
    width = local_ref.shape[1]
    folds = width // LANES
    correction = select(table_ref[...], get_slab(returned_ref, folds))
    image = local_ref[...] + product((high_ref[...], low_ref[...]), parts(correction))
    image_ref[...] = image
    put_faces(image_ref, rows, FIRST, face_refs)
    tail = jnp.sum(returned_ref[:, folds * CAP :, :], axis=0)
    if pair_depth:
        sums_ref[...] = tail
    else:
        sums_ref[...] = jnp.broadcast_to(tail[None], sums_ref.shape)


def with_got(ref, at, got, move):
    return ref[at, :] + got[move][...] if move in got else ref[at, :]


def new_direction(len_ref, beta, image_ref, prev_ref, got, move, rows):
    face = served(*move)
    at = rows_of(face, rows)
    precond = 0.5 * with_got(image_ref, at, got, move)
    return jnp.where(live_rows(len_ref, face, rows), precond + beta * prev_ref[at, :], 0.0)


def near_kernel(pair_depth, scale, keys, len_ref, sums_ref, prev_rho_ref, image_ref, prev_ref, high_ref, low_ref, *refs):
    got, refs = dict(zip(keys, refs)), refs[len(keys) :]
    if pair_depth:
        sums, refs = sums_ref[...] + refs[0][...], refs[1:]
    else:
        sums = jnp.sum(sums_ref[...], axis=0)
    rho_out, beta_out, square_out, near_ref, image_out = refs
    rows = image_ref.shape[0] // 6
    folds = image_ref.shape[1] // LANES
    rho = scale * unfolded(sums, 0, folds)
    beta = rho / prev_rho_ref[...]
    rho_out[...] = rho
    beta_out[...] = beta
    square_out[...] = unfolded(sums, folds, folds)
    for i, move in enumerate(NEAR):
        near_ref[i * rows : (i + 1) * rows, :] = new_direction(
            len_ref, beta, image_ref, prev_ref, got, move, rows
        )
    first = len(NEAR) * rows
    image_out[...] = product((high_ref[:, :first], low_ref[:, :first]), parts(near_ref[...]))


def far_kernel(keys, len_ref, beta_ref, image_ref, prev_ref, high_ref, low_ref, near_ref, near_image_ref, *refs):
    got, refs = dict(zip(keys, refs)), refs[len(keys) :]
    far_ref, schur_out, *face_refs = refs
    rows = image_ref.shape[0] // 6
    beta = beta_ref[...]
    for i, move in enumerate(FAR):
        far_ref[i * rows : (i + 1) * rows, :] = new_direction(
            len_ref, beta, image_ref, prev_ref, got, move, rows
        )
    first = len(NEAR) * rows
    image = near_image_ref[...] + product(
        (high_ref[:, first:], low_ref[:, first:]), parts(far_ref[...])
    )
    schur_out[...] = image
    put_faces(schur_out, rows, SECOND, face_refs)


def store_kernel(near_ref, far_ref, direction_out, sems):
    rows = far_ref.shape[0] // len(FAR)
    copies = []
    for ref, served_moves in ((near_ref, NEAR), (far_ref, FAR)):
        for i, move in enumerate(served_moves):
            copies.append(
                pltpu.make_async_copy(
                    ref.at[pl.ds(i * rows, rows)],
                    direction_out.at[rows_of(served(*move), rows)],
                    sems.at[len(copies)],
                )
            )
    for copy in copies:
        copy.start()
    for copy in copies:
        copy.wait()


def products_kernel(len_ref, near_ref, far_ref, schur_ref, residual_ref, arrived, stored, out_ref):
    rows = schur_ref.shape[0] // 6
    curve = cross = jnp.zeros((1, schur_ref.shape[1]), f32)
    for ref, served_moves in ((near_ref, NEAR), (far_ref, FAR)):
        for i, move in enumerate(served_moves):
            face = served(*move)
            at = rows_of(face, rows)
            image = schur_ref[at, :]
            live = jnp.where(live_rows(len_ref, face, rows), residual_ref[at, :], 0.0)
            direction = ref[i * rows : (i + 1) * rows, :]
            curve += 2.0 * jnp.sum(direction * image, axis=0, keepdims=True)
            cross += 2.0 * jnp.sum(live * image, axis=0, keepdims=True)
    for j, piece in enumerate(folded(curve) + folded(cross)):
        out_ref[j : j + 1, :] = piece


def applied_kernel(pair_depth, len_ref, schur_ref, *refs):
    keys = moves(SECOND)
    got, refs = dict(zip(keys, refs)), refs[len(keys) :]
    products, (applied_ref, spread_ref) = refs[:-2], refs[-2:]
    rows = schur_ref.shape[0] // 6
    folds = schur_ref.shape[1] // LANES
    total = jnp.zeros((1, schur_ref.shape[1]), f32)
    for move in SECOND:
        face = served(*move)
        at = rows_of(face, rows)
        applied = with_got(schur_ref, at, got, move)
        applied = jnp.where(live_rows(len_ref, face, rows), applied, 0.0)
        applied_ref[at, :] = applied
        total += jnp.sum(applied * applied, axis=0, keepdims=True)
    products = sum(ref[...] for ref in products)
    halves = [products[:folds], products[folds : 2 * folds]]
    if pair_depth:
        halves = [jnp.where(lax.axis_index("depth") == 0, *halves)]
    block = jnp.concatenate([*halves, *folded(total)], axis=0)
    spread_ref[...] = jnp.broadcast_to(block[None], spread_ref.shape)


def finish_kernel(pair_depth, scale, len_ref, sums_ref, rho_ref, square_ref, residual_ref, applied_ref, new_out, alpha_ref, norm_ref, new_ref, sems):
    rows = applied_ref.shape[0] // 6
    devices, height, _ = sums_ref.shape
    if pair_depth:
        folds = height // 2
        layers = [jnp.sum(sums_ref[: devices // 2], axis=0), jnp.sum(sums_ref[devices // 2 :], axis=0)]
        curve, cross = [unfolded(layer, 0, folds) for layer in layers]
        applied_square = unfolded(layers[0] + layers[1], folds, folds)
    else:
        folds = height // 3
        total = jnp.sum(sums_ref[...], axis=0)
        curve, cross, applied_square = [unfolded(total, i * folds, folds) for i in range(3)]
    alpha = rho_ref[...] / (scale * curve)
    alpha_ref[...] = alpha
    norm_ref[...] = scale * (
        square_ref[...] - 2.0 * alpha * cross + alpha * alpha * applied_square
    )
    copies = []
    for face in range(6):
        at = slice(face * rows, (face + 1) * rows)
        new_ref[at, :] = masked(len_ref, residual_ref, face, rows) - alpha * applied_ref[at, :]
        where = pl.ds(face * rows, rows)
        copies.append(pltpu.make_async_copy(new_ref.at[where], new_out.at[where], sems.at[face]))
        copies[-1].start()
    for copy in copies:
        copy.wait()


def to_all(x, axes):
    return lax.all_to_all(x, axes, split_axis=0, concat_axis=0, tiled=True)


def shards(
    face_len,
    residual,
    prev_direction,
    prev_rho,
    schur,
    neumann,
    coarse_basis,
    coarse_inverse,
    prim_owner,
    coarse_row,
):
    height, width = residual.shape[3:]
    rows = height // 6
    primal = coarse_basis.shape[4]
    owned = coarse_inverse.shape[3]
    owners = lax.axis_size(LAYER)
    slots = owners * CAP
    devices = lax.axis_size(AXES)
    layers = lax.axis_size("depth")
    pair_depth = layers == 2
    scale = 0.5 / (devices * height)
    folds = width // LANES
    tail = tiles(2 * folds)
    id_tail = tiles(id_rows(slots))

    lengths = face_len.reshape(6)
    residual = residual.reshape(height, width)
    prev_direction = prev_direction.reshape(height, width)
    schur = schur.reshape(height, height)
    neumann = neumann.reshape(height, height)
    basis = coarse_basis.reshape(height, primal)
    inverse = coarse_inverse.reshape(owned, owned)
    owner = prim_owner.reshape(1, primal)
    wanted = coarse_row.reshape(1, primal)
    whole = shape_of(height, width)
    row = shape_of(1, width)
    face = shape_of(rows, width)

    (outgoing,) = call(
        pack_kernel,
        [shape_of(owners, folds * CAP + id_tail, LANES)],
        [lengths, owner, wanted, residual, basis],
        far=range(5),
        flops=6 * height * primal * width,
        moved=4 * (height * (width + primal) + slots * width),
        scratch=[
            pltpu.SMEM((6,), jnp.int32),
            pltpu.VMEM((1, primal), jnp.int32),
            pltpu.VMEM((1, primal), jnp.int32),
            pltpu.VMEM((height, width), f32),
            pltpu.VMEM((height, primal), f32),
            pltpu.SemaphoreType.DMA((3, 2)),
            pltpu.SemaphoreType.DMA((3,)),
        ],
    )
    incoming = to_all(outgoing, LAYER)
    local, local_part, square, table, *halves = call(
        local_kernel,
        [whole, row, row, shape_of(primal, slots, dtype=bf16)]
        + [shape_of(height, primal, dtype=bf16)] * 2
        + [shape_of(height, height, dtype=bf16)] * 2,
        [lengths, residual, neumann, owner, basis, schur],
        smem=(0,),
        flops=6 * height * height * width,
        moved=4 * height * (3 * height + 2 * width),
    )
    basis_halves, schur_halves = halves[:2], halves[2:]
    (answers,) = call(
        solve_kernel,
        [shape_of(owners, folds * CAP + tail, LANES)],
        [incoming, inverse, local_part, square],
        far=range(2),
        flops=(8 * slots + 6 * owned) * owned * width,
        moved=8 * slots * width,
        scratch=[
            pltpu.VMEM((owners, id_tail, LANES), f32),
            pltpu.VMEM((owners, folds * CAP, LANES), f32),
            pltpu.VMEM((owned, owned), f32),
            pltpu.SemaphoreType.DMA((4,)),
        ],
    )
    returned = to_all(answers, LAYER)
    keys = moves(FIRST)
    faces = [face] * len(keys)
    image, sums, *outward = call(
        functools.partial(image_kernel, pair_depth),
        [whole, shape_of(tail, LANES) if pair_depth else shape_of(layers, tail, LANES), *faces],
        [returned, table, *basis_halves, local],
        flops=(6 * height + 4 * slots) * primal * width,
        moved=16 * height * width,
    )
    got = dict(zip(keys, exchange(outward, FIRST)))
    if pair_depth:
        sums = [sums, lax.ppermute(sums, "depth", route("depth", 0))]
    else:
        sums = [to_all(sums, "depth")]
    near_keys, far_keys = moves(NEAR), moves(FAR)
    rho, beta, square, near, near_image = call(
        functools.partial(near_kernel, pair_depth, scale, near_keys),
        [row, row, row, shape_of(len(NEAR) * rows, width), whole],
        [lengths, sums[0], prev_rho.reshape(1, width), image, prev_direction, *schur_halves]
        + [got[key] for key in near_keys]
        + sums[1:],
        smem=(0,),
        flops=4 * height * height * width,
        moved=4 * height * (height + 4 * width),
    )
    far, schur_image, *outward = call(
        functools.partial(far_kernel, far_keys),
        [shape_of(len(FAR) * rows, width), whole, *faces],
        [lengths, beta, image, prev_direction, *schur_halves, near, near_image]
        + [got[key] for key in far_keys],
        smem=(0,),
        flops=2 * height * height * width,
        moved=4 * height * (height + 4 * width),
    )
    got = exchange(outward, SECOND)
    (direction,) = call(
        store_kernel,
        [whole],
        [near, far],
        far_out=(0,),
        moved=8 * height * width,
        scratch=[pltpu.SemaphoreType.DMA((6,))],
    )
    (products,) = call(
        products_kernel,
        [shape_of(2 * folds, LANES)],
        [lengths, near, far, schur_image, residual, got[0], direction],
        smem=(0,),
        loose=(5,),
        far=(6,),
        flops=4 * height * width,
        moved=12 * height * width,
    )
    products = [products]
    if pair_depth:
        products.append(lax.ppermute(products[0], "depth", route("depth", 0)))
    applied, spread_sums = call(
        functools.partial(applied_kernel, pair_depth),
        [whole, shape_of(devices, (2 if pair_depth else 3) * folds, LANES)],
        [lengths, schur_image, *got, *products],
        smem=(0,),
        flops=4 * height * width,
        moved=12 * height * width,
    )
    new_residual, alpha, norm = call(
        functools.partial(finish_kernel, pair_depth, scale),
        [whole, row, row],
        [lengths, to_all(spread_sums, AXES), rho, square, residual, applied],
        smem=(0,),
        far_out=(0,),
        flops=4 * height * width,
        moved=12 * height * width,
        scratch=[pltpu.VMEM((height, width), f32), pltpu.SemaphoreType.DMA((6,))],
    )
    out_shape = (1, 1, 1, height, width)
    return (
        new_residual.reshape(out_shape),
        direction.reshape(out_shape),
        rho.reshape(width),
        alpha.reshape(width),
        norm.reshape(width),
    )


def solution(mesh):
    tall = P("blk", "lat", "depth", None, None)
    flat = P("blk", "lat", "depth", None)
    in_specs = (flat, tall, tall, P(), tall, tall, tall, tall, tall, flat)
    out_specs = (tall, tall, P(), P(), P())
    return jax.shard_map(shards, mesh=mesh, in_specs=in_specs, out_specs=out_specs, check_vma=False)
```

```python
import functools

import jax
import jax.numpy as jnp
from jax import lax
from jax.experimental import pallas as pl
from jax.experimental.pallas import tpu as pltpu
from jax.sharding import PartitionSpec as P

CAP = 24
AXES = ("depth", "blk", "lat")
LAYER = ("blk", "lat")
LANES = 128
TILE = 8
f32 = jnp.float32
bf16 = jnp.bfloat16

VMEM = pl.BlockSpec(memory_space=pltpu.VMEM)
SMEM = pl.BlockSpec(memory_space=pltpu.SMEM)
ANY = pl.BlockSpec(memory_space=pl.ANY)


def shape_of(*dims, dtype=f32):
    return jax.ShapeDtypeStruct(dims, dtype)


def call(body, outs, operands, smem=(), far=(), loose=(), far_out=(), flops=0, moved=0, scratch=(), room=32):
    in_specs = [
        SMEM if i in smem else ANY if i in far or i in loose else VMEM
        for i in range(len(operands))
    ]
    operands = [
        pltpu.with_memory_space_constraint(x, pltpu.HBM) if i in far else x
        for i, x in enumerate(operands)
    ]
    out_specs = [ANY if i in far_out else VMEM for i in range(len(outs))]
    return pl.pallas_call(
        body,
        out_shape=list(outs),
        in_specs=in_specs,
        out_specs=out_specs,
        scratch_shapes=list(scratch),
        compiler_params=pltpu.CompilerParams(vmem_limit_bytes=room << 20),
        cost_estimate=pl.CostEstimate(flops=flops, bytes_accessed=moved, transcendentals=0),
    )(*operands)


def parts(x):
    high = x.astype(bf16)
    low = (x - high.astype(f32)).astype(bf16)
    return high, low


def mul(a, b, dims):
    return lax.dot_general(a, b, (dims, ((), ())), preferred_element_type=f32)


PLAIN = ((1,), (0,))


def product(a, b, dims=PLAIN):
    (ah, al), (bh, bl) = a, b
    return mul(ah, bh, dims) + (mul(ah, bl, dims) + mul(al, bh, dims))


def select(table, x, dims=PLAIN):
    high, low = parts(x)
    return mul(table, high, dims) + mul(table, low, dims)


def one_hot(hit):
    return jnp.where(hit, 1.0, 0.0).astype(bf16)


def live_rows(len_ref, face, rows):
    return lax.broadcasted_iota(jnp.int32, (rows, 1), 0) < len_ref[face]


def masked(len_ref, ref, face, rows):
    block = ref[face * rows : (face + 1) * rows, :]
    return jnp.where(live_rows(len_ref, face, rows), block, 0.0)


def folded(vector):
    pieces = vector.shape[1] // LANES
    return [vector[:, j * LANES : (j + 1) * LANES] for j in range(pieces)]


def unfolded(block, first, pieces):
    return jnp.concatenate([block[first + j : first + j + 1, :] for j in range(pieces)], axis=1)


def id_rows(slots):
    return -(-slots // LANES)


def tiles(rows):
    return -(-rows // TILE) * TILE


def put_slab(out_ref, block):
    owners = out_ref.shape[0]
    for j in range(block.shape[1] // LANES):
        piece = block[:, j * LANES : (j + 1) * LANES]
        out_ref[:, j * CAP : (j + 1) * CAP, :] = piece.reshape(owners, CAP, LANES)


def get_slab(ref, pieces, first=0, last=None):
    last = ref.shape[0] if last is None else last
    columns_of = [ref[first:last, j * CAP : (j + 1) * CAP, :] for j in range(pieces)]
    return jnp.concatenate([x.reshape((last - first) * CAP, LANES) for x in columns_of], axis=1)


def columns(*rows):
    spare = [jnp.zeros_like(rows[0])] * (TILE - len(rows))
    turned = jnp.transpose(jnp.concatenate([*rows, *spare], axis=0))
    return [turned[:, i : i + 1] for i in range(len(rows))]


def turn(lat):
    return lat ^ (lat >> 1)


def position(owner):
    lats = lax.axis_size("lat")
    owner = owner.astype(f32)
    lat = owner - lats * jnp.floor((owner + 0.5) * (1.0 / lats))
    for one in range(lats):
        owner = owner + jnp.where(lat == one, float(turn(one) - one), 0.0)
    return owner


def own_position():
    lat = lax.axis_index("lat")
    return lax.axis_index("blk") * lax.axis_size("lat") + turn(lat)


def to_layer(x):
    lats = lax.axis_size("lat")
    order = [
        blk * lats + lat
        for blk in range(lax.axis_size("blk"))
        for lat in sorted(range(lats), key=turn)
    ]
    return lax.all_to_all(x, LAYER, 0, 0, axis_index_groups=[order], tiled=True)


def ranks(own_row):
    primal = own_row.shape[1]
    (own_col,) = columns(own_row)
    row_at = lax.broadcasted_iota(jnp.int32, (primal, primal), 0)
    col_at = lax.broadcasted_iota(jnp.int32, (primal, primal), 1)
    before = (own_row == own_col) & (row_at < col_at)
    return jnp.sum(jnp.where(before, 1.0, 0.0), axis=0, keepdims=True), own_col


def pack_kernel(len_any, owner_any, row_any, residual_any, basis_any, slab_ref, *refs):
    len_ref, owner_ref, row_ref, residual_ref, basis_ref, sems, small_sems = refs
    rows = residual_ref.shape[0] // 6
    primal = basis_ref.shape[1]
    owners = slab_ref.shape[0]
    slots = owners * CAP
    small = [
        pltpu.make_async_copy(src, dst, small_sems.at[i])
        for i, (src, dst) in enumerate(
            [(owner_any, owner_ref), (row_any, row_ref), (len_any, len_ref)]
        )
    ]
    large = []
    for pair in range(3):
        at = pl.ds(2 * pair * rows, 2 * rows)
        large.append(
            (
                pltpu.make_async_copy(residual_any.at[at], residual_ref.at[at], sems.at[pair, 0]),
                pltpu.make_async_copy(basis_any.at[at], basis_ref.at[at], sems.at[pair, 1]),
            )
        )
    for copy in small:
        copy.start()
    for pair in large:
        for copy in pair:
            copy.start()
    for copy in small:
        copy.wait()

    def term_of(*pairs):
        for pair in pairs:
            for copy in large[pair]:
                copy.wait()
        first, last = 2 * pairs[0], 2 * pairs[-1] + 2
        weighted = jnp.concatenate(
            [0.5 * masked(len_ref, residual_ref, face, rows) for face in range(first, last)],
            axis=0,
        )
        basis = basis_ref[first * rows : last * rows, :]
        return product(parts(jnp.transpose(basis)), parts(weighted))

    terms = term_of(0)
    own_row = position(owner_ref[...])
    wanted_row = row_ref[...].astype(f32) + 1.0
    rank_row, _ = ranks(own_row)
    slot_row = (own_row * CAP + rank_row).astype(jnp.int32)
    rank_col, wanted_col = columns(rank_row, wanted_row)
    packer = one_hot(lax.broadcasted_iota(jnp.int32, (slots, primal), 0) == slot_row)
    to_owner = one_hot(
        lax.broadcasted_iota(jnp.int32, (owners, primal), 0) == own_row.astype(jnp.int32)
    )
    at_owner = own_position() * CAP + rank_col.astype(jnp.int32)
    place = lax.broadcasted_iota(jnp.int32, (primal, id_rows(slots) * LANES), 1)
    names = select(to_owner, jnp.where(place == at_owner, wanted_col, 0.0))
    terms += term_of(1, 2)
    put_slab(slab_ref, select(packer, terms))
    tail = slab_ref.shape[1] - tiles(id_rows(slots))
    names = jnp.concatenate(
        [names, jnp.zeros((owners, (slab_ref.shape[1] - tail) * LANES - names.shape[1]), f32)], axis=1
    )
    for j in range(slab_ref.shape[1] - tail):
        slab_ref[:, tail + j, :] = names[:, j * LANES : (j + 1) * LANES]


def local_kernel(len_ref, residual_ref, matrix_ref, owner_ref, *refs):
    whole, refs = refs[:2], refs[2:]
    local_ref, part_ref, square_ref, table_ref, refs = *refs[:4], refs[4:]
    rows = residual_ref.shape[0] // 6
    live = jnp.concatenate(
        [masked(len_ref, residual_ref, face, rows) for face in range(6)], axis=0
    )
    local = product(parts(matrix_ref[...]), parts(0.5 * live))
    local_ref[...] = local
    part_ref[...] = jnp.sum(live * local, axis=0, keepdims=True)
    square_ref[...] = jnp.sum(live * live, axis=0, keepdims=True)
    refs[0][...], refs[1][...] = parts(whole[0][...])
    for i, move in enumerate(NEAR + FAR):
        at = slice(i * rows, (i + 1) * rows)
        refs[2][:, at], refs[3][:, at] = parts(whole[1][:, rows_of(served(*move), rows)])
    primal, slots = table_ref.shape
    rank_row, own_col = ranks(position(owner_ref[...]))
    (rank_col,) = columns(rank_row)
    slot_col = (own_col * CAP + rank_col).astype(jnp.int32)
    table_ref[...] = one_hot(lax.broadcasted_iota(jnp.int32, (primal, slots), 1) == slot_col)


def solve_kernel(incoming_any, inverse_any, local_part_ref, square_ref, answer_ref, *refs):
    names_ref, slab_ref, inverse_ref, sems = refs
    owners, height, _ = slab_ref.shape
    pieces = height // CAP
    slots, owned = owners * CAP, inverse_ref.shape[0]
    cut = 2 * slots // 3 // LANES * LANES
    lead = -(-cut // CAP)
    copies = [
        pltpu.make_async_copy(
            incoming_any.at[:, pl.ds(height, names_ref.shape[1])], names_ref, sems.at[0]
        ),
        pltpu.make_async_copy(
            incoming_any.at[pl.ds(0, lead), pl.ds(0, height)],
            slab_ref.at[pl.ds(0, lead)],
            sems.at[1],
        ),
        pltpu.make_async_copy(
            incoming_any.at[pl.ds(lead, owners - lead), pl.ds(0, height)],
            slab_ref.at[pl.ds(lead, owners - lead)],
            sems.at[2],
        ),
        pltpu.make_async_copy(inverse_any, inverse_ref, sems.at[3]),
    ]
    for copy in copies:
        copy.start()
    copies[0].wait()
    wanted = unfolded(jnp.sum(names_ref[...], axis=0), 0, id_rows(slots))[:, :slots]
    (wanted_col,) = columns(wanted)
    row_at = lax.broadcasted_iota(jnp.int32, (owned, slots), 0).astype(f32) + 1.0
    col_at = lax.broadcasted_iota(jnp.int32, (slots, owned), 1).astype(f32) + 1.0
    gather = one_hot(row_at == wanted)
    table = one_hot(col_at == wanted_col)
    copies[3].wait()
    inverse = parts(inverse_ref[...])
    copies[1].wait()
    head = get_slab(slab_ref, pieces, 0, lead)
    summed = select(gather[:, :cut], head[:cut])
    copies[2].wait()
    rest = jnp.concatenate([head[cut:], get_slab(slab_ref, pieces, lead, owners)], axis=0)
    summed += select(gather[:, cut:], rest)
    solved = product(inverse, parts(summed))
    put_slab(answer_ref, select(table, solved))
    total = local_part_ref[...] + 2.0 * jnp.sum(summed * solved, axis=0, keepdims=True)
    sums = folded(total) + folded(square_ref[...])
    sums += [jnp.zeros((1, LANES), f32)] * (tiles(len(sums)) - len(sums))
    answer_ref[:, pieces * CAP :, :] = jnp.broadcast_to(
        jnp.concatenate(sums, axis=0)[None], (owners, len(sums), LANES)
    )


NEAR = (("blk", "up"), ("lat", 0), ("depth", 0), ("depth", 1))
FAR = (("blk", "down"), ("lat", 1))
FIRST = NEAR + FAR
SECOND = (("blk", "up"), ("lat", 0), ("blk", "down"), ("lat", 1), ("depth", 0), ("depth", 1))


def moves(order):
    return [(axis, way) for axis, way in order if route(axis, way)]


def route(axis, way):
    devices = lax.axis_size(axis)
    if way in ("up", "down"):
        by = 1 if way == "up" else -1
        return [(i, (i + by) % devices) for i in range(devices)]
    return [pair for i in range(way, devices - 1, 2) for pair in ((i, i + 1), (i + 1, i))]


def served(axis, way):
    if way in ("up", "down"):
        return 0 if way == "up" else 1
    plus = (lax.rem(lax.axis_index(axis), 2) == way).astype(jnp.int32)
    return (2 if axis == "lat" else 4) + plus


def sent(axis, way):
    return 1 - served(axis, way) if axis == "blk" else served(axis, way)


def rows_of(face, rows):
    if isinstance(face, int):
        return pl.ds(face * rows, rows)
    return pl.ds(pl.multiple_of(face * rows, rows), rows)


def put_faces(image_ref, rows, order, face_refs):
    for ref, move in zip(face_refs, moves(order), strict=True):
        ref[...] = image_ref[rows_of(sent(*move), rows), :]


def exchange(faces, order):
    return [
        lax.ppermute(block, axis, route(axis, way))
        for block, (axis, way) in zip(faces, moves(order), strict=True)
    ]


def image_kernel(pair_depth, returned_ref, table_ref, high_ref, low_ref, local_ref, image_ref, sums_ref, *face_refs):
    rows = local_ref.shape[0] // 6
    width = local_ref.shape[1]
    folds = width // LANES
    correction = select(table_ref[...], get_slab(returned_ref, folds))
    image = local_ref[...] + product((high_ref[...], low_ref[...]), parts(correction))
    image_ref[...] = image
    put_faces(image_ref, rows, FIRST, face_refs)
    tail = jnp.sum(returned_ref[:, folds * CAP :, :], axis=0)
    if pair_depth:
        sums_ref[...] = tail
    else:
        sums_ref[...] = jnp.broadcast_to(tail[None], sums_ref.shape)


def with_got(ref, at, got, move):
    return ref[at, :] + got[move][...] if move in got else ref[at, :]


def new_direction(len_ref, beta, image_ref, prev_ref, got, move, rows):
    face = served(*move)
    at = rows_of(face, rows)
    precond = 0.5 * with_got(image_ref, at, got, move)
    return jnp.where(live_rows(len_ref, face, rows), precond + beta * prev_ref[at, :], 0.0)


def near_kernel(pair_depth, scale, keys, len_ref, sums_ref, prev_rho_ref, image_ref, prev_ref, high_ref, low_ref, *refs):
    got, refs = dict(zip(keys, refs)), refs[len(keys) :]
    if pair_depth:
        sums, refs = sums_ref[...] + refs[0][...], refs[1:]
    else:
        sums = jnp.sum(sums_ref[...], axis=0)
    rho_out, beta_out, square_out, near_ref, image_out = refs
    rows = image_ref.shape[0] // 6
    folds = image_ref.shape[1] // LANES
    rho = scale * unfolded(sums, 0, folds)
    beta = rho / prev_rho_ref[...]
    rho_out[...] = rho
    beta_out[...] = beta
    square_out[...] = unfolded(sums, folds, folds)
    for i, move in enumerate(NEAR):
        near_ref[i * rows : (i + 1) * rows, :] = new_direction(
            len_ref, beta, image_ref, prev_ref, got, move, rows
        )
    first = len(NEAR) * rows
    image_out[...] = product((high_ref[:, :first], low_ref[:, :first]), parts(near_ref[...]))


def far_kernel(keys, len_ref, beta_ref, image_ref, prev_ref, high_ref, low_ref, near_image_ref, *refs):
    got, refs = dict(zip(keys, refs)), refs[len(keys) :]
    far_ref, blk_ref, plus_ref = refs
    rows = image_ref.shape[0] // 6
    beta = beta_ref[...]
    for i, move in enumerate(FAR):
        far_ref[i * rows : (i + 1) * rows, :] = new_direction(
            len_ref, beta, image_ref, prev_ref, got, move, rows
        )
    first, height = len(NEAR) * rows, 2 * rows
    image = near_image_ref[:height, :] + product(
        (high_ref[:height, first:], low_ref[:height, first:]), parts(far_ref[...])
    )
    blk_ref[...] = image
    plus_ref[...] = image[rows:]


def rest_kernel(high_ref, low_ref, near_image_ref, far_ref, blk_ref, schur_out, *face_refs):
    rows = near_image_ref.shape[0] // 6
    first, height = len(NEAR) * rows, 2 * rows
    schur_out[:height, :] = blk_ref[...]
    schur_out[height:, :] = near_image_ref[height:, :] + product(
        (high_ref[height:, first:], low_ref[height:, first:]), parts(far_ref[...])
    )
    for ref, move in zip(face_refs, sideways(), strict=True):
        ref[...] = schur_out[rows_of(sent(*move), rows), :]


def sideways():
    return [move for move in moves(SECOND) if move != ("blk", "up")]


def store_kernel(near_ref, far_ref, direction_out, sems):
    rows = far_ref.shape[0] // len(FAR)
    copies = []
    for ref, served_moves in ((near_ref, NEAR), (far_ref, FAR)):
        for i, move in enumerate(served_moves):
            copies.append(
                pltpu.make_async_copy(
                    ref.at[pl.ds(i * rows, rows)],
                    direction_out.at[rows_of(served(*move), rows)],
                    sems.at[len(copies)],
                )
            )
    for copy in copies:
        copy.start()
    for copy in copies:
        copy.wait()


def products_kernel(len_ref, near_ref, far_ref, schur_ref, residual_ref, arrived, out_ref):
    rows = schur_ref.shape[0] // 6
    curve = cross = jnp.zeros((1, schur_ref.shape[1]), f32)
    for ref, served_moves in ((near_ref, NEAR), (far_ref, FAR)):
        for i, move in enumerate(served_moves):
            face = served(*move)
            at = rows_of(face, rows)
            image = schur_ref[at, :]
            live = jnp.where(live_rows(len_ref, face, rows), residual_ref[at, :], 0.0)
            direction = ref[i * rows : (i + 1) * rows, :]
            curve += 2.0 * jnp.sum(direction * image, axis=0, keepdims=True)
            cross += 2.0 * jnp.sum(live * image, axis=0, keepdims=True)
    for j, piece in enumerate(folded(curve) + folded(cross)):
        out_ref[j : j + 1, :] = piece


def applied_kernel(pair_depth, len_ref, stored, schur_ref, *refs):
    keys = moves(SECOND)
    got, refs = dict(zip(keys, refs)), refs[len(keys) :]
    products, (applied_ref, spread_ref) = refs[:-2], refs[-2:]
    rows = schur_ref.shape[0] // 6
    folds = schur_ref.shape[1] // LANES
    total = jnp.zeros((1, schur_ref.shape[1]), f32)
    for move in SECOND:
        face = served(*move)
        at = rows_of(face, rows)
        applied = with_got(schur_ref, at, got, move)
        applied = jnp.where(live_rows(len_ref, face, rows), applied, 0.0)
        applied_ref[at, :] = applied
        total += jnp.sum(applied * applied, axis=0, keepdims=True)
    products = sum(ref[...] for ref in products)
    halves = [products[:folds], products[folds : 2 * folds]]
    if pair_depth:
        halves = [jnp.where(lax.axis_index("depth") == 0, *halves)]
    block = jnp.concatenate([*halves, *folded(total)], axis=0)
    spread_ref[...] = jnp.broadcast_to(block[None], spread_ref.shape)


def finish_kernel(pair_depth, scale, len_ref, sums_ref, rho_ref, square_ref, residual_ref, applied_ref, new_out, alpha_ref, norm_ref, new_ref, sems):
    rows = applied_ref.shape[0] // 6
    devices, height, _ = sums_ref.shape
    if pair_depth:
        folds = height // 2
        layers = [jnp.sum(sums_ref[: devices // 2], axis=0), jnp.sum(sums_ref[devices // 2 :], axis=0)]
        curve, cross = [unfolded(layer, 0, folds) for layer in layers]
        applied_square = unfolded(layers[0] + layers[1], folds, folds)
    else:
        folds = height // 3
        total = jnp.sum(sums_ref[...], axis=0)
        curve, cross, applied_square = [unfolded(total, i * folds, folds) for i in range(3)]
    alpha = rho_ref[...] / (scale * curve)
    alpha_ref[...] = alpha
    norm_ref[...] = scale * (
        square_ref[...] - 2.0 * alpha * cross + alpha * alpha * applied_square
    )
    copies = []
    for face in range(6):
        at = slice(face * rows, (face + 1) * rows)
        new_ref[at, :] = masked(len_ref, residual_ref, face, rows) - alpha * applied_ref[at, :]
        where = pl.ds(face * rows, rows)
        copies.append(pltpu.make_async_copy(new_ref.at[where], new_out.at[where], sems.at[face]))
        copies[-1].start()
    for copy in copies:
        copy.wait()


def to_all(x, axes):
    return lax.all_to_all(x, axes, split_axis=0, concat_axis=0, tiled=True)


def shards(
    face_len,
    residual,
    prev_direction,
    prev_rho,
    schur,
    neumann,
    coarse_basis,
    coarse_inverse,
    prim_owner,
    coarse_row,
):
    height, width = residual.shape[3:]
    rows = height // 6
    primal = coarse_basis.shape[4]
    owned = coarse_inverse.shape[3]
    owners = lax.axis_size(LAYER)
    slots = owners * CAP
    devices = lax.axis_size(AXES)
    layers = lax.axis_size("depth")
    pair_depth = layers == 2
    scale = 0.5 / (devices * height)
    folds = width // LANES
    tail = tiles(2 * folds)
    id_tail = tiles(id_rows(slots))

    lengths = face_len.reshape(6)
    residual = residual.reshape(height, width)
    prev_direction = prev_direction.reshape(height, width)
    schur = schur.reshape(height, height)
    neumann = neumann.reshape(height, height)
    basis = coarse_basis.reshape(height, primal)
    inverse = coarse_inverse.reshape(owned, owned)
    owner = prim_owner.reshape(1, primal)
    wanted = coarse_row.reshape(1, primal)
    whole = shape_of(height, width)
    row = shape_of(1, width)
    face = shape_of(rows, width)

    (outgoing,) = call(
        pack_kernel,
        [shape_of(owners, folds * CAP + id_tail, LANES)],
        [lengths, owner, wanted, residual, basis],
        far=range(5),
        flops=6 * height * primal * width,
        moved=4 * (height * (width + primal) + slots * width),
        scratch=[
            pltpu.SMEM((6,), jnp.int32),
            pltpu.VMEM((1, primal), jnp.int32),
            pltpu.VMEM((1, primal), jnp.int32),
            pltpu.VMEM((height, width), f32),
            pltpu.VMEM((height, primal), f32),
            pltpu.SemaphoreType.DMA((3, 2)),
            pltpu.SemaphoreType.DMA((3,)),
        ],
    )
    incoming = to_layer(outgoing)
    local, local_part, square, table, *halves = call(
        local_kernel,
        [whole, row, row, shape_of(primal, slots, dtype=bf16)]
        + [shape_of(height, primal, dtype=bf16)] * 2
        + [shape_of(height, height, dtype=bf16)] * 2,
        [lengths, residual, neumann, owner, basis, schur],
        smem=(0,),
        flops=6 * height * height * width,
        moved=4 * height * (3 * height + 2 * width),
    )
    basis_halves, schur_halves = halves[:2], halves[2:]
    (answers,) = call(
        solve_kernel,
        [shape_of(owners, folds * CAP + tail, LANES)],
        [incoming, inverse, local_part, square],
        far=range(2),
        flops=(8 * slots + 6 * owned) * owned * width,
        moved=8 * slots * width,
        scratch=[
            pltpu.VMEM((owners, id_tail, LANES), f32),
            pltpu.VMEM((owners, folds * CAP, LANES), f32),
            pltpu.VMEM((owned, owned), f32),
            pltpu.SemaphoreType.DMA((4,)),
        ],
    )
    returned = to_layer(answers)
    keys = moves(FIRST)
    faces = [face] * len(keys)
    image, sums, *outward = call(
        functools.partial(image_kernel, pair_depth),
        [whole, shape_of(tail, LANES) if pair_depth else shape_of(layers, tail, LANES), *faces],
        [returned, table, *basis_halves, local],
        flops=(6 * height + 4 * slots) * primal * width,
        moved=16 * height * width,
    )
    got = dict(zip(keys, exchange(outward, FIRST)))
    if pair_depth:
        sums = [sums, lax.ppermute(sums, "depth", route("depth", 0))]
    else:
        sums = [to_all(sums, "depth")]
    near_keys, far_keys = moves(NEAR), moves(FAR)
    rho, beta, square, near, near_image = call(
        functools.partial(near_kernel, pair_depth, scale, near_keys),
        [row, row, row, shape_of(len(NEAR) * rows, width), whole],
        [lengths, sums[0], prev_rho.reshape(1, width), image, prev_direction, *schur_halves]
        + [got[key] for key in near_keys]
        + sums[1:],
        smem=(0,),
        flops=4 * height * height * width,
        moved=4 * height * (height + 4 * width),
    )
    far, blk_image, plus = call(
        functools.partial(far_kernel, far_keys),
        [shape_of(len(FAR) * rows, width), shape_of(2 * rows, width), face],
        [lengths, beta, image, prev_direction, *schur_halves, near_image]
        + [got[key] for key in far_keys],
        smem=(0,),
        flops=2 * height * rows * width,
        moved=8 * height * width,
    )
    schur_image, *others = call(
        rest_kernel,
        [whole] + [face] * len(sideways()),
        [*schur_halves, near_image, far, blk_image],
        flops=4 * height * rows * width,
        moved=8 * height * width,
    )
    outward = dict(zip(sideways(), others))
    outward["blk", "up"] = plus
    outward = [outward[move] for move in moves(SECOND)]
    got = exchange(outward, SECOND)
    (products,) = call(
        products_kernel,
        [shape_of(2 * folds, LANES)],
        [lengths, near, far, schur_image, residual, got[0]],
        smem=(0,),
        loose=(5,),
        flops=4 * height * width,
        moved=12 * height * width,
    )
    products = [products]
    if pair_depth:
        products.append(lax.ppermute(products[0], "depth", route("depth", 0)))
    (direction,) = call(
        store_kernel,
        [whole],
        [near, far],
        far_out=(0,),
        moved=8 * height * width,
        scratch=[pltpu.SemaphoreType.DMA((6,))],
    )
    applied, spread_sums = call(
        functools.partial(applied_kernel, pair_depth),
        [whole, shape_of(devices, (2 if pair_depth else 3) * folds, LANES)],
        [lengths, direction, schur_image, *got, *products],
        smem=(0,),
        far=(1,),
        flops=4 * height * width,
        moved=12 * height * width,
    )
    new_residual, alpha, norm = call(
        functools.partial(finish_kernel, pair_depth, scale),
        [whole, row, row],
        [lengths, to_all(spread_sums, AXES), rho, square, residual, applied],
        smem=(0,),
        far_out=(0,),
        flops=4 * height * width,
        moved=12 * height * width,
        scratch=[pltpu.VMEM((height, width), f32), pltpu.SemaphoreType.DMA((6,))],
    )
    out_shape = (1, 1, 1, height, width)
    return (
        new_residual.reshape(out_shape),
        direction.reshape(out_shape),
        rho.reshape(width),
        alpha.reshape(width),
        norm.reshape(width),
    )


def solution(mesh):
    tall = P("blk", "lat", "depth", None, None)
    flat = P("blk", "lat", "depth", None)
    in_specs = (flat, tall, tall, P(), tall, tall, tall, tall, tall, flat)
    out_specs = (tall, tall, P(), P(), P())
    return jax.shard_map(shards, mesh=mesh, in_specs=in_specs, out_specs=out_specs, check_vma=False)
```

```python
import functools

import jax
import jax.numpy as jnp
from jax import lax
from jax.experimental import pallas as pl
from jax.experimental.pallas import tpu as pltpu
from jax.sharding import PartitionSpec as P

CAP = 24
AXES = ("depth", "blk", "lat")
LAYER = ("blk", "lat")
LANES = 128
TILE = 8
f32 = jnp.float32
bf16 = jnp.bfloat16

VMEM = pl.BlockSpec(memory_space=pltpu.VMEM)
SMEM = pl.BlockSpec(memory_space=pltpu.SMEM)
ANY = pl.BlockSpec(memory_space=pl.ANY)


def shape_of(*dims, dtype=f32):
    return jax.ShapeDtypeStruct(dims, dtype)


def call(body, outs, operands, smem=(), far=(), loose=(), far_out=(), flops=0, moved=0, scratch=(), room=32):
    in_specs = [
        SMEM if i in smem else ANY if i in far or i in loose else VMEM
        for i in range(len(operands))
    ]
    operands = [
        pltpu.with_memory_space_constraint(x, pltpu.HBM) if i in far else x
        for i, x in enumerate(operands)
    ]
    out_specs = [ANY if i in far_out else VMEM for i in range(len(outs))]
    return pl.pallas_call(
        body,
        out_shape=list(outs),
        in_specs=in_specs,
        out_specs=out_specs,
        scratch_shapes=list(scratch),
        compiler_params=pltpu.CompilerParams(vmem_limit_bytes=room << 20),
        cost_estimate=pl.CostEstimate(flops=flops, bytes_accessed=moved, transcendentals=0),
    )(*operands)


def parts(x):
    high = x.astype(bf16)
    low = (x - high.astype(f32)).astype(bf16)
    return high, low


def mul(a, b, dims):
    return lax.dot_general(a, b, (dims, ((), ())), preferred_element_type=f32)


PLAIN = ((1,), (0,))


def product(a, b, dims=PLAIN):
    (ah, al), (bh, bl) = a, b
    return mul(ah, bh, dims) + (mul(ah, bl, dims) + mul(al, bh, dims))


def select(table, x, dims=PLAIN):
    high, low = parts(x)
    return mul(table, high, dims) + mul(table, low, dims)


def one_hot(hit):
    return jnp.where(hit, 1.0, 0.0).astype(bf16)


def live_rows(len_ref, face, rows):
    return lax.broadcasted_iota(jnp.int32, (rows, 1), 0) < len_ref[face]


def masked(len_ref, ref, face, rows):
    block = ref[face * rows : (face + 1) * rows, :]
    return jnp.where(live_rows(len_ref, face, rows), block, 0.0)


def folded(vector):
    pieces = vector.shape[1] // LANES
    return [vector[:, j * LANES : (j + 1) * LANES] for j in range(pieces)]


def unfolded(block, first, pieces):
    return jnp.concatenate([block[first + j : first + j + 1, :] for j in range(pieces)], axis=1)


def id_rows(slots):
    return -(-slots // LANES)


def tiles(rows):
    return -(-rows // TILE) * TILE


def put_slab(out_ref, block):
    owners = out_ref.shape[0]
    for j in range(block.shape[1] // LANES):
        piece = block[:, j * LANES : (j + 1) * LANES]
        out_ref[:, j * CAP : (j + 1) * CAP, :] = piece.reshape(owners, CAP, LANES)


def get_slab(ref, pieces, first=0, last=None):
    last = ref.shape[0] if last is None else last
    columns_of = [ref[first:last, j * CAP : (j + 1) * CAP, :] for j in range(pieces)]
    return jnp.concatenate([x.reshape((last - first) * CAP, LANES) for x in columns_of], axis=1)


def columns(*rows):
    spare = [jnp.zeros_like(rows[0])] * (TILE - len(rows))
    turned = jnp.transpose(jnp.concatenate([*rows, *spare], axis=0))
    return [turned[:, i : i + 1] for i in range(len(rows))]


def turn(lat):
    return lat ^ (lat >> 1)


def position(owner):
    lats = lax.axis_size("lat")
    owner = owner.astype(f32)
    lat = owner - lats * jnp.floor((owner + 0.5) * (1.0 / lats))
    for one in range(lats):
        owner = owner + jnp.where(lat == one, float(turn(one) - one), 0.0)
    return owner


def own_position():
    lat = lax.axis_index("lat")
    return lax.axis_index("blk") * lax.axis_size("lat") + turn(lat)


def to_layer(x):
    lats = lax.axis_size("lat")
    order = [
        blk * lats + lat
        for blk in range(lax.axis_size("blk"))
        for lat in sorted(range(lats), key=turn)
    ]
    return lax.all_to_all(x, LAYER, 0, 0, axis_index_groups=[order], tiled=True)


def ranks(own_row):
    primal = own_row.shape[1]
    (own_col,) = columns(own_row)
    row_at = lax.broadcasted_iota(jnp.int32, (primal, primal), 0)
    col_at = lax.broadcasted_iota(jnp.int32, (primal, primal), 1)
    before = (own_row == own_col) & (row_at < col_at)
    return jnp.sum(jnp.where(before, 1.0, 0.0), axis=0, keepdims=True), own_col


def pack_kernel(len_any, owner_any, row_any, residual_any, basis_any, slab_ref, *refs):
    len_ref, owner_ref, row_ref, residual_ref, basis_ref, sems, small_sems = refs
    rows = residual_ref.shape[0] // 6
    primal = basis_ref.shape[1]
    owners = slab_ref.shape[0]
    slots = owners * CAP
    small = [
        pltpu.make_async_copy(src, dst, small_sems.at[i])
        for i, (src, dst) in enumerate(
            [(owner_any, owner_ref), (row_any, row_ref), (len_any, len_ref)]
        )
    ]
    large = []
    for pair in range(3):
        at = pl.ds(2 * pair * rows, 2 * rows)
        large.append(
            (
                pltpu.make_async_copy(residual_any.at[at], residual_ref.at[at], sems.at[pair, 0]),
                pltpu.make_async_copy(basis_any.at[at], basis_ref.at[at], sems.at[pair, 1]),
            )
        )
    for copy in small:
        copy.start()
    for pair in large:
        for copy in pair:
            copy.start()
    for copy in small:
        copy.wait()

    def term_of(*pairs):
        for pair in pairs:
            for copy in large[pair]:
                copy.wait()
        first, last = 2 * pairs[0], 2 * pairs[-1] + 2
        weighted = jnp.concatenate(
            [0.5 * masked(len_ref, residual_ref, face, rows) for face in range(first, last)],
            axis=0,
        )
        basis = basis_ref[first * rows : last * rows, :]
        return product(parts(jnp.transpose(basis)), parts(weighted))

    terms = term_of(0)
    own_row = position(owner_ref[...])
    wanted_row = row_ref[...].astype(f32) + 1.0
    rank_row, _ = ranks(own_row)
    slot_row = (own_row * CAP + rank_row).astype(jnp.int32)
    rank_col, wanted_col = columns(rank_row, wanted_row)
    packer = one_hot(lax.broadcasted_iota(jnp.int32, (slots, primal), 0) == slot_row)
    to_owner = one_hot(
        lax.broadcasted_iota(jnp.int32, (owners, primal), 0) == own_row.astype(jnp.int32)
    )
    at_owner = own_position() * CAP + rank_col.astype(jnp.int32)
    place = lax.broadcasted_iota(jnp.int32, (primal, id_rows(slots) * LANES), 1)
    names = select(to_owner, jnp.where(place == at_owner, wanted_col, 0.0))
    terms += term_of(1, 2)
    put_slab(slab_ref, select(packer, terms))
    tail = slab_ref.shape[1] - tiles(id_rows(slots))
    names = jnp.concatenate(
        [names, jnp.zeros((owners, (slab_ref.shape[1] - tail) * LANES - names.shape[1]), f32)], axis=1
    )
    for j in range(slab_ref.shape[1] - tail):
        slab_ref[:, tail + j, :] = names[:, j * LANES : (j + 1) * LANES]


def local_kernel(len_ref, residual_ref, matrix_ref, owner_ref, *refs):
    whole, refs = refs[:2], refs[2:]
    local_ref, part_ref, square_ref, table_ref, refs = *refs[:4], refs[4:]
    rows = residual_ref.shape[0] // 6
    live = jnp.concatenate(
        [masked(len_ref, residual_ref, face, rows) for face in range(6)], axis=0
    )
    local = product(parts(matrix_ref[...]), parts(0.5 * live))
    local_ref[...] = local
    part_ref[...] = jnp.sum(live * local, axis=0, keepdims=True)
    square_ref[...] = jnp.sum(live * live, axis=0, keepdims=True)
    refs[0][...], refs[1][...] = parts(whole[0][...])
    for i, move in enumerate(NEAR + FAR):
        at = slice(i * rows, (i + 1) * rows)
        refs[2][:, at], refs[3][:, at] = parts(whole[1][:, rows_of(served(*move), rows)])
    primal, slots = table_ref.shape
    rank_row, own_col = ranks(position(owner_ref[...]))
    (rank_col,) = columns(rank_row)
    slot_col = (own_col * CAP + rank_col).astype(jnp.int32)
    table_ref[...] = one_hot(lax.broadcasted_iota(jnp.int32, (primal, slots), 1) == slot_col)


def solve_kernel(incoming_any, inverse_any, local_part_ref, square_ref, answer_ref, *refs):
    names_ref, slab_ref, inverse_ref, sems = refs
    owners, height, _ = slab_ref.shape
    pieces = height // CAP
    slots, owned = owners * CAP, inverse_ref.shape[0]
    cut = 2 * slots // 3 // LANES * LANES
    lead = -(-cut // CAP)
    copies = [
        pltpu.make_async_copy(
            incoming_any.at[:, pl.ds(height, names_ref.shape[1])], names_ref, sems.at[0]
        ),
        pltpu.make_async_copy(
            incoming_any.at[pl.ds(0, lead), pl.ds(0, height)],
            slab_ref.at[pl.ds(0, lead)],
            sems.at[1],
        ),
        pltpu.make_async_copy(
            incoming_any.at[pl.ds(lead, owners - lead), pl.ds(0, height)],
            slab_ref.at[pl.ds(lead, owners - lead)],
            sems.at[2],
        ),
        pltpu.make_async_copy(inverse_any, inverse_ref, sems.at[3]),
    ]
    for copy in copies:
        copy.start()
    copies[0].wait()
    wanted = unfolded(jnp.sum(names_ref[...], axis=0), 0, id_rows(slots))[:, :slots]
    (wanted_col,) = columns(wanted)
    row_at = lax.broadcasted_iota(jnp.int32, (owned, slots), 0).astype(f32) + 1.0
    col_at = lax.broadcasted_iota(jnp.int32, (slots, owned), 1).astype(f32) + 1.0
    gather = one_hot(row_at == wanted)
    table = one_hot(col_at == wanted_col)
    copies[3].wait()
    inverse = parts(inverse_ref[...])
    copies[1].wait()
    head = get_slab(slab_ref, pieces, 0, lead)
    summed = select(gather[:, :cut], head[:cut])
    copies[2].wait()
    rest = jnp.concatenate([head[cut:], get_slab(slab_ref, pieces, lead, owners)], axis=0)
    summed += select(gather[:, cut:], rest)
    solved = product(inverse, parts(summed))
    put_slab(answer_ref, select(table, solved))
    total = local_part_ref[...] + 2.0 * jnp.sum(summed * solved, axis=0, keepdims=True)
    sums = folded(total) + folded(square_ref[...])
    sums += [jnp.zeros((1, LANES), f32)] * (tiles(len(sums)) - len(sums))
    answer_ref[:, pieces * CAP :, :] = jnp.broadcast_to(
        jnp.concatenate(sums, axis=0)[None], (owners, len(sums), LANES)
    )


NEAR = (("blk", "up"), ("lat", 0), ("depth", 0), ("depth", 1))
FAR = (("blk", "down"), ("lat", 1))
FIRST = NEAR + FAR
SECOND = (("blk", "up"), ("lat", 0), ("blk", "down"), ("lat", 1), ("depth", 0), ("depth", 1))


def moves(order):
    return [(axis, way) for axis, way in order if route(axis, way)]


def route(axis, way):
    devices = lax.axis_size(axis)
    if way in ("up", "down"):
        by = 1 if way == "up" else -1
        return [(i, (i + by) % devices) for i in range(devices)]
    return [pair for i in range(way, devices - 1, 2) for pair in ((i, i + 1), (i + 1, i))]


def served(axis, way):
    if way in ("up", "down"):
        return 0 if way == "up" else 1
    plus = (lax.rem(lax.axis_index(axis), 2) == way).astype(jnp.int32)
    return (2 if axis == "lat" else 4) + plus


def sent(axis, way):
    return 1 - served(axis, way) if axis == "blk" else served(axis, way)


def rows_of(face, rows):
    if isinstance(face, int):
        return pl.ds(face * rows, rows)
    return pl.ds(pl.multiple_of(face * rows, rows), rows)


def put_faces(image_ref, rows, order, face_refs):
    for ref, move in zip(face_refs, moves(order), strict=True):
        ref[...] = image_ref[rows_of(sent(*move), rows), :]


def exchange(faces, order):
    return [
        lax.ppermute(block, axis, route(axis, way))
        for block, (axis, way) in zip(faces, moves(order), strict=True)
    ]


def image_kernel(pair_depth, returned_ref, table_ref, high_ref, low_ref, local_ref, image_ref, sums_ref, *face_refs):
    rows = local_ref.shape[0] // 6
    width = local_ref.shape[1]
    folds = width // LANES
    correction = select(table_ref[...], get_slab(returned_ref, folds))
    image = local_ref[...] + product((high_ref[...], low_ref[...]), parts(correction))
    image_ref[...] = image
    put_faces(image_ref, rows, FIRST, face_refs)
    tail = jnp.sum(returned_ref[:, folds * CAP :, :], axis=0)
    if pair_depth:
        sums_ref[...] = tail
    else:
        sums_ref[...] = jnp.broadcast_to(tail[None], sums_ref.shape)


def with_got(ref, at, got, move):
    return ref[at, :] + got[move][...] if move in got else ref[at, :]


def new_direction(len_ref, beta, image_ref, prev_ref, got, move, rows):
    face = served(*move)
    at = rows_of(face, rows)
    precond = 0.5 * with_got(image_ref, at, got, move)
    return jnp.where(live_rows(len_ref, face, rows), precond + beta * prev_ref[at, :], 0.0)


def near_kernel(pair_depth, scale, keys, len_ref, sums_ref, prev_rho_ref, image_ref, prev_ref, high_ref, low_ref, *refs):
    got, refs = dict(zip(keys, refs)), refs[len(keys) :]
    if pair_depth:
        sums, refs = sums_ref[...] + refs[0][...], refs[1:]
    else:
        sums = jnp.sum(sums_ref[...], axis=0)
    rho_out, beta_out, square_out, near_ref, image_out = refs
    rows = image_ref.shape[0] // 6
    folds = image_ref.shape[1] // LANES
    rho = scale * unfolded(sums, 0, folds)
    beta = rho / prev_rho_ref[...]
    rho_out[...] = rho
    beta_out[...] = beta
    square_out[...] = unfolded(sums, folds, folds)
    for i, move in enumerate(NEAR):
        near_ref[i * rows : (i + 1) * rows, :] = new_direction(
            len_ref, beta, image_ref, prev_ref, got, move, rows
        )
    first = len(NEAR) * rows
    image_out[...] = product((high_ref[:, :first], low_ref[:, :first]), parts(near_ref[...]))


def far_kernel(keys, len_ref, beta_ref, image_ref, prev_ref, high_ref, low_ref, near_image_ref, *refs):
    got, refs = dict(zip(keys, refs)), refs[len(keys) :]
    far_ref, blk_ref, plus_ref = refs
    rows = image_ref.shape[0] // 6
    beta = beta_ref[...]
    for i, move in enumerate(FAR):
        far_ref[i * rows : (i + 1) * rows, :] = new_direction(
            len_ref, beta, image_ref, prev_ref, got, move, rows
        )
    first, height = len(NEAR) * rows, 2 * rows
    image = near_image_ref[:height, :] + product(
        (high_ref[:height, first:], low_ref[:height, first:]), parts(far_ref[...])
    )
    blk_ref[...] = image
    plus_ref[...] = image[rows:]


def rest_kernel(high_ref, low_ref, near_image_ref, far_ref, blk_ref, schur_out, *face_refs):
    rows = near_image_ref.shape[0] // 6
    first, height = len(NEAR) * rows, 2 * rows
    schur_out[:height, :] = blk_ref[...]
    schur_out[height:, :] = near_image_ref[height:, :] + product(
        (high_ref[height:, first:], low_ref[height:, first:]), parts(far_ref[...])
    )
    for ref, move in zip(face_refs, sideways(), strict=True):
        ref[...] = schur_out[rows_of(sent(*move), rows), :]


def sideways():
    return [move for move in moves(SECOND) if move != ("blk", "up")]


def store_kernel(near_ref, far_ref, direction_out, sems):
    rows = far_ref.shape[0] // len(FAR)
    copies = []
    for ref, served_moves in ((near_ref, NEAR), (far_ref, FAR)):
        for i, move in enumerate(served_moves):
            copies.append(
                pltpu.make_async_copy(
                    ref.at[pl.ds(i * rows, rows)],
                    direction_out.at[rows_of(served(*move), rows)],
                    sems.at[len(copies)],
                )
            )
    for copy in copies:
        copy.start()
    for copy in copies:
        copy.wait()


def products_kernel(len_ref, near_ref, far_ref, schur_ref, residual_ref, arrived, stored, out_ref):
    rows = schur_ref.shape[0] // 6
    curve = cross = jnp.zeros((1, schur_ref.shape[1]), f32)
    for ref, served_moves in ((near_ref, NEAR), (far_ref, FAR)):
        for i, move in enumerate(served_moves):
            face = served(*move)
            at = rows_of(face, rows)
            image = schur_ref[at, :]
            live = jnp.where(live_rows(len_ref, face, rows), residual_ref[at, :], 0.0)
            direction = ref[i * rows : (i + 1) * rows, :]
            curve += 2.0 * jnp.sum(direction * image, axis=0, keepdims=True)
            cross += 2.0 * jnp.sum(live * image, axis=0, keepdims=True)
    for j, piece in enumerate(folded(curve) + folded(cross)):
        out_ref[j : j + 1, :] = piece


def applied_kernel(pair_depth, len_ref, schur_ref, *refs):
    keys = moves(SECOND)
    got, refs = dict(zip(keys, refs)), refs[len(keys) :]
    products, (applied_ref, spread_ref) = refs[:-2], refs[-2:]
    rows = schur_ref.shape[0] // 6
    folds = schur_ref.shape[1] // LANES
    total = jnp.zeros((1, schur_ref.shape[1]), f32)
    for move in SECOND:
        face = served(*move)
        at = rows_of(face, rows)
        applied = with_got(schur_ref, at, got, move)
        applied = jnp.where(live_rows(len_ref, face, rows), applied, 0.0)
        applied_ref[at, :] = applied
        total += jnp.sum(applied * applied, axis=0, keepdims=True)
    products = sum(ref[...] for ref in products)
    halves = [products[:folds], products[folds : 2 * folds]]
    if pair_depth:
        halves = [jnp.where(lax.axis_index("depth") == 0, *halves)]
    block = jnp.concatenate([*halves, *folded(total)], axis=0)
    spread_ref[...] = jnp.broadcast_to(block[None], spread_ref.shape)


def finish_kernel(pair_depth, scale, len_ref, sums_ref, rho_ref, square_ref, residual_ref, applied_ref, new_out, alpha_ref, norm_ref, new_ref, sems):
    rows = applied_ref.shape[0] // 6
    devices, height, _ = sums_ref.shape
    if pair_depth:
        folds = height // 2
        layers = [jnp.sum(sums_ref[: devices // 2], axis=0), jnp.sum(sums_ref[devices // 2 :], axis=0)]
        curve, cross = [unfolded(layer, 0, folds) for layer in layers]
        applied_square = unfolded(layers[0] + layers[1], folds, folds)
    else:
        folds = height // 3
        total = jnp.sum(sums_ref[...], axis=0)
        curve, cross, applied_square = [unfolded(total, i * folds, folds) for i in range(3)]
    alpha = rho_ref[...] / (scale * curve)
    alpha_ref[...] = alpha
    norm_ref[...] = scale * (
        square_ref[...] - 2.0 * alpha * cross + alpha * alpha * applied_square
    )
    copies = []
    for face in range(6):
        at = slice(face * rows, (face + 1) * rows)
        new_ref[at, :] = masked(len_ref, residual_ref, face, rows) - alpha * applied_ref[at, :]
        where = pl.ds(face * rows, rows)
        copies.append(pltpu.make_async_copy(new_ref.at[where], new_out.at[where], sems.at[face]))
        copies[-1].start()
    for copy in copies:
        copy.wait()


def to_all(x, axes):
    return lax.all_to_all(x, axes, split_axis=0, concat_axis=0, tiled=True)


def shards(
    face_len,
    residual,
    prev_direction,
    prev_rho,
    schur,
    neumann,
    coarse_basis,
    coarse_inverse,
    prim_owner,
    coarse_row,
):
    height, width = residual.shape[3:]
    rows = height // 6
    primal = coarse_basis.shape[4]
    owned = coarse_inverse.shape[3]
    owners = lax.axis_size(LAYER)
    slots = owners * CAP
    devices = lax.axis_size(AXES)
    layers = lax.axis_size("depth")
    pair_depth = layers == 2
    scale = 0.5 / (devices * height)
    folds = width // LANES
    tail = tiles(2 * folds)
    id_tail = tiles(id_rows(slots))

    lengths = face_len.reshape(6)
    residual = residual.reshape(height, width)
    prev_direction = prev_direction.reshape(height, width)
    schur = schur.reshape(height, height)
    neumann = neumann.reshape(height, height)
    basis = coarse_basis.reshape(height, primal)
    inverse = coarse_inverse.reshape(owned, owned)
    owner = prim_owner.reshape(1, primal)
    wanted = coarse_row.reshape(1, primal)
    whole = shape_of(height, width)
    row = shape_of(1, width)
    face = shape_of(rows, width)

    (outgoing,) = call(
        pack_kernel,
        [shape_of(owners, folds * CAP + id_tail, LANES)],
        [lengths, owner, wanted, residual, basis],
        far=range(5),
        flops=6 * height * primal * width,
        moved=4 * (height * (width + primal) + slots * width),
        scratch=[
            pltpu.SMEM((6,), jnp.int32),
            pltpu.VMEM((1, primal), jnp.int32),
            pltpu.VMEM((1, primal), jnp.int32),
            pltpu.VMEM((height, width), f32),
            pltpu.VMEM((height, primal), f32),
            pltpu.SemaphoreType.DMA((3, 2)),
            pltpu.SemaphoreType.DMA((3,)),
        ],
    )
    incoming = to_layer(outgoing)
    local, local_part, square, table, *halves = call(
        local_kernel,
        [whole, row, row, shape_of(primal, slots, dtype=bf16)]
        + [shape_of(height, primal, dtype=bf16)] * 2
        + [shape_of(height, height, dtype=bf16)] * 2,
        [lengths, residual, neumann, owner, basis, schur],
        smem=(0,),
        flops=6 * height * height * width,
        moved=4 * height * (3 * height + 2 * width),
    )
    basis_halves, schur_halves = halves[:2], halves[2:]
    (answers,) = call(
        solve_kernel,
        [shape_of(owners, folds * CAP + tail, LANES)],
        [incoming, inverse, local_part, square],
        far=range(2),
        flops=(8 * slots + 6 * owned) * owned * width,
        moved=8 * slots * width,
        scratch=[
            pltpu.VMEM((owners, id_tail, LANES), f32),
            pltpu.VMEM((owners, folds * CAP, LANES), f32),
            pltpu.VMEM((owned, owned), f32),
            pltpu.SemaphoreType.DMA((4,)),
        ],
    )
    returned = to_layer(answers)
    keys = moves(FIRST)
    faces = [face] * len(keys)
    image, sums, *outward = call(
        functools.partial(image_kernel, pair_depth),
        [whole, shape_of(tail, LANES) if pair_depth else shape_of(layers, tail, LANES), *faces],
        [returned, table, *basis_halves, local],
        flops=(6 * height + 4 * slots) * primal * width,
        moved=16 * height * width,
    )
    got = dict(zip(keys, exchange(outward, FIRST)))
    if pair_depth:
        sums = [sums, lax.ppermute(sums, "depth", route("depth", 0))]
    else:
        sums = [to_all(sums, "depth")]
    near_keys, far_keys = moves(NEAR), moves(FAR)
    rho, beta, square, near, near_image = call(
        functools.partial(near_kernel, pair_depth, scale, near_keys),
        [row, row, row, shape_of(len(NEAR) * rows, width), whole],
        [lengths, sums[0], prev_rho.reshape(1, width), image, prev_direction, *schur_halves]
        + [got[key] for key in near_keys]
        + sums[1:],
        smem=(0,),
        flops=4 * height * height * width,
        moved=4 * height * (height + 4 * width),
    )
    far, blk_image, plus = call(
        functools.partial(far_kernel, far_keys),
        [shape_of(len(FAR) * rows, width), shape_of(2 * rows, width), face],
        [lengths, beta, image, prev_direction, *schur_halves, near_image]
        + [got[key] for key in far_keys],
        smem=(0,),
        flops=2 * height * rows * width,
        moved=8 * height * width,
    )
    schur_image, *others = call(
        rest_kernel,
        [whole] + [face] * len(sideways()),
        [*schur_halves, near_image, far, blk_image],
        flops=4 * height * rows * width,
        moved=8 * height * width,
    )
    outward = dict(zip(sideways(), others))
    outward["blk", "up"] = plus
    outward = [outward[move] for move in moves(SECOND)]
    got = exchange(outward, SECOND)
    (direction,) = call(
        store_kernel,
        [whole],
        [near, far],
        far_out=(0,),
        moved=8 * height * width,
        scratch=[pltpu.SemaphoreType.DMA((6,))],
    )
    (products,) = call(
        products_kernel,
        [shape_of(2 * folds, LANES)],
        [lengths, near, far, schur_image, residual, got[0], direction],
        smem=(0,),
        loose=(5,),
        far=(6,),
        flops=4 * height * width,
        moved=12 * height * width,
    )
    products = [products]
    if pair_depth:
        products.append(lax.ppermute(products[0], "depth", route("depth", 0)))
    applied, spread_sums = call(
        functools.partial(applied_kernel, pair_depth),
        [whole, shape_of(devices, (2 if pair_depth else 3) * folds, LANES)],
        [lengths, schur_image, *got, *products],
        smem=(0,),
        flops=4 * height * width,
        moved=12 * height * width,
    )
    new_residual, alpha, norm = call(
        functools.partial(finish_kernel, pair_depth, scale),
        [whole, row, row],
        [lengths, to_all(spread_sums, AXES), rho, square, residual, applied],
        smem=(0,),
        far_out=(0,),
        flops=4 * height * width,
        moved=12 * height * width,
        scratch=[pltpu.VMEM((height, width), f32), pltpu.SemaphoreType.DMA((6,))],
    )
    out_shape = (1, 1, 1, height, width)
    return (
        new_residual.reshape(out_shape),
        direction.reshape(out_shape),
        rho.reshape(width),
        alpha.reshape(width),
        norm.reshape(width),
    )


def solution(mesh):
    tall = P("blk", "lat", "depth", None, None)
    flat = P("blk", "lat", "depth", None)
    in_specs = (flat, tall, tall, P(), tall, tall, tall, tall, tall, flat)
    out_specs = (tall, tall, P(), P(), P())
    return jax.shard_map(shards, mesh=mesh, in_specs=in_specs, out_specs=out_specs, check_vma=False)
```
